32 devices in a mesh: rep: 2 (over x), pg: 16 (over z, y, core).
Axes of the slice: x: 2, y: 2, z: 4, core: 2. Of those that a mesh axis runs over, the one named last changes fastest.
Arguments:
- queries: bfloat16 [32, 128, 4096], P(('rep', 'pg')), parts along dimension 0, may hold values from -6 to 6
- block_kv: bfloat16 [32, 128, 1024], P(('rep', 'pg')), parts along dimension 0, may hold values from -6 to 6
- pool_kv: bfloat16 [32, 16, 32, 1024], P(('rep', 'pg')), parts along dimension 0, may hold values from -6 to 6
- prefix_len: int32 [32], P('rep'), parts along dimension 0, may hold values from 0 to 512, as said below
- assignment: int32 [32], P('rep'), parts along dimension 0, may hold values from 0 to 15, each once
- stripe_map: int32 [32, 16], P('rep'), parts along dimension 0, may hold values from 0 to 15, each once within a row
- owner_map: int32 [32, 16], P('rep'), parts along dimension 0, may hold values from 0 to 15, each once within a row
Outputs:
- attended: bfloat16 [32, 128, 4096], P(('rep', 'pg')), parts along dimension 0
- decode_kv: bfloat16 [32, 16, 8, 1024], P(('rep', 'pg')), parts along dimension 0
The draws below stay inside these ranges and needn't reach their ends.
There are 2 independent parts, one for each index of `rep`. The reference program is written for one: setup_inputs(seed, part) draws one part's arguments, and reference() takes and returns one part's arrays. A program takes and returns all parts, laid end to end along the dimension named above; each array names one. Nothing has to cross between parts.
Inputs may be any that keep to these rules, and one draw needn't show every extreme that they name: `prefix_len`: some request has exactly 512. `assignment`: each group computes a different request. `stripe_map`: each row names every device once. `owner_map`: each row names every device once.
All inputs are finite; a program needn't handle non-finite values.
Results may differ from the reference program's by a relative error of at most 0.0079.
Values may be sent and summed in bfloat16 or wider, within the bound.
No kernel may reach another device: no remote copies, remote signals or barrier semaphores. Data moves between devices by JAX's collectives and lax.ppermute only.
A program may use at most 64 MiB of HBM per device.

```python
import jax
import jax.numpy as jnp
from jax import lax

Q_HEADS = 32
KV_HEADS = 4
HEAD_DIM = 128
NEW_TOK = 128
PREFIX_MAX = 512
GROUPS = 16
PREFIX_SLOTS = 32


def draw_queries(key, part):
    key = jax.random.fold_in(key, 7)
    shape = (GROUPS, NEW_TOK, Q_HEADS * HEAD_DIM)
    values = jnp.clip(1.5 * jax.random.normal(key, shape, jnp.float32), -6.0, 6.0)
    return values.astype(jnp.bfloat16)


def draw_block_kv(key, part):
    key = jax.random.fold_in(key, 13)
    kv_width = KV_HEADS * HEAD_DIM
    shape = (GROUPS, NEW_TOK, 2 * kv_width)
    values = jnp.clip(1.5 * jax.random.normal(key, shape, jnp.float32), -6.0, 6.0)
    return values.astype(jnp.bfloat16)


def draw_prefix_len(key, part):
    key = jax.random.fold_in(key, 29)
    key_counts, key_longest = jax.random.split(key)
    lengths = jax.random.randint(key_counts, (GROUPS,), 0, PREFIX_MAX + 1)
    longest = jax.random.randint(key_longest, (), 0, GROUPS)
    lengths = jnp.where(jnp.arange(GROUPS) == longest, PREFIX_MAX, lengths)
    return lengths.astype(jnp.int32)


def levels(key, dims, shards, low, largest):
    gain, own = 1.0, jax.random.fold_in(key, 6)
    for axis_at, parts in shards:
        draws = jnp.exp(jax.random.uniform(jax.random.fold_in(own, axis_at), (parts,), jnp.float32, low / len(shards), largest / len(shards)))
        gain = gain * jnp.repeat(draws, dims[axis_at] // parts).reshape([-1 if axis == axis_at else 1 for axis in range(len(dims))])
    return gain


def noise(rng, extent, deviation, most, shards=(), kind=jnp.bfloat16):
    drawn = jax.random.normal(rng, extent, jnp.float32) * deviation
    if len(shards) > 0:
        drawn = levels(rng, extent, shards, -0.22, 0.18) * drawn
    return jnp.clip(drawn, min=-most, max=most).astype(kind)


def setup_inputs(seed: int = 0, part: int = 0) -> dict:
    arg_keys = jax.random.split(jax.random.key(seed), 8)
    part_splits = jax.random.split(jax.random.fold_in(arg_keys[7], part), 8)
    return {
        "queries": draw_queries(jax.random.fold_in(jax.random.fold_in(arg_keys[7], part), 71), part),
        "block_kv": draw_block_kv(jax.random.fold_in(jax.random.fold_in(arg_keys[7], part), 71), part),
        "pool_kv": noise(part_splits[2], (GROUPS, GROUPS, PREFIX_SLOTS, 2 * KV_HEADS * HEAD_DIM), 1.2, 6.0, ((0, 16),)),
        "prefix_len": draw_prefix_len(jax.random.fold_in(jax.random.fold_in(arg_keys[7], part), 71), part),
        "assignment": jax.random.permutation(part_splits[4], GROUPS).astype(jnp.int32),
        "stripe_map": jax.vmap(lambda own: jax.random.permutation(own, GROUPS))(jax.random.split(part_splits[5], GROUPS)).reshape((GROUPS, GROUPS)).astype(jnp.int32),
        "owner_map": jax.vmap(lambda own: jax.random.permutation(own, GROUPS))(jax.random.split(part_splits[6], GROUPS)).reshape((GROUPS, GROUPS)).astype(jnp.int32),
    }


ROPE_BASE = 1000000.0
MASKED = -1e+30

def invert(table):
    count = table.shape[-1]
    places = jnp.arange(count, dtype=jnp.int32)
    hits = table[..., None, :] == places[:, None]
    return lax.optimization_barrier(jnp.sum(jnp.where(hits, places, 0), axis=-1)).astype(jnp.int32)

def rotate(rows, positions, heads):
    head_width = rows.shape[-1] // heads
    half_width = head_width // 2
    freqs = ROPE_BASE ** (-jnp.arange(half_width, dtype=jnp.float32) / half_width)
    angles = positions.astype(jnp.float32)[:, None] * freqs[None, :]
    cosine = jnp.concatenate([jnp.cos(angles), jnp.cos(angles)], axis=-1)[:, None, :]
    sine = jnp.concatenate([jnp.sin(angles), jnp.sin(angles)], axis=-1)[:, None, :]
    split_rows = rows.astype(jnp.float32).reshape(rows.shape[0], heads, head_width)
    turned = jnp.concatenate([-split_rows[..., half_width:], split_rows[..., :half_width]], axis=-1)
    return (split_rows * cosine + turned * sine).reshape(rows.shape).astype(jnp.bfloat16)

def group_attention(q_rot, new_kv, prefix_kv, prefix_live):
    kv_width = KV_HEADS * HEAD_DIM
    per_group = Q_HEADS // KV_HEADS
    offsets = jnp.arange(NEW_TOK, dtype=jnp.int32)
    causal = offsets[None, :] <= offsets[:, None]
    live = jnp.concatenate([jnp.broadcast_to(prefix_live[None, :], (NEW_TOK, prefix_live.shape[0])), causal], axis=1)
    all_keys = jnp.concatenate([prefix_kv, new_kv], axis=0)
    query_stack = jnp.transpose(q_rot.reshape(NEW_TOK, KV_HEADS, per_group, HEAD_DIM), (1, 0, 2, 3))
    key_stack = jnp.transpose(all_keys[:, :kv_width].reshape(-1, KV_HEADS, HEAD_DIM), (1, 0, 2))
    value_stack = jnp.transpose(all_keys[:, kv_width:].reshape(-1, KV_HEADS, HEAD_DIM), (1, 0, 2))

    def one_head(item):
        query_head, key_head, value_head = item
        scores = jnp.einsum('tgd,kd->tgk', query_head.astype(jnp.float32), key_head.astype(jnp.float32)) / jnp.sqrt(jnp.float32(HEAD_DIM))
        scores = jnp.where(live[:, None, :], scores, MASKED)
        highest = lax.optimization_barrier(jnp.max(scores, axis=-1, keepdims=True))
        weights = jnp.where(live[:, None, :], jnp.exp(scores - highest), 0.0)
        totals = lax.optimization_barrier(jnp.sum(weights, axis=-1))
        rounded = weights.astype(jnp.bfloat16)
        summed = jnp.einsum('tgk,kd->tgd', rounded.astype(jnp.float32), value_head.astype(jnp.float32))
        return summed / totals[..., None]
    outputs = lax.map(one_head, (query_stack, key_stack, value_stack))
    return jnp.transpose(outputs, (1, 0, 2, 3)).reshape(NEW_TOK, Q_HEADS * HEAD_DIM).astype(jnp.bfloat16)

def reference(queries, block_kv, pool_kv, prefix_len, assignment, stripe_map, owner_map):
    kv_width = KV_HEADS * HEAD_DIM
    offsets = jnp.arange(NEW_TOK, dtype=jnp.int32)
    slot_index = jnp.arange(PREFIX_SLOTS, dtype=jnp.int32)
    residues = invert(stripe_map)

    def per_group(item):
        query_rows, kv_rows, request = item
        length = prefix_len[request]
        positions = length + offsets
        q_rot = rotate(query_rows, positions, Q_HEADS)
        new_kv = jnp.concatenate([rotate(kv_rows[:, :kv_width], positions, KV_HEADS), kv_rows[:, kv_width:]], axis=1)
        prefix_kv = jnp.take(pool_kv, request, axis=1).reshape(GROUPS * PREFIX_SLOTS, 2 * kv_width)
        located = slot_index[None, :] * GROUPS + residues[request][:, None]
        prefix_live = (located < length).reshape(-1)
        return (group_attention(q_rot, new_kv, prefix_kv, prefix_live), new_kv)
    attended, fresh = lax.map(per_group, (queries, block_kv, assignment))
    by_request = fresh[invert(assignment)]
    spread = jnp.transpose(by_request.reshape(GROUPS, NEW_TOK // GROUPS, GROUPS, 2 * kv_width), (0, 2, 1, 3))
    targets = invert(owner_map)
    request_rows = jnp.arange(GROUPS, dtype=jnp.int32)[:, None]
    picked = spread[request_rows, targets]
    decode_kv = jnp.transpose(picked, (1, 0, 2, 3))
    return (attended, decode_kv)
```

```python
import functools

import jax
import jax.numpy as jnp
from jax import lax
from jax.experimental import pallas as pl
from jax.experimental.pallas import tpu as pltpu
from jax.sharding import PartitionSpec as P

Q_HEADS = 32
KV_HEADS = 4
HEAD_DIM = 128
PER_KV = Q_HEADS // KV_HEADS
KV_WIDTH = KV_HEADS * HEAD_DIM

ROPE_BASE = 1000000.0
MASKED = -1e30
VMEM_LIMIT = 48 * 1024 * 1024

SMEM = pl.BlockSpec(memory_space=pltpu.SMEM)
VMEM = pl.BlockSpec(memory_space=pltpu.VMEM)
ANY = pl.BlockSpec(memory_space=pl.ANY)


def params():
    return pltpu.CompilerParams(vmem_limit_bytes=VMEM_LIMIT)


def pack_kernel(assign_ref, pool_ref, out_ref, sems):
    groups = out_ref.shape[0]

    def copy(g):
        return pltpu.make_async_copy(pool_ref.at[assign_ref[g]], out_ref.at[g], sems.at[g])

    def start(g, carry):
        copy(g).start()
        return carry

    def wait(g, carry):
        copy(g).wait()
        return carry

    lax.fori_loop(0, groups, start, 0)
    lax.fori_loop(0, groups, wait, 0)


def pack(assignment, pool):
    return pl.pallas_call(
        pack_kernel,
        out_shape=jax.ShapeDtypeStruct(pool.shape, pool.dtype),
        in_specs=[SMEM, ANY],
        out_specs=ANY,
        scratch_shapes=[pltpu.SemaphoreType.DMA((pool.shape[0],))],
        compiler_params=params(),
        name="pack_pool",
    )(assignment, pool)


def unpack_kernel(assign_ref, got_ref, out_ref, sems):
    groups = out_ref.shape[0]

    def copy(g):
        return pltpu.make_async_copy(got_ref.at[g], out_ref.at[assign_ref[g]], sems.at[g])

    def start(g, carry):
        copy(g).start()
        return carry

    def wait(g, carry):
        copy(g).wait()
        return carry

    lax.fori_loop(0, groups, start, 0)
    lax.fori_loop(0, groups, wait, 0)


def unpack(assignment, got):
    return pl.pallas_call(
        unpack_kernel,
        out_shape=jax.ShapeDtypeStruct(got.shape, got.dtype),
        in_specs=[SMEM, ANY],
        out_specs=ANY,
        scratch_shapes=[pltpu.SemaphoreType.DMA((got.shape[0],))],
        compiler_params=params(),
        name="unpack_decode",
    )(assignment, got)


def turn(x, cosine, sine):
    return x * cosine + pltpu.roll(x, HEAD_DIM // 2, 1) * sine


def fresh_kernel(
    me_ref, assign_ref, length_ref, owner_ref, block_ref, new_ref, fresh_ref, cos_ref, sin_ref, rows_ref
):
    groups, count = fresh_ref.shape[:2]
    new_count = block_ref.shape[0]
    request = assign_ref[me_ref[0]]
    length = length_ref[request]
    half = HEAD_DIM // 2
    lane = lax.broadcasted_iota(jnp.int32, (1, HEAD_DIM), 1)
    step = jnp.where(lane < half, lane, lane - half).astype(jnp.float32)
    freqs = jnp.exp(step * jnp.float32(-jnp.log(ROPE_BASE) / half))
    positions = (length + lax.broadcasted_iota(jnp.int32, (new_count, HEAD_DIM), 0)).astype(jnp.float32)
    angles = positions * freqs
    cosine = jnp.cos(angles)
    sine = jnp.where(lane < half, -1.0, 1.0) * jnp.sin(angles)
    cos_ref[...] = cosine
    sin_ref[...] = sine
    for head in range(KV_HEADS):
        at = slice(head * HEAD_DIM, (head + 1) * HEAD_DIM)
        turned = turn(block_ref[:, at].astype(jnp.float32), cosine, sine).astype(jnp.bfloat16)
        new_ref[:, at] = turned
        rows_ref[head] = turned.astype(jnp.float32)
    for head in range(KV_HEADS, 2 * KV_HEADS):
        at = slice(head * HEAD_DIM, (head + 1) * HEAD_DIM)
        new_ref[:, at] = block_ref[:, at]
        rows_ref[head] = block_ref[:, at].astype(jnp.float32)
    for residue in range(groups):
        owner = owner_ref[request, residue]
        for head in range(2 * KV_HEADS):
            picked = rows_ref[head, pl.ds(residue, count, stride=groups), :]
            fresh_ref[owner, :, head * HEAD_DIM : (head + 1) * HEAD_DIM] = picked.astype(jnp.bfloat16)


def fresh(me, assignment, prefix_len, owner_map, block_kv):
    groups = assignment.shape[0]
    new_count, width = block_kv.shape
    return pl.pallas_call(
        fresh_kernel,
        out_shape=(
            jax.ShapeDtypeStruct(block_kv.shape, jnp.bfloat16),
            jax.ShapeDtypeStruct((groups, new_count // groups, width), jnp.bfloat16),
            jax.ShapeDtypeStruct((new_count, HEAD_DIM), jnp.float32),
            jax.ShapeDtypeStruct((new_count, HEAD_DIM), jnp.float32),
        ),
        in_specs=[SMEM, SMEM, SMEM, SMEM, VMEM],
        out_specs=(VMEM, VMEM, VMEM, VMEM),
        scratch_shapes=[pltpu.VMEM((2 * KV_HEADS, new_count, HEAD_DIM), jnp.float32)],
        compiler_params=params(),
        name="fresh_kv",
    )(me, assignment, prefix_len, owner_map, block_kv)


SCALE = HEAD_DIM ** -0.5


def own_kernel(
    me_ref, assign_ref, length_ref, stripe_ref, q_ref, key_ref, value_ref, cos_ref, sin_ref,
    rot_ref, high_ref, total_ref, sum_ref, bias_ref,
):
    new_count = q_ref.shape[0]
    groups = assign_ref.shape[0]
    span = bias_ref.shape[1]
    slots = span // groups

    @pl.when(pl.program_id(0) == 0)
    def _():
        request = assign_ref[me_ref[0]]
        length = length_ref[request]
        lane = lax.broadcasted_iota(jnp.int32, (8, span), 1)
        holder, slot = lane // slots, lane % slots

        def visit(residue, bias):
            live = (holder == stripe_ref[request, residue]) & (slot * groups + residue < length)
            return jnp.where(live, 0.0, bias)

        bias_ref[...] = lax.fori_loop(0, groups, visit, jnp.full((8, span), MASKED, jnp.float32))

    cosine, sine = cos_ref[...], sin_ref[...]
    causal = lax.broadcasted_iota(jnp.int32, (new_count, new_count), 1) <= lax.broadcasted_iota(
        jnp.int32, (new_count, new_count), 0
    )
    for head in range(PER_KV):
        at = slice(head * HEAD_DIM, (head + 1) * HEAD_DIM)
        rows = slice(head * new_count, (head + 1) * new_count)
        query = turn(q_ref[:, at].astype(jnp.float32), cosine, sine).astype(jnp.bfloat16)
        rot_ref[0, rows, :] = query
        scores = lax.dot_general(
            query, key_ref[...], (((1,), (1,)), ((), ())), preferred_element_type=jnp.float32
        ) * SCALE
        scores = jnp.where(causal, scores, MASKED)
        high = jnp.max(scores, axis=1, keepdims=True)
        weights = jnp.exp(scores - high)
        total = jnp.sum(weights, axis=1, keepdims=True)
        high_ref[0, rows, :] = jnp.broadcast_to(high, (new_count, HEAD_DIM))
        total_ref[0, rows, :] = jnp.broadcast_to(total, (new_count, HEAD_DIM))
        sum_ref[0, rows, :] = jnp.dot(
            weights.astype(jnp.bfloat16), value_ref[...], preferred_element_type=jnp.float32
        )


def own(me, assignment, prefix_len, stripe_map, queries, new_kv, cosine, sine, span):
    new_count = queries.shape[0]
    stacked = (KV_HEADS, PER_KV * new_count, HEAD_DIM)
    per_head = pl.BlockSpec((1, PER_KV * new_count, HEAD_DIM), lambda h: (h, 0, 0))
    whole = pl.BlockSpec((new_count, HEAD_DIM), lambda h: (0, 0))
    return pl.pallas_call(
        own_kernel,
        grid=(KV_HEADS,),
        out_shape=(
            jax.ShapeDtypeStruct(stacked, jnp.bfloat16),
            jax.ShapeDtypeStruct(stacked, jnp.float32),
            jax.ShapeDtypeStruct(stacked, jnp.float32),
            jax.ShapeDtypeStruct(stacked, jnp.float32),
            jax.ShapeDtypeStruct((8, span), jnp.float32),
        ),
        in_specs=[
            SMEM, SMEM, SMEM, SMEM,
            pl.BlockSpec((new_count, PER_KV * HEAD_DIM), lambda h: (0, h)),
            pl.BlockSpec((new_count, HEAD_DIM), lambda h: (0, h)),
            pl.BlockSpec((new_count, HEAD_DIM), lambda h: (0, KV_HEADS + h)),
            whole,
            whole,
        ],
        out_specs=(per_head, per_head, per_head, per_head, pl.BlockSpec((8, span), lambda h: (0, 0))),
        compiler_params=params(),
        name="own_attention",
    )(me, assignment, prefix_len, stripe_map, queries, new_kv, new_kv, cosine, sine)


def prefix_kernel(rot_ref, high_ref, total_ref, sum_ref, bias_ref, key_ref, value_ref, out_ref):
    new_count = out_ref.shape[0]
    bias = bias_ref[0:1, :]
    for head in range(PER_KV):
        rows = slice(head * new_count, (head + 1) * new_count)
        scores = lax.dot_general(
            rot_ref[0, rows, :], key_ref[...], (((1,), (1,)), ((), ())), preferred_element_type=jnp.float32
        ) * SCALE + bias
        own_high = high_ref[0, rows, :]
        high = jnp.maximum(own_high, jnp.max(scores, axis=1, keepdims=True))
        factor = jnp.exp(own_high - high)
        weights = jnp.exp(scores - high[:, 0:1])
        total = jnp.sum(weights, axis=1, keepdims=True) + total_ref[0, rows, :] * factor
        summed = jnp.dot(weights.astype(jnp.bfloat16), value_ref[...], preferred_element_type=jnp.float32)
        summed = summed + sum_ref[0, rows, :] * factor
        out_ref[:, head * HEAD_DIM : (head + 1) * HEAD_DIM] = (summed / total).astype(jnp.bfloat16)


def attend(rot, high, total, summed, bias, keys, new_count):
    span = keys.shape[0]
    per_head = pl.BlockSpec((1, PER_KV * new_count, HEAD_DIM), lambda h: (h, 0, 0))
    return pl.pallas_call(
        prefix_kernel,
        grid=(KV_HEADS,),
        out_shape=jax.ShapeDtypeStruct((new_count, Q_HEADS * HEAD_DIM), jnp.bfloat16),
        in_specs=[
            per_head, per_head, per_head, per_head,
            pl.BlockSpec((8, span), lambda h: (0, 0)),
            pl.BlockSpec((span, HEAD_DIM), lambda h: (0, h)),
            pl.BlockSpec((span, HEAD_DIM), lambda h: (0, KV_HEADS + h)),
        ],
        out_specs=pl.BlockSpec((new_count, PER_KV * HEAD_DIM), lambda h: (0, h)),
        compiler_params=params(),
        name="prefix_attention",
    )(rot, high, total, summed, bias, keys, keys)


def shards(queries, block_kv, pool_kv, prefix_len, assignment, stripe_map, owner_map):
    new_count = queries.shape[1]
    groups, slots, width = pool_kv.shape[1:]
    span = groups * slots
    me = lax.axis_index("pg").astype(jnp.int32).reshape(1)
    outgoing = pack(assignment, pool_kv[0])
    incoming = lax.all_to_all(outgoing, "pg", split_axis=0, concat_axis=0, tiled=True)
    new_kv, fresh_out, cosine, sine = fresh(me, assignment, prefix_len, owner_map, block_kv[0])
    arrived = lax.all_to_all(fresh_out, "pg", split_axis=0, concat_axis=0, tiled=True)
    rot, high, total, summed, bias = own(
        me, assignment, prefix_len, stripe_map, queries[0], new_kv, cosine, sine, span
    )
    attended = attend(rot, high, total, summed, bias, incoming.reshape(span, width), new_count)
    decode_kv = unpack(assignment, arrived)
    return (attended[None], decode_kv[None])


def solution(mesh):
    return jax.shard_map(
        shards,
        mesh=mesh,
        in_specs=(
            P(("rep", "pg"), None, None),
            P(("rep", "pg"), None, None),
            P(("rep", "pg"), None, None, None),
            P("rep"),
            P("rep"),
            P("rep", None),
            P("rep", None),
        ),
        out_specs=(P(("rep", "pg"), None, None), P(("rep", "pg"), None, None, None)),
        check_vma=False,
    )
```

```python
import math

import jax
import jax.numpy as jnp
from jax import lax
from jax.experimental import pallas as pl
from jax.experimental.pallas import tpu as pltpu
from jax.sharding import PartitionSpec as P

Q_HEADS = 32
KV_HEADS = 4
HEAD_DIM = 128
PER_KV = Q_HEADS // KV_HEADS
KV_WIDTH = KV_HEADS * HEAD_DIM

ROPE_BASE = 1000000.0
MASKED = -1e30
SCALE = HEAD_DIM ** -0.5 / math.log(2.0)
CHUNK = 256

SMEM = pl.BlockSpec(memory_space=pltpu.SMEM)
VMEM = pl.BlockSpec(memory_space=pltpu.VMEM)
ANY = pl.BlockSpec(memory_space=pl.ANY)


def params(mib):
    return pltpu.CompilerParams(vmem_limit_bytes=mib * 1024 * 1024)


def column(head):
    return slice(head * HEAD_DIM, (head + 1) * HEAD_DIM)


def angle_tables(length, rows):
    half = HEAD_DIM // 2
    lane = lax.broadcasted_iota(jnp.int32, (1, HEAD_DIM), 1)
    step = jnp.where(lane < half, lane, lane - half).astype(jnp.float32)
    freqs = jnp.exp(step * (-math.log(ROPE_BASE) / half))
    positions = (length + lax.broadcasted_iota(jnp.int32, (rows, HEAD_DIM), 0)).astype(jnp.float32)
    angles = positions * freqs
    return jnp.cos(angles), jnp.where(lane < half, -1.0, 1.0) * jnp.sin(angles)


def turn(x, cosine, sine):
    x = x.astype(jnp.float32)
    return (x * cosine + pltpu.roll(x, HEAD_DIM // 2, 1) * sine).astype(jnp.bfloat16)


def front_kernel(
    me_ref, assign_any, length_any, owner_any, block_any, pool_ref,
    new_ref, cos_ref, sin_ref, send_ref,
    assign_ref, length_ref, owner_ref, block_ref, rows_ref, fresh_ref, small_sems, pool_sems, fresh_sems,
):
    groups, _, width = send_ref.shape
    slots = pool_ref.shape[1]
    new_count = block_any.shape[0]
    count = new_count // groups
    smalls = [
        pltpu.make_async_copy(assign_any, assign_ref, small_sems.at[0]),
        pltpu.make_async_copy(length_any, length_ref, small_sems.at[1]),
        pltpu.make_async_copy(owner_any, owner_ref, small_sems.at[2]),
        pltpu.make_async_copy(block_any, block_ref, small_sems.at[3]),
    ]
    for copy in smalls:
        copy.start()
    smalls[0].wait()

    def pool_copy(g, part):
        return pltpu.make_async_copy(
            pool_ref.at[assign_ref[g], :, pl.ds(part * width, width)],
            send_ref.at[g, pl.ds(part * slots, slots), :],
            pool_sems.at[part, g],
        )

    for g in range(groups):
        pool_copy(g, 0).start()
        pool_copy(g, 1).start()
    for copy in smalls[1:]:
        copy.wait()
    request = assign_ref[me_ref[0]]
    cosine, sine = angle_tables(length_ref[request], new_count)
    cos_ref[...] = cosine
    sin_ref[...] = sine
    for head in range(KV_HEADS):
        turned = turn(block_ref[:, column(head)], cosine, sine)
        new_ref[:, column(head)] = turned
        rows_ref[head] = turned.astype(jnp.float32)
    for head in range(KV_HEADS, 2 * KV_HEADS):
        new_ref[:, column(head)] = block_ref[:, column(head)]
        rows_ref[head] = block_ref[:, column(head)].astype(jnp.float32)

    def fresh_copy(residue):
        return pltpu.make_async_copy(
            fresh_ref.at[residue],
            send_ref.at[owner_ref[request, residue], pl.ds(2 * slots, 2 * count), :],
            fresh_sems.at[residue],
        )

    for residue in range(groups):
        for head in range(KV_HEADS):
            pair = [
                rows_ref[part * KV_HEADS + head, pl.ds(residue, count, stride=groups), :] for part in range(2)
            ]
            fresh_ref[residue, :, column(head)] = jnp.concatenate(pair, axis=0).astype(jnp.bfloat16)
        fresh_copy(residue).start()
    for g in range(groups):
        pool_copy(g, 0).wait()
        pool_copy(g, 1).wait()
        fresh_copy(g).wait()


def front(me, assignment, prefix_len, owner_map, block_kv, pool):
    groups, slots, width = pool.shape
    new_count = block_kv.shape[0]
    count = new_count // groups
    table = jax.ShapeDtypeStruct((new_count, HEAD_DIM), jnp.float32)
    return pl.pallas_call(
        front_kernel,
        out_shape=(
            jax.ShapeDtypeStruct(block_kv.shape, jnp.bfloat16),
            table,
            table,
            jax.ShapeDtypeStruct((groups, 2 * slots + 2 * count, width // 2), jnp.bfloat16),
        ),
        in_specs=[SMEM, ANY, ANY, ANY, ANY, ANY],
        out_specs=(VMEM, VMEM, VMEM, ANY),
        scratch_shapes=[
            pltpu.SMEM(assignment.shape, jnp.int32),
            pltpu.SMEM(prefix_len.shape, jnp.int32),
            pltpu.SMEM(owner_map.shape, jnp.int32),
            pltpu.VMEM(block_kv.shape, jnp.bfloat16),
            pltpu.VMEM((2 * KV_HEADS, new_count, HEAD_DIM), jnp.float32),
            pltpu.VMEM((groups, 2 * count, width // 2), jnp.bfloat16),
            pltpu.SemaphoreType.DMA((4,)),
            pltpu.SemaphoreType.DMA((2, groups)),
            pltpu.SemaphoreType.DMA((groups,)),
        ],
        compiler_params=params(60),
        name="front",
    )(me, assignment, prefix_len, owner_map, block_kv, pool)


def query_kernel(me_ref, assign_ref, length_ref, stripe_ref, q_ref, cos_ref, sin_ref, rot_ref, bias_ref):
    new_count = q_ref.shape[0]
    groups = assign_ref.shape[0]
    span = bias_ref.shape[1]
    slots = span // groups
    request = assign_ref[me_ref[0]]
    length = length_ref[request]
    lane = lax.broadcasted_iota(jnp.int32, (8, span), 1)
    holder, slot = lane // slots, lane % slots

    def visit(residue, bias):
        live = (holder == stripe_ref[request, residue]) & (slot * groups + residue < length)
        return jnp.where(live, 0.0, bias)

    bias_ref[...] = lax.fori_loop(0, groups, visit, jnp.full((8, span), MASKED, jnp.float32))
    cosine, sine = cos_ref[...], sin_ref[...]
    for head in range(Q_HEADS):
        rows = slice((head % PER_KV) * new_count, (head % PER_KV + 1) * new_count)
        rot_ref[head // PER_KV, rows, :] = turn(q_ref[:, column(head)], cosine, sine)


def rotate_queries(me, assignment, prefix_len, stripe_map, queries, cosine, sine, span):
    new_count = queries.shape[0]
    return pl.pallas_call(
        query_kernel,
        out_shape=(
            jax.ShapeDtypeStruct((KV_HEADS, PER_KV * new_count, HEAD_DIM), jnp.bfloat16),
            jax.ShapeDtypeStruct((8, span), jnp.float32),
        ),
        in_specs=[SMEM, SMEM, SMEM, SMEM, VMEM, VMEM, VMEM],
        out_specs=(VMEM, VMEM),
        compiler_params=params(32),
        name="rotate_queries",
    )(me, assignment, prefix_len, stripe_map, queries, cosine, sine)


def attend_kernel(assign_ref, rot_ref, bias_ref, new_ref, got_ref, out_ref, decode_ref, done_ref, out_sems):
    new_count = new_ref.shape[0]
    pieces, rows_in, _ = got_ref.shape
    groups = assign_ref.shape[0]
    span = bias_ref.shape[1]
    slots = span // pieces
    count = new_count // groups
    if decode_ref is not None:
        for g in range(groups):
            for part in range(2):
                decode_ref[assign_ref[g], :, part * KV_WIDTH : (part + 1) * KV_WIDTH] = got_ref[
                    g, 2 * slots : 2 * slots + 2 * count, :
                ][part * count : (part + 1) * count]
    bias = bias_ref[0:1, :]
    token = lax.broadcasted_iota(jnp.int32, (CHUNK, new_count), 0) % new_count
    causal = jnp.where(lax.broadcasted_iota(jnp.int32, (CHUNK, new_count), 1) <= token, 0.0, MASKED)
    ones = jnp.ones((span + new_count, HEAD_DIM), jnp.bfloat16)
    per_head = PER_KV * new_count // CHUNK
    keys, values = {}, {}

    def scores_of(at):
        head, chunk = divmod(at, per_head)
        if chunk == 0:
            lanes = column(head)
            parts = [got_ref[i, 0:slots, lanes] for i in range(pieces)] + [new_ref[:, lanes]]
            keys[head] = jnp.concatenate(parts, axis=0)
            parts = [got_ref[i, slots : 2 * slots, lanes] for i in range(pieces)]
            parts.append(new_ref[:, column(KV_HEADS + head)])
            values[head] = jnp.concatenate([jnp.concatenate(parts, axis=0), ones], axis=1)
        query = rot_ref[head, chunk * CHUNK : (chunk + 1) * CHUNK, :]
        return lax.dot_general(query, keys[head], (((1,), (1,)), ((), ())), preferred_element_type=jnp.float32)

    def out_copy(head):
        width = PER_KV * HEAD_DIM
        return pltpu.make_async_copy(
            done_ref.at[head], out_ref.at[:, pl.ds(head * width, width)], out_sems.at[head]
        )

    total_chunks = KV_HEADS * per_head
    ahead = scores_of(0)
    for at in range(total_chunks):
        scores = ahead
        if at + 1 < total_chunks:
            ahead = scores_of(at + 1)
        head, chunk = divmod(at, per_head)
        scores = jnp.concatenate([scores[:, :span] * SCALE + bias, scores[:, span:] * SCALE + causal], axis=1)
        weights = jnp.exp2(scores - jnp.max(scores, axis=1, keepdims=True)).astype(jnp.bfloat16)
        summed = jnp.dot(weights, values[head], preferred_element_type=jnp.float32)
        result = (summed[:, :HEAD_DIM] / summed[:, HEAD_DIM:]).astype(jnp.bfloat16)
        for row in range(CHUNK // new_count):
            done_ref[head, :, column(chunk * (CHUNK // new_count) + row)] = result[
                row * new_count : (row + 1) * new_count
            ]
        if chunk == per_head - 1:
            out_copy(head).start()
    for head in range(KV_HEADS):
        out_copy(head).wait()


def attend(assignment, rot, bias, new_kv, got, unpack):
    new_count = new_kv.shape[0]
    groups = assignment.shape[0]
    shapes = [jax.ShapeDtypeStruct((new_count, Q_HEADS * HEAD_DIM), jnp.bfloat16)]
    if unpack:
        shapes.append(jax.ShapeDtypeStruct((groups, new_count // groups, 2 * KV_WIDTH), jnp.bfloat16))

    def kernel(*refs):
        refs = list(refs)
        if not unpack:
            refs.insert(6, None)
        attend_kernel(*refs)

    return pl.pallas_call(
        kernel,
        out_shape=tuple(shapes),
        in_specs=[SMEM, VMEM, VMEM, VMEM, VMEM],
        out_specs=(ANY, VMEM)[: len(shapes)],
        scratch_shapes=[
            pltpu.VMEM((KV_HEADS, new_count, PER_KV * HEAD_DIM), jnp.bfloat16),
            pltpu.SemaphoreType.DMA((KV_HEADS,)),
        ],
        compiler_params=params(32),
        name="attend",
    )(assignment, rot, bias, new_kv, got)


def new_rows_kernel(me_ref, assign_ref, length_ref, block_ref, new_ref, cos_ref, sin_ref):
    cosine, sine = angle_tables(length_ref[assign_ref[me_ref[0]]], block_ref.shape[0])
    cos_ref[...] = cosine
    sin_ref[...] = sine
    for head in range(KV_HEADS):
        new_ref[:, column(head)] = turn(block_ref[:, column(head)], cosine, sine)
    new_ref[:, KV_WIDTH:] = block_ref[:, KV_WIDTH:]


def inverse(table):
    places = jnp.arange(table.shape[0], dtype=jnp.int32)
    return jnp.sum(jnp.where(table[None, :] == places[:, None], places, 0), axis=1)


def small_pieces(me, assignment, prefix_len, stripe_map, owner_map, queries, block_kv, pool):
    groups, slots, width = pool.shape
    new_count = block_kv.shape[0]
    count = new_count // groups
    table = jax.ShapeDtypeStruct((new_count, HEAD_DIM), jnp.float32)
    new_kv, cosine, sine = pl.pallas_call(
        new_rows_kernel,
        out_shape=(jax.ShapeDtypeStruct(block_kv.shape, jnp.bfloat16), table, table),
        in_specs=[SMEM, SMEM, SMEM, VMEM],
        out_specs=(VMEM, VMEM, VMEM),
        compiler_params=params(32),
        name="new_rows",
    )(me, assignment, prefix_len, block_kv)
    spread = jnp.transpose(new_kv.reshape(count, groups, width), (1, 0, 2))
    fresh = spread[inverse(owner_map[assignment[me[0]]])]
    send = jnp.concatenate([pool[assignment], fresh], axis=1)
    got = lax.all_to_all(send, "pg", split_axis=0, concat_axis=0, tiled=True)
    rot, bias = rotate_queries(
        me, assignment, prefix_len, stripe_map, queries, cosine, sine, groups * slots
    )
    keys = got[:, :slots].reshape(groups * slots, width)
    keys = jnp.concatenate([keys[:, :KV_WIDTH], keys[:, KV_WIDTH:]], axis=0)[None]
    (attended,) = attend(assignment, rot, bias, new_kv, keys, False)
    return attended, got[inverse(assignment), slots:]


def shards(queries, block_kv, pool_kv, prefix_len, assignment, stripe_map, owner_map):
    queries, block_kv, pool = queries[0], block_kv[0], pool_kv[0]
    groups, slots, _ = pool.shape
    me = lax.axis_index("pg").astype(jnp.int32).reshape(1)
    if slots % 16 or (2 * queries.shape[0] // groups) % 16:
        attended, decode_kv = small_pieces(
            me, assignment, prefix_len, stripe_map, owner_map, queries, block_kv, pool
        )
        return (attended[None], decode_kv[None])
    new_kv, cosine, sine, send = front(me, assignment, prefix_len, owner_map, block_kv, pool)
    got = lax.all_to_all(send, "pg", split_axis=0, concat_axis=0, tiled=True)
    rot, bias = rotate_queries(
        me, assignment, prefix_len, stripe_map, queries, cosine, sine, groups * slots
    )
    attended, decode_kv = attend(assignment, rot, bias, new_kv, got, True)
    return (attended[None], decode_kv[None])


def solution(mesh):
    return jax.shard_map(
        shards,
        mesh=mesh,
        in_specs=(
            P(("rep", "pg"), None, None),
            P(("rep", "pg"), None, None),
            P(("rep", "pg"), None, None, None),
            P("rep"),
            P("rep"),
            P("rep", None),
            P("rep", None),
        ),
        out_specs=(P(("rep", "pg"), None, None), P(("rep", "pg"), None, None, None)),
        check_vma=False,
    )
```

```python
import functools
import math

import jax
import jax.numpy as jnp
from jax import lax
from jax.experimental import pallas as pl
from jax.experimental.pallas import tpu as pltpu
from jax.sharding import PartitionSpec as P

Q_HEADS = 32
KV_HEADS = 4
HEAD_DIM = 128
PER_KV = Q_HEADS // KV_HEADS
KV_WIDTH = KV_HEADS * HEAD_DIM

ROPE_BASE = 1000000.0
MASKED = -1e30
SCALE = HEAD_DIM ** -0.5 / math.log(2.0)
CHUNK = 256

SMEM = pl.BlockSpec(memory_space=pltpu.SMEM)
VMEM = pl.BlockSpec(memory_space=pltpu.VMEM)
ANY = pl.BlockSpec(memory_space=pl.ANY)


def params(mib):
    return pltpu.CompilerParams(vmem_limit_bytes=mib * 1024 * 1024)


def column(head):
    return slice(head * HEAD_DIM, (head + 1) * HEAD_DIM)


def angle_tables(length, rows):
    half = HEAD_DIM // 2
    lane = lax.broadcasted_iota(jnp.int32, (1, HEAD_DIM), 1)
    step = jnp.where(lane < half, lane, lane - half).astype(jnp.float32)
    freqs = jnp.exp(step * (-math.log(ROPE_BASE) / half))
    positions = (length + lax.broadcasted_iota(jnp.int32, (rows, HEAD_DIM), 0)).astype(jnp.float32)
    angles = positions * freqs
    return jnp.cos(angles), jnp.where(lane < half, -1.0, 1.0) * jnp.sin(angles)


def turn(x, cosine, sine):
    x = x.astype(jnp.float32)
    return (x * cosine + pltpu.roll(x, HEAD_DIM // 2, 1) * sine).astype(jnp.bfloat16)


def front_kernel(
    me_ref, assign_any, length_any, owner_any, block_any, pool_any, *refs
):
    groups, slots, _ = pool_any.shape
    send_refs, refs = refs[:groups], refs[groups:]
    assign_ref, length_ref, owner_ref, residue_ref, block_ref, rows_ref, small_sems, pool_sems = refs
    width = send_refs[0].shape[1]
    new_count = block_any.shape[0]
    count = new_count // groups
    smalls = [
        pltpu.make_async_copy(assign_any, assign_ref, small_sems.at[0]),
        pltpu.make_async_copy(length_any, length_ref, small_sems.at[1]),
        pltpu.make_async_copy(owner_any, owner_ref, small_sems.at[2]),
        pltpu.make_async_copy(block_any, block_ref, small_sems.at[3]),
    ]
    for copy in smalls:
        copy.start()
    me = me_ref[0]
    smalls[0].wait()

    def pool_copy(t, part):
        return pltpu.make_async_copy(
            pool_any.at[assign_ref[me ^ t], :, pl.ds(part * width, width)],
            send_refs[t].at[pl.ds(part * slots, slots), :],
            pool_sems.at[part, t],
        )

    for t in range(groups):
        pool_copy(t, 0).start()
        pool_copy(t, 1).start()
    for copy in smalls[1:]:
        copy.wait()
    request = assign_ref[me]
    for residue in range(groups):
        residue_ref[owner_ref[request, residue]] = residue
    cosine, sine = angle_tables(length_ref[request], new_count)
    for head in range(KV_HEADS):
        turned = turn(block_ref[:, column(head)], cosine, sine)
        rows_ref[head] = turned.astype(jnp.float32)
        rows_ref[KV_HEADS + head] = block_ref[:, column(KV_HEADS + head)].astype(jnp.float32)
    for t in range(groups):
        residue = residue_ref[me ^ t]
        for head in range(KV_HEADS):
            pair = [
                rows_ref[part * KV_HEADS + head, pl.ds(residue, count, stride=groups), :] for part in range(2)
            ]
            send_refs[t][2 * slots : 2 * slots + 2 * count, column(head)] = jnp.concatenate(
                pair, axis=0
            ).astype(jnp.bfloat16)
    for t in range(groups):
        pool_copy(t, 0).wait()
        pool_copy(t, 1).wait()


def front(me, assignment, prefix_len, owner_map, block_kv, pool):
    groups, slots, width = pool.shape
    new_count = block_kv.shape[0]
    count = new_count // groups
    return pl.pallas_call(
        front_kernel,
        out_shape=[jax.ShapeDtypeStruct((2 * slots + 2 * count, width // 2), jnp.bfloat16)] * groups,
        in_specs=[SMEM, ANY, ANY, ANY, ANY, ANY],
        out_specs=[VMEM] * groups,
        scratch_shapes=[
            pltpu.SMEM(assignment.shape, jnp.int32),
            pltpu.SMEM(prefix_len.shape, jnp.int32),
            pltpu.SMEM(owner_map.shape, jnp.int32),
            pltpu.SMEM(assignment.shape, jnp.int32),
            pltpu.VMEM(block_kv.shape, jnp.bfloat16),
            pltpu.VMEM((2 * KV_HEADS, new_count, HEAD_DIM), jnp.float32),
            pltpu.SemaphoreType.DMA((4,)),
            pltpu.SemaphoreType.DMA((2, groups)),
        ],
        compiler_params=params(60),
        name="front",
    )(me, assignment, prefix_len, owner_map, block_kv, pool)


def query_kernel(me_ref, assign_ref, length_ref, stripe_ref, q_ref, block_ref, rot_ref, bias_ref, new_ref, order_ref):
    new_count = q_ref.shape[0]
    groups = assign_ref.shape[0]
    span = bias_ref.shape[1]
    slots = span // groups
    me = me_ref[0]
    request = assign_ref[me]
    length = length_ref[request]
    lane = lax.broadcasted_iota(jnp.int32, (8, span), 1)
    holder, slot = (lane // slots) ^ me, lane % slots

    def visit(residue, bias):
        live = (holder == stripe_ref[request, residue]) & (slot * groups + residue < length)
        return jnp.where(live, 0.0, bias)

    bias_ref[...] = lax.fori_loop(0, groups, visit, jnp.full((8, span), MASKED, jnp.float32))
    place = lax.broadcasted_iota(jnp.int32, order_ref.shape, 1)

    def name(t, order):
        return jnp.where(place == t, assign_ref[me ^ t], order)

    order_ref[...] = lax.fori_loop(0, groups, name, jnp.zeros(order_ref.shape, jnp.int32))
    cosine, sine = angle_tables(length, new_count)
    for head in range(KV_HEADS):
        new_ref[:, column(head)] = turn(block_ref[:, column(head)], cosine, sine)
    new_ref[:, KV_WIDTH:] = block_ref[:, KV_WIDTH:]
    for head in range(Q_HEADS):
        rows = slice((head % PER_KV) * new_count, (head % PER_KV + 1) * new_count)
        rot_ref[head // PER_KV, rows, :] = turn(q_ref[:, column(head)], cosine, sine)


def rotate_queries(me, assignment, prefix_len, stripe_map, queries, block_kv, span):
    new_count = queries.shape[0]
    return pl.pallas_call(
        query_kernel,
        out_shape=(
            jax.ShapeDtypeStruct((KV_HEADS, PER_KV * new_count, HEAD_DIM), jnp.bfloat16),
            jax.ShapeDtypeStruct((8, span), jnp.float32),
            jax.ShapeDtypeStruct(block_kv.shape, jnp.bfloat16),
            jax.ShapeDtypeStruct((8, HEAD_DIM), jnp.int32),
        ),
        in_specs=[SMEM, SMEM, SMEM, SMEM, VMEM, VMEM],
        out_specs=(VMEM, VMEM, VMEM, VMEM),
        compiler_params=params(32),
        name="rotate_queries",
    )(me, assignment, prefix_len, stripe_map, queries, block_kv)


def attend_kernel(unpack, pieces, order_vmem, rot_ref, bias_ref, new_ref, *refs):
    got_refs, refs = refs[:pieces], refs[pieces:]
    out_ref, refs = refs[0], refs[1:]
    if unpack:
        decode_ref, refs = refs[0], refs[1:]
    done_ref, order_ref, out_sems, order_sem = refs
    new_count = new_ref.shape[0]
    span = bias_ref.shape[1]
    slots = span // pieces
    order_copy = pltpu.make_async_copy(order_vmem, order_ref, order_sem)
    order_copy.start()
    bias = bias_ref[0:1, :]
    token = lax.broadcasted_iota(jnp.int32, (CHUNK, new_count), 0) % new_count
    causal = jnp.where(lax.broadcasted_iota(jnp.int32, (CHUNK, new_count), 1) <= token, 0.0, MASKED)
    ones = jnp.ones((span + new_count, HEAD_DIM), jnp.bfloat16)
    per_head = PER_KV * new_count // CHUNK
    keys, values = {}, {}

    def scores_of(at):
        head, chunk = divmod(at, per_head)
        if chunk == 0:
            lanes = column(head)
            parts = [got[0:slots, lanes] for got in got_refs] + [new_ref[:, lanes]]
            keys[head] = jnp.concatenate(parts, axis=0)
            parts = [got[slots : 2 * slots, lanes] for got in got_refs]
            parts.append(new_ref[:, column(KV_HEADS + head)])
            values[head] = jnp.concatenate([jnp.concatenate(parts, axis=0), ones], axis=1)
        query = rot_ref[head, chunk * CHUNK : (chunk + 1) * CHUNK, :]
        return lax.dot_general(query, keys[head], (((1,), (1,)), ((), ())), preferred_element_type=jnp.float32)

    def out_copy(head):
        width = PER_KV * HEAD_DIM
        return pltpu.make_async_copy(
            done_ref.at[head], out_ref.at[:, pl.ds(head * width, width)], out_sems.at[head]
        )

    total_chunks = KV_HEADS * per_head
    ahead = scores_of(0)
    for at in range(total_chunks):
        scores = ahead
        if at + 1 < total_chunks:
            ahead = scores_of(at + 1)
        head, chunk = divmod(at, per_head)
        scores = jnp.concatenate([scores[:, :span] * SCALE + bias, scores[:, span:] * SCALE + causal], axis=1)
        weights = jnp.exp2(scores - jnp.max(scores, axis=1, keepdims=True)).astype(jnp.bfloat16)
        summed = jnp.dot(weights, values[head], preferred_element_type=jnp.float32)
        result = (summed[:, :HEAD_DIM] / summed[:, HEAD_DIM:]).astype(jnp.bfloat16)
        for row in range(CHUNK // new_count):
            done_ref[head, :, column(chunk * (CHUNK // new_count) + row)] = result[
                row * new_count : (row + 1) * new_count
            ]
        if chunk == per_head - 1:
            out_copy(head).start()
    order_copy.wait()
    if unpack:
        count = decode_ref.shape[1]
        for t, got in enumerate(got_refs):
            rows = got[2 * slots : 2 * slots + 2 * count, :]
            for part in range(2):
                decode_ref[order_ref[0, t], :, part * KV_WIDTH : (part + 1) * KV_WIDTH] = rows[
                    part * count : (part + 1) * count
                ]
    for head in range(KV_HEADS):
        out_copy(head).wait()


def attend(order, rot, bias, new_kv, got, count):
    new_count = new_kv.shape[0]
    shapes = [jax.ShapeDtypeStruct((new_count, Q_HEADS * HEAD_DIM), jnp.bfloat16)]
    if count:
        shapes.append(jax.ShapeDtypeStruct((new_count // count, count, 2 * KV_WIDTH), jnp.bfloat16))
    return pl.pallas_call(
        functools.partial(attend_kernel, count > 0, len(got)),
        out_shape=tuple(shapes),
        in_specs=[VMEM] * (4 + len(got)),
        out_specs=(ANY, VMEM)[: len(shapes)],
        scratch_shapes=[
            pltpu.VMEM((KV_HEADS, new_count, PER_KV * HEAD_DIM), jnp.bfloat16),
            pltpu.SMEM(order.shape, jnp.int32),
            pltpu.SemaphoreType.DMA((KV_HEADS,)),
            pltpu.SemaphoreType.DMA,
        ],
        compiler_params=params(32),
        name="attend",
    )(order, rot, bias, new_kv, *got)


def inverse(table):
    places = jnp.arange(table.shape[0], dtype=jnp.int32)
    return jnp.sum(jnp.where(table[None, :] == places[:, None], places, 0), axis=1)


def small_pieces(me, assignment, prefix_len, stripe_map, owner_map, queries, block_kv, pool):
    groups, slots, width = pool.shape
    count = block_kv.shape[0] // groups
    rot, bias, new_kv, order = rotate_queries(
        me, assignment, prefix_len, stripe_map, queries, block_kv, groups * slots
    )
    spread = jnp.transpose(new_kv.reshape(count, groups, width), (1, 0, 2))
    fresh = spread[inverse(owner_map[assignment[me[0]]])]
    send = jnp.concatenate([pool[assignment], fresh], axis=1)
    got = lax.all_to_all(send, "pg", split_axis=0, concat_axis=0, tiled=True)
    places = jnp.arange(groups, dtype=jnp.int32) ^ me[0]
    keys = got[places, :slots].reshape(groups * slots, width)
    keys = jnp.concatenate([keys[:, :KV_WIDTH], keys[:, KV_WIDTH:]], axis=0)
    (attended,) = attend(order, rot, bias, new_kv, [keys], 0)
    return attended, got[inverse(assignment), slots:]


def exchange(blocks):
    got = [blocks[0]]
    for t in range(len(blocks) - 1, 0, -1):
        pairs = [(source, source ^ t) for source in range(len(blocks))]
        got.insert(1, lax.ppermute(blocks[t], "pg", pairs))
    return got


def shards(queries, block_kv, pool_kv, prefix_len, assignment, stripe_map, owner_map):
    queries, block_kv, pool = queries[0], block_kv[0], pool_kv[0]
    groups, slots, _ = pool.shape
    count = queries.shape[0] // groups
    me = lax.axis_index("pg").astype(jnp.int32).reshape(1)
    if slots % 16 or (2 * count) % 16 or groups > 16:
        attended, decode_kv = small_pieces(
            me, assignment, prefix_len, stripe_map, owner_map, queries, block_kv, pool
        )
        return (attended[None], decode_kv[None])
    got = exchange(front(me, assignment, prefix_len, owner_map, block_kv, pool))
    rot, bias, new_kv, order = rotate_queries(
        me, assignment, prefix_len, stripe_map, queries, block_kv, groups * slots
    )
    attended, decode_kv = attend(order, rot, bias, new_kv, got, count)
    return (attended[None], decode_kv[None])


def solution(mesh):
    return jax.shard_map(
        shards,
        mesh=mesh,
        in_specs=(
            P(("rep", "pg"), None, None),
            P(("rep", "pg"), None, None),
            P(("rep", "pg"), None, None, None),
            P("rep"),
            P("rep"),
            P("rep", None),
            P("rep", None),
        ),
        out_specs=(P(("rep", "pg"), None, None), P(("rep", "pg"), None, None, None)),
        check_vma=False,
    )
```

```python
import functools
import math

import jax
import jax.numpy as jnp
from jax import lax
from jax.experimental import pallas as pl
from jax.experimental.pallas import tpu as pltpu
from jax.sharding import PartitionSpec as P

Q_HEADS = 32
KV_HEADS = 4
HEAD_DIM = 128
PER_KV = Q_HEADS // KV_HEADS
KV_WIDTH = KV_HEADS * HEAD_DIM

ROPE_BASE = 1000000.0
MASKED = -1e30
SCALE = HEAD_DIM ** -0.5 / math.log(2.0)
CHUNK = 256

SMEM = pl.BlockSpec(memory_space=pltpu.SMEM)
VMEM = pl.BlockSpec(memory_space=pltpu.VMEM)
ANY = pl.BlockSpec(memory_space=pl.ANY)


def params(mib):
    return pltpu.CompilerParams(vmem_limit_bytes=mib * 1024 * 1024)


def column(head):
    return slice(head * HEAD_DIM, (head + 1) * HEAD_DIM)


def angle_tables(length, rows):
    half = HEAD_DIM // 2
    lane = lax.broadcasted_iota(jnp.int32, (1, HEAD_DIM), 1)
    step = jnp.where(lane < half, lane, lane - half).astype(jnp.float32)
    freqs = jnp.exp(step * (-math.log(ROPE_BASE) / half))
    positions = (length + lax.broadcasted_iota(jnp.int32, (rows, HEAD_DIM), 0)).astype(jnp.float32)
    angles = positions * freqs
    return jnp.cos(angles), jnp.where(lane < half, -1.0, 1.0) * jnp.sin(angles)


def turn(x, cosine, sine):
    x = x.astype(jnp.float32)
    return (x * cosine + pltpu.roll(x, HEAD_DIM // 2, 1) * sine).astype(jnp.bfloat16)


def front_kernel(
    me_ref, assign_any, length_any, owner_any, block_any, pool_any, *refs
):
    groups, slots, _ = pool_any.shape
    send_refs, refs = refs[:groups], refs[groups:]
    assign_ref, length_ref, owner_ref, residue_ref, block_ref, rows_ref, small_sems, pool_sems = refs
    width = send_refs[0].shape[1]
    new_count = block_any.shape[0]
    count = new_count // groups
    smalls = [
        pltpu.make_async_copy(assign_any, assign_ref, small_sems.at[0]),
        pltpu.make_async_copy(length_any, length_ref, small_sems.at[1]),
        pltpu.make_async_copy(owner_any, owner_ref, small_sems.at[2]),
        pltpu.make_async_copy(block_any, block_ref, small_sems.at[3]),
    ]
    for copy in smalls:
        copy.start()
    me = me_ref[0]
    smalls[0].wait()

    def pool_copy(t, part):
        return pltpu.make_async_copy(
            pool_any.at[assign_ref[me ^ t], :, pl.ds(part * width, width)],
            send_refs[t].at[pl.ds(part * slots, slots), :],
            pool_sems.at[part, t],
        )

    for t in range(groups):
        pool_copy(t, 0).start()
        pool_copy(t, 1).start()
    for copy in smalls[1:]:
        copy.wait()
    request = assign_ref[me]
    for residue in range(groups):
        residue_ref[owner_ref[request, residue]] = residue
    cosine, sine = angle_tables(length_ref[request], new_count)
    for head in range(KV_HEADS):
        turned = turn(block_ref[:, column(head)], cosine, sine)
        rows_ref[head] = turned.astype(jnp.float32)
        rows_ref[KV_HEADS + head] = block_ref[:, column(KV_HEADS + head)].astype(jnp.float32)
    for t in range(groups):
        residue = residue_ref[me ^ t]
        for head in range(KV_HEADS):
            pair = [
                rows_ref[part * KV_HEADS + head, pl.ds(residue, count, stride=groups), :] for part in range(2)
            ]
            send_refs[t][2 * slots : 2 * slots + 2 * count, column(head)] = jnp.concatenate(
                pair, axis=0
            ).astype(jnp.bfloat16)
    for t in range(groups):
        pool_copy(t, 0).wait()
        pool_copy(t, 1).wait()


def front(me, assignment, prefix_len, owner_map, block_kv, pool):
    groups, slots, width = pool.shape
    new_count = block_kv.shape[0]
    count = new_count // groups
    return pl.pallas_call(
        front_kernel,
        out_shape=[jax.ShapeDtypeStruct((2 * slots + 2 * count, width // 2), jnp.bfloat16)] * groups,
        in_specs=[SMEM, ANY, ANY, ANY, ANY, ANY],
        out_specs=[VMEM] * groups,
        scratch_shapes=[
            pltpu.SMEM(assignment.shape, jnp.int32),
            pltpu.SMEM(prefix_len.shape, jnp.int32),
            pltpu.SMEM(owner_map.shape, jnp.int32),
            pltpu.SMEM(assignment.shape, jnp.int32),
            pltpu.VMEM(block_kv.shape, jnp.bfloat16),
            pltpu.VMEM((2 * KV_HEADS, new_count, HEAD_DIM), jnp.float32),
            pltpu.SemaphoreType.DMA((4,)),
            pltpu.SemaphoreType.DMA((2, groups)),
        ],
        compiler_params=params(60),
        name="front",
    )(me, assignment, prefix_len, owner_map, block_kv, pool)


def query_kernel(me_ref, assign_ref, length_ref, stripe_ref, q_ref, block_ref, rot_ref, bias_ref, new_ref, order_ref):
    new_count = q_ref.shape[0]
    groups = assign_ref.shape[0]
    span = bias_ref.shape[1]
    slots = span // groups
    me = me_ref[0]
    request = assign_ref[me]
    length = length_ref[request]
    lane = lax.broadcasted_iota(jnp.int32, (8, span), 1)
    holder, slot = (lane // slots) ^ me, lane % slots

    def visit(residue, bias):
        live = (holder == stripe_ref[request, residue]) & (slot * groups + residue < length)
        return jnp.where(live, 0.0, bias)

    bias_ref[...] = lax.fori_loop(0, groups, visit, jnp.full((8, span), MASKED, jnp.float32))
    place = lax.broadcasted_iota(jnp.int32, order_ref.shape, 1)

    def name(t, order):
        return jnp.where(place == t, assign_ref[me ^ t], order)

    order_ref[...] = lax.fori_loop(0, groups, name, jnp.zeros(order_ref.shape, jnp.int32))
    cosine, sine = angle_tables(length, new_count)
    for head in range(KV_HEADS):
        new_ref[:, column(head)] = turn(block_ref[:, column(head)], cosine, sine)
    new_ref[:, KV_WIDTH:] = block_ref[:, KV_WIDTH:]
    for head in range(Q_HEADS):
        rows = slice((head % PER_KV) * new_count, (head % PER_KV + 1) * new_count)
        rot_ref[head // PER_KV, rows, :] = turn(q_ref[:, column(head)], cosine, sine)


def rotate_queries(me, assignment, prefix_len, stripe_map, queries, block_kv, span):
    new_count = queries.shape[0]
    return pl.pallas_call(
        query_kernel,
        out_shape=(
            jax.ShapeDtypeStruct((KV_HEADS, PER_KV * new_count, HEAD_DIM), jnp.bfloat16),
            jax.ShapeDtypeStruct((8, span), jnp.float32),
            jax.ShapeDtypeStruct(block_kv.shape, jnp.bfloat16),
            jax.ShapeDtypeStruct((8, HEAD_DIM), jnp.int32),
        ),
        in_specs=[SMEM, SMEM, SMEM, SMEM, VMEM, VMEM],
        out_specs=(VMEM, VMEM, VMEM, VMEM),
        compiler_params=params(32),
        name="rotate_queries",
    )(me, assignment, prefix_len, stripe_map, queries, block_kv)


def attend_kernel(unpack, pieces, order_vmem, rot_ref, bias_ref, new_ref, *refs):
    got_refs, refs = refs[:pieces], refs[pieces:]
    out_ref, refs = refs[0], refs[1:]
    if unpack:
        decode_ref, refs = refs[0], refs[1:]
    done_ref, order_ref, out_sems, order_sem = refs
    new_count = new_ref.shape[0]
    span = bias_ref.shape[1]
    slots = span // pieces
    order_copy = pltpu.make_async_copy(order_vmem, order_ref, order_sem)
    order_copy.start()
    bias = bias_ref[0:1, :]
    token = lax.broadcasted_iota(jnp.int32, (CHUNK, new_count), 0) % new_count
    causal = jnp.where(lax.broadcasted_iota(jnp.int32, (CHUNK, new_count), 1) <= token, 0.0, MASKED)
    ones = jnp.ones((span + new_count, HEAD_DIM), jnp.bfloat16)
    per_head = PER_KV * new_count // CHUNK
    keys, values = {}, {}

    def scores_of(at):
        head, chunk = divmod(at, per_head)
        if chunk == 0:
            lanes = column(head)
            parts = [got[0:slots, lanes] for got in got_refs] + [new_ref[:, lanes]]
            keys[head] = jnp.concatenate(parts, axis=0)
            parts = [got[slots : 2 * slots, lanes] for got in got_refs]
            parts.append(new_ref[:, column(KV_HEADS + head)])
            values[head] = jnp.concatenate([jnp.concatenate(parts, axis=0), ones], axis=1)
        query = rot_ref[head, chunk * CHUNK : (chunk + 1) * CHUNK, :]
        return lax.dot_general(query, keys[head], (((1,), (1,)), ((), ())), preferred_element_type=jnp.float32)

    def out_copy(head):
        width = PER_KV * HEAD_DIM
        return pltpu.make_async_copy(
            done_ref.at[head], out_ref.at[:, pl.ds(head * width, width)], out_sems.at[head]
        )

    total_chunks = KV_HEADS * per_head
    ahead = scores_of(0)
    for at in range(total_chunks):
        scores = ahead
        if at + 1 < total_chunks:
            ahead = scores_of(at + 1)
        head, chunk = divmod(at, per_head)
        scores = jnp.concatenate([scores[:, :span] * SCALE + bias, scores[:, span:] * SCALE + causal], axis=1)
        weights = jnp.exp2(scores - jnp.max(scores, axis=1, keepdims=True)).astype(jnp.bfloat16)
        summed = jnp.dot(weights, values[head], preferred_element_type=jnp.float32)
        result = (summed[:, :HEAD_DIM] / summed[:, HEAD_DIM:]).astype(jnp.bfloat16)
        for row in range(CHUNK // new_count):
            done_ref[head, :, column(chunk * (CHUNK // new_count) + row)] = result[
                row * new_count : (row + 1) * new_count
            ]
        if chunk == per_head - 1:
            out_copy(head).start()
    order_copy.wait()
    if unpack:
        count = decode_ref.shape[1]
        for t, got in enumerate(got_refs):
            rows = got[2 * slots : 2 * slots + 2 * count, :]
            for part in range(2):
                decode_ref[order_ref[0, t], :, part * KV_WIDTH : (part + 1) * KV_WIDTH] = rows[
                    part * count : (part + 1) * count
                ]
    for head in range(KV_HEADS):
        out_copy(head).wait()


def attend(order, rot, bias, new_kv, got, count):
    new_count = new_kv.shape[0]
    shapes = [jax.ShapeDtypeStruct((new_count, Q_HEADS * HEAD_DIM), jnp.bfloat16)]
    if count:
        shapes.append(jax.ShapeDtypeStruct((new_count // count, count, 2 * KV_WIDTH), jnp.bfloat16))
    return pl.pallas_call(
        functools.partial(attend_kernel, count > 0, len(got)),
        out_shape=tuple(shapes),
        in_specs=[VMEM] * (4 + len(got)),
        out_specs=(ANY, VMEM)[: len(shapes)],
        scratch_shapes=[
            pltpu.VMEM((KV_HEADS, new_count, PER_KV * HEAD_DIM), jnp.bfloat16),
            pltpu.SMEM(order.shape, jnp.int32),
            pltpu.SemaphoreType.DMA((KV_HEADS,)),
            pltpu.SemaphoreType.DMA,
        ],
        compiler_params=params(32),
        name="attend",
    )(order, rot, bias, new_kv, *got)


def inverse(table):
    places = jnp.arange(table.shape[0], dtype=jnp.int32)
    return jnp.sum(jnp.where(table[None, :] == places[:, None], places, 0), axis=1)


def small_pieces(me, assignment, prefix_len, stripe_map, owner_map, queries, block_kv, pool):
    groups, slots, width = pool.shape
    count = block_kv.shape[0] // groups
    rot, bias, new_kv, order = rotate_queries(
        me, assignment, prefix_len, stripe_map, queries, block_kv, groups * slots
    )
    spread = jnp.transpose(new_kv.reshape(count, groups, width), (1, 0, 2))
    fresh = spread[inverse(owner_map[assignment[me[0]]])]
    send = jnp.concatenate([pool[assignment], fresh], axis=1)
    got = lax.all_to_all(send, "pg", split_axis=0, concat_axis=0, tiled=True)
    places = jnp.arange(groups, dtype=jnp.int32) ^ me[0]
    keys = got[places, :slots].reshape(groups * slots, width)
    keys = jnp.concatenate([keys[:, :KV_WIDTH], keys[:, KV_WIDTH:]], axis=0)
    (attended,) = attend(order, rot, bias, new_kv, [keys], 0)
    return attended, got[inverse(assignment), slots:]


def exchange(blocks):
    got = list(blocks)
    half = len(blocks) // 2
    far, near = list(range(half, 2 * half)), list(range(half - 1, 0, -1))
    order = [t for pair in zip(far, near + [None]) for t in pair if t is not None]
    for t in order:
        pairs = [(source, source ^ t) for source in range(len(blocks))]
        got[t] = lax.ppermute(blocks[t], "pg", pairs)
    return got


def shards(queries, block_kv, pool_kv, prefix_len, assignment, stripe_map, owner_map):
    queries, block_kv, pool = queries[0], block_kv[0], pool_kv[0]
    groups, slots, _ = pool.shape
    count = queries.shape[0] // groups
    me = lax.axis_index("pg").astype(jnp.int32).reshape(1)
    if slots % 16 or (2 * count) % 16 or groups > 16:
        attended, decode_kv = small_pieces(
            me, assignment, prefix_len, stripe_map, owner_map, queries, block_kv, pool
        )
        return (attended[None], decode_kv[None])
    got = exchange(front(me, assignment, prefix_len, owner_map, block_kv, pool))
    rot, bias, new_kv, order = rotate_queries(
        me, assignment, prefix_len, stripe_map, queries, block_kv, groups * slots
    )
    attended, decode_kv = attend(order, rot, bias, new_kv, got, count)
    return (attended[None], decode_kv[None])


def solution(mesh):
    return jax.shard_map(
        shards,
        mesh=mesh,
        in_specs=(
            P(("rep", "pg"), None, None),
            P(("rep", "pg"), None, None),
            P(("rep", "pg"), None, None, None),
            P("rep"),
            P("rep"),
            P("rep", None),
            P("rep", None),
        ),
        out_specs=(P(("rep", "pg"), None, None), P(("rep", "pg"), None, None, None)),
        check_vma=False,
    )
```

```python
import functools
import math

import jax
import jax.numpy as jnp
import numpy as np
from jax import lax
from jax.experimental import pallas as pl
from jax.experimental.pallas import tpu as pltpu
from jax.sharding import PartitionSpec as P

Q_HEADS = 32
KV_HEADS = 4
HEAD_DIM = 128
PER_KV = Q_HEADS // KV_HEADS
KV_WIDTH = KV_HEADS * HEAD_DIM
WIDTH = 2 * KV_WIDTH

ROPE_BASE = 1000000.0
MASKED = -1e30
SCALE = HEAD_DIM ** -0.5 / math.log(2.0)
CHUNK = 256
LATE = 4

SMEM = pl.BlockSpec(memory_space=pltpu.SMEM)
VMEM = pl.BlockSpec(memory_space=pltpu.VMEM)
ANY = pl.BlockSpec(memory_space=pl.ANY)


def params(mib):
    return pltpu.CompilerParams(vmem_limit_bytes=mib * 1024 * 1024)


def column(head):
    return slice(head * HEAD_DIM, (head + 1) * HEAD_DIM)


def order_of(groups):
    half = groups // 2
    far, near = list(range(half, 2 * half)), list(range(half - 1, 0, -1))
    order = [0]
    for at in range(half):
        order += far[at : at + 1] + near[at : at + 1]
    return order


def rotation_tables(rows):
    half = HEAD_DIM // 2
    freqs = np.tile(ROPE_BASE ** (-np.arange(half, dtype=np.float64) / half), 2)
    angles = np.arange(rows, dtype=np.float64)[:, None] * freqs[None, :]
    parts = [np.cos(angles), np.sin(angles), np.tile(freqs, (8, 1))]
    return jnp.asarray(np.concatenate(parts, axis=0).astype(np.float32))


def rotation(table_ref, length):
    rows = (table_ref.shape[0] - 8) // 2
    start = length.astype(jnp.float32) * table_ref[2 * rows : 2 * rows + 8, :]
    cos_start, sin_start = jnp.cos(start)[0:1], jnp.sin(start)[0:1]
    cos_row, sin_row = table_ref[0:rows, :], table_ref[rows : 2 * rows, :]
    lane = lax.broadcasted_iota(jnp.int32, (1, HEAD_DIM), 1)
    sign = jnp.where(lane < HEAD_DIM // 2, -1.0, 1.0)
    cosine = cos_row * cos_start - sin_row * sin_start
    return cosine, sin_row * (cos_start * sign) + cos_row * (sin_start * sign)


def turn(x, cosine, sine):
    x = x.astype(jnp.float32)
    return (x * cosine + pltpu.roll(x, HEAD_DIM // 2, 1) * sine).astype(jnp.bfloat16)


def front_kernel(order, me_ref, assign_any, length_any, owner_any, block_any, table_any, pool_any, *refs):
    groups, slots, width = pool_any.shape
    send_refs, refs = refs[:groups], refs[groups:]
    assign_ref, length_ref, owner_ref, residue_ref, block_ref, table_ref, rows_ref, small_sems, pool_sems = refs
    new_count = block_any.shape[0]
    count = new_count // groups
    smalls = [
        pltpu.make_async_copy(assign_any, assign_ref, small_sems.at[0]),
        pltpu.make_async_copy(length_any, length_ref, small_sems.at[1]),
        pltpu.make_async_copy(owner_any, owner_ref, small_sems.at[2]),
        pltpu.make_async_copy(block_any, block_ref, small_sems.at[3]),
        pltpu.make_async_copy(table_any, table_ref, small_sems.at[4]),
    ]
    for copy in smalls:
        copy.start()
    me = me_ref[0]
    smalls[0].wait()

    def pool_copy(p):
        return pltpu.make_async_copy(
            pool_any.at[assign_ref[me ^ order[p]]], send_refs[p].at[:, pl.ds(0, width)], pool_sems.at[p]
        )

    for p in range(groups):
        pool_copy(p).start()
    for copy in smalls[1:]:
        copy.wait()
    request = assign_ref[me]
    for residue in range(groups):
        residue_ref[owner_ref[request, residue]] = residue
    cosine, sine = rotation(table_ref, length_ref[request])
    for head in range(KV_HEADS):
        rows_ref[head] = turn(block_ref[:, column(head)], cosine, sine).astype(jnp.float32)
        rows_ref[KV_HEADS + head] = block_ref[:, column(KV_HEADS + head)].astype(jnp.float32)
    quarter = width * count // slots // HEAD_DIM
    for p in range(groups):
        residue = residue_ref[me ^ order[p]]
        for lanes in range(quarter):
            stack = [
                rows_ref[at + lanes, pl.ds(residue, count, stride=groups), :]
                for at in range(0, 2 * KV_HEADS, quarter)
            ]
            send_refs[p][:, width + lanes * HEAD_DIM : width + (lanes + 1) * HEAD_DIM] = jnp.concatenate(
                stack, axis=0
            ).astype(jnp.bfloat16)
    for p in range(groups):
        pool_copy(p).wait()


def front(order, me, assignment, prefix_len, owner_map, block_kv, table, pool):
    groups, slots, width = pool.shape
    new_count = block_kv.shape[0]
    count = new_count // groups
    block = jax.ShapeDtypeStruct((slots, width + width * count // slots), jnp.bfloat16)
    return pl.pallas_call(
        functools.partial(front_kernel, order),
        out_shape=[block] * groups,
        in_specs=[SMEM] + [ANY] * 6,
        out_specs=[VMEM] * groups,
        scratch_shapes=[
            pltpu.SMEM(assignment.shape, jnp.int32),
            pltpu.SMEM(prefix_len.shape, jnp.int32),
            pltpu.SMEM(owner_map.shape, jnp.int32),
            pltpu.SMEM(assignment.shape, jnp.int32),
            pltpu.VMEM(block_kv.shape, jnp.bfloat16),
            pltpu.VMEM(table.shape, jnp.float32),
            pltpu.VMEM((2 * KV_HEADS, new_count, HEAD_DIM), jnp.float32),
            pltpu.SemaphoreType.DMA((5,)),
            pltpu.SemaphoreType.DMA((groups,)),
        ],
        compiler_params=params(60),
        name="front",
    )(me, assignment, prefix_len, owner_map, block_kv, table, pool)


def query_kernel(
    order, me_ref, assign_ref, length_ref, stripe_ref, q_ref, block_ref, table_ref,
    rot_ref, bias_ref, new_ref, request_ref,
):
    new_count = q_ref.shape[0]
    groups = assign_ref.shape[0]
    span = bias_ref.shape[1]
    slots = span // groups
    me = me_ref[0]
    request = assign_ref[me]
    length = length_ref[request]
    lane = lax.broadcasted_iota(jnp.int32, (8, span), 1)
    piece, slot = lane // slots, lane % slots
    place = lax.broadcasted_iota(jnp.int32, request_ref.shape, 1)
    if order is None:
        holder = piece
    else:
        holder, requests = jnp.zeros_like(piece), jnp.zeros_like(place)
        for p in range(groups):
            holder = jnp.where(piece == p, me ^ order[p], holder)
            requests = jnp.where(place == p, assign_ref[me ^ order[p]], requests)
        request_ref[...] = requests

    def visit(residue, bias):
        live = (holder == stripe_ref[request, residue]) & (slot * groups + residue < length)
        return jnp.where(live, 0.0, bias)

    bias_ref[...] = lax.fori_loop(0, groups, visit, jnp.full((8, span), MASKED, jnp.float32))
    cosine, sine = rotation(table_ref, length)
    for head in range(KV_HEADS):
        new_ref[:, column(head)] = turn(block_ref[:, column(head)], cosine, sine)
    new_ref[:, KV_WIDTH:] = block_ref[:, KV_WIDTH:]
    for head in range(Q_HEADS):
        rows = slice((head % PER_KV) * new_count, (head % PER_KV + 1) * new_count)
        rot_ref[head // PER_KV, rows, :] = turn(q_ref[:, column(head)], cosine, sine)


def rotate_queries(order, me, assignment, prefix_len, stripe_map, queries, block_kv, table, span):
    new_count = queries.shape[0]
    return pl.pallas_call(
        functools.partial(query_kernel, order),
        out_shape=(
            jax.ShapeDtypeStruct((KV_HEADS, PER_KV * new_count, HEAD_DIM), jnp.bfloat16),
            jax.ShapeDtypeStruct((8, span), jnp.float32),
            jax.ShapeDtypeStruct(block_kv.shape, jnp.bfloat16),
            jax.ShapeDtypeStruct((8, HEAD_DIM), jnp.int32),
        ),
        in_specs=[SMEM, SMEM, SMEM, SMEM, VMEM, VMEM, VMEM],
        out_specs=(VMEM, VMEM, VMEM, VMEM),
        compiler_params=params(32),
        name="rotate_queries",
    )(me, assignment, prefix_len, stripe_map, queries, block_kv, table)


def attend_kernel(pieces, first, early, final, unpack, *refs):
    rot_ref, bias_ref, refs = refs[0], refs[1], refs[2:]
    if early:
        (sum_in, total_in, high_in), refs = refs[:3], refs[3:]
    else:
        new_ref, refs = refs[0], refs[1:]
    got_refs, refs = refs[:pieces], refs[pieces:]
    if unpack:
        request_vmem, refs = refs[0], refs[1:]
        if early:
            refs = refs[1:]
    if final:
        out_ref, refs = refs[0], refs[1:]
    else:
        (sum_out, total_out, high_out), refs = refs[:3], refs[3:]
    if unpack:
        (decode_ref, rows_ref, request_ref, request_sem, decode_sems), refs = refs[:5], refs[5:]
        count = rows_ref.shape[1]
        request_copy = pltpu.make_async_copy(request_vmem, request_ref, request_sem)
        request_copy.start()
    if final:
        done_ref, out_sems = refs
        new_count = done_ref.shape[1]
    else:
        new_count = rot_ref.shape[1] // PER_KV
    slots = got_refs[0].shape[0]
    span = pieces * slots
    bias = bias_ref[0:1, first * slots : first * slots + span]
    if not early:
        token = lax.broadcasted_iota(jnp.int32, (CHUNK, new_count), 0) % new_count
        causal = jnp.where(lax.broadcasted_iota(jnp.int32, (CHUNK, new_count), 1) <= token, 0.0, MASKED)
    per_head = PER_KV * new_count // CHUNK
    keys, values = {}, {}

    def scores_of(at):
        head, chunk = divmod(at, per_head)
        if chunk == 0:
            key_parts = [got[:, column(head)] for got in got_refs]
            value_parts = [got[:, column(KV_HEADS + head)] for got in got_refs]
            if not early:
                key_parts.append(new_ref[:, column(head)])
                value_parts.append(new_ref[:, column(KV_HEADS + head)])
            keys[head] = jnp.concatenate(key_parts, axis=0)
            value = jnp.concatenate(value_parts, axis=0)
            values[head] = jnp.concatenate([value, jnp.ones_like(value)], axis=1)
        query = rot_ref[head, chunk * CHUNK : (chunk + 1) * CHUNK, :]
        return lax.dot_general(query, keys[head], (((1,), (1,)), ((), ())), preferred_element_type=jnp.float32)

    def out_copy(head):
        width = PER_KV * HEAD_DIM
        return pltpu.make_async_copy(
            done_ref.at[head], out_ref.at[:, pl.ds(head * width, width)], out_sems.at[head]
        )

    def decode_copy(p):
        return pltpu.make_async_copy(
            rows_ref.at[p], decode_ref.at[request_ref[0, first + p]], decode_sems.at[p]
        )

    total_chunks = KV_HEADS * per_head
    ahead = scores_of(0)
    for at in range(total_chunks):
        scores = ahead
        if at + 1 < total_chunks:
            ahead = scores_of(at + 1)
        head, chunk = divmod(at, per_head)
        rows = slice(chunk * CHUNK, (chunk + 1) * CHUNK)
        if early:
            scores = scores * SCALE + bias
        else:
            scores = jnp.concatenate([scores[:, :span] * SCALE + bias, scores[:, span:] * SCALE + causal], axis=1)
        high = jnp.max(scores, axis=1, keepdims=True)
        if early:
            high_before = high_in[head, rows, :]
            high_joint = jnp.maximum(high_before, high)
            factor = jnp.exp2(high_before - high_joint)
            high = high_joint[:, 0:1]
        weights = jnp.exp2(scores - high).astype(jnp.bfloat16)
        summed = jnp.dot(weights, values[head], preferred_element_type=jnp.float32)
        summed, total = summed[:, :HEAD_DIM], summed[:, HEAD_DIM:]
        if early:
            summed = summed + sum_in[head, rows, :] * factor
            total = total + total_in[head, rows, :] * factor
        if final:
            result = (summed / total).astype(jnp.bfloat16)
            for row in range(CHUNK // new_count):
                done_ref[head, :, column(chunk * (CHUNK // new_count) + row)] = result[
                    row * new_count : (row + 1) * new_count
                ]
            if chunk == per_head - 1:
                out_copy(head).start()
        else:
            sum_out[head, rows, :] = summed
            total_out[head, rows, :] = total
            high_out[head, rows, :] = jnp.broadcast_to(high, (CHUNK, HEAD_DIM))
        if unpack and at == per_head - 1:
            request_copy.wait()
            for p, got in enumerate(got_refs):
                stack = got[:, WIDTH:]
                quarter = stack.shape[1]
                for part in range(slots // count):
                    rows_ref[p, :, part * quarter : (part + 1) * quarter] = stack[
                        part * count : (part + 1) * count
                    ]
                decode_copy(p).start()
    if unpack:
        for p in range(pieces):
            decode_copy(p).wait()
    if final:
        for head in range(KV_HEADS):
            out_copy(head).wait()


def attend(rot, bias, new_kv, got, first=0, sums=None, final=True, requests=None, decode=None):
    rows = rot.shape[1]
    new_count = rows // PER_KV
    pieces = len(got)
    early, unpack = sums is not None, requests is not None
    operands = [rot, bias] + (list(sums) if early else [new_kv]) + list(got)
    specs = [VMEM] * len(operands)
    shapes, out_specs, scratch, aliases = [], [], [], {}
    if unpack:
        operands.append(requests)
        specs.append(VMEM)
        if early:
            operands.append(decode)
            specs.append(ANY)
            aliases = {len(operands) - 1: 1 if final else 3}
    if final:
        shapes.append(jax.ShapeDtypeStruct((new_count, Q_HEADS * HEAD_DIM), jnp.bfloat16))
        out_specs.append(ANY)
    else:
        shapes += [jax.ShapeDtypeStruct((KV_HEADS, rows, HEAD_DIM), jnp.float32)] * 3
        out_specs += [VMEM] * 3
    if unpack:
        slots = got[0].shape[0]
        count = (got[0].shape[1] - WIDTH) * slots // WIDTH
        shapes.append(jax.ShapeDtypeStruct((new_count // count, count, WIDTH), jnp.bfloat16))
        out_specs.append(ANY)
        scratch += [
            pltpu.VMEM((pieces, count, WIDTH), jnp.bfloat16),
            pltpu.SMEM(requests.shape, jnp.int32),
            pltpu.SemaphoreType.DMA,
            pltpu.SemaphoreType.DMA((pieces,)),
        ]
    if final:
        scratch += [
            pltpu.VMEM((KV_HEADS, new_count, PER_KV * HEAD_DIM), jnp.bfloat16),
            pltpu.SemaphoreType.DMA((KV_HEADS,)),
        ]
    return pl.pallas_call(
        functools.partial(attend_kernel, pieces, first, early, final, unpack),
        out_shape=tuple(shapes),
        in_specs=specs,
        out_specs=tuple(out_specs),
        scratch_shapes=scratch,
        input_output_aliases=aliases,
        compiler_params=params(32),
        name="attend_late" if early else "attend",
    )(*operands)


def inverse(table):
    places = jnp.arange(table.shape[0], dtype=jnp.int32)
    return jnp.sum(jnp.where(table[None, :] == places[:, None], places, 0), axis=1)


def small_pieces(me, assignment, prefix_len, stripe_map, owner_map, queries, block_kv, table, pool):
    groups, slots, width = pool.shape
    count = block_kv.shape[0] // groups
    rot, bias, new_kv, _ = rotate_queries(
        None, me, assignment, prefix_len, stripe_map, queries, block_kv, table, groups * slots
    )
    spread = jnp.transpose(new_kv.reshape(count, groups, width), (1, 0, 2))
    fresh = spread[inverse(owner_map[assignment[me[0]]])]
    send = jnp.concatenate([pool[assignment], fresh], axis=1)
    got = lax.all_to_all(send, "pg", split_axis=0, concat_axis=0, tiled=True)
    keys = got[:, :slots].reshape(groups * slots, width)
    (attended,) = attend(rot, bias, new_kv, [keys])
    return attended, got[inverse(assignment), slots:]


def shards(queries, block_kv, pool_kv, prefix_len, assignment, stripe_map, owner_map):
    queries, block_kv, pool = queries[0], block_kv[0], pool_kv[0]
    groups, slots, _ = pool.shape
    new_count = queries.shape[0]
    count = new_count // groups
    me = lax.axis_index("pg").astype(jnp.int32).reshape(1)
    table = rotation_tables(new_count)
    if slots % 16 or count % 8 or slots % count or groups != 16:
        attended, decode_kv = small_pieces(
            me, assignment, prefix_len, stripe_map, owner_map, queries, block_kv, table, pool
        )
        return (attended[None], decode_kv[None])
    order = order_of(groups)
    blocks = front(order, me, assignment, prefix_len, owner_map, block_kv, table, pool)
    got = [blocks[0]]
    for p in range(1, groups):
        pairs = [(source, source ^ order[p]) for source in range(groups)]
        got.append(lax.ppermute(blocks[p], "pg", pairs))
    rot, bias, new_kv, requests = rotate_queries(
        order, me, assignment, prefix_len, stripe_map, queries, block_kv, table, groups * slots
    )
    soon = groups - LATE
    *sums, decode_kv = attend(rot, bias, new_kv, got[:soon], final=False, requests=requests)
    attended, decode_kv = attend(
        rot, bias, new_kv, got[soon:], first=soon, sums=sums, requests=requests, decode=decode_kv
    )
    return (attended[None], decode_kv[None])


def solution(mesh):
    return jax.shard_map(
        shards,
        mesh=mesh,
        in_specs=(
            P(("rep", "pg"), None, None),
            P(("rep", "pg"), None, None),
            P(("rep", "pg"), None, None, None),
            P("rep"),
            P("rep"),
            P("rep", None),
            P("rep", None),
        ),
        out_specs=(P(("rep", "pg"), None, None), P(("rep", "pg"), None, None, None)),
        check_vma=False,
    )
```

```python
import functools
import math

import jax
import jax.numpy as jnp
import numpy as np
from jax import lax
from jax.experimental import pallas as pl
from jax.experimental.pallas import tpu as pltpu
from jax.sharding import PartitionSpec as P

Q_HEADS = 32
KV_HEADS = 4
HEAD_DIM = 128
PER_KV = Q_HEADS // KV_HEADS
KV_WIDTH = KV_HEADS * HEAD_DIM
WIDTH = 2 * KV_WIDTH

ROPE_BASE = 1000000.0
MASKED = -1e30
SCALE = HEAD_DIM ** -0.5 / math.log(2.0)
CHUNK = 256
LATE = 4
LATE_CHUNK = 512
AHEAD = 4

SMEM = pl.BlockSpec(memory_space=pltpu.SMEM)
VMEM = pl.BlockSpec(memory_space=pltpu.VMEM)
ANY = pl.BlockSpec(memory_space=pl.ANY)


def params(mib):
    return pltpu.CompilerParams(vmem_limit_bytes=mib * 1024 * 1024)


def column(head):
    return slice(head * HEAD_DIM, (head + 1) * HEAD_DIM)


def order_of(groups):
    half = groups // 2
    far, near = list(range(half, 2 * half)), list(range(half - 1, 0, -1))
    order = []
    for at in range(half):
        order += far[at : at + 1] + near[at : at + 1]
    order.insert(groups - LATE - 1, 0)
    return order


def rotation_tables(rows):
    half = HEAD_DIM // 2
    freqs = np.tile(ROPE_BASE ** (-np.arange(half, dtype=np.float64) / half), 2)
    angles = np.arange(rows, dtype=np.float64)[:, None] * freqs[None, :]
    parts = [np.cos(angles), np.sin(angles), np.tile(freqs, (8, 1))]
    return jnp.asarray(np.concatenate(parts, axis=0).astype(np.float32))


def rotation(table_ref, length):
    rows = (table_ref.shape[0] - 8) // 2
    start = length.astype(jnp.float32) * table_ref[2 * rows : 2 * rows + 8, :]
    cos_start, sin_start = jnp.cos(start)[0:1], jnp.sin(start)[0:1]
    cos_row, sin_row = table_ref[0:rows, :], table_ref[rows : 2 * rows, :]
    lane = lax.broadcasted_iota(jnp.int32, (1, HEAD_DIM), 1)
    sign = jnp.where(lane < HEAD_DIM // 2, -1.0, 1.0)
    cosine = cos_row * cos_start - sin_row * sin_start
    return cosine, sin_row * (cos_start * sign) + cos_row * (sin_start * sign)


def turn(x, cosine, sine):
    x = x.astype(jnp.float32)
    return (x * cosine + pltpu.roll(x, HEAD_DIM // 2, 1) * sine).astype(jnp.bfloat16)


def info_rows(groups, slots, new_count, spare):
    sizes = [
        ("cos", new_count),
        ("sin", new_count),
        ("bias", 8),
        ("request", 8),
        ("new", 2 * KV_HEADS * new_count),
        ("own", 2 * KV_HEADS * slots),
        ("fresh", spare * slots),
    ]
    at, rows = 0, {}
    for name, size in sizes:
        rows[name] = at
        at += size
    return rows, at


def front_kernel(
    order, me_ref, assign_any, length_any, owner_any, stripe_any, block_any, table_any, pool_any, *refs
):
    groups, slots, width = pool_any.shape
    send_refs, info_any, refs = refs[: groups - 1], refs[groups - 1], refs[groups:]
    (assign_ref, length_ref, owner_ref, stripe_ref, residue_ref, block_ref, table_ref, pool_ref, pack_ref, info_ref,
     small_sems, pool_sems, send_sems, info_sem) = refs
    new_count = block_any.shape[0]
    count = new_count // groups
    quarter = width * count // slots // HEAD_DIM
    at, _ = info_rows(groups, slots, new_count, quarter)
    pool_copies = [
        pltpu.make_async_copy(pool_any.at[pl.ds(r, 4)], pool_ref.at[pl.ds(r, 4)], pool_sems.at[r // 4])
        for r in range(0, groups, 4)
    ]
    pairs = [
        (length_any, length_ref), (assign_any, assign_ref), (owner_any, owner_ref), (stripe_any, stripe_ref),
        (block_any, block_ref), (table_any, table_ref),
    ]
    smalls = [pltpu.make_async_copy(*pair, small_sems.at[i]) for i, pair in enumerate(pairs)]
    for copy in smalls + pool_copies:
        copy.start()
    me = me_ref[0]
    for copy in smalls:
        copy.wait()
    request = assign_ref[me]
    length = length_ref[request]
    for residue in range(groups):
        residue_ref[owner_ref[request, residue]] = residue
    cosine, sine = rotation(table_ref, length)
    for head in range(KV_HEADS):
        rows = at["new"] + head * new_count
        info_ref[rows : rows + new_count] = turn(block_ref[:, column(head)], cosine, sine).astype(jnp.float32)
        rows += KV_HEADS * new_count
        info_ref[rows : rows + new_count] = block_ref[:, column(KV_HEADS + head)].astype(jnp.float32)

    def fresh_rows(p, lanes):
        residue = residue_ref[me ^ order[p]]
        stack = [
            info_ref[pl.ds(at["new"] + (base + lanes) * new_count + residue, count, stride=groups), :]
            for base in range(0, 2 * KV_HEADS, quarter)
        ]
        return jnp.concatenate(stack, axis=0)

    for copy in pool_copies:
        copy.wait()
    sends = []
    for p in range(groups):
        if order[p] == 0:
            continue
        slot = len(sends)
        pack_ref[slot, :, 0:width] = pool_ref[assign_ref[me ^ order[p]]]
        for lanes in range(quarter):
            pack_ref[slot, :, width + lanes * HEAD_DIM : width + (lanes + 1) * HEAD_DIM] = fresh_rows(
                p, lanes
            ).astype(jnp.bfloat16)
        sends.append(pltpu.make_async_copy(pack_ref.at[slot], send_refs[slot], send_sems.at[slot]))
        sends[-1].start()
    info_ref[at["cos"] : at["cos"] + new_count] = cosine
    info_ref[at["sin"] : at["sin"] + new_count] = sine
    mine = pool_ref[request]
    for head in range(2 * KV_HEADS):
        rows = at["own"] + head * slots
        info_ref[rows : rows + slots] = mine[:, column(head)].astype(jnp.float32)
    for lanes in range(quarter):
        rows = at["fresh"] + lanes * slots
        info_ref[rows : rows + slots] = fresh_rows(order.index(0), lanes)
    per_row = HEAD_DIM // slots
    row = lax.broadcasted_iota(jnp.int32, (8, HEAD_DIM), 0)
    lane = lax.broadcasted_iota(jnp.int32, (8, HEAD_DIM), 1)
    piece, slot = row * per_row + lane // slots, lane % slots
    holder, requests = jnp.zeros_like(lane), jnp.zeros_like(lane)
    for p in range(groups):
        holder = jnp.where(piece == p, me ^ order[p], holder)
        requests = jnp.where(lane == p, assign_ref[me ^ order[p]], requests)
    bias = jnp.full((8, HEAD_DIM), MASKED, jnp.float32)
    for residue in range(groups):
        live = (holder == stripe_ref[request, residue]) & (slot * groups + residue < length)
        bias = jnp.where(live, 0.0, bias)
    info_ref[at["bias"] : at["bias"] + 8] = bias
    info_ref[at["request"] : at["request"] + 8] = requests.astype(jnp.float32)
    info_copy = pltpu.make_async_copy(info_ref, info_any, info_sem)
    info_copy.start()
    for copy in sends:
        copy.wait()
    info_copy.wait()


def front(order, me, assignment, prefix_len, owner_map, stripe_map, block_kv, table, pool):
    groups, slots, width = pool.shape
    new_count = block_kv.shape[0]
    count = new_count // groups
    block = jax.ShapeDtypeStruct((slots, width + width * count // slots), jnp.bfloat16)
    _, rows = info_rows(groups, slots, new_count, width * count // slots // HEAD_DIM)
    info = jax.ShapeDtypeStruct((rows, HEAD_DIM), jnp.float32)
    *blocks, info = pl.pallas_call(
        functools.partial(front_kernel, order),
        out_shape=[block] * (groups - 1) + [info],
        in_specs=[SMEM] + [ANY] * 7,
        out_specs=[ANY] * groups,
        scratch_shapes=[
            pltpu.SMEM(assignment.shape, jnp.int32),
            pltpu.SMEM(prefix_len.shape, jnp.int32),
            pltpu.SMEM(owner_map.shape, jnp.int32),
            pltpu.SMEM(stripe_map.shape, jnp.int32),
            pltpu.SMEM(assignment.shape, jnp.int32),
            pltpu.VMEM(block_kv.shape, jnp.bfloat16),
            pltpu.VMEM(table.shape, jnp.float32),
            pltpu.VMEM(pool.shape, jnp.bfloat16),
            pltpu.VMEM((groups - 1,) + block.shape, jnp.bfloat16),
            pltpu.VMEM(info.shape, jnp.float32),
            pltpu.SemaphoreType.DMA((6,)),
            pltpu.SemaphoreType.DMA((groups // 4,)),
            pltpu.SemaphoreType.DMA((groups - 1,)),
            pltpu.SemaphoreType.DMA,
        ],
        compiler_params=params(60),
        name="front",
    )(me, assignment, prefix_len, owner_map, stripe_map, block_kv, table, pool)
    return blocks, info


def query_kernel(at, info_ref, q_ref, rot_ref, own_ref, fresh_ref, bias_ref, request_ref):
    new_count = q_ref.shape[0]
    slots = fresh_ref.shape[0]
    cosine = info_ref[at["cos"] : at["cos"] + new_count]
    sine = info_ref[at["sin"] : at["sin"] + new_count]
    for lanes in range(fresh_ref.shape[1] // HEAD_DIM):
        rows = at["fresh"] + lanes * slots
        fresh_ref[:, column(lanes)] = info_ref[rows : rows + slots].astype(jnp.bfloat16)
    for row in range(bias_ref.shape[1] // HEAD_DIM):
        line = info_ref[at["bias"] + row : at["bias"] + row + 1]
        bias_ref[:, column(row)] = jnp.broadcast_to(line, (8, HEAD_DIM))
    request_ref[...] = info_ref[at["request"] : at["request"] + 8].astype(jnp.int32)
    for head in range(2 * KV_HEADS):
        rows = at["own"] + head * slots
        own_ref[head, 0:slots] = info_ref[rows : rows + slots].astype(jnp.bfloat16)
        rows = at["new"] + head * new_count
        own_ref[head, slots : slots + new_count] = info_ref[rows : rows + new_count].astype(jnp.bfloat16)
    for head in range(Q_HEADS):
        rows = slice((head % PER_KV) * new_count, (head % PER_KV + 1) * new_count)
        rot_ref[head // PER_KV, rows, :] = turn(q_ref[:, column(head)], cosine, sine)


def rotate_queries(info, queries, groups, slots, spare):
    new_count = queries.shape[0]
    at, _ = info_rows(groups, slots, new_count, spare)
    return pl.pallas_call(
        functools.partial(query_kernel, at),
        out_shape=(
            jax.ShapeDtypeStruct((KV_HEADS, PER_KV * new_count, HEAD_DIM), jnp.bfloat16),
            jax.ShapeDtypeStruct((2 * KV_HEADS, slots + new_count, HEAD_DIM), jnp.bfloat16),
            jax.ShapeDtypeStruct((slots, spare * HEAD_DIM), jnp.bfloat16),
            jax.ShapeDtypeStruct((8, groups * slots), jnp.float32),
            jax.ShapeDtypeStruct((8, HEAD_DIM), jnp.int32),
        ),
        in_specs=[VMEM, VMEM],
        out_specs=[VMEM] * 5,
        compiler_params=params(32),
        name="rotate_queries",
    )(info, queries)


def attend_kernel(pieces, first, early, final, unpack, size, *refs):
    rot_ref, bias_ref, refs = refs[0], refs[1], refs[2:]
    if early:
        (sum_in, total_in, high_in), refs = refs[:3], refs[3:]
    else:
        own_ref, refs = refs[0], refs[1:]
    got_refs, refs = refs[:pieces], refs[pieces:]
    fresh_refs = [got.at[:, pl.ds(WIDTH, got.shape[1] - WIDTH)] for got in got_refs] if unpack else []
    if unpack:
        request_vmem, refs = refs[0], refs[1:]
        if early:
            refs = refs[1:]
        else:
            fresh_refs, refs = fresh_refs + [refs[0]], refs[1:]
    if final:
        out_ref, refs = refs[0], refs[1:]
    else:
        (sum_out, total_out, high_out), refs = refs[:3], refs[3:]
    if unpack:
        (decode_ref, rows_ref, request_ref, request_sem, decode_sems), refs = refs[:5], refs[5:]
        count = rows_ref.shape[1]
        request_copy = pltpu.make_async_copy(request_vmem, request_ref, request_sem)
        request_copy.start()
    if final:
        done_ref, out_sems = refs
    new_count = rot_ref.shape[1] // PER_KV
    slots = got_refs[0].shape[0]
    span = pieces * slots
    if not early:
        span += own_ref.shape[1] - new_count
        token = lax.broadcasted_iota(jnp.int32, (size, new_count), 0) % new_count
        causal = jnp.where(lax.broadcasted_iota(jnp.int32, (size, new_count), 1) <= token, 0.0, MASKED)
    bias = bias_ref[0:1, first * slots : first * slots + span]
    per_head = PER_KV * new_count // size
    total_chunks = KV_HEADS * per_head
    heads_in = size // new_count
    keys, values = {}, {}
    scores, weights, factors = {}, {}, {}

    def place(at):
        head, chunk = divmod(at, per_head)
        return head, chunk, slice(chunk * size, (chunk + 1) * size)

    def score(at):
        head, chunk, rows = place(at)
        if chunk == 0:
            key_parts = [got[:, column(head)] for got in got_refs]
            value_parts = [got[:, column(KV_HEADS + head)] for got in got_refs]
            if not early:
                key_parts.append(own_ref[head])
                value_parts.append(own_ref[KV_HEADS + head])
            keys[head] = jnp.concatenate(key_parts, axis=0)
            value = jnp.concatenate(value_parts, axis=0)
            values[head] = jnp.concatenate([value, jnp.ones_like(value)], axis=1)
        scores[at] = lax.dot_general(
            rot_ref[head, rows, :], keys[head], (((1,), (1,)), ((), ())), preferred_element_type=jnp.float32
        )

    def weigh(at):
        head, chunk, rows = place(at)
        values_at = scores.pop(at)
        if early:
            values_at = values_at * SCALE + bias
        else:
            values_at = jnp.concatenate(
                [values_at[:, :span] * SCALE + bias, values_at[:, span:] * SCALE + causal], axis=1
            )
        high = jnp.max(values_at, axis=1, keepdims=True)
        if early:
            high_before = high_in[head, rows, :]
            high = jnp.maximum(high_before, high)
            factors[at] = jnp.exp2(high_before - high)
            high = high[:, 0:1]
        else:
            high_out_at = jnp.broadcast_to(high, (size, HEAD_DIM))
            if not final:
                high_out[head, rows, :] = high_out_at
        weights[at] = jnp.exp2(values_at - high).astype(jnp.bfloat16)

    def out_copy(at):
        head, chunk, rows = place(at)
        width = heads_in * HEAD_DIM
        return pltpu.make_async_copy(
            done_ref.at[at], out_ref.at[:, pl.ds(at * width, width)], out_sems.at[at]
        )

    def finish(at, summed):
        head, chunk, rows = place(at)
        summed, total = summed[:, :HEAD_DIM], summed[:, HEAD_DIM:]
        if early:
            factor = factors.pop(at)
            summed = summed + sum_in[head, rows, :] * factor
            total = total + total_in[head, rows, :] * factor
        if not final:
            sum_out[head, rows, :] = summed
            total_out[head, rows, :] = total
            return
        about = pl.reciprocal(total, approx=True)
        result = (summed * (about * (2.0 - total * about))).astype(jnp.bfloat16)
        for row in range(heads_in):
            done_ref[at, :, column(row)] = result[row * new_count : (row + 1) * new_count]
        out_copy(at).start()

    def decode_copy(p):
        return pltpu.make_async_copy(
            rows_ref.at[p], decode_ref.at[request_ref[0, first + p]], decode_sems.at[p]
        )

    score(0)
    for at in range(total_chunks + 1):
        if at + 1 < total_chunks:
            score(at + 1)
        if at >= 1:
            summed = jnp.dot(
                weights.pop(at - 1), values[(at - 1) // per_head], preferred_element_type=jnp.float32
            )
        if at < total_chunks:
            weigh(at)
        if at >= 1:
            finish(at - 1, summed)
        if unpack and at == 1:
            request_copy.wait()
            for p, fresh_ref in enumerate(fresh_refs):
                stack = fresh_ref[...]
                quarter = stack.shape[1]
                for part in range(stack.shape[0] // count):
                    rows_ref[p, :, part * quarter : (part + 1) * quarter] = stack[
                        part * count : (part + 1) * count
                    ]
                decode_copy(p).start()
    for p in range(len(fresh_refs)):
        decode_copy(p).wait()
    if final:
        for at in range(total_chunks):
            out_copy(at).wait()


def attend(rot, bias, own, got, first=0, sums=None, final=True, requests=None, fresh=None, decode=None, size=CHUNK):
    rows = rot.shape[1]
    new_count = rows // PER_KV
    pieces = len(got)
    early, unpack = sums is not None, requests is not None
    operands = [rot, bias] + (list(sums) if early else [own]) + list(got)
    specs = [VMEM] * len(operands)
    shapes, out_specs, scratch, aliases = [], [], [], {}
    if unpack:
        operands.append(requests)
        specs.append(VMEM)
        if early:
            operands.append(decode)
            specs.append(ANY)
            aliases = {len(operands) - 1: 1 if final else 3}
        else:
            operands.append(fresh)
            specs.append(VMEM)
    if final:
        shapes.append(jax.ShapeDtypeStruct((new_count, Q_HEADS * HEAD_DIM), jnp.bfloat16))
        out_specs.append(ANY)
    else:
        shapes += [jax.ShapeDtypeStruct((KV_HEADS, rows, HEAD_DIM), jnp.float32)] * 3
        out_specs += [VMEM] * 3
    if unpack:
        slots = got[0].shape[0]
        count = (got[0].shape[1] - WIDTH) * slots // WIDTH
        unpacked = pieces if early else pieces + 1
        shapes.append(jax.ShapeDtypeStruct((new_count // count, count, WIDTH), jnp.bfloat16))
        out_specs.append(ANY)
        scratch += [
            pltpu.VMEM((unpacked, count, WIDTH), jnp.bfloat16),
            pltpu.SMEM(requests.shape, jnp.int32),
            pltpu.SemaphoreType.DMA,
            pltpu.SemaphoreType.DMA((unpacked,)),
        ]
    if final:
        chunks = KV_HEADS * rows // size
        scratch += [
            pltpu.VMEM((chunks, new_count, size // new_count * HEAD_DIM), jnp.bfloat16),
            pltpu.SemaphoreType.DMA((chunks,)),
        ]
    return pl.pallas_call(
        functools.partial(attend_kernel, pieces, first, early, final, unpack, size),
        out_shape=tuple(shapes),
        in_specs=specs,
        out_specs=tuple(out_specs),
        scratch_shapes=scratch,
        input_output_aliases=aliases,
        compiler_params=params(32),
        name="attend_late" if early else "attend",
    )(*operands)


def inverse(table):
    places = jnp.arange(table.shape[0], dtype=jnp.int32)
    return jnp.sum(jnp.where(table[None, :] == places[:, None], places, 0), axis=1)


def rotate(rows, positions, heads):
    half = HEAD_DIM // 2
    freqs = ROPE_BASE ** (-jnp.arange(half, dtype=jnp.float32) / half)
    angles = positions.astype(jnp.float32)[:, None] * freqs[None, :]
    cosine = jnp.concatenate([jnp.cos(angles)] * 2, axis=-1)[:, None, :]
    sine = jnp.concatenate([-jnp.sin(angles), jnp.sin(angles)], axis=-1)[:, None, :]
    split = rows.astype(jnp.float32).reshape(rows.shape[0], heads, HEAD_DIM)
    turned = jnp.roll(split, half, axis=-1)
    return (split * cosine + turned * sine).astype(jnp.bfloat16)


def small_pieces(me, assignment, prefix_len, stripe_map, owner_map, queries, block_kv, pool):
    groups, slots, width = pool.shape
    new_count = block_kv.shape[0]
    count = new_count // groups
    request = assignment[me[0]]
    length = prefix_len[request]
    positions = length + jnp.arange(new_count, dtype=jnp.int32)
    rot = rotate(queries, positions, Q_HEADS).reshape(new_count, KV_HEADS, PER_KV, HEAD_DIM)
    rot = jnp.transpose(rot, (1, 2, 0, 3)).reshape(KV_HEADS, PER_KV * new_count, HEAD_DIM)
    new_keys = rotate(block_kv[:, :KV_WIDTH], positions, KV_HEADS).reshape(new_count, KV_WIDTH)
    new_kv = jnp.concatenate([new_keys, block_kv[:, KV_WIDTH:]], axis=1)
    own = jnp.transpose(new_kv.reshape(new_count, 2 * KV_HEADS, HEAD_DIM), (1, 0, 2))
    spread = jnp.transpose(new_kv.reshape(count, groups, width), (1, 0, 2))
    send = jnp.concatenate([pool[assignment], spread[inverse(owner_map[request])]], axis=1)
    got = lax.all_to_all(send, "pg", split_axis=0, concat_axis=0, tiled=True)
    located = jnp.arange(slots, dtype=jnp.int32)[None, :] * groups + inverse(stripe_map[request])[:, None]
    bias = jnp.where(located < length, 0.0, MASKED).astype(jnp.float32).reshape(1, groups * slots)
    keys = got[:, :slots].reshape(groups * slots, width)
    (attended,) = attend(rot, jnp.broadcast_to(bias, (8, groups * slots)), own, [keys])
    return attended, got[inverse(assignment), slots:]


def shards(queries, block_kv, pool_kv, prefix_len, assignment, stripe_map, owner_map):
    queries, block_kv, pool = queries[0], block_kv[0], pool_kv[0]
    groups, slots, width = pool.shape
    new_count = queries.shape[0]
    count = new_count // groups
    me = lax.axis_index("pg").astype(jnp.int32).reshape(1)
    if groups != 16 or slots % 16 or HEAD_DIM % slots or count % 8 or slots % count:
        attended, decode_kv = small_pieces(
            me, assignment, prefix_len, stripe_map, owner_map, queries, block_kv, pool
        )
        return (attended[None], decode_kv[None])
    order = order_of(groups)
    table = rotation_tables(new_count)
    blocks, info = front(order, me, assignment, prefix_len, owner_map, stripe_map, block_kv, table, pool)
    spare = width * count // slots // HEAD_DIM
    rot, own, fresh, bias, requests = rotate_queries(info, queries, groups, slots, spare)
    rot, *later = lax.optimization_barrier((rot, *blocks[AHEAD:]))
    got = []
    for block, t in zip(blocks[:AHEAD] + list(later), [t for t in order if t]):
        got.append(lax.ppermute(block, "pg", [(source, source ^ t) for source in range(groups)]))
    soon = groups - LATE - 1
    *sums, decode_kv = attend(rot, bias, own, got[:soon], final=False, requests=requests, fresh=fresh)
    attended, decode_kv = attend(
        rot, bias, None, got[soon:], first=soon + 1, sums=sums, requests=requests, decode=decode_kv, size=LATE_CHUNK
    )
    return (attended[None], decode_kv[None])


def solution(mesh):
    return jax.shard_map(
        shards,
        mesh=mesh,
        in_specs=(
            P(("rep", "pg"), None, None),
            P(("rep", "pg"), None, None),
            P(("rep", "pg"), None, None, None),
            P("rep"),
            P("rep"),
            P("rep", None),
            P("rep", None),
        ),
        out_specs=(P(("rep", "pg"), None, None), P(("rep", "pg"), None, None, None)),
        check_vma=False,
    )
```

```python
import functools
import math

import jax
import jax.numpy as jnp
import numpy as np
from jax import lax
from jax.experimental import pallas as pl
from jax.experimental.pallas import tpu as pltpu
from jax.sharding import PartitionSpec as P

Q_HEADS = 32
KV_HEADS = 4
HEAD_DIM = 128
PER_KV = Q_HEADS // KV_HEADS
KV_WIDTH = KV_HEADS * HEAD_DIM
WIDTH = 2 * KV_WIDTH

ROPE_BASE = 1000000.0
MASKED = -1e30
SCALE = HEAD_DIM ** -0.5 / math.log(2.0)
CHUNK = 256
LATE = 4
LATE_CHUNK = 256
AHEAD = 4

SMEM = pl.BlockSpec(memory_space=pltpu.SMEM)
VMEM = pl.BlockSpec(memory_space=pltpu.VMEM)
ANY = pl.BlockSpec(memory_space=pl.ANY)


def params(mib):
    return pltpu.CompilerParams(vmem_limit_bytes=mib * 1024 * 1024)


def column(head):
    return slice(head * HEAD_DIM, (head + 1) * HEAD_DIM)


def order_of(groups):
    half = groups // 2
    far, near = list(range(half, 2 * half)), list(range(half - 1, 0, -1))
    order = [(far if kind == "f" else near).pop(0) for kind in "fffnfnfnfnnffnn"]
    order.insert(groups - LATE - 1, 0)
    return order


def rotation_tables(rows):
    half = HEAD_DIM // 2
    freqs = np.tile(ROPE_BASE ** (-np.arange(half, dtype=np.float64) / half), 2)
    angles = np.arange(rows, dtype=np.float64)[:, None] * freqs[None, :]
    parts = [np.cos(angles), np.sin(angles), np.tile(freqs, (8, 1))]
    return jnp.asarray(np.concatenate(parts, axis=0).astype(np.float32))


def rotation(table_ref, length):
    rows = (table_ref.shape[0] - 8) // 2
    start = length.astype(jnp.float32) * table_ref[2 * rows : 2 * rows + 8, :]
    cos_start, sin_start = jnp.cos(start)[0:1], jnp.sin(start)[0:1]
    cos_row, sin_row = table_ref[0:rows, :], table_ref[rows : 2 * rows, :]
    lane = lax.broadcasted_iota(jnp.int32, (1, HEAD_DIM), 1)
    sign = jnp.where(lane < HEAD_DIM // 2, -1.0, 1.0)
    cosine = cos_row * cos_start - sin_row * sin_start
    return cosine, sin_row * (cos_start * sign) + cos_row * (sin_start * sign)


def turn(x, cosine, sine):
    x = x.astype(jnp.float32)
    return (x * cosine + pltpu.roll(x, HEAD_DIM // 2, 1) * sine).astype(jnp.bfloat16)


def info_rows(new_count):
    sizes = [("cos", new_count), ("sin", new_count), ("bias", 8), ("scalars", 8), ("new", 2 * KV_HEADS * new_count)]
    at, rows = 0, {}
    for name, size in sizes:
        rows[name] = at
        at += size
    return rows, at


def fresh_rows(info_ref, base, residue, new_count, count, quarter, lanes):
    groups = new_count // count
    stack = [
        info_ref[pl.ds(base + (head + lanes) * new_count + residue, count, stride=groups), :]
        for head in range(0, 2 * KV_HEADS, quarter)
    ]
    return jnp.concatenate(stack, axis=0)


def front_kernel(
    order, me_ref, assign_any, length_any, owner_any, stripe_any, block_any, table_any, pool_any, *refs
):
    groups, slots, width = pool_any.shape
    send_refs, info_any, refs = refs[:AHEAD], refs[AHEAD], refs[AHEAD + 1 :]
    (assign_ref, length_ref, owner_ref, stripe_ref, residue_ref, block_ref, table_ref, pack_ref, info_ref,
     small_sems, pool_sems, send_sems, info_sems) = refs
    new_count = block_any.shape[0]
    count = new_count // groups
    quarter = width * count // slots // HEAD_DIM
    at, rows = info_rows(new_count)
    pairs = [
        (assign_any, assign_ref), (length_any, length_ref), (owner_any, owner_ref), (stripe_any, stripe_ref),
        (block_any, block_ref), (table_any, table_ref),
    ]
    smalls = [pltpu.make_async_copy(*pair, small_sems.at[i]) for i, pair in enumerate(pairs)]
    for copy in smalls:
        copy.start()
    me = me_ref[0]
    smalls[0].wait()
    pool_copies = [
        pltpu.make_async_copy(
            pool_any.at[assign_ref[me ^ order[p]]], pack_ref.at[p, :, pl.ds(0, width)], pool_sems.at[p]
        )
        for p in range(AHEAD)
    ]
    for copy in pool_copies:
        copy.start()
    for copy in smalls[1:]:
        copy.wait()
    request = assign_ref[me]
    length = length_ref[request]
    for residue in range(groups):
        residue_ref[owner_ref[request, residue]] = residue
    cosine, sine = rotation(table_ref, length)
    for head in range(KV_HEADS):
        low = at["new"] + head * new_count
        info_ref[low : low + new_count] = turn(block_ref[:, column(head)], cosine, sine).astype(jnp.float32)
        low += KV_HEADS * new_count
        info_ref[low : low + new_count] = block_ref[:, column(KV_HEADS + head)].astype(jnp.float32)

    def info_copy(part, low, high):
        part_rows = pl.ds(low, high - low)
        return pltpu.make_async_copy(info_ref.at[part_rows], info_any.at[part_rows], info_sems.at[part])

    info_copy(0, at["new"], rows).start()
    sends = []
    for p in range(AHEAD):
        for lanes in range(quarter):
            pack_ref[p, :, width + lanes * HEAD_DIM : width + (lanes + 1) * HEAD_DIM] = fresh_rows(
                info_ref, at["new"], residue_ref[me ^ order[p]], new_count, count, quarter, lanes
            ).astype(jnp.bfloat16)
        pool_copies[p].wait()
        sends.append(pltpu.make_async_copy(pack_ref.at[p], send_refs[p], send_sems.at[p]))
        sends[-1].start()
    info_ref[at["cos"] : at["cos"] + new_count] = cosine
    info_ref[at["sin"] : at["sin"] + new_count] = sine
    per_row = HEAD_DIM // slots
    row = lax.broadcasted_iota(jnp.int32, (8, HEAD_DIM), 0)
    lane = lax.broadcasted_iota(jnp.int32, (8, HEAD_DIM), 1)
    piece, slot = row * per_row + lane // slots, lane % slots
    holder, requests, residues = jnp.zeros_like(lane), jnp.zeros_like(lane), jnp.zeros_like(lane)
    for p in range(groups):
        other = me ^ order[p]
        holder = jnp.where(piece == p, other, holder)
        requests = jnp.where(lane == p, assign_ref[other], requests)
        residues = jnp.where(lane == p, residue_ref[other], residues)
    bias = jnp.full((8, HEAD_DIM), MASKED, jnp.float32)
    for residue in range(groups):
        live = (holder == stripe_ref[request, residue]) & (slot * groups + residue < length)
        bias = jnp.where(live, 0.0, bias)
    info_ref[at["bias"] : at["bias"] + 8] = bias
    scalars = jnp.where(row == 0, requests, residues)
    info_ref[at["scalars"] : at["scalars"] + 8] = scalars.astype(jnp.float32)
    info_copy(1, 0, at["new"]).start()
    for copy in sends:
        copy.wait()
    info_copy(0, at["new"], rows).wait()
    info_copy(1, 0, at["new"]).wait()


def front(order, me, assignment, prefix_len, owner_map, stripe_map, block_kv, table, pool):
    groups, slots, width = pool.shape
    new_count = block_kv.shape[0]
    count = new_count // groups
    block = jax.ShapeDtypeStruct((slots, width + width * count // slots), jnp.bfloat16)
    info = jax.ShapeDtypeStruct((info_rows(new_count)[1], HEAD_DIM), jnp.float32)
    *blocks, info = pl.pallas_call(
        functools.partial(front_kernel, order),
        out_shape=[block] * AHEAD + [info],
        in_specs=[SMEM] + [ANY] * 7,
        out_specs=[ANY] * (AHEAD + 1),
        scratch_shapes=[
            pltpu.SMEM(assignment.shape, jnp.int32),
            pltpu.SMEM(prefix_len.shape, jnp.int32),
            pltpu.SMEM(owner_map.shape, jnp.int32),
            pltpu.SMEM(stripe_map.shape, jnp.int32),
            pltpu.SMEM(assignment.shape, jnp.int32),
            pltpu.VMEM(block_kv.shape, jnp.bfloat16),
            pltpu.VMEM(table.shape, jnp.float32),
            pltpu.VMEM((AHEAD,) + block.shape, jnp.bfloat16),
            pltpu.VMEM(info.shape, jnp.float32),
            pltpu.SemaphoreType.DMA((6,)),
            pltpu.SemaphoreType.DMA((AHEAD,)),
            pltpu.SemaphoreType.DMA((AHEAD,)),
            pltpu.SemaphoreType.DMA((2,)),
        ],
        compiler_params=params(60),
        name="front",
    )(me, assignment, prefix_len, owner_map, stripe_map, block_kv, table, pool)
    return blocks, info


def query_kernel(order, info_ref, q_ref, pool_ref, *refs):
    groups, slots, width = pool_ref.shape
    sent = groups - 1 - AHEAD
    send_refs, refs = refs[:sent], refs[sent:]
    rot_ref, own_ref, fresh_ref, bias_ref, request_ref, scalar_ref, scalar_sem = refs
    new_count = q_ref.shape[0]
    count = new_count // groups
    quarter = fresh_ref.shape[1] // HEAD_DIM
    at, _ = info_rows(new_count)
    scalar_copy = pltpu.make_async_copy(info_ref.at[pl.ds(at["scalars"], 8)], scalar_ref, scalar_sem)
    scalar_copy.start()
    cosine = info_ref[at["cos"] : at["cos"] + new_count]
    sine = info_ref[at["sin"] : at["sin"] + new_count]
    for row in range(bias_ref.shape[1] // HEAD_DIM):
        line = info_ref[at["bias"] + row : at["bias"] + row + 1]
        bias_ref[:, column(row)] = jnp.broadcast_to(line, (8, HEAD_DIM))
    request_ref[...] = info_ref[at["scalars"] : at["scalars"] + 8].astype(jnp.int32)
    for head in range(2 * KV_HEADS):
        rows = at["new"] + head * new_count
        own_ref[head, slots : slots + new_count] = info_ref[rows : rows + new_count].astype(jnp.bfloat16)
    for head in range(Q_HEADS):
        rows = slice((head % PER_KV) * new_count, (head % PER_KV + 1) * new_count)
        rot_ref[head // PER_KV, rows, :] = turn(q_ref[:, column(head)], cosine, sine)
    scalar_copy.wait()
    sends = list(send_refs)
    for p in range(AHEAD, groups):
        request = scalar_ref[0, p].astype(jnp.int32)
        residue = scalar_ref[1, p].astype(jnp.int32)
        if order[p] == 0:
            target, base = fresh_ref, 0
            for head in range(2 * KV_HEADS):
                own_ref[head, 0:slots] = pool_ref[request, :, column(head)]
        else:
            target, base = sends.pop(0), width
            target[:, 0:width] = pool_ref[request]
        for lanes in range(quarter):
            target[:, base + lanes * HEAD_DIM : base + (lanes + 1) * HEAD_DIM] = fresh_rows(
                info_ref, at["new"], residue, new_count, count, quarter, lanes
            ).astype(jnp.bfloat16)


def rotate_queries(order, info, queries, pool):
    groups, slots, width = pool.shape
    new_count = queries.shape[0]
    spare = width * (new_count // groups) // slots
    sent = groups - 1 - AHEAD
    outs = pl.pallas_call(
        functools.partial(query_kernel, order),
        out_shape=[jax.ShapeDtypeStruct((slots, width + spare), jnp.bfloat16)] * sent
        + [
            jax.ShapeDtypeStruct((KV_HEADS, PER_KV * new_count, HEAD_DIM), jnp.bfloat16),
            jax.ShapeDtypeStruct((2 * KV_HEADS, slots + new_count, HEAD_DIM), jnp.bfloat16),
            jax.ShapeDtypeStruct((slots, spare), jnp.bfloat16),
            jax.ShapeDtypeStruct((8, groups * slots), jnp.float32),
            jax.ShapeDtypeStruct((8, HEAD_DIM), jnp.int32),
        ],
        in_specs=[VMEM] * 3,
        out_specs=[VMEM] * (sent + 5),
        scratch_shapes=[pltpu.SMEM((8, HEAD_DIM), jnp.float32), pltpu.SemaphoreType.DMA],
        compiler_params=params(32),
        name="rotate_queries",
    )(info, queries, pool)
    return outs[:sent], outs[sent:]


def attend_kernel(pieces, first, early, final, unpack, size, *refs):
    rot_ref, bias_ref, refs = refs[0], refs[1], refs[2:]
    if early:
        (sum_in, total_in, high_in), refs = refs[:3], refs[3:]
    else:
        own_ref, refs = refs[0], refs[1:]
    got_refs, refs = refs[:pieces], refs[pieces:]
    fresh_refs = [got.at[:, pl.ds(WIDTH, got.shape[1] - WIDTH)] for got in got_refs] if unpack else []
    if unpack:
        request_vmem, refs = refs[0], refs[1:]
        if early:
            refs = refs[1:]
        else:
            fresh_refs, refs = fresh_refs + [refs[0]], refs[1:]
    if final:
        out_ref, refs = refs[0], refs[1:]
    else:
        (sum_out, total_out, high_out), refs = refs[:3], refs[3:]
    if unpack:
        (decode_ref, rows_ref, request_ref, request_sem, decode_sems), refs = refs[:5], refs[5:]
        count = rows_ref.shape[1]
        request_copy = pltpu.make_async_copy(request_vmem, request_ref, request_sem)
        request_copy.start()
    if final:
        done_ref, out_sems = refs
    new_count = rot_ref.shape[1] // PER_KV
    slots = got_refs[0].shape[0]
    span = pieces * slots
    if not early:
        span += own_ref.shape[1] - new_count
        token = lax.broadcasted_iota(jnp.int32, (size, new_count), 0) % new_count
        causal = jnp.where(lax.broadcasted_iota(jnp.int32, (size, new_count), 1) <= token, 0.0, MASKED)
    bias = bias_ref[0:1, first * slots : first * slots + span]
    per_head = PER_KV * new_count // size
    total_chunks = KV_HEADS * per_head
    heads_in = size // new_count
    keys, values = {}, {}
    scores, weights, factors = {}, {}, {}

    def place(at):
        head, chunk = divmod(at, per_head)
        return head, chunk, slice(chunk * size, (chunk + 1) * size)

    def score(at):
        head, chunk, rows = place(at)
        if chunk == 0:
            key_parts = [got[:, column(head)] for got in got_refs]
            value_parts = [got[:, column(KV_HEADS + head)] for got in got_refs]
            if not early:
                key_parts.append(own_ref[head])
                value_parts.append(own_ref[KV_HEADS + head])
            keys[head] = jnp.concatenate(key_parts, axis=0)
            value = jnp.concatenate(value_parts, axis=0)
            values[head] = jnp.concatenate([value, jnp.ones_like(value)], axis=1)
        scores[at] = lax.dot_general(
            rot_ref[head, rows, :], keys[head], (((1,), (1,)), ((), ())), preferred_element_type=jnp.float32
        )

    def weigh(at):
        head, chunk, rows = place(at)
        values_at = scores.pop(at)
        if early:
            values_at = values_at * SCALE + bias
        else:
            values_at = jnp.concatenate(
                [values_at[:, :span] * SCALE + bias, values_at[:, span:] * SCALE + causal], axis=1
            )
        high = jnp.max(values_at, axis=1, keepdims=True)
        if early:
            high_before = high_in[head, rows, :]
            high = jnp.maximum(high_before, high)
            factors[at] = jnp.exp2(high_before - high)
            high = jnp.concatenate([high] * (span // HEAD_DIM), axis=1)
        elif not final:
            high_out[head, rows, :] = jnp.broadcast_to(high, (size, HEAD_DIM))
        weights[at] = jnp.exp2(values_at - high).astype(jnp.bfloat16)

    def out_copy(at):
        head, chunk, rows = place(at)
        width = heads_in * HEAD_DIM
        return pltpu.make_async_copy(
            done_ref.at[at], out_ref.at[:, pl.ds(at * width, width)], out_sems.at[at]
        )

    def finish(at, summed):
        head, chunk, rows = place(at)
        summed, total = summed[:, :HEAD_DIM], summed[:, HEAD_DIM:]
        if early:
            factor = factors.pop(at)
            summed = summed + sum_in[head, rows, :] * factor
            total = total + total_in[head, rows, :] * factor
        if not final:
            sum_out[head, rows, :] = summed
            total_out[head, rows, :] = total
            return
        about = pl.reciprocal(total, approx=True)
        result = (summed * (about * (2.0 - total * about))).astype(jnp.bfloat16)
        for row in range(heads_in):
            done_ref[at, :, column(row)] = result[row * new_count : (row + 1) * new_count]
        out_copy(at).start()

    def decode_copy(p):
        return pltpu.make_async_copy(
            rows_ref.at[p], decode_ref.at[request_ref[0, first + p]], decode_sems.at[p]
        )

    score(0)
    for at in range(total_chunks + 1):
        if at + 1 < total_chunks:
            score(at + 1)
        if at >= 1:
            summed = jnp.dot(
                weights.pop(at - 1), values[(at - 1) // per_head], preferred_element_type=jnp.float32
            )
        if at < total_chunks:
            weigh(at)
        if at >= 1:
            finish(at - 1, summed)
        if unpack and at == 1:
            request_copy.wait()
            for p, fresh_ref in enumerate(fresh_refs):
                stack = fresh_ref[...]
                quarter = stack.shape[1]
                for part in range(stack.shape[0] // count):
                    rows_ref[p, :, part * quarter : (part + 1) * quarter] = stack[
                        part * count : (part + 1) * count
                    ]
                decode_copy(p).start()
    for p in range(len(fresh_refs)):
        decode_copy(p).wait()
    if final:
        for at in range(total_chunks):
            out_copy(at).wait()


def attend(rot, bias, own, got, first=0, sums=None, final=True, requests=None, fresh=None, decode=None, size=CHUNK):
    rows = rot.shape[1]
    new_count = rows // PER_KV
    pieces = len(got)
    early, unpack = sums is not None, requests is not None
    operands = [rot, bias] + (list(sums) if early else [own]) + list(got)
    specs = [VMEM] * len(operands)
    shapes, out_specs, scratch, aliases = [], [], [], {}
    if unpack:
        operands.append(requests)
        specs.append(VMEM)
        if early:
            operands.append(decode)
            specs.append(ANY)
            aliases = {len(operands) - 1: 1 if final else 3}
        else:
            operands.append(fresh)
            specs.append(VMEM)
    if final:
        shapes.append(jax.ShapeDtypeStruct((new_count, Q_HEADS * HEAD_DIM), jnp.bfloat16))
        out_specs.append(ANY)
    else:
        shapes += [jax.ShapeDtypeStruct((KV_HEADS, rows, HEAD_DIM), jnp.float32)] * 3
        out_specs += [VMEM] * 3
    if unpack:
        slots = got[0].shape[0]
        count = (got[0].shape[1] - WIDTH) * slots // WIDTH
        unpacked = pieces if early else pieces + 1
        shapes.append(jax.ShapeDtypeStruct((new_count // count, count, WIDTH), jnp.bfloat16))
        out_specs.append(ANY)
        scratch += [
            pltpu.VMEM((unpacked, count, WIDTH), jnp.bfloat16),
            pltpu.SMEM(requests.shape, jnp.int32),
            pltpu.SemaphoreType.DMA,
            pltpu.SemaphoreType.DMA((unpacked,)),
        ]
    if final:
        chunks = KV_HEADS * rows // size
        scratch += [
            pltpu.VMEM((chunks, new_count, size // new_count * HEAD_DIM), jnp.bfloat16),
            pltpu.SemaphoreType.DMA((chunks,)),
        ]
    return pl.pallas_call(
        functools.partial(attend_kernel, pieces, first, early, final, unpack, size),
        out_shape=tuple(shapes),
        in_specs=specs,
        out_specs=tuple(out_specs),
        scratch_shapes=scratch,
        input_output_aliases=aliases,
        compiler_params=params(32),
        name="attend_late" if early else "attend",
    )(*operands)


def inverse(table):
    places = jnp.arange(table.shape[0], dtype=jnp.int32)
    return jnp.sum(jnp.where(table[None, :] == places[:, None], places, 0), axis=1)


def rotate(rows, positions, heads):
    half = HEAD_DIM // 2
    freqs = ROPE_BASE ** (-jnp.arange(half, dtype=jnp.float32) / half)
    angles = positions.astype(jnp.float32)[:, None] * freqs[None, :]
    cosine = jnp.concatenate([jnp.cos(angles)] * 2, axis=-1)[:, None, :]
    sine = jnp.concatenate([-jnp.sin(angles), jnp.sin(angles)], axis=-1)[:, None, :]
    split = rows.astype(jnp.float32).reshape(rows.shape[0], heads, HEAD_DIM)
    turned = jnp.roll(split, half, axis=-1)
    return (split * cosine + turned * sine).astype(jnp.bfloat16)


def small_pieces(me, assignment, prefix_len, stripe_map, owner_map, queries, block_kv, pool):
    groups, slots, width = pool.shape
    new_count = block_kv.shape[0]
    count = new_count // groups
    request = assignment[me[0]]
    length = prefix_len[request]
    positions = length + jnp.arange(new_count, dtype=jnp.int32)
    rot = rotate(queries, positions, Q_HEADS).reshape(new_count, KV_HEADS, PER_KV, HEAD_DIM)
    rot = jnp.transpose(rot, (1, 2, 0, 3)).reshape(KV_HEADS, PER_KV * new_count, HEAD_DIM)
    new_keys = rotate(block_kv[:, :KV_WIDTH], positions, KV_HEADS).reshape(new_count, KV_WIDTH)
    new_kv = jnp.concatenate([new_keys, block_kv[:, KV_WIDTH:]], axis=1)
    own = jnp.transpose(new_kv.reshape(new_count, 2 * KV_HEADS, HEAD_DIM), (1, 0, 2))
    spread = jnp.transpose(new_kv.reshape(count, groups, width), (1, 0, 2))
    send = jnp.concatenate([pool[assignment], spread[inverse(owner_map[request])]], axis=1)
    got = lax.all_to_all(send, "pg", split_axis=0, concat_axis=0, tiled=True)
    located = jnp.arange(slots, dtype=jnp.int32)[None, :] * groups + inverse(stripe_map[request])[:, None]
    bias = jnp.where(located < length, 0.0, MASKED).astype(jnp.float32).reshape(1, groups * slots)
    keys = got[:, :slots].reshape(groups * slots, width)
    (attended,) = attend(rot, jnp.broadcast_to(bias, (8, groups * slots)), own, [keys])
    return attended, got[inverse(assignment), slots:]


def shards(queries, block_kv, pool_kv, prefix_len, assignment, stripe_map, owner_map):
    queries, block_kv, pool = queries[0], block_kv[0], pool_kv[0]
    groups, slots, width = pool.shape
    new_count = queries.shape[0]
    count = new_count // groups
    me = lax.axis_index("pg").astype(jnp.int32).reshape(1)
    if groups != 16 or slots % 16 or HEAD_DIM % slots or count % 8 or slots % count:
        attended, decode_kv = small_pieces(
            me, assignment, prefix_len, stripe_map, owner_map, queries, block_kv, pool
        )
        return (attended[None], decode_kv[None])
    order = order_of(groups)
    table = rotation_tables(new_count)
    first_blocks, info = front(order, me, assignment, prefix_len, owner_map, stripe_map, block_kv, table, pool)
    other_blocks, (rot, own, fresh, bias, requests) = rotate_queries(order, info, queries, pool)
    got = []
    for block, t in zip(list(first_blocks) + list(other_blocks), [t for t in order if t]):
        got.append(lax.ppermute(block, "pg", [(source, source ^ t) for source in range(groups)]))
    soon = groups - LATE - 1
    *sums, decode_kv = attend(rot, bias, own, got[:soon], final=False, requests=requests, fresh=fresh)
    attended, decode_kv = attend(
        rot, bias, None, got[soon:], first=soon + 1, sums=sums, requests=requests, decode=decode_kv, size=LATE_CHUNK
    )
    return (attended[None], decode_kv[None])


def solution(mesh):
    return jax.shard_map(
        shards,
        mesh=mesh,
        in_specs=(
            P(("rep", "pg"), None, None),
            P(("rep", "pg"), None, None),
            P(("rep", "pg"), None, None, None),
            P("rep"),
            P("rep"),
            P("rep", None),
            P("rep", None),
        ),
        out_specs=(P(("rep", "pg"), None, None), P(("rep", "pg"), None, None, None)),
        check_vma=False,
    )
```

```python
import functools
import math

import jax
import jax.numpy as jnp
import numpy as np
from jax import lax
from jax.experimental import pallas as pl
from jax.experimental.pallas import tpu as pltpu
from jax.sharding import PartitionSpec as P

Q_HEADS = 32
KV_HEADS = 4
HEAD_DIM = 128
PER_KV = Q_HEADS // KV_HEADS
KV_WIDTH = KV_HEADS * HEAD_DIM
WIDTH = 2 * KV_WIDTH

ROPE_BASE = 1000000.0
MASKED = -1e30
SCALE = HEAD_DIM ** -0.5 / math.log(2.0)
CHUNK = 256
LATE = 4
LATE_CHUNK = 256
AHEAD = 4

SMEM = pl.BlockSpec(memory_space=pltpu.SMEM)
VMEM = pl.BlockSpec(memory_space=pltpu.VMEM)
ANY = pl.BlockSpec(memory_space=pl.ANY)


def params(mib):
    return pltpu.CompilerParams(vmem_limit_bytes=mib * 1024 * 1024)


def column(head):
    return slice(head * HEAD_DIM, (head + 1) * HEAD_DIM)


def order_of(groups):
    half = groups // 2
    far, near = list(range(half, 2 * half)), list(range(half - 1, 0, -1))
    order = [(far if kind == "f" else near).pop(0) for kind in "fnfnfnfnfnnffnf"]
    order.insert(groups - LATE - 1, 0)
    return order


def rotation_tables(rows):
    half = HEAD_DIM // 2
    freqs = np.tile(ROPE_BASE ** (-np.arange(half, dtype=np.float64) / half), 2)
    angles = np.arange(rows, dtype=np.float64)[:, None] * freqs[None, :]
    parts = [np.cos(angles), np.sin(angles), np.tile(freqs, (8, 1))]
    return jnp.asarray(np.concatenate(parts, axis=0).astype(np.float32))


def rotation(table_ref, length):
    rows = (table_ref.shape[0] - 8) // 2
    start = length.astype(jnp.float32) * table_ref[2 * rows : 2 * rows + 8, :]
    cos_start, sin_start = jnp.cos(start)[0:1], jnp.sin(start)[0:1]
    cos_row, sin_row = table_ref[0:rows, :], table_ref[rows : 2 * rows, :]
    lane = lax.broadcasted_iota(jnp.int32, (1, HEAD_DIM), 1)
    sign = jnp.where(lane < HEAD_DIM // 2, -1.0, 1.0)
    cosine = cos_row * cos_start - sin_row * sin_start
    return cosine, sin_row * (cos_start * sign) + cos_row * (sin_start * sign)


def turn(x, cosine, sine):
    x = x.astype(jnp.float32)
    return (x * cosine + pltpu.roll(x, HEAD_DIM // 2, 1) * sine).astype(jnp.bfloat16)


def info_rows(new_count):
    sizes = [("cos", new_count), ("sin", new_count), ("bias", 8), ("scalars", 8), ("new", 2 * KV_HEADS * new_count)]
    at, rows = 0, {}
    for name, size in sizes:
        rows[name] = at
        at += size
    return rows, at


def fresh_rows(info_ref, base, residue, new_count, count, quarter, lanes):
    groups = new_count // count
    stack = [
        info_ref[pl.ds(base + (head + lanes) * new_count + residue, count, stride=groups), :]
        for head in range(0, 2 * KV_HEADS, quarter)
    ]
    return jnp.concatenate(stack, axis=0)


def front_kernel(
    order, me_ref, assign_any, length_any, owner_any, stripe_any, block_any, table_any, pool_any, *refs
):
    groups, slots, width = pool_any.shape
    send_refs, info_any, refs = refs[:AHEAD], refs[AHEAD], refs[AHEAD + 1 :]
    (assign_ref, length_ref, owner_ref, stripe_ref, residue_ref, block_ref, table_ref, pool_ref, pack_ref, info_ref,
     small_sems, pool_sems, send_sems, info_sems) = refs
    new_count = block_any.shape[0]
    count = new_count // groups
    quarter = width * count // slots // HEAD_DIM
    at, rows = info_rows(new_count)
    pairs = [
        (assign_any, assign_ref), (length_any, length_ref), (owner_any, owner_ref), (stripe_any, stripe_ref),
        (block_any, block_ref), (table_any, table_ref),
    ]
    smalls = [pltpu.make_async_copy(*pair, small_sems.at[i]) for i, pair in enumerate(pairs)]
    for copy in smalls:
        copy.start()
    pool_copies = [
        pltpu.make_async_copy(pool_any.at[pl.ds(low, 4)], pool_ref.at[pl.ds(low, 4)], pool_sems.at[low // 4])
        for low in range(0, groups, 4)
    ]
    for copy in pool_copies:
        copy.start()
    me = me_ref[0]
    for copy in smalls:
        copy.wait()
    request = assign_ref[me]
    length = length_ref[request]
    for residue in range(groups):
        residue_ref[owner_ref[request, residue]] = residue
    cosine, sine = rotation(table_ref, length)
    for head in range(KV_HEADS):
        low = at["new"] + head * new_count
        info_ref[low : low + new_count] = turn(block_ref[:, column(head)], cosine, sine).astype(jnp.float32)
        low += KV_HEADS * new_count
        info_ref[low : low + new_count] = block_ref[:, column(KV_HEADS + head)].astype(jnp.float32)

    def info_copy(part, low, high):
        part_rows = pl.ds(low, high - low)
        return pltpu.make_async_copy(info_ref.at[part_rows], info_any.at[part_rows], info_sems.at[part])

    info_copy(0, at["new"], rows).start()
    for copy in pool_copies:
        copy.wait()
    sends = []
    for p in range(AHEAD):
        pack_ref[p, :, 0:width] = pool_ref[assign_ref[me ^ order[p]]]
        for lanes in range(quarter):
            pack_ref[p, :, width + lanes * HEAD_DIM : width + (lanes + 1) * HEAD_DIM] = fresh_rows(
                info_ref, at["new"], residue_ref[me ^ order[p]], new_count, count, quarter, lanes
            ).astype(jnp.bfloat16)
        sends.append(pltpu.make_async_copy(pack_ref.at[p], send_refs[p], send_sems.at[p]))
        sends[-1].start()
    info_ref[at["cos"] : at["cos"] + new_count] = cosine
    info_ref[at["sin"] : at["sin"] + new_count] = sine
    per_row = HEAD_DIM // slots
    row = lax.broadcasted_iota(jnp.int32, (8, HEAD_DIM), 0)
    lane = lax.broadcasted_iota(jnp.int32, (8, HEAD_DIM), 1)
    piece, slot = row * per_row + lane // slots, lane % slots
    holder, requests, residues = jnp.zeros_like(lane), jnp.zeros_like(lane), jnp.zeros_like(lane)
    for p in range(groups):
        other = me ^ order[p]
        holder = jnp.where(piece == p, other, holder)
        requests = jnp.where(lane == p, assign_ref[other], requests)
        residues = jnp.where(lane == p, residue_ref[other], residues)
    bias = jnp.full((8, HEAD_DIM), MASKED, jnp.float32)
    for residue in range(groups):
        live = (holder == stripe_ref[request, residue]) & (slot * groups + residue < length)
        bias = jnp.where(live, 0.0, bias)
    info_ref[at["bias"] : at["bias"] + 8] = bias
    scalars = jnp.where(row == 0, requests, residues)
    info_ref[at["scalars"] : at["scalars"] + 8] = scalars.astype(jnp.float32)
    info_copy(1, 0, at["new"]).start()
    for copy in sends:
        copy.wait()
    info_copy(0, at["new"], rows).wait()
    info_copy(1, 0, at["new"]).wait()


def front(order, me, assignment, prefix_len, owner_map, stripe_map, block_kv, table, pool):
    groups, slots, width = pool.shape
    new_count = block_kv.shape[0]
    count = new_count // groups
    block = jax.ShapeDtypeStruct((slots, width + width * count // slots), jnp.bfloat16)
    info = jax.ShapeDtypeStruct((info_rows(new_count)[1], HEAD_DIM), jnp.float32)
    *blocks, info = pl.pallas_call(
        functools.partial(front_kernel, order),
        out_shape=[block] * AHEAD + [info],
        in_specs=[SMEM] + [ANY] * 7,
        out_specs=[ANY] * (AHEAD + 1),
        scratch_shapes=[
            pltpu.SMEM(assignment.shape, jnp.int32),
            pltpu.SMEM(prefix_len.shape, jnp.int32),
            pltpu.SMEM(owner_map.shape, jnp.int32),
            pltpu.SMEM(stripe_map.shape, jnp.int32),
            pltpu.SMEM(assignment.shape, jnp.int32),
            pltpu.VMEM(block_kv.shape, jnp.bfloat16),
            pltpu.VMEM(table.shape, jnp.float32),
            pltpu.VMEM(pool.shape, jnp.bfloat16),
            pltpu.VMEM((AHEAD,) + block.shape, jnp.bfloat16),
            pltpu.VMEM(info.shape, jnp.float32),
            pltpu.SemaphoreType.DMA((6,)),
            pltpu.SemaphoreType.DMA((groups // 4,)),
            pltpu.SemaphoreType.DMA((AHEAD,)),
            pltpu.SemaphoreType.DMA((2,)),
        ],
        compiler_params=params(60),
        name="front",
    )(me, assignment, prefix_len, owner_map, stripe_map, block_kv, table, pool)
    return blocks, info


def query_kernel(order, info_ref, q_ref, pool_ref, *refs):
    groups, slots, width = pool_ref.shape
    sent = groups - 1 - AHEAD
    send_refs, refs = refs[:sent], refs[sent:]
    rot_ref, own_ref, fresh_ref, bias_ref, request_ref, scalar_ref, scalar_sem = refs
    new_count = q_ref.shape[0]
    count = new_count // groups
    quarter = fresh_ref.shape[1] // HEAD_DIM
    at, _ = info_rows(new_count)
    scalar_copy = pltpu.make_async_copy(info_ref.at[pl.ds(at["scalars"], 8)], scalar_ref, scalar_sem)
    scalar_copy.start()
    cosine = info_ref[at["cos"] : at["cos"] + new_count]
    sine = info_ref[at["sin"] : at["sin"] + new_count]
    for row in range(bias_ref.shape[1] // HEAD_DIM):
        line = info_ref[at["bias"] + row : at["bias"] + row + 1]
        bias_ref[:, column(row)] = jnp.broadcast_to(line, (8, HEAD_DIM))
    request_ref[...] = info_ref[at["scalars"] : at["scalars"] + 8].astype(jnp.int32)
    for head in range(2 * KV_HEADS):
        rows = at["new"] + head * new_count
        own_ref[head, slots : slots + new_count] = info_ref[rows : rows + new_count].astype(jnp.bfloat16)
    for head in range(Q_HEADS):
        rows = slice((head % PER_KV) * new_count, (head % PER_KV + 1) * new_count)
        rot_ref[head // PER_KV, rows, :] = turn(q_ref[:, column(head)], cosine, sine)
    scalar_copy.wait()
    sends = list(send_refs)
    for p in range(AHEAD, groups):
        request = scalar_ref[0, p].astype(jnp.int32)
        residue = scalar_ref[1, p].astype(jnp.int32)
        if order[p] == 0:
            target, base = fresh_ref, 0
            for head in range(2 * KV_HEADS):
                own_ref[head, 0:slots] = pool_ref[request, :, column(head)]
        else:
            target, base = sends.pop(0), width
            target[:, 0:width] = pool_ref[request]
        for lanes in range(quarter):
            target[:, base + lanes * HEAD_DIM : base + (lanes + 1) * HEAD_DIM] = fresh_rows(
                info_ref, at["new"], residue, new_count, count, quarter, lanes
            ).astype(jnp.bfloat16)


def rotate_queries(order, info, queries, pool):
    groups, slots, width = pool.shape
    new_count = queries.shape[0]
    spare = width * (new_count // groups) // slots
    sent = groups - 1 - AHEAD
    outs = pl.pallas_call(
        functools.partial(query_kernel, order),
        out_shape=[jax.ShapeDtypeStruct((slots, width + spare), jnp.bfloat16)] * sent
        + [
            jax.ShapeDtypeStruct((KV_HEADS, PER_KV * new_count, HEAD_DIM), jnp.bfloat16),
            jax.ShapeDtypeStruct((2 * KV_HEADS, slots + new_count, HEAD_DIM), jnp.bfloat16),
            jax.ShapeDtypeStruct((slots, spare), jnp.bfloat16),
            jax.ShapeDtypeStruct((8, groups * slots), jnp.float32),
            jax.ShapeDtypeStruct((8, HEAD_DIM), jnp.int32),
        ],
        in_specs=[VMEM] * 3,
        out_specs=[VMEM] * (sent + 5),
        scratch_shapes=[pltpu.SMEM((8, HEAD_DIM), jnp.float32), pltpu.SemaphoreType.DMA],
        compiler_params=params(32),
        name="rotate_queries",
    )(info, queries, pool)
    return outs[:sent], outs[sent:]


def quotient(summed, total):
    about = pl.reciprocal(total, approx=True)
    return summed * (about * (2.0 - total * about))


def join_keys(keys, values, got_refs, own_ref, head):
    key_parts = [got[:, column(head)] for got in got_refs]
    value_parts = [got[:, column(KV_HEADS + head)] for got in got_refs]
    if own_ref is not None:
        key_parts.append(own_ref[head])
        value_parts.append(own_ref[KV_HEADS + head])
    keys[head] = jnp.concatenate(key_parts, axis=0)
    value = jnp.concatenate(value_parts, axis=0)
    values[head] = jnp.concatenate([value, jnp.ones_like(value)], axis=1)


def dot_keys(query, keys):
    return lax.dot_general(query, keys, (((1,), (1,)), ((), ())), preferred_element_type=jnp.float32)


def staged(total, score, weigh, mix, finish, beside=None):
    scores, weights = {0: score(0)}, {}
    for at in range(total + 1):
        if at + 1 < total:
            scores[at + 1] = score(at + 1)
        if at >= 1:
            mixed = mix(at - 1, weights.pop(at - 1))
        if at < total:
            weights[at] = weigh(at, scores.pop(at))
        if at >= 1:
            finish(at - 1, mixed)
        if at == 1 and beside is not None:
            beside()


def unpacking(fresh_refs, first, request_vmem, decode_ref, rows_ref, request_ref, request_sem, decode_sems):
    count = rows_ref.shape[1]
    request_copy = pltpu.make_async_copy(request_vmem, request_ref, request_sem)
    request_copy.start()

    def decode_copy(p):
        return pltpu.make_async_copy(
            rows_ref.at[p], decode_ref.at[request_ref[0, first + p]], decode_sems.at[p]
        )

    def start():
        request_copy.wait()
        for p, fresh_ref in enumerate(fresh_refs):
            stack = fresh_ref[...]
            quarter = stack.shape[1]
            for part in range(stack.shape[0] // count):
                rows_ref[p, :, part * quarter : (part + 1) * quarter] = stack[part * count : (part + 1) * count]
            decode_copy(p).start()

    def wait():
        for p in range(len(fresh_refs)):
            decode_copy(p).wait()

    return start, wait


def spare_part(got):
    return got.at[:, pl.ds(WIDTH, got.shape[1] - WIDTH)]


def attend_kernel(pieces, unpack, rot_ref, bias_ref, own_ref, *refs):
    got_refs, refs = refs[:pieces], refs[pieces:]
    start, wait = None, None
    if unpack:
        request_vmem, fresh_ref, result_ref, level_ref, decode_ref, *scratch = refs
        fresh_refs = [spare_part(got) for got in got_refs] + [fresh_ref]
        start, wait = unpacking(fresh_refs, 0, request_vmem, decode_ref, *scratch)
    else:
        result_ref, level_ref = refs
    new_count = rot_ref.shape[1] // PER_KV
    span = pieces * got_refs[0].shape[0] + own_ref.shape[1] - new_count
    token = lax.broadcasted_iota(jnp.int32, (CHUNK, new_count), 0) % new_count
    causal = jnp.where(lax.broadcasted_iota(jnp.int32, (CHUNK, new_count), 1) <= token, 0.0, MASKED)
    bias = bias_ref[0:1, 0:span]
    per_head = PER_KV * new_count // CHUNK
    keys, values, highs = {}, {}, {}

    def place(at):
        return at // per_head, slice(at % per_head * CHUNK, (at % per_head + 1) * CHUNK)

    def score(at):
        head, rows = place(at)
        if at % per_head == 0:
            join_keys(keys, values, got_refs, own_ref, head)
        return dot_keys(rot_ref[head, rows, :], keys[head])

    def weigh(at, scores):
        scores = jnp.concatenate([scores[:, :span] * SCALE + bias, scores[:, span:] * SCALE + causal], axis=1)
        highs[at] = jnp.max(scores, axis=1, keepdims=True)
        return jnp.exp2(scores - highs[at]).astype(jnp.bfloat16)

    def mix(at, weights):
        return jnp.dot(weights, values[at // per_head], preferred_element_type=jnp.float32)

    def finish(at, mixed):
        head, rows = place(at)
        total = mixed[:, HEAD_DIM:]
        result_ref[head, rows, :] = quotient(mixed[:, :HEAD_DIM], total)
        level_ref[head, rows, :] = highs.pop(at) + jnp.log2(total)

    staged(KV_HEADS * per_head, score, weigh, mix, finish, start)
    if unpack:
        wait()


def attend(rot, bias, own, got, requests=None, fresh=None):
    rows, new_count = rot.shape[1], rot.shape[1] // PER_KV
    operands = [rot, bias, own, *got]
    shapes = [jax.ShapeDtypeStruct((KV_HEADS, rows, HEAD_DIM), jnp.float32)] * 2
    out_specs, scratch = [VMEM] * 2, []
    if requests is not None:
        operands += [requests, fresh]
        slots = got[0].shape[0]
        count = (got[0].shape[1] - WIDTH) * slots // WIDTH
        shapes.append(jax.ShapeDtypeStruct((new_count // count, count, WIDTH), jnp.bfloat16))
        out_specs.append(ANY)
        scratch = unpack_scratch(len(got) + 1, count, requests)
    return pl.pallas_call(
        functools.partial(attend_kernel, len(got), requests is not None),
        out_shape=tuple(shapes),
        in_specs=[VMEM] * len(operands),
        out_specs=tuple(out_specs),
        scratch_shapes=scratch,
        compiler_params=params(32),
        name="attend",
    )(*operands)


def unpack_scratch(pieces, count, requests):
    return [
        pltpu.VMEM((pieces, count, WIDTH), jnp.bfloat16),
        pltpu.SMEM(requests.shape, jnp.int32),
        pltpu.SemaphoreType.DMA,
        pltpu.SemaphoreType.DMA((pieces,)),
    ]


HEADROOM = 96.0


def late_kernel(pieces, first, rot_ref, bias_ref, result_ref, level_ref, *refs):
    got_refs, refs = refs[:pieces], refs[pieces:]
    request_vmem, _, out_ref, decode_ref, done_ref, out_sems, *scratch = refs
    start, wait = unpacking([spare_part(got) for got in got_refs], first, request_vmem, decode_ref, *scratch)
    slots = got_refs[0].shape[0]
    new_count = out_ref.shape[0]
    size = LATE_CHUNK
    heads_in = size // new_count
    bias = bias_ref[0:1, first * slots : (first + pieces) * slots]
    per_head = PER_KV * new_count // size
    chunks = KV_HEADS * per_head
    keys, values, excess = {}, {}, []

    def place(at):
        return at // per_head, slice(at % per_head * size, (at % per_head + 1) * size)

    def out_copy(at):
        width = heads_in * HEAD_DIM
        return pltpu.make_async_copy(
            done_ref.at[at], out_ref.at[:, pl.ds(pl.multiple_of(at * width, width), width)], out_sems.at[at]
        )

    def store(at, result):
        for row in range(heads_in):
            done_ref[at, :, column(row)] = result[row * new_count : (row + 1) * new_count].astype(jnp.bfloat16)
        out_copy(at).start()

    def score(at):
        head, rows = place(at)
        if at % per_head == 0:
            join_keys(keys, values, got_refs, None, head)
        return dot_keys(rot_ref[head, rows, :], keys[head])

    def weigh(at, scores):
        head, rows = place(at)
        powers = scores * SCALE + bias - level_ref[head, rows, :]
        excess.append(jnp.max(powers.reshape(size // 8, 8, HEAD_DIM), axis=0))
        return jnp.exp2(powers).astype(jnp.bfloat16)

    def mix(at, weights):
        return jnp.dot(weights, values[at // per_head], preferred_element_type=jnp.float32)

    def finish(at, mixed):
        head, rows = place(at)
        store(at, quotient(result_ref[head, rows, :] + mixed[:, :HEAD_DIM], 1.0 + mixed[:, HEAD_DIM:]))

    staged(chunks, score, weigh, mix, finish, start)
    most = jnp.max(functools.reduce(jnp.maximum, excess))
    wait()
    for at in range(chunks):
        out_copy(at).wait()

    @pl.when(most > HEADROOM)
    def _():
        for head in range(KV_HEADS):

            def again(chunk, carry, head=head):
                rows = pl.ds(pl.multiple_of(chunk * size, size), size)
                scores = dot_keys(rot_ref[head, rows, :], keys[head]) * SCALE + bias
                level = level_ref[head, rows, :]
                high = jnp.maximum(level, jnp.max(scores, axis=1, keepdims=True))
                factor = jnp.exp2(level - high)
                weights = jnp.exp2(scores - high).astype(jnp.bfloat16)
                mixed = jnp.dot(weights, values[head], preferred_element_type=jnp.float32)
                at = head * per_head + chunk
                summed = result_ref[head, rows, :] * factor + mixed[:, :HEAD_DIM]
                store(at, quotient(summed, factor + mixed[:, HEAD_DIM:]))
                out_copy(at).wait()
                return carry

            lax.fori_loop(0, per_head, again, 0)


def attend_late(rot, bias, result, level, got, first, requests, decode):
    rows, new_count = rot.shape[1], rot.shape[1] // PER_KV
    operands = [rot, bias, result, level, *got, requests, decode]
    chunks = KV_HEADS * rows // LATE_CHUNK
    return pl.pallas_call(
        functools.partial(late_kernel, len(got), first),
        out_shape=(
            jax.ShapeDtypeStruct((new_count, Q_HEADS * HEAD_DIM), jnp.bfloat16),
            jax.ShapeDtypeStruct(decode.shape, jnp.bfloat16),
        ),
        in_specs=[VMEM] * (len(operands) - 1) + [ANY],
        out_specs=(ANY, ANY),
        scratch_shapes=[
            pltpu.VMEM((chunks, new_count, LATE_CHUNK // new_count * HEAD_DIM), jnp.bfloat16),
            pltpu.SemaphoreType.DMA((chunks,)),
        ]
        + unpack_scratch(len(got), decode.shape[1], requests),
        input_output_aliases={len(operands) - 1: 1},
        compiler_params=params(32),
        name="attend_late",
    )(*operands)


def inverse(table):
    places = jnp.arange(table.shape[0], dtype=jnp.int32)
    return jnp.sum(jnp.where(table[None, :] == places[:, None], places, 0), axis=1)


def rotate(rows, positions, heads):
    half = HEAD_DIM // 2
    freqs = ROPE_BASE ** (-jnp.arange(half, dtype=jnp.float32) / half)
    angles = positions.astype(jnp.float32)[:, None] * freqs[None, :]
    cosine = jnp.concatenate([jnp.cos(angles)] * 2, axis=-1)[:, None, :]
    sine = jnp.concatenate([-jnp.sin(angles), jnp.sin(angles)], axis=-1)[:, None, :]
    split = rows.astype(jnp.float32).reshape(rows.shape[0], heads, HEAD_DIM)
    turned = jnp.roll(split, half, axis=-1)
    return (split * cosine + turned * sine).astype(jnp.bfloat16)


def small_pieces(me, assignment, prefix_len, stripe_map, owner_map, queries, block_kv, pool):
    groups, slots, width = pool.shape
    new_count = block_kv.shape[0]
    count = new_count // groups
    request = assignment[me[0]]
    length = prefix_len[request]
    positions = length + jnp.arange(new_count, dtype=jnp.int32)
    rot = rotate(queries, positions, Q_HEADS).reshape(new_count, KV_HEADS, PER_KV, HEAD_DIM)
    rot = jnp.transpose(rot, (1, 2, 0, 3)).reshape(KV_HEADS, PER_KV * new_count, HEAD_DIM)
    new_keys = rotate(block_kv[:, :KV_WIDTH], positions, KV_HEADS).reshape(new_count, KV_WIDTH)
    new_kv = jnp.concatenate([new_keys, block_kv[:, KV_WIDTH:]], axis=1)
    own = jnp.transpose(new_kv.reshape(new_count, 2 * KV_HEADS, HEAD_DIM), (1, 0, 2))
    spread = jnp.transpose(new_kv.reshape(count, groups, width), (1, 0, 2))
    send = jnp.concatenate([pool[assignment], spread[inverse(owner_map[request])]], axis=1)
    got = lax.all_to_all(send, "pg", split_axis=0, concat_axis=0, tiled=True)
    located = jnp.arange(slots, dtype=jnp.int32)[None, :] * groups + inverse(stripe_map[request])[:, None]
    bias = jnp.where(located < length, 0.0, MASKED).astype(jnp.float32).reshape(1, groups * slots)
    keys = got[:, :slots].reshape(groups * slots, width)
    result, _ = attend(rot, jnp.broadcast_to(bias, (8, groups * slots)), own, [keys])
    result = result.astype(jnp.bfloat16).reshape(KV_HEADS, PER_KV, new_count, HEAD_DIM)
    attended = jnp.transpose(result, (2, 0, 1, 3)).reshape(new_count, Q_HEADS * HEAD_DIM)
    return attended, got[inverse(assignment), slots:]


def shards(queries, block_kv, pool_kv, prefix_len, assignment, stripe_map, owner_map):
    queries, block_kv, pool = queries[0], block_kv[0], pool_kv[0]
    groups, slots, width = pool.shape
    new_count = queries.shape[0]
    count = new_count // groups
    me = lax.axis_index("pg").astype(jnp.int32).reshape(1)
    if groups != 16 or slots % 16 or HEAD_DIM % slots or count % 8 or slots % count:
        attended, decode_kv = small_pieces(
            me, assignment, prefix_len, stripe_map, owner_map, queries, block_kv, pool
        )
        return (attended[None], decode_kv[None])
    order = order_of(groups)
    table = rotation_tables(new_count)
    first_blocks, info = front(order, me, assignment, prefix_len, owner_map, stripe_map, block_kv, table, pool)
    other_blocks, (rot, own, fresh, bias, requests) = rotate_queries(order, info, queries, pool)
    got = []
    for block, t in zip(list(first_blocks) + list(other_blocks), [t for t in order if t]):
        got.append(lax.ppermute(block, "pg", [(source, source ^ t) for source in range(groups)]))
    soon = groups - LATE - 1
    result, level, decode_kv = attend(rot, bias, own, got[:soon], requests, fresh)
    attended, decode_kv = attend_late(rot, bias, result, level, got[soon:], soon + 1, requests, decode_kv)
    return (attended[None], decode_kv[None])


def solution(mesh):
    return jax.shard_map(
        shards,
        mesh=mesh,
        in_specs=(
            P(("rep", "pg"), None, None),
            P(("rep", "pg"), None, None),
            P(("rep", "pg"), None, None, None),
            P("rep"),
            P("rep"),
            P("rep", None),
            P("rep", None),
        ),
        out_specs=(P(("rep", "pg"), None, None), P(("rep", "pg"), None, None, None)),
        check_vma=False,
    )
```

```python
import functools
import math

import jax
import jax.numpy as jnp
import numpy as np
from jax import lax
from jax.experimental import pallas as pl
from jax.experimental.pallas import tpu as pltpu
from jax.sharding import PartitionSpec as P

Q_HEADS = 32
KV_HEADS = 4
HEAD_DIM = 128
PER_KV = Q_HEADS // KV_HEADS
KV_WIDTH = KV_HEADS * HEAD_DIM
WIDTH = 2 * KV_WIDTH

ROPE_BASE = 1000000.0
MASKED = -1e30
SCALE = HEAD_DIM ** -0.5 / math.log(2.0)
CHUNK = 256
LATE_CHUNK = 256
AHEAD = 4

SMEM = pl.BlockSpec(memory_space=pltpu.SMEM)
VMEM = pl.BlockSpec(memory_space=pltpu.VMEM)
ANY = pl.BlockSpec(memory_space=pl.ANY)


def params(mib):
    return pltpu.CompilerParams(vmem_limit_bytes=mib * 1024 * 1024)


def column(head):
    return slice(head * HEAD_DIM, (head + 1) * HEAD_DIM)


def far_partners(groups):
    quarter = groups // 4
    next_to, beyond = list(range(2 * quarter, 3 * quarter)), list(range(3 * quarter, 4 * quarter))
    order = []
    for at in range(quarter):
        order += [next_to[at ^ (at >> 1)], beyond[(at ^ (at >> 1)) ^ 1]]
    return order


def holder_of(p, me, groups, far):
    half = groups // 2
    return me // half * half + p if p < half else me ^ far[p - half]


def rotation_tables(rows):
    half = HEAD_DIM // 2
    freqs = np.tile(ROPE_BASE ** (-np.arange(half, dtype=np.float64) / half), 2)
    angles = np.arange(rows, dtype=np.float64)[:, None] * freqs[None, :]
    parts = [np.cos(angles), np.sin(angles), np.tile(freqs, (8, 1))]
    return jnp.asarray(np.concatenate(parts, axis=0).astype(np.float32))


def rotation(table_ref, length):
    rows = (table_ref.shape[0] - 8) // 2
    start = length.astype(jnp.float32) * table_ref[2 * rows : 2 * rows + 8, :]
    cos_start, sin_start = jnp.cos(start)[0:1], jnp.sin(start)[0:1]
    cos_row, sin_row = table_ref[0:rows, :], table_ref[rows : 2 * rows, :]
    lane = lax.broadcasted_iota(jnp.int32, (1, HEAD_DIM), 1)
    sign = jnp.where(lane < HEAD_DIM // 2, -1.0, 1.0)
    cosine = cos_row * cos_start - sin_row * sin_start
    return cosine, sin_row * (cos_start * sign) + cos_row * (sin_start * sign)


def turn(x, cosine, sine):
    x = x.astype(jnp.float32)
    return (x * cosine + pltpu.roll(x, HEAD_DIM // 2, 1) * sine).astype(jnp.bfloat16)


def info_rows(new_count):
    sizes = [("cos", new_count), ("sin", new_count), ("bias", 8), ("scalars", 8), ("new", 2 * KV_HEADS * new_count)]
    at, rows = 0, {}
    for name, size in sizes:
        rows[name] = at
        at += size
    return rows, at


def fresh_rows(info_ref, base, residue, new_count, count, quarter, lanes):
    groups = new_count // count
    stack = [
        info_ref[pl.ds(base + (head + lanes) * new_count + residue, count, stride=groups), :]
        for head in range(0, 2 * KV_HEADS, quarter)
    ]
    return jnp.concatenate(stack, axis=0)


def front_kernel(
    far, me_ref, assign_any, length_any, owner_any, stripe_any, block_any, table_any, pool_any, *refs
):
    groups, slots, width = pool_any.shape
    send_refs, info_any, refs = refs[:AHEAD], refs[AHEAD], refs[AHEAD + 1 :]
    (assign_ref, length_ref, owner_ref, stripe_ref, residue_ref, block_ref, table_ref, pool_ref, pack_ref, info_ref,
     small_sems, pool_sems, send_sems, info_sems) = refs
    new_count = block_any.shape[0]
    count = new_count // groups
    quarter = width * count // slots // HEAD_DIM
    at, rows = info_rows(new_count)
    pairs = [
        (assign_any, assign_ref), (length_any, length_ref), (owner_any, owner_ref), (stripe_any, stripe_ref),
        (block_any, block_ref), (table_any, table_ref),
    ]
    smalls = [pltpu.make_async_copy(*pair, small_sems.at[i]) for i, pair in enumerate(pairs)]
    for copy in smalls:
        copy.start()
    pool_copies = [
        pltpu.make_async_copy(pool_any.at[pl.ds(low, 4)], pool_ref.at[pl.ds(low, 4)], pool_sems.at[low // 4])
        for low in range(0, groups, 4)
    ]
    for copy in pool_copies:
        copy.start()
    me = me_ref[0]
    for copy in smalls:
        copy.wait()
    request = assign_ref[me]
    length = length_ref[request]
    for residue in range(groups):
        residue_ref[owner_ref[request, residue]] = residue
    cosine, sine = rotation(table_ref, length)
    for head in range(KV_HEADS):
        low = at["new"] + head * new_count
        info_ref[low : low + new_count] = turn(block_ref[:, column(head)], cosine, sine).astype(jnp.float32)
        low += KV_HEADS * new_count
        info_ref[low : low + new_count] = block_ref[:, column(KV_HEADS + head)].astype(jnp.float32)

    def info_copy(part, low, high):
        part_rows = pl.ds(low, high - low)
        return pltpu.make_async_copy(info_ref.at[part_rows], info_any.at[part_rows], info_sems.at[part])

    info_copy(0, at["new"], rows).start()
    for copy in pool_copies:
        copy.wait()
    sends = []
    for p in range(AHEAD):
        pack_ref[p, :, 0:width] = pool_ref[assign_ref[me ^ far[p]]]
        for lanes in range(quarter):
            pack_ref[p, :, width + lanes * HEAD_DIM : width + (lanes + 1) * HEAD_DIM] = fresh_rows(
                info_ref, at["new"], residue_ref[me ^ far[p]], new_count, count, quarter, lanes
            ).astype(jnp.bfloat16)
        sends.append(pltpu.make_async_copy(pack_ref.at[p], send_refs[p], send_sems.at[p]))
        sends[-1].start()
    info_ref[at["cos"] : at["cos"] + new_count] = cosine
    info_ref[at["sin"] : at["sin"] + new_count] = sine
    per_row = HEAD_DIM // slots
    row = lax.broadcasted_iota(jnp.int32, (8, HEAD_DIM), 0)
    lane = lax.broadcasted_iota(jnp.int32, (8, HEAD_DIM), 1)
    piece, slot = row * per_row + lane // slots, lane % slots
    holder, requests, residues = jnp.zeros_like(lane), jnp.zeros_like(lane), jnp.zeros_like(lane)
    for p in range(groups):
        other = holder_of(p, me, groups, far)
        holder = jnp.where(piece == p, other, holder)
        requests = jnp.where(lane == p, assign_ref[other], requests)
        residues = jnp.where(lane == p, residue_ref[other], residues)
    bias = jnp.full((8, HEAD_DIM), MASKED, jnp.float32)
    for residue in range(groups):
        live = (holder == stripe_ref[request, residue]) & (slot * groups + residue < length)
        bias = jnp.where(live, 0.0, bias)
    info_ref[at["bias"] : at["bias"] + 8] = bias
    scalars = jnp.where(row == 0, requests, residues)
    info_ref[at["scalars"] : at["scalars"] + 8] = scalars.astype(jnp.float32)
    info_copy(1, 0, at["new"]).start()
    for copy in sends:
        copy.wait()
    info_copy(0, at["new"], rows).wait()
    info_copy(1, 0, at["new"]).wait()


def front(far, me, assignment, prefix_len, owner_map, stripe_map, block_kv, table, pool):
    groups, slots, width = pool.shape
    new_count = block_kv.shape[0]
    count = new_count // groups
    block = jax.ShapeDtypeStruct((slots, width + width * count // slots), jnp.bfloat16)
    info = jax.ShapeDtypeStruct((info_rows(new_count)[1], HEAD_DIM), jnp.float32)
    *blocks, info = pl.pallas_call(
        functools.partial(front_kernel, far),
        out_shape=[block] * AHEAD + [info],
        in_specs=[SMEM] + [ANY] * 7,
        out_specs=[ANY] * (AHEAD + 1),
        scratch_shapes=[
            pltpu.SMEM(assignment.shape, jnp.int32),
            pltpu.SMEM(prefix_len.shape, jnp.int32),
            pltpu.SMEM(owner_map.shape, jnp.int32),
            pltpu.SMEM(stripe_map.shape, jnp.int32),
            pltpu.SMEM(assignment.shape, jnp.int32),
            pltpu.VMEM(block_kv.shape, jnp.bfloat16),
            pltpu.VMEM(table.shape, jnp.float32),
            pltpu.VMEM(pool.shape, jnp.bfloat16),
            pltpu.VMEM((AHEAD,) + block.shape, jnp.bfloat16),
            pltpu.VMEM(info.shape, jnp.float32),
            pltpu.SemaphoreType.DMA((6,)),
            pltpu.SemaphoreType.DMA((groups // 4,)),
            pltpu.SemaphoreType.DMA((AHEAD,)),
            pltpu.SemaphoreType.DMA((2,)),
        ],
        compiler_params=params(60),
        name="front",
    )(me, assignment, prefix_len, owner_map, stripe_map, block_kv, table, pool)
    return blocks, info


def query_kernel(info_ref, q_ref, pool_ref, near_ref, *refs):
    groups, slots, width = pool_ref.shape
    half = groups // 2
    send_refs, refs = refs[: half - AHEAD], refs[half - AHEAD :]
    rot_ref, own_ref, bias_ref, request_ref, scalar_ref, scalar_sem = refs
    new_count = q_ref.shape[0]
    count = new_count // groups
    quarter = width * count // slots // HEAD_DIM
    at, _ = info_rows(new_count)
    scalar_copy = pltpu.make_async_copy(info_ref.at[pl.ds(at["scalars"], 8)], scalar_ref, scalar_sem)
    scalar_copy.start()
    cosine = info_ref[at["cos"] : at["cos"] + new_count]
    sine = info_ref[at["sin"] : at["sin"] + new_count]
    for row in range(bias_ref.shape[1] // HEAD_DIM):
        line = info_ref[at["bias"] + row : at["bias"] + row + 1]
        bias_ref[:, column(row)] = jnp.broadcast_to(line, (8, HEAD_DIM))
    request_ref[...] = info_ref[at["scalars"] : at["scalars"] + 8].astype(jnp.int32)
    for head in range(2 * KV_HEADS):
        rows = at["new"] + head * new_count
        own_ref[head] = info_ref[rows : rows + new_count].astype(jnp.bfloat16)
    for head in range(Q_HEADS):
        rows = slice((head % PER_KV) * new_count, (head % PER_KV + 1) * new_count)
        rot_ref[head // PER_KV, rows, :] = turn(q_ref[:, column(head)], cosine, sine)
    scalar_copy.wait()
    targets = [near_ref.at[p] for p in range(half)] + [None] * AHEAD + list(send_refs)
    for p, target in enumerate(targets):
        if target is None:
            continue
        target[:, 0:width] = pool_ref[scalar_ref[0, p].astype(jnp.int32)]
        residue = scalar_ref[1, p].astype(jnp.int32)
        for lanes in range(quarter):
            target[:, width + lanes * HEAD_DIM : width + (lanes + 1) * HEAD_DIM] = fresh_rows(
                info_ref, at["new"], residue, new_count, count, quarter, lanes
            ).astype(jnp.bfloat16)


def rotate_queries(info, queries, pool):
    groups, slots, width = pool.shape
    new_count = queries.shape[0]
    block = (slots, width + width * (new_count // groups) // slots)
    sent = groups // 2 - AHEAD
    near, *outs = pl.pallas_call(
        query_kernel,
        out_shape=[jax.ShapeDtypeStruct((groups // 2,) + block, jnp.bfloat16)]
        + [jax.ShapeDtypeStruct(block, jnp.bfloat16)] * sent
        + [
            jax.ShapeDtypeStruct((KV_HEADS, PER_KV * new_count, HEAD_DIM), jnp.bfloat16),
            jax.ShapeDtypeStruct((2 * KV_HEADS, new_count, HEAD_DIM), jnp.bfloat16),
            jax.ShapeDtypeStruct((8, groups * slots), jnp.float32),
            jax.ShapeDtypeStruct((8, HEAD_DIM), jnp.int32),
        ],
        in_specs=[VMEM] * 3,
        out_specs=[VMEM] * (sent + 5),
        scratch_shapes=[pltpu.SMEM((8, HEAD_DIM), jnp.float32), pltpu.SemaphoreType.DMA],
        compiler_params=params(32),
        name="rotate_queries",
    )(info, queries, pool)
    return near, outs[:sent], outs[sent:]


def quotient(summed, total):
    about = pl.reciprocal(total, approx=True)
    return summed * (about * (2.0 - total * about))


def join_keys(keys, values, got_refs, own_ref, head):
    key_parts = [got[:, column(head)] for got in got_refs]
    value_parts = [got[:, column(KV_HEADS + head)] for got in got_refs]
    if own_ref is not None:
        key_parts.append(own_ref[head])
        value_parts.append(own_ref[KV_HEADS + head])
    keys[head] = jnp.concatenate(key_parts, axis=0)
    value = jnp.concatenate(value_parts, axis=0)
    values[head] = jnp.concatenate([value, jnp.ones_like(value)], axis=1)


def dot_keys(query, keys):
    return lax.dot_general(query, keys, (((1,), (1,)), ((), ())), preferred_element_type=jnp.float32)


def staged(total, score, weigh, mix, finish, beside=None):
    scores, weights = {0: score(0)}, {}
    for at in range(total + 1):
        if at + 1 < total:
            scores[at + 1] = score(at + 1)
        if at >= 1:
            mixed = mix(at - 1, weights.pop(at - 1))
        if at < total:
            weights[at] = weigh(at, scores.pop(at))
        if at >= 1:
            finish(at - 1, mixed)
        if at == 1 and beside is not None:
            beside()


def unpacking(fresh_refs, first, request_vmem, decode_ref, rows_ref, request_ref, request_sem, decode_sems):
    count = rows_ref.shape[1]
    request_copy = pltpu.make_async_copy(request_vmem, request_ref, request_sem)
    request_copy.start()

    def decode_copy(p):
        return pltpu.make_async_copy(
            rows_ref.at[p], decode_ref.at[request_ref[0, first + p]], decode_sems.at[p]
        )

    def start():
        request_copy.wait()
        for p, fresh_ref in enumerate(fresh_refs):
            stack = fresh_ref[...]
            quarter = stack.shape[1]
            for part in range(stack.shape[0] // count):
                rows_ref[p, :, part * quarter : (part + 1) * quarter] = stack[part * count : (part + 1) * count]
            decode_copy(p).start()

    def wait():
        for p in range(len(fresh_refs)):
            decode_copy(p).wait()

    return start, wait


def spare_part(got):
    return got.at[:, pl.ds(WIDTH, got.shape[1] - WIDTH)]


def pieces_of(refs):
    pieces = []
    for ref in refs:
        pieces += [ref] if len(ref.shape) == 2 else [ref.at[i] for i in range(ref.shape[0])]
    return pieces


def attend_kernel(arrays, unpack, rot_ref, bias_ref, own_ref, *refs):
    got_refs, refs = pieces_of(refs[:arrays]), refs[arrays:]
    start, wait = None, None
    if unpack:
        request_vmem, result_ref, level_ref, decode_ref, *scratch = refs
        start, wait = unpacking([spare_part(got) for got in got_refs], 0, request_vmem, decode_ref, *scratch)
    else:
        result_ref, level_ref = refs
    new_count = rot_ref.shape[1] // PER_KV
    span = len(got_refs) * got_refs[0].shape[0]
    token = lax.broadcasted_iota(jnp.int32, (CHUNK, new_count), 0) % new_count
    causal = jnp.where(lax.broadcasted_iota(jnp.int32, (CHUNK, new_count), 1) <= token, 0.0, MASKED)
    bias = bias_ref[0:1, 0:span]
    per_head = PER_KV * new_count // CHUNK
    keys, values, highs = {}, {}, {}

    def place(at):
        return at // per_head, slice(at % per_head * CHUNK, (at % per_head + 1) * CHUNK)

    def score(at):
        head, rows = place(at)
        if at % per_head == 0:
            join_keys(keys, values, got_refs, own_ref, head)
        return dot_keys(rot_ref[head, rows, :], keys[head])

    def weigh(at, scores):
        scores = jnp.concatenate([scores[:, :span] * SCALE + bias, scores[:, span:] * SCALE + causal], axis=1)
        highs[at] = jnp.max(scores, axis=1, keepdims=True)
        return jnp.exp2(scores - highs[at]).astype(jnp.bfloat16)

    def mix(at, weights):
        return jnp.dot(weights, values[at // per_head], preferred_element_type=jnp.float32)

    def finish(at, mixed):
        head, rows = place(at)
        total = mixed[:, HEAD_DIM:]
        result_ref[head, rows, :] = quotient(mixed[:, :HEAD_DIM], total)
        level_ref[head, rows, :] = highs.pop(at) + jnp.log2(total)

    staged(KV_HEADS * per_head, score, weigh, mix, finish, start)
    if unpack:
        wait()


def attend(rot, bias, own, got, requests=None):
    rows, new_count = rot.shape[1], rot.shape[1] // PER_KV
    operands = [rot, bias, own, *got]
    shapes = [jax.ShapeDtypeStruct((KV_HEADS, rows, HEAD_DIM), jnp.float32)] * 2
    out_specs, scratch = [VMEM] * 2, []
    if requests is not None:
        operands.append(requests)
        slots, width = got[-1].shape
        count = (width - WIDTH) * slots // WIDTH
        shapes.append(jax.ShapeDtypeStruct((new_count // count, count, WIDTH), jnp.bfloat16))
        out_specs.append(ANY)
        scratch = unpack_scratch(len(pieces_of(got)), count, requests)
    return pl.pallas_call(
        functools.partial(attend_kernel, len(got), requests is not None),
        out_shape=tuple(shapes),
        in_specs=[VMEM] * len(operands),
        out_specs=tuple(out_specs),
        scratch_shapes=scratch,
        compiler_params=params(32),
        name="attend",
    )(*operands)


def unpack_scratch(pieces, count, requests):
    return [
        pltpu.VMEM((pieces, count, WIDTH), jnp.bfloat16),
        pltpu.SMEM(requests.shape, jnp.int32),
        pltpu.SemaphoreType.DMA,
        pltpu.SemaphoreType.DMA((pieces,)),
    ]


HEADROOM = 96.0


def late_kernel(pieces, first, rot_ref, bias_ref, result_ref, level_ref, *refs):
    got_refs, refs = refs[:pieces], refs[pieces:]
    request_vmem, _, out_ref, decode_ref, done_ref, out_sems, *scratch = refs
    start, wait = unpacking([spare_part(got) for got in got_refs], first, request_vmem, decode_ref, *scratch)
    slots = got_refs[0].shape[0]
    new_count = out_ref.shape[0]
    size = LATE_CHUNK
    heads_in = size // new_count
    bias = bias_ref[0:1, first * slots : (first + pieces) * slots]
    per_head = PER_KV * new_count // size
    chunks = KV_HEADS * per_head
    keys, values, excess = {}, {}, []

    def place(at):
        return at // per_head, slice(at % per_head * size, (at % per_head + 1) * size)

    def out_copy(at):
        width = heads_in * HEAD_DIM
        return pltpu.make_async_copy(
            done_ref.at[at], out_ref.at[:, pl.ds(pl.multiple_of(at * width, width), width)], out_sems.at[at]
        )

    def store(at, result):
        for row in range(heads_in):
            done_ref[at, :, column(row)] = result[row * new_count : (row + 1) * new_count].astype(jnp.bfloat16)
        out_copy(at).start()

    def score(at):
        head, rows = place(at)
        if at % per_head == 0:
            join_keys(keys, values, got_refs, None, head)
        return dot_keys(rot_ref[head, rows, :], keys[head])

    def weigh(at, scores):
        head, rows = place(at)
        powers = scores * SCALE + bias - level_ref[head, rows, :]
        excess.append(jnp.max(powers.reshape(size // 8, 8, HEAD_DIM), axis=0))
        return jnp.exp2(powers).astype(jnp.bfloat16)

    def mix(at, weights):
        return jnp.dot(weights, values[at // per_head], preferred_element_type=jnp.float32)

    def finish(at, mixed):
        head, rows = place(at)
        store(at, quotient(result_ref[head, rows, :] + mixed[:, :HEAD_DIM], 1.0 + mixed[:, HEAD_DIM:]))

    staged(chunks, score, weigh, mix, finish, start)
    most = jnp.max(functools.reduce(jnp.maximum, excess))
    wait()
    for at in range(chunks):
        out_copy(at).wait()

    @pl.when(most > HEADROOM)
    def _():
        for head in range(KV_HEADS):

            def again(chunk, carry, head=head):
                rows = pl.ds(pl.multiple_of(chunk * size, size), size)
                scores = dot_keys(rot_ref[head, rows, :], keys[head]) * SCALE + bias
                level = level_ref[head, rows, :]
                high = jnp.maximum(level, jnp.max(scores, axis=1, keepdims=True))
                factor = jnp.exp2(level - high)
                weights = jnp.exp2(scores - high).astype(jnp.bfloat16)
                mixed = jnp.dot(weights, values[head], preferred_element_type=jnp.float32)
                at = head * per_head + chunk
                summed = result_ref[head, rows, :] * factor + mixed[:, :HEAD_DIM]
                store(at, quotient(summed, factor + mixed[:, HEAD_DIM:]))
                out_copy(at).wait()
                return carry

            lax.fori_loop(0, per_head, again, 0)


def attend_late(rot, bias, result, level, got, first, requests, decode):
    rows, new_count = rot.shape[1], rot.shape[1] // PER_KV
    operands = [rot, bias, result, level, *got, requests, decode]
    chunks = KV_HEADS * rows // LATE_CHUNK
    return pl.pallas_call(
        functools.partial(late_kernel, len(got), first),
        out_shape=(
            jax.ShapeDtypeStruct((new_count, Q_HEADS * HEAD_DIM), jnp.bfloat16),
            jax.ShapeDtypeStruct(decode.shape, jnp.bfloat16),
        ),
        in_specs=[VMEM] * (len(operands) - 1) + [ANY],
        out_specs=(ANY, ANY),
        scratch_shapes=[
            pltpu.VMEM((chunks, new_count, LATE_CHUNK // new_count * HEAD_DIM), jnp.bfloat16),
            pltpu.SemaphoreType.DMA((chunks,)),
        ]
        + unpack_scratch(len(got), decode.shape[1], requests),
        input_output_aliases={len(operands) - 1: 1},
        compiler_params=params(32),
        name="attend_late",
    )(*operands)


def inverse(table):
    places = jnp.arange(table.shape[0], dtype=jnp.int32)
    return jnp.sum(jnp.where(table[None, :] == places[:, None], places, 0), axis=1)


def rotate(rows, positions, heads):
    half = HEAD_DIM // 2
    freqs = ROPE_BASE ** (-jnp.arange(half, dtype=jnp.float32) / half)
    angles = positions.astype(jnp.float32)[:, None] * freqs[None, :]
    cosine = jnp.concatenate([jnp.cos(angles)] * 2, axis=-1)[:, None, :]
    sine = jnp.concatenate([-jnp.sin(angles), jnp.sin(angles)], axis=-1)[:, None, :]
    split = rows.astype(jnp.float32).reshape(rows.shape[0], heads, HEAD_DIM)
    turned = jnp.roll(split, half, axis=-1)
    return (split * cosine + turned * sine).astype(jnp.bfloat16)


def small_pieces(me, assignment, prefix_len, stripe_map, owner_map, queries, block_kv, pool):
    groups, slots, width = pool.shape
    new_count = block_kv.shape[0]
    count = new_count // groups
    request = assignment[me[0]]
    length = prefix_len[request]
    positions = length + jnp.arange(new_count, dtype=jnp.int32)
    rot = rotate(queries, positions, Q_HEADS).reshape(new_count, KV_HEADS, PER_KV, HEAD_DIM)
    rot = jnp.transpose(rot, (1, 2, 0, 3)).reshape(KV_HEADS, PER_KV * new_count, HEAD_DIM)
    new_keys = rotate(block_kv[:, :KV_WIDTH], positions, KV_HEADS).reshape(new_count, KV_WIDTH)
    new_kv = jnp.concatenate([new_keys, block_kv[:, KV_WIDTH:]], axis=1)
    own = jnp.transpose(new_kv.reshape(new_count, 2 * KV_HEADS, HEAD_DIM), (1, 0, 2))
    spread = jnp.transpose(new_kv.reshape(count, groups, width), (1, 0, 2))
    send = jnp.concatenate([pool[assignment], spread[inverse(owner_map[request])]], axis=1)
    got = lax.all_to_all(send, "pg", split_axis=0, concat_axis=0, tiled=True)
    located = jnp.arange(slots, dtype=jnp.int32)[None, :] * groups + inverse(stripe_map[request])[:, None]
    bias = jnp.where(located < length, 0.0, MASKED).astype(jnp.float32).reshape(1, groups * slots)
    keys = got[:, :slots].reshape(groups * slots, width)
    result, _ = attend(rot, jnp.broadcast_to(bias, (8, groups * slots)), own, [keys])
    result = result.astype(jnp.bfloat16).reshape(KV_HEADS, PER_KV, new_count, HEAD_DIM)
    attended = jnp.transpose(result, (2, 0, 1, 3)).reshape(new_count, Q_HEADS * HEAD_DIM)
    return attended, got[inverse(assignment), slots:]


def shards(queries, block_kv, pool_kv, prefix_len, assignment, stripe_map, owner_map):
    queries, block_kv, pool = queries[0], block_kv[0], pool_kv[0]
    groups, slots, width = pool.shape
    new_count = queries.shape[0]
    count = new_count // groups
    me = lax.axis_index("pg").astype(jnp.int32).reshape(1)
    if groups != 16 or slots % 16 or HEAD_DIM % slots or count % 8 or slots % count:
        attended, decode_kv = small_pieces(
            me, assignment, prefix_len, stripe_map, owner_map, queries, block_kv, pool
        )
        return (attended[None], decode_kv[None])
    half = groups // 2
    far = far_partners(groups)
    table = rotation_tables(new_count)
    blocks, info = front(far, me, assignment, prefix_len, owner_map, stripe_map, block_kv, table, pool)
    near, other_blocks, (rot, own, bias, requests) = rotate_queries(info, queries, pool)
    got = []
    for block, t in zip(list(blocks) + list(other_blocks), far):
        got.append(lax.ppermute(block, "pg", [(source, source ^ t) for source in range(groups)]))
    halves = [list(range(low, low + half)) for low in range(0, groups, half)]
    got_near = lax.all_to_all(near, "pg", split_axis=0, concat_axis=0, axis_index_groups=halves, tiled=True)
    result, level, decode_kv = attend(rot, bias, own, [got_near] + got[:AHEAD], requests)
    attended, decode_kv = attend_late(rot, bias, result, level, got[AHEAD:], half + AHEAD, requests, decode_kv)
    return (attended[None], decode_kv[None])


def solution(mesh):
    return jax.shard_map(
        shards,
        mesh=mesh,
        in_specs=(
            P(("rep", "pg"), None, None),
            P(("rep", "pg"), None, None),
            P(("rep", "pg"), None, None, None),
            P("rep"),
            P("rep"),
            P("rep", None),
            P("rep", None),
        ),
        out_specs=(P(("rep", "pg"), None, None), P(("rep", "pg"), None, None, None)),
        check_vma=False,
    )
```

```python
import functools
import math

import jax
import jax.numpy as jnp
import numpy as np
from jax import lax
from jax.experimental import pallas as pl
from jax.experimental.pallas import tpu as pltpu
from jax.sharding import PartitionSpec as P

Q_HEADS = 32
KV_HEADS = 4
HEAD_DIM = 128
PER_KV = Q_HEADS // KV_HEADS
KV_WIDTH = KV_HEADS * HEAD_DIM
WIDTH = 2 * KV_WIDTH

ROPE_BASE = 1000000.0
MASKED = -1e30
SCALE = HEAD_DIM ** -0.5 / math.log(2.0)
CHUNK = 256
LATE_CHUNK = 256
AHEAD = 4

SMEM = pl.BlockSpec(memory_space=pltpu.SMEM)
VMEM = pl.BlockSpec(memory_space=pltpu.VMEM)
ANY = pl.BlockSpec(memory_space=pl.ANY)


def params(mib):
    return pltpu.CompilerParams(vmem_limit_bytes=mib * 1024 * 1024)


def column(head):
    return slice(head * HEAD_DIM, (head + 1) * HEAD_DIM)


def far_partners(groups):
    quarter = groups // 4
    next_to, beyond = list(range(2 * quarter, 3 * quarter)), list(range(3 * quarter, 4 * quarter))
    order = []
    for at in range(quarter):
        order += [next_to[at ^ (at >> 1)], beyond[(at ^ (at >> 1)) ^ 1]]
    return order


def holder_of(p, me, groups, far):
    half = groups // 2
    return me // half * half + p if p < half else me ^ far[p - half]


def rotation_tables(rows):
    half = HEAD_DIM // 2
    freqs = np.tile(ROPE_BASE ** (-np.arange(half, dtype=np.float64) / half), 2)
    angles = np.arange(rows, dtype=np.float64)[:, None] * freqs[None, :]
    parts = [np.cos(angles), np.sin(angles), np.tile(freqs, (8, 1))]
    return jnp.asarray(np.concatenate(parts, axis=0).astype(np.float32))


def rotation(table_ref, length):
    rows = (table_ref.shape[0] - 8) // 2
    start = length.astype(jnp.float32) * table_ref[2 * rows : 2 * rows + 8, :]
    cos_start, sin_start = jnp.cos(start)[0:1], jnp.sin(start)[0:1]
    cos_row, sin_row = table_ref[0:rows, :], table_ref[rows : 2 * rows, :]
    lane = lax.broadcasted_iota(jnp.int32, (1, HEAD_DIM), 1)
    sign = jnp.where(lane < HEAD_DIM // 2, -1.0, 1.0)
    cosine = cos_row * cos_start - sin_row * sin_start
    return cosine, sin_row * (cos_start * sign) + cos_row * (sin_start * sign)


def turn(x, cosine, sine):
    x = x.astype(jnp.float32)
    return (x * cosine + pltpu.roll(x, HEAD_DIM // 2, 1) * sine).astype(jnp.bfloat16)


def info_rows(new_count):
    sizes = [("cos", new_count), ("sin", new_count), ("bias", 8), ("scalars", 8), ("new", 2 * KV_HEADS * new_count)]
    at, rows = 0, {}
    for name, size in sizes:
        rows[name] = at
        at += size
    return rows, at


def fresh_rows(info_ref, base, residue, new_count, count, quarter, lanes):
    groups = new_count // count
    stack = [
        info_ref[pl.ds(base + (head + lanes) * new_count + residue, count, stride=groups), :]
        for head in range(0, 2 * KV_HEADS, quarter)
    ]
    return jnp.concatenate(stack, axis=0)


def front_kernel(
    far, me_ref, assign_any, length_any, owner_any, stripe_any, block_any, table_any, pool_any, *refs
):
    groups, slots, width = pool_any.shape
    send_refs, info_any, refs = refs[:AHEAD], refs[AHEAD], refs[AHEAD + 1 :]
    (assign_ref, length_ref, owner_ref, stripe_ref, residue_ref, block_ref, table_ref, pool_ref, pack_ref, info_ref,
     small_sems, pool_sems, send_sems, info_sems) = refs
    new_count = block_any.shape[0]
    count = new_count // groups
    quarter = width * count // slots // HEAD_DIM
    at, rows = info_rows(new_count)
    pairs = [
        (assign_any, assign_ref), (length_any, length_ref), (owner_any, owner_ref), (stripe_any, stripe_ref),
        (block_any, block_ref), (table_any, table_ref),
    ]
    smalls = [pltpu.make_async_copy(*pair, small_sems.at[i]) for i, pair in enumerate(pairs)]
    for copy in smalls:
        copy.start()
    pool_copies = [
        pltpu.make_async_copy(pool_any.at[pl.ds(low, 4)], pool_ref.at[pl.ds(low, 4)], pool_sems.at[low // 4])
        for low in range(0, groups, 4)
    ]
    for copy in pool_copies:
        copy.start()
    me = me_ref[0]
    for copy in smalls:
        copy.wait()
    request = assign_ref[me]
    length = length_ref[request]
    for residue in range(groups):
        residue_ref[owner_ref[request, residue]] = residue
    cosine, sine = rotation(table_ref, length)
    for head in range(KV_HEADS):
        low = at["new"] + head * new_count
        info_ref[low : low + new_count] = turn(block_ref[:, column(head)], cosine, sine).astype(jnp.float32)
        low += KV_HEADS * new_count
        info_ref[low : low + new_count] = block_ref[:, column(KV_HEADS + head)].astype(jnp.float32)

    def info_copy(part, low, high):
        part_rows = pl.ds(low, high - low)
        return pltpu.make_async_copy(info_ref.at[part_rows], info_any.at[part_rows], info_sems.at[part])

    info_copy(0, at["new"], rows).start()
    for copy in pool_copies:
        copy.wait()
    sends = []
    for p in range(AHEAD):
        pack_ref[p, :, 0:width] = pool_ref[assign_ref[me ^ far[p]]]
        for lanes in range(quarter):
            pack_ref[p, :, width + lanes * HEAD_DIM : width + (lanes + 1) * HEAD_DIM] = fresh_rows(
                info_ref, at["new"], residue_ref[me ^ far[p]], new_count, count, quarter, lanes
            ).astype(jnp.bfloat16)
        sends.append(pltpu.make_async_copy(pack_ref.at[p], send_refs[p], send_sems.at[p]))
        sends[-1].start()
    info_ref[at["cos"] : at["cos"] + new_count] = cosine
    info_ref[at["sin"] : at["sin"] + new_count] = sine
    per_row = HEAD_DIM // slots
    row = lax.broadcasted_iota(jnp.int32, (8, HEAD_DIM), 0)
    lane = lax.broadcasted_iota(jnp.int32, (8, HEAD_DIM), 1)
    piece, slot = row * per_row + lane // slots, lane % slots
    holder, requests, residues = jnp.zeros_like(lane), jnp.zeros_like(lane), jnp.zeros_like(lane)
    for p in range(groups):
        other = holder_of(p, me, groups, far)
        holder = jnp.where(piece == p, other, holder)
        requests = jnp.where(lane == p, assign_ref[other], requests)
        residues = jnp.where(lane == p, residue_ref[other], residues)
    bias = jnp.full((8, HEAD_DIM), MASKED, jnp.float32)
    for residue in range(groups):
        live = (holder == stripe_ref[request, residue]) & (slot * groups + residue < length)
        bias = jnp.where(live, 0.0, bias)
    info_ref[at["bias"] : at["bias"] + 8] = bias
    scalars = jnp.where(row == 0, requests, residues)
    info_ref[at["scalars"] : at["scalars"] + 8] = scalars.astype(jnp.float32)
    info_copy(1, 0, at["new"]).start()
    for copy in sends:
        copy.wait()
    info_copy(0, at["new"], rows).wait()
    info_copy(1, 0, at["new"]).wait()


def front(far, me, assignment, prefix_len, owner_map, stripe_map, block_kv, table, pool):
    groups, slots, width = pool.shape
    new_count = block_kv.shape[0]
    count = new_count // groups
    block = jax.ShapeDtypeStruct((slots, width + width * count // slots), jnp.bfloat16)
    info = jax.ShapeDtypeStruct((info_rows(new_count)[1], HEAD_DIM), jnp.float32)
    *blocks, info = pl.pallas_call(
        functools.partial(front_kernel, far),
        out_shape=[block] * AHEAD + [info],
        in_specs=[SMEM] + [ANY] * 7,
        out_specs=[ANY] * (AHEAD + 1),
        scratch_shapes=[
            pltpu.SMEM(assignment.shape, jnp.int32),
            pltpu.SMEM(prefix_len.shape, jnp.int32),
            pltpu.SMEM(owner_map.shape, jnp.int32),
            pltpu.SMEM(stripe_map.shape, jnp.int32),
            pltpu.SMEM(assignment.shape, jnp.int32),
            pltpu.VMEM(block_kv.shape, jnp.bfloat16),
            pltpu.VMEM(table.shape, jnp.float32),
            pltpu.VMEM(pool.shape, jnp.bfloat16),
            pltpu.VMEM((AHEAD,) + block.shape, jnp.bfloat16),
            pltpu.VMEM(info.shape, jnp.float32),
            pltpu.SemaphoreType.DMA((6,)),
            pltpu.SemaphoreType.DMA((groups // 4,)),
            pltpu.SemaphoreType.DMA((AHEAD,)),
            pltpu.SemaphoreType.DMA((2,)),
        ],
        compiler_params=params(60),
        name="front",
    )(me, assignment, prefix_len, owner_map, stripe_map, block_kv, table, pool)
    return blocks, info


def query_kernel(info_ref, q_ref, pool_ref, near_ref, *refs):
    groups, slots, width = pool_ref.shape
    half = groups // 2
    send_refs, refs = refs[: half - AHEAD], refs[half - AHEAD :]
    rot_ref, own_ref, bias_ref, request_ref, scalar_ref, scalar_sem = refs
    new_count = q_ref.shape[0]
    count = new_count // groups
    quarter = width * count // slots // HEAD_DIM
    at, _ = info_rows(new_count)
    scalar_copy = pltpu.make_async_copy(info_ref.at[pl.ds(at["scalars"], 8)], scalar_ref, scalar_sem)
    scalar_copy.start()
    cosine = info_ref[at["cos"] : at["cos"] + new_count]
    sine = info_ref[at["sin"] : at["sin"] + new_count]
    for row in range(bias_ref.shape[1] // HEAD_DIM):
        line = info_ref[at["bias"] + row : at["bias"] + row + 1]
        bias_ref[:, column(row)] = jnp.broadcast_to(line, (8, HEAD_DIM))
    request_ref[...] = info_ref[at["scalars"] : at["scalars"] + 8].astype(jnp.int32)
    for head in range(2 * KV_HEADS):
        rows = at["new"] + head * new_count
        own_ref[head] = info_ref[rows : rows + new_count].astype(jnp.bfloat16)
    for head in range(Q_HEADS):
        rows = slice((head % PER_KV) * new_count, (head % PER_KV + 1) * new_count)
        rot_ref[head // PER_KV, rows, :] = turn(q_ref[:, column(head)], cosine, sine)
    scalar_copy.wait()
    targets = [near_ref.at[p] for p in range(half)] + [None] * AHEAD + list(send_refs)
    for p, target in enumerate(targets):
        if target is None:
            continue
        target[:, 0:width] = pool_ref[scalar_ref[0, p].astype(jnp.int32)]
        residue = scalar_ref[1, p].astype(jnp.int32)
        for lanes in range(quarter):
            target[:, width + lanes * HEAD_DIM : width + (lanes + 1) * HEAD_DIM] = fresh_rows(
                info_ref, at["new"], residue, new_count, count, quarter, lanes
            ).astype(jnp.bfloat16)


def rotate_queries(info, queries, pool):
    groups, slots, width = pool.shape
    new_count = queries.shape[0]
    block = (slots, width + width * (new_count // groups) // slots)
    sent = groups // 2 - AHEAD
    near, *outs = pl.pallas_call(
        query_kernel,
        out_shape=[jax.ShapeDtypeStruct((groups // 2,) + block, jnp.bfloat16)]
        + [jax.ShapeDtypeStruct(block, jnp.bfloat16)] * sent
        + [
            jax.ShapeDtypeStruct((KV_HEADS, PER_KV * new_count, HEAD_DIM), jnp.bfloat16),
            jax.ShapeDtypeStruct((2 * KV_HEADS, new_count, HEAD_DIM), jnp.bfloat16),
            jax.ShapeDtypeStruct((8, groups * slots), jnp.float32),
            jax.ShapeDtypeStruct((8, HEAD_DIM), jnp.int32),
        ],
        in_specs=[VMEM] * 3,
        out_specs=[VMEM] * (sent + 5),
        scratch_shapes=[pltpu.SMEM((8, HEAD_DIM), jnp.float32), pltpu.SemaphoreType.DMA],
        compiler_params=params(32),
        name="rotate_queries",
    )(info, queries, pool)
    return near, outs[:sent], outs[sent:]


def quotient(summed, total):
    about = pl.reciprocal(total, approx=True)
    return summed * (about * (2.0 - total * about))


def join_keys(keys, values, got_refs, own_ref, head):
    key_parts = [got[:, column(head)] for got in got_refs]
    value_parts = [got[:, column(KV_HEADS + head)] for got in got_refs]
    if own_ref is not None:
        key_parts.append(own_ref[head])
        value_parts.append(own_ref[KV_HEADS + head])
    keys[head] = jnp.concatenate(key_parts, axis=0)
    value = jnp.concatenate(value_parts, axis=0)
    values[head] = jnp.concatenate([value, jnp.ones_like(value)], axis=1)


def dot_keys(query, keys):
    return lax.dot_general(query, keys, (((1,), (1,)), ((), ())), preferred_element_type=jnp.float32)


def staged(total, score, weigh, mix, finish, beside=None):
    scores, weights = {0: score(0)}, {}
    for at in range(total + 1):
        if at + 1 < total:
            scores[at + 1] = score(at + 1)
        if at >= 1:
            mixed = mix(at - 1, weights.pop(at - 1))
        if at < total:
            weights[at] = weigh(at, scores.pop(at))
        if at >= 1:
            finish(at - 1, mixed)
        if at == 1 and beside is not None:
            beside()


def unpacking(fresh_refs, first, request_vmem, decode_ref, rows_ref, request_ref, request_sem, decode_sems):
    count = rows_ref.shape[1]
    request_copy = pltpu.make_async_copy(request_vmem, request_ref, request_sem)
    request_copy.start()

    def decode_copy(p):
        return pltpu.make_async_copy(
            rows_ref.at[p], decode_ref.at[request_ref[0, first + p]], decode_sems.at[p]
        )

    def start():
        request_copy.wait()
        for p, fresh_ref in enumerate(fresh_refs):
            stack = fresh_ref[...]
            quarter = stack.shape[1]
            for part in range(stack.shape[0] // count):
                rows_ref[p, :, part * quarter : (part + 1) * quarter] = stack[part * count : (part + 1) * count]
            decode_copy(p).start()

    def wait():
        for p in range(len(fresh_refs)):
            decode_copy(p).wait()

    return start, wait


def spare_part(got):
    return got.at[:, pl.ds(WIDTH, got.shape[1] - WIDTH)]


def pieces_of(refs):
    pieces = []
    for ref in refs:
        pieces += [ref] if len(ref.shape) == 2 else [ref.at[i] for i in range(ref.shape[0])]
    return pieces


def attend_kernel(arrays, unpack, rot_ref, bias_ref, own_ref, *refs):
    got_refs, refs = pieces_of(refs[:arrays]), refs[arrays:]
    start, wait = None, None
    if unpack:
        request_vmem, result_ref, level_ref, decode_ref, *scratch = refs
        start, wait = unpacking([spare_part(got) for got in got_refs], 0, request_vmem, decode_ref, *scratch)
    else:
        result_ref, level_ref = refs
    new_count = rot_ref.shape[1] // PER_KV
    span = len(got_refs) * got_refs[0].shape[0]
    token = lax.broadcasted_iota(jnp.int32, (CHUNK, new_count), 0) % new_count
    causal = jnp.where(lax.broadcasted_iota(jnp.int32, (CHUNK, new_count), 1) <= token, 0.0, MASKED)
    bias = bias_ref[0:1, 0:span]
    per_head = PER_KV * new_count // CHUNK
    keys, values, highs = {}, {}, {}

    def place(at):
        return at // per_head, slice(at % per_head * CHUNK, (at % per_head + 1) * CHUNK)

    def score(at):
        head, rows = place(at)
        if at % per_head == 0:
            join_keys(keys, values, got_refs, own_ref, head)
        return dot_keys(rot_ref[head, rows, :], keys[head])

    def weigh(at, scores):
        scores = jnp.concatenate([scores[:, :span] * SCALE + bias, scores[:, span:] * SCALE + causal], axis=1)
        highs[at] = jnp.max(scores, axis=1, keepdims=True)
        return jnp.exp2(scores - highs[at]).astype(jnp.bfloat16)

    def mix(at, weights):
        return jnp.dot(weights, values[at // per_head], preferred_element_type=jnp.float32)

    def finish(at, mixed):
        head, rows = place(at)
        total = mixed[:, HEAD_DIM:]
        result_ref[head, rows, :] = quotient(mixed[:, :HEAD_DIM], total)
        level_ref[head, rows, :] = highs.pop(at) + jnp.log2(total)

    staged(KV_HEADS * per_head, score, weigh, mix, finish, start)
    if unpack:
        wait()


def attend(rot, bias, own, got, requests=None):
    rows, new_count = rot.shape[1], rot.shape[1] // PER_KV
    operands = [rot, bias, own, *got]
    shapes = [jax.ShapeDtypeStruct((KV_HEADS, rows, HEAD_DIM), jnp.float32)] * 2
    out_specs, scratch = [VMEM] * 2, []
    if requests is not None:
        operands.append(requests)
        slots, width = got[-1].shape
        count = (width - WIDTH) * slots // WIDTH
        shapes.append(jax.ShapeDtypeStruct((new_count // count, count, WIDTH), jnp.bfloat16))
        out_specs.append(ANY)
        scratch = unpack_scratch(len(pieces_of(got)), count, requests)
    return pl.pallas_call(
        functools.partial(attend_kernel, len(got), requests is not None),
        out_shape=tuple(shapes),
        in_specs=[VMEM] * len(operands),
        out_specs=tuple(out_specs),
        scratch_shapes=scratch,
        compiler_params=params(32),
        name="attend",
    )(*operands)


def unpack_scratch(pieces, count, requests):
    return [
        pltpu.VMEM((pieces, count, WIDTH), jnp.bfloat16),
        pltpu.SMEM(requests.shape, jnp.int32),
        pltpu.SemaphoreType.DMA,
        pltpu.SemaphoreType.DMA((pieces,)),
    ]


HEADROOM = 96.0


def late_kernel(pieces, first, rot_ref, bias_ref, result_ref, level_ref, *refs):
    got_refs, refs = refs[:pieces], refs[pieces:]
    request_vmem, _, out_ref, decode_ref, done_ref, out_sems, *scratch = refs
    start, wait = unpacking([spare_part(got) for got in got_refs], first, request_vmem, decode_ref, *scratch)
    slots = got_refs[0].shape[0]
    new_count = out_ref.shape[0]
    size = LATE_CHUNK
    heads_in = size // new_count
    bias = bias_ref[0:1, first * slots : (first + pieces) * slots]
    per_head = PER_KV * new_count // size
    chunks = KV_HEADS * per_head
    keys, values, excess = {}, {}, []

    def place(at):
        return at // per_head, slice(at % per_head * size, (at % per_head + 1) * size)

    def out_copy(at):
        width = heads_in * HEAD_DIM
        return pltpu.make_async_copy(
            done_ref.at[at], out_ref.at[:, pl.ds(pl.multiple_of(at * width, width), width)], out_sems.at[at]
        )

    def store(at, result):
        for row in range(heads_in):
            done_ref[at, :, column(row)] = result[row * new_count : (row + 1) * new_count].astype(jnp.bfloat16)
        out_copy(at).start()

    def score(at):
        head, rows = place(at)
        if at % per_head == 0:
            join_keys(keys, values, got_refs, None, head)
        return dot_keys(rot_ref[head, rows, :], keys[head])

    def weigh(at, scores):
        head, rows = place(at)
        powers = scores * SCALE + bias - level_ref[head, rows, :]
        excess.append(jnp.max(powers.reshape(size // 8, 8, HEAD_DIM), axis=0))
        return jnp.exp2(powers).astype(jnp.bfloat16)

    def mix(at, weights):
        return jnp.dot(weights, values[at // per_head], preferred_element_type=jnp.float32)

    def finish(at, mixed):
        head, rows = place(at)
        store(at, quotient(result_ref[head, rows, :] + mixed[:, :HEAD_DIM], 1.0 + mixed[:, HEAD_DIM:]))

    staged(chunks, score, weigh, mix, finish, start)
    most = jnp.max(functools.reduce(jnp.maximum, excess))
    wait()
    for at in range(chunks):
        out_copy(at).wait()

    @pl.when(most > HEADROOM)
    def _():
        for head in range(KV_HEADS):

            def again(chunk, carry, head=head):
                rows = pl.ds(pl.multiple_of(chunk * size, size), size)
                scores = dot_keys(rot_ref[head, rows, :], keys[head]) * SCALE + bias
                level = level_ref[head, rows, :]
                high = jnp.maximum(level, jnp.max(scores, axis=1, keepdims=True))
                factor = jnp.exp2(level - high)
                weights = jnp.exp2(scores - high).astype(jnp.bfloat16)
                mixed = jnp.dot(weights, values[head], preferred_element_type=jnp.float32)
                at = head * per_head + chunk
                summed = result_ref[head, rows, :] * factor + mixed[:, :HEAD_DIM]
                store(at, quotient(summed, factor + mixed[:, HEAD_DIM:]))
                out_copy(at).wait()
                return carry

            lax.fori_loop(0, per_head, again, 0)


def attend_late(rot, bias, result, level, got, first, requests, decode):
    rows, new_count = rot.shape[1], rot.shape[1] // PER_KV
    operands = [rot, bias, result, level, *got, requests, decode]
    chunks = KV_HEADS * rows // LATE_CHUNK
    return pl.pallas_call(
        functools.partial(late_kernel, len(got), first),
        out_shape=(
            jax.ShapeDtypeStruct((new_count, Q_HEADS * HEAD_DIM), jnp.bfloat16),
            jax.ShapeDtypeStruct(decode.shape, jnp.bfloat16),
        ),
        in_specs=[VMEM] * (len(operands) - 1) + [ANY],
        out_specs=(ANY, ANY),
        scratch_shapes=[
            pltpu.VMEM((chunks, new_count, LATE_CHUNK // new_count * HEAD_DIM), jnp.bfloat16),
            pltpu.SemaphoreType.DMA((chunks,)),
        ]
        + unpack_scratch(len(got), decode.shape[1], requests),
        input_output_aliases={len(operands) - 1: 1},
        compiler_params=params(32),
        name="attend_late",
    )(*operands)


def inverse(table):
    places = jnp.arange(table.shape[0], dtype=jnp.int32)
    return jnp.sum(jnp.where(table[None, :] == places[:, None], places, 0), axis=1)


def rotate(rows, positions, heads):
    half = HEAD_DIM // 2
    freqs = ROPE_BASE ** (-jnp.arange(half, dtype=jnp.float32) / half)
    angles = positions.astype(jnp.float32)[:, None] * freqs[None, :]
    cosine = jnp.concatenate([jnp.cos(angles)] * 2, axis=-1)[:, None, :]
    sine = jnp.concatenate([-jnp.sin(angles), jnp.sin(angles)], axis=-1)[:, None, :]
    split = rows.astype(jnp.float32).reshape(rows.shape[0], heads, HEAD_DIM)
    turned = jnp.roll(split, half, axis=-1)
    return (split * cosine + turned * sine).astype(jnp.bfloat16)


def small_pieces(me, assignment, prefix_len, stripe_map, owner_map, queries, block_kv, pool):
    groups, slots, width = pool.shape
    new_count = block_kv.shape[0]
    count = new_count // groups
    request = assignment[me[0]]
    length = prefix_len[request]
    positions = length + jnp.arange(new_count, dtype=jnp.int32)
    rot = rotate(queries, positions, Q_HEADS).reshape(new_count, KV_HEADS, PER_KV, HEAD_DIM)
    rot = jnp.transpose(rot, (1, 2, 0, 3)).reshape(KV_HEADS, PER_KV * new_count, HEAD_DIM)
    new_keys = rotate(block_kv[:, :KV_WIDTH], positions, KV_HEADS).reshape(new_count, KV_WIDTH)
    new_kv = jnp.concatenate([new_keys, block_kv[:, KV_WIDTH:]], axis=1)
    own = jnp.transpose(new_kv.reshape(new_count, 2 * KV_HEADS, HEAD_DIM), (1, 0, 2))
    spread = jnp.transpose(new_kv.reshape(count, groups, width), (1, 0, 2))
    send = jnp.concatenate([pool[assignment], spread[inverse(owner_map[request])]], axis=1)
    got = lax.all_to_all(send, "pg", split_axis=0, concat_axis=0, tiled=True)
    located = jnp.arange(slots, dtype=jnp.int32)[None, :] * groups + inverse(stripe_map[request])[:, None]
    bias = jnp.where(located < length, 0.0, MASKED).astype(jnp.float32).reshape(1, groups * slots)
    keys = got[:, :slots].reshape(groups * slots, width)
    result, _ = attend(rot, jnp.broadcast_to(bias, (8, groups * slots)), own, [keys])
    result = result.astype(jnp.bfloat16).reshape(KV_HEADS, PER_KV, new_count, HEAD_DIM)
    attended = jnp.transpose(result, (2, 0, 1, 3)).reshape(new_count, Q_HEADS * HEAD_DIM)
    return attended, got[inverse(assignment), slots:]


def shards(queries, block_kv, pool_kv, prefix_len, assignment, stripe_map, owner_map):
    queries, block_kv, pool = queries[0], block_kv[0], pool_kv[0]
    groups, slots, width = pool.shape
    new_count = queries.shape[0]
    count = new_count // groups
    me = lax.axis_index("pg").astype(jnp.int32).reshape(1)
    if groups != 16 or slots % 16 or HEAD_DIM % slots or count % 8 or slots % count:
        attended, decode_kv = small_pieces(
            me, assignment, prefix_len, stripe_map, owner_map, queries, block_kv, pool
        )
        return (attended[None], decode_kv[None])
    half = groups // 2
    far = far_partners(groups)
    table = rotation_tables(new_count)
    blocks, info = front(far, me, assignment, prefix_len, owner_map, stripe_map, block_kv, table, pool)
    near, other_blocks, (rot, own, bias, requests) = rotate_queries(info, queries, pool)
    got = []
    for block, t in zip(list(blocks) + list(other_blocks), far):
        got.append(lax.ppermute(block, "pg", [(source, source ^ t) for source in range(groups)]))
    near, *got[:2] = lax.optimization_barrier((near, *got[:2]))
    halves = [list(range(low, low + half)) for low in range(0, groups, half)]
    got_near = lax.all_to_all(near, "pg", split_axis=0, concat_axis=0, axis_index_groups=halves, tiled=True)
    result, level, decode_kv = attend(rot, bias, own, [got_near] + got[:AHEAD], requests)
    attended, decode_kv = attend_late(rot, bias, result, level, got[AHEAD:], half + AHEAD, requests, decode_kv)
    return (attended[None], decode_kv[None])


def solution(mesh):
    return jax.shard_map(
        shards,
        mesh=mesh,
        in_specs=(
            P(("rep", "pg"), None, None),
            P(("rep", "pg"), None, None),
            P(("rep", "pg"), None, None, None),
            P("rep"),
            P("rep"),
            P("rep", None),
            P("rep", None),
        ),
        out_specs=(P(("rep", "pg"), None, None), P(("rep", "pg"), None, None, None)),
        check_vma=False,
    )
```

```python
import functools
import math

import jax
import jax.numpy as jnp
import numpy as np
from jax import lax
from jax.experimental import pallas as pl
from jax.experimental.pallas import tpu as pltpu
from jax.sharding import PartitionSpec as P

Q_HEADS = 32
KV_HEADS = 4
HEAD_DIM = 128
PER_KV = Q_HEADS // KV_HEADS
KV_WIDTH = KV_HEADS * HEAD_DIM
WIDTH = 2 * KV_WIDTH

ROPE_BASE = 1000000.0
MASKED = -1e30
SCALE = HEAD_DIM ** -0.5 / math.log(2.0)
CHUNK = 256
LATE = 4
LATE_CHUNK = 256
AHEAD = 4

SMEM = pl.BlockSpec(memory_space=pltpu.SMEM)
VMEM = pl.BlockSpec(memory_space=pltpu.VMEM)
ANY = pl.BlockSpec(memory_space=pl.ANY)


def params(mib):
    return pltpu.CompilerParams(vmem_limit_bytes=mib * 1024 * 1024)


def column(head):
    return slice(head * HEAD_DIM, (head + 1) * HEAD_DIM)


def order_of(groups):
    half = groups // 2
    far, near = list(range(half, 2 * half)), list(range(half - 1, 0, -1))
    order = [(far if kind == "f" else near).pop(0) for kind in "ffnfnfnfnfnfnfn"]
    order.insert(groups - LATE - 1, 0)
    return order


def rotation_tables(rows):
    half = HEAD_DIM // 2
    freqs = np.tile(ROPE_BASE ** (-np.arange(half, dtype=np.float64) / half), 2)
    angles = np.arange(rows, dtype=np.float64)[:, None] * freqs[None, :]
    parts = [np.cos(angles), np.sin(angles), np.tile(freqs, (8, 1))]
    return jnp.asarray(np.concatenate(parts, axis=0).astype(np.float32))


def rotation(table_ref, length):
    rows = (table_ref.shape[0] - 8) // 2
    start = length.astype(jnp.float32) * table_ref[2 * rows : 2 * rows + 8, :]
    cos_start, sin_start = jnp.cos(start)[0:1], jnp.sin(start)[0:1]
    cos_row, sin_row = table_ref[0:rows, :], table_ref[rows : 2 * rows, :]
    lane = lax.broadcasted_iota(jnp.int32, (1, HEAD_DIM), 1)
    sign = jnp.where(lane < HEAD_DIM // 2, -1.0, 1.0)
    cosine = cos_row * cos_start - sin_row * sin_start
    return cosine, sin_row * (cos_start * sign) + cos_row * (sin_start * sign)


def turn(x, cosine, sine):
    x = x.astype(jnp.float32)
    return (x * cosine + pltpu.roll(x, HEAD_DIM // 2, 1) * sine).astype(jnp.bfloat16)


def info_rows(new_count):
    sizes = [("cos", new_count), ("sin", new_count), ("bias", 8), ("scalars", 8), ("new", 2 * KV_HEADS * new_count)]
    at, rows = 0, {}
    for name, size in sizes:
        rows[name] = at
        at += size
    return rows, at


def fresh_rows(info_ref, base, residue, new_count, count, quarter, lanes):
    groups = new_count // count
    stack = [
        info_ref[pl.ds(base + (head + lanes) * new_count + residue, count, stride=groups), :]
        for head in range(0, 2 * KV_HEADS, quarter)
    ]
    return jnp.concatenate(stack, axis=0)


def front_kernel(
    order, me_ref, assign_any, length_any, owner_any, stripe_any, block_any, table_any, pool_any, *refs
):
    groups, slots, width = pool_any.shape
    send_refs, info_any, refs = refs[:AHEAD], refs[AHEAD], refs[AHEAD + 1 :]
    (assign_ref, length_ref, owner_ref, stripe_ref, residue_ref, block_ref, table_ref, pool_ref, pack_ref, info_ref,
     small_sems, pool_sems, send_sems, info_sems) = refs
    new_count = block_any.shape[0]
    count = new_count // groups
    quarter = width * count // slots // HEAD_DIM
    at, rows = info_rows(new_count)
    pairs = [
        (assign_any, assign_ref), (length_any, length_ref), (owner_any, owner_ref), (stripe_any, stripe_ref),
        (block_any, block_ref), (table_any, table_ref),
    ]
    smalls = [pltpu.make_async_copy(*pair, small_sems.at[i]) for i, pair in enumerate(pairs)]
    for copy in smalls:
        copy.start()
    pool_copies = [
        pltpu.make_async_copy(pool_any.at[pl.ds(low, 4)], pool_ref.at[pl.ds(low, 4)], pool_sems.at[low // 4])
        for low in range(0, groups, 4)
    ]
    for copy in pool_copies:
        copy.start()
    me = me_ref[0]
    for copy in smalls:
        copy.wait()
    request = assign_ref[me]
    length = length_ref[request]
    for residue in range(groups):
        residue_ref[owner_ref[request, residue]] = residue
    cosine, sine = rotation(table_ref, length)
    for head in range(KV_HEADS):
        low = at["new"] + head * new_count
        info_ref[low : low + new_count] = turn(block_ref[:, column(head)], cosine, sine).astype(jnp.float32)
        low += KV_HEADS * new_count
        info_ref[low : low + new_count] = block_ref[:, column(KV_HEADS + head)].astype(jnp.float32)

    def info_copy(part, low, high):
        part_rows = pl.ds(low, high - low)
        return pltpu.make_async_copy(info_ref.at[part_rows], info_any.at[part_rows], info_sems.at[part])

    info_copy(0, at["new"], rows).start()
    for copy in pool_copies:
        copy.wait()
    sends = []
    for p in range(AHEAD):
        pack_ref[p, :, 0:width] = pool_ref[assign_ref[me ^ order[p]]]
        for lanes in range(quarter):
            pack_ref[p, :, width + lanes * HEAD_DIM : width + (lanes + 1) * HEAD_DIM] = fresh_rows(
                info_ref, at["new"], residue_ref[me ^ order[p]], new_count, count, quarter, lanes
            ).astype(jnp.bfloat16)
        sends.append(pltpu.make_async_copy(pack_ref.at[p], send_refs[p], send_sems.at[p]))
        sends[-1].start()
    info_ref[at["cos"] : at["cos"] + new_count] = cosine
    info_ref[at["sin"] : at["sin"] + new_count] = sine
    per_row = HEAD_DIM // slots
    row = lax.broadcasted_iota(jnp.int32, (8, HEAD_DIM), 0)
    lane = lax.broadcasted_iota(jnp.int32, (8, HEAD_DIM), 1)
    piece, slot = row * per_row + lane // slots, lane % slots
    holder, requests, residues = jnp.zeros_like(lane), jnp.zeros_like(lane), jnp.zeros_like(lane)
    for p in range(groups):
        other = me ^ order[p]
        holder = jnp.where(piece == p, other, holder)
        requests = jnp.where(lane == p, assign_ref[other], requests)
        residues = jnp.where(lane == p, residue_ref[other], residues)
    bias = jnp.full((8, HEAD_DIM), MASKED, jnp.float32)
    for residue in range(groups):
        live = (holder == stripe_ref[request, residue]) & (slot * groups + residue < length)
        bias = jnp.where(live, 0.0, bias)
    info_ref[at["bias"] : at["bias"] + 8] = bias
    scalars = jnp.where(row == 0, requests, residues)
    info_ref[at["scalars"] : at["scalars"] + 8] = scalars.astype(jnp.float32)
    info_copy(1, 0, at["new"]).start()
    for copy in sends:
        copy.wait()
    info_copy(0, at["new"], rows).wait()
    info_copy(1, 0, at["new"]).wait()


def front(order, me, assignment, prefix_len, owner_map, stripe_map, block_kv, table, pool):
    groups, slots, width = pool.shape
    new_count = block_kv.shape[0]
    count = new_count // groups
    block = jax.ShapeDtypeStruct((slots, width + width * count // slots), jnp.bfloat16)
    info = jax.ShapeDtypeStruct((info_rows(new_count)[1], HEAD_DIM), jnp.float32)
    *blocks, info = pl.pallas_call(
        functools.partial(front_kernel, order),
        out_shape=[block] * AHEAD + [info],
        in_specs=[SMEM] + [ANY] * 7,
        out_specs=[ANY] * (AHEAD + 1),
        scratch_shapes=[
            pltpu.SMEM(assignment.shape, jnp.int32),
            pltpu.SMEM(prefix_len.shape, jnp.int32),
            pltpu.SMEM(owner_map.shape, jnp.int32),
            pltpu.SMEM(stripe_map.shape, jnp.int32),
            pltpu.SMEM(assignment.shape, jnp.int32),
            pltpu.VMEM(block_kv.shape, jnp.bfloat16),
            pltpu.VMEM(table.shape, jnp.float32),
            pltpu.VMEM(pool.shape, jnp.bfloat16),
            pltpu.VMEM((AHEAD,) + block.shape, jnp.bfloat16),
            pltpu.VMEM(info.shape, jnp.float32),
            pltpu.SemaphoreType.DMA((6,)),
            pltpu.SemaphoreType.DMA((groups // 4,)),
            pltpu.SemaphoreType.DMA((AHEAD,)),
            pltpu.SemaphoreType.DMA((2,)),
        ],
        compiler_params=params(60),
        name="front",
    )(me, assignment, prefix_len, owner_map, stripe_map, block_kv, table, pool)
    return blocks, info


def query_kernel(order, info_ref, q_ref, pool_ref, *refs):
    groups, slots, width = pool_ref.shape
    sent = groups - 1 - AHEAD
    send_refs, refs = refs[:sent], refs[sent:]
    rot_ref, own_ref, fresh_ref, bias_ref, request_ref, scalar_ref, scalar_sem = refs
    new_count = q_ref.shape[0]
    count = new_count // groups
    quarter = fresh_ref.shape[1] // HEAD_DIM
    at, _ = info_rows(new_count)
    scalar_copy = pltpu.make_async_copy(info_ref.at[pl.ds(at["scalars"], 8)], scalar_ref, scalar_sem)
    scalar_copy.start()
    cosine = info_ref[at["cos"] : at["cos"] + new_count]
    sine = info_ref[at["sin"] : at["sin"] + new_count]
    for row in range(bias_ref.shape[1] // HEAD_DIM):
        line = info_ref[at["bias"] + row : at["bias"] + row + 1]
        bias_ref[:, column(row)] = jnp.broadcast_to(line, (8, HEAD_DIM))
    request_ref[...] = info_ref[at["scalars"] : at["scalars"] + 8].astype(jnp.int32)
    for head in range(2 * KV_HEADS):
        rows = at["new"] + head * new_count
        own_ref[head, slots : slots + new_count] = info_ref[rows : rows + new_count].astype(jnp.bfloat16)
    for head in range(Q_HEADS):
        rows = slice((head % PER_KV) * new_count, (head % PER_KV + 1) * new_count)
        rot_ref[head // PER_KV, rows, :] = turn(q_ref[:, column(head)], cosine, sine)
    scalar_copy.wait()
    sends = list(send_refs)
    for p in range(AHEAD, groups):
        request = scalar_ref[0, p].astype(jnp.int32)
        residue = scalar_ref[1, p].astype(jnp.int32)
        if order[p] == 0:
            target, base = fresh_ref, 0
            for head in range(2 * KV_HEADS):
                own_ref[head, 0:slots] = pool_ref[request, :, column(head)]
        else:
            target, base = sends.pop(0), width
            target[:, 0:width] = pool_ref[request]
        for lanes in range(quarter):
            target[:, base + lanes * HEAD_DIM : base + (lanes + 1) * HEAD_DIM] = fresh_rows(
                info_ref, at["new"], residue, new_count, count, quarter, lanes
            ).astype(jnp.bfloat16)


def rotate_queries(order, info, queries, pool):
    groups, slots, width = pool.shape
    new_count = queries.shape[0]
    spare = width * (new_count // groups) // slots
    sent = groups - 1 - AHEAD
    outs = pl.pallas_call(
        functools.partial(query_kernel, order),
        out_shape=[jax.ShapeDtypeStruct((slots, width + spare), jnp.bfloat16)] * sent
        + [
            jax.ShapeDtypeStruct((KV_HEADS, PER_KV * new_count, HEAD_DIM), jnp.bfloat16),
            jax.ShapeDtypeStruct((2 * KV_HEADS, slots + new_count, HEAD_DIM), jnp.bfloat16),
            jax.ShapeDtypeStruct((slots, spare), jnp.bfloat16),
            jax.ShapeDtypeStruct((8, groups * slots), jnp.float32),
            jax.ShapeDtypeStruct((8, HEAD_DIM), jnp.int32),
        ],
        in_specs=[VMEM] * 3,
        out_specs=[VMEM] * (sent + 5),
        scratch_shapes=[pltpu.SMEM((8, HEAD_DIM), jnp.float32), pltpu.SemaphoreType.DMA],
        compiler_params=params(32),
        name="rotate_queries",
    )(info, queries, pool)
    return outs[:sent], outs[sent:]


def quotient(summed, total):
    about = pl.reciprocal(total, approx=True)
    return summed * (about * (2.0 - total * about))


def join_keys(keys, values, got_refs, own_ref, head):
    key_parts = [got[:, column(head)] for got in got_refs]
    value_parts = [got[:, column(KV_HEADS + head)] for got in got_refs]
    if own_ref is not None:
        key_parts.append(own_ref[head])
        value_parts.append(own_ref[KV_HEADS + head])
    keys[head] = jnp.concatenate(key_parts, axis=0)
    value = jnp.concatenate(value_parts, axis=0)
    values[head] = jnp.concatenate([value, jnp.ones_like(value)], axis=1)


def dot_keys(query, keys):
    return lax.dot_general(query, keys, (((1,), (1,)), ((), ())), preferred_element_type=jnp.float32)


def staged(total, score, weigh, mix, finish, beside=None):
    scores, weights = {0: score(0)}, {}
    for at in range(total + 1):
        if at + 1 < total:
            scores[at + 1] = score(at + 1)
        if at >= 1:
            mixed = mix(at - 1, weights.pop(at - 1))
        if at < total:
            weights[at] = weigh(at, scores.pop(at))
        if at >= 1:
            finish(at - 1, mixed)
        if at == 1 and beside is not None:
            beside()


def unpacking(fresh_refs, first, request_vmem, decode_ref, rows_ref, request_ref, request_sem, decode_sems):
    count = rows_ref.shape[1]
    request_copy = pltpu.make_async_copy(request_vmem, request_ref, request_sem)
    request_copy.start()

    def decode_copy(p):
        return pltpu.make_async_copy(
            rows_ref.at[p], decode_ref.at[request_ref[0, first + p]], decode_sems.at[p]
        )

    def start():
        request_copy.wait()
        for p, fresh_ref in enumerate(fresh_refs):
            stack = fresh_ref[...]
            quarter = stack.shape[1]
            for part in range(stack.shape[0] // count):
                rows_ref[p, :, part * quarter : (part + 1) * quarter] = stack[part * count : (part + 1) * count]
            decode_copy(p).start()

    def wait():
        for p in range(len(fresh_refs)):
            decode_copy(p).wait()

    return start, wait


def spare_part(got):
    return got.at[:, pl.ds(WIDTH, got.shape[1] - WIDTH)]


def attend_kernel(pieces, unpack, rot_ref, bias_ref, own_ref, *refs):
    got_refs, refs = refs[:pieces], refs[pieces:]
    start, wait = None, None
    if unpack:
        request_vmem, fresh_ref, result_ref, level_ref, decode_ref, *scratch = refs
        fresh_refs = [spare_part(got) for got in got_refs] + [fresh_ref]
        start, wait = unpacking(fresh_refs, 0, request_vmem, decode_ref, *scratch)
    else:
        result_ref, level_ref = refs
    new_count = rot_ref.shape[1] // PER_KV
    span = pieces * got_refs[0].shape[0] + own_ref.shape[1] - new_count
    token = lax.broadcasted_iota(jnp.int32, (CHUNK, new_count), 0) % new_count
    causal = jnp.where(lax.broadcasted_iota(jnp.int32, (CHUNK, new_count), 1) <= token, 0.0, MASKED)
    bias = bias_ref[0:1, 0:span]
    per_head = PER_KV * new_count // CHUNK
    keys, values, highs = {}, {}, {}

    def place(at):
        return at // per_head, slice(at % per_head * CHUNK, (at % per_head + 1) * CHUNK)

    def score(at):
        head, rows = place(at)
        if at % per_head == 0:
            join_keys(keys, values, got_refs, own_ref, head)
        return dot_keys(rot_ref[head, rows, :], keys[head])

    def weigh(at, scores):
        scores = jnp.concatenate([scores[:, :span] * SCALE + bias, scores[:, span:] * SCALE + causal], axis=1)
        highs[at] = jnp.max(scores, axis=1, keepdims=True)
        return jnp.exp2(scores - highs[at]).astype(jnp.bfloat16)

    def mix(at, weights):
        return jnp.dot(weights, values[at // per_head], preferred_element_type=jnp.float32)

    def finish(at, mixed):
        head, rows = place(at)
        total = mixed[:, HEAD_DIM:]
        result_ref[head, rows, :] = quotient(mixed[:, :HEAD_DIM], total)
        level_ref[head, rows, :] = highs.pop(at) + jnp.log2(total)

    staged(KV_HEADS * per_head, score, weigh, mix, finish, start)
    if unpack:
        wait()


def attend(rot, bias, own, got, requests=None, fresh=None):
    rows, new_count = rot.shape[1], rot.shape[1] // PER_KV
    operands = [rot, bias, own, *got]
    shapes = [jax.ShapeDtypeStruct((KV_HEADS, rows, HEAD_DIM), jnp.float32)] * 2
    out_specs, scratch = [VMEM] * 2, []
    if requests is not None:
        operands += [requests, fresh]
        slots = got[0].shape[0]
        count = (got[0].shape[1] - WIDTH) * slots // WIDTH
        shapes.append(jax.ShapeDtypeStruct((new_count // count, count, WIDTH), jnp.bfloat16))
        out_specs.append(ANY)
        scratch = unpack_scratch(len(got) + 1, count, requests)
    return pl.pallas_call(
        functools.partial(attend_kernel, len(got), requests is not None),
        out_shape=tuple(shapes),
        in_specs=[VMEM] * len(operands),
        out_specs=tuple(out_specs),
        scratch_shapes=scratch,
        compiler_params=params(32),
        name="attend",
    )(*operands)


def unpack_scratch(pieces, count, requests):
    return [
        pltpu.VMEM((pieces, count, WIDTH), jnp.bfloat16),
        pltpu.SMEM(requests.shape, jnp.int32),
        pltpu.SemaphoreType.DMA,
        pltpu.SemaphoreType.DMA((pieces,)),
    ]


HEADROOM = 96.0


def late_kernel(pieces, first, rot_ref, bias_ref, result_ref, level_ref, *refs):
    got_refs, refs = refs[:pieces], refs[pieces:]
    request_vmem, _, out_ref, decode_ref, done_ref, out_sems, *scratch = refs
    start, wait = unpacking([spare_part(got) for got in got_refs], first, request_vmem, decode_ref, *scratch)
    slots = got_refs[0].shape[0]
    new_count = out_ref.shape[0]
    size = LATE_CHUNK
    heads_in = size // new_count
    bias = bias_ref[0:1, first * slots : (first + pieces) * slots]
    per_head = PER_KV * new_count // size
    chunks = KV_HEADS * per_head
    keys, values, excess = {}, {}, []

    def place(at):
        return at // per_head, slice(at % per_head * size, (at % per_head + 1) * size)

    def out_copy(at):
        width = heads_in * HEAD_DIM
        return pltpu.make_async_copy(
            done_ref.at[at], out_ref.at[:, pl.ds(pl.multiple_of(at * width, width), width)], out_sems.at[at]
        )

    def store(at, result):
        for row in range(heads_in):
            done_ref[at, :, column(row)] = result[row * new_count : (row + 1) * new_count].astype(jnp.bfloat16)
        out_copy(at).start()

    def score(at):
        head, rows = place(at)
        if at % per_head == 0:
            join_keys(keys, values, got_refs, None, head)
        return dot_keys(rot_ref[head, rows, :], keys[head])

    def weigh(at, scores):
        head, rows = place(at)
        powers = scores * SCALE + bias - level_ref[head, rows, :]
        excess.append(jnp.max(powers.reshape(size // 8, 8, HEAD_DIM), axis=0))
        return jnp.exp2(powers).astype(jnp.bfloat16)

    def mix(at, weights):
        return jnp.dot(weights, values[at // per_head], preferred_element_type=jnp.float32)

    def finish(at, mixed):
        head, rows = place(at)
        store(at, quotient(result_ref[head, rows, :] + mixed[:, :HEAD_DIM], 1.0 + mixed[:, HEAD_DIM:]))

    staged(chunks, score, weigh, mix, finish, start)
    most = jnp.max(functools.reduce(jnp.maximum, excess))
    wait()
    for at in range(chunks):
        out_copy(at).wait()

    @pl.when(most > HEADROOM)
    def _():
        for head in range(KV_HEADS):

            def again(chunk, carry, head=head):
                rows = pl.ds(pl.multiple_of(chunk * size, size), size)
                scores = dot_keys(rot_ref[head, rows, :], keys[head]) * SCALE + bias
                level = level_ref[head, rows, :]
                high = jnp.maximum(level, jnp.max(scores, axis=1, keepdims=True))
                factor = jnp.exp2(level - high)
                weights = jnp.exp2(scores - high).astype(jnp.bfloat16)
                mixed = jnp.dot(weights, values[head], preferred_element_type=jnp.float32)
                at = head * per_head + chunk
                summed = result_ref[head, rows, :] * factor + mixed[:, :HEAD_DIM]
                store(at, quotient(summed, factor + mixed[:, HEAD_DIM:]))
                out_copy(at).wait()
                return carry

            lax.fori_loop(0, per_head, again, 0)


def attend_late(rot, bias, result, level, got, first, requests, decode):
    rows, new_count = rot.shape[1], rot.shape[1] // PER_KV
    operands = [rot, bias, result, level, *got, requests, decode]
    chunks = KV_HEADS * rows // LATE_CHUNK
    return pl.pallas_call(
        functools.partial(late_kernel, len(got), first),
        out_shape=(
            jax.ShapeDtypeStruct((new_count, Q_HEADS * HEAD_DIM), jnp.bfloat16),
            jax.ShapeDtypeStruct(decode.shape, jnp.bfloat16),
        ),
        in_specs=[VMEM] * (len(operands) - 1) + [ANY],
        out_specs=(ANY, ANY),
        scratch_shapes=[
            pltpu.VMEM((chunks, new_count, LATE_CHUNK // new_count * HEAD_DIM), jnp.bfloat16),
            pltpu.SemaphoreType.DMA((chunks,)),
        ]
        + unpack_scratch(len(got), decode.shape[1], requests),
        input_output_aliases={len(operands) - 1: 1},
        compiler_params=params(32),
        name="attend_late",
    )(*operands)


def inverse(table):
    places = jnp.arange(table.shape[0], dtype=jnp.int32)
    return jnp.sum(jnp.where(table[None, :] == places[:, None], places, 0), axis=1)


def rotate(rows, positions, heads):
    half = HEAD_DIM // 2
    freqs = ROPE_BASE ** (-jnp.arange(half, dtype=jnp.float32) / half)
    angles = positions.astype(jnp.float32)[:, None] * freqs[None, :]
    cosine = jnp.concatenate([jnp.cos(angles)] * 2, axis=-1)[:, None, :]
    sine = jnp.concatenate([-jnp.sin(angles), jnp.sin(angles)], axis=-1)[:, None, :]
    split = rows.astype(jnp.float32).reshape(rows.shape[0], heads, HEAD_DIM)
    turned = jnp.roll(split, half, axis=-1)
    return (split * cosine + turned * sine).astype(jnp.bfloat16)


def small_pieces(me, assignment, prefix_len, stripe_map, owner_map, queries, block_kv, pool):
    groups, slots, width = pool.shape
    new_count = block_kv.shape[0]
    count = new_count // groups
    request = assignment[me[0]]
    length = prefix_len[request]
    positions = length + jnp.arange(new_count, dtype=jnp.int32)
    rot = rotate(queries, positions, Q_HEADS).reshape(new_count, KV_HEADS, PER_KV, HEAD_DIM)
    rot = jnp.transpose(rot, (1, 2, 0, 3)).reshape(KV_HEADS, PER_KV * new_count, HEAD_DIM)
    new_keys = rotate(block_kv[:, :KV_WIDTH], positions, KV_HEADS).reshape(new_count, KV_WIDTH)
    new_kv = jnp.concatenate([new_keys, block_kv[:, KV_WIDTH:]], axis=1)
    own = jnp.transpose(new_kv.reshape(new_count, 2 * KV_HEADS, HEAD_DIM), (1, 0, 2))
    spread = jnp.transpose(new_kv.reshape(count, groups, width), (1, 0, 2))
    send = jnp.concatenate([pool[assignment], spread[inverse(owner_map[request])]], axis=1)
    got = lax.all_to_all(send, "pg", split_axis=0, concat_axis=0, tiled=True)
    located = jnp.arange(slots, dtype=jnp.int32)[None, :] * groups + inverse(stripe_map[request])[:, None]
    bias = jnp.where(located < length, 0.0, MASKED).astype(jnp.float32).reshape(1, groups * slots)
    keys = got[:, :slots].reshape(groups * slots, width)
    result, _ = attend(rot, jnp.broadcast_to(bias, (8, groups * slots)), own, [keys])
    result = result.astype(jnp.bfloat16).reshape(KV_HEADS, PER_KV, new_count, HEAD_DIM)
    attended = jnp.transpose(result, (2, 0, 1, 3)).reshape(new_count, Q_HEADS * HEAD_DIM)
    return attended, got[inverse(assignment), slots:]


def shards(queries, block_kv, pool_kv, prefix_len, assignment, stripe_map, owner_map):
    queries, block_kv, pool = queries[0], block_kv[0], pool_kv[0]
    groups, slots, width = pool.shape
    new_count = queries.shape[0]
    count = new_count // groups
    me = lax.axis_index("pg").astype(jnp.int32).reshape(1)
    if groups != 16 or slots % 16 or HEAD_DIM % slots or count % 8 or slots % count:
        attended, decode_kv = small_pieces(
            me, assignment, prefix_len, stripe_map, owner_map, queries, block_kv, pool
        )
        return (attended[None], decode_kv[None])
    order = order_of(groups)
    table = rotation_tables(new_count)
    first_blocks, info = front(order, me, assignment, prefix_len, owner_map, stripe_map, block_kv, table, pool)
    other_blocks, (rot, own, fresh, bias, requests) = rotate_queries(order, info, queries, pool)
    got = []
    for block, t in zip(list(first_blocks) + list(other_blocks), [t for t in order if t]):
        got.append(lax.ppermute(block, "pg", [(source, source ^ t) for source in range(groups)]))
    soon = groups - LATE - 1
    result, level, decode_kv = attend(rot, bias, own, got[:soon], requests, fresh)
    attended, decode_kv = attend_late(rot, bias, result, level, got[soon:], soon + 1, requests, decode_kv)
    return (attended[None], decode_kv[None])


def solution(mesh):
    return jax.shard_map(
        shards,
        mesh=mesh,
        in_specs=(
            P(("rep", "pg"), None, None),
            P(("rep", "pg"), None, None),
            P(("rep", "pg"), None, None, None),
            P("rep"),
            P("rep"),
            P("rep", None),
            P("rep", None),
        ),
        out_specs=(P(("rep", "pg"), None, None), P(("rep", "pg"), None, None, None)),
        check_vma=False,
    )
```

```python
import functools
import math

import jax
import jax.numpy as jnp
import numpy as np
from jax import lax
from jax.experimental import pallas as pl
from jax.experimental.pallas import tpu as pltpu
from jax.sharding import PartitionSpec as P

Q_HEADS = 32
KV_HEADS = 4
HEAD_DIM = 128
PER_KV = Q_HEADS // KV_HEADS
KV_WIDTH = KV_HEADS * HEAD_DIM
WIDTH = 2 * KV_WIDTH

ROPE_BASE = 1000000.0
MASKED = -1e30
SCALE = HEAD_DIM ** -0.5 / math.log(2.0)
CHUNK = 256
LATE = 4
LATE_CHUNK = 256
AHEAD = 4
AHEAD_OF_QUERIES = 8

SMEM = pl.BlockSpec(memory_space=pltpu.SMEM)
VMEM = pl.BlockSpec(memory_space=pltpu.VMEM)
ANY = pl.BlockSpec(memory_space=pl.ANY)


def params(mib):
    return pltpu.CompilerParams(vmem_limit_bytes=mib * 1024 * 1024)


def column(head):
    return slice(head * HEAD_DIM, (head + 1) * HEAD_DIM)


def order_of(groups):
    half = groups // 2
    far, near = list(range(half, 2 * half)), list(range(half - 1, 0, -1))
    order = [(far if kind == "f" else near).pop(0) for kind in "fnfnfnfnfnnffnf"]
    order.insert(groups - LATE - 1, 0)
    return order


def rotation_tables(rows):
    half = HEAD_DIM // 2
    freqs = np.tile(ROPE_BASE ** (-np.arange(half, dtype=np.float64) / half), 2)
    angles = np.arange(rows, dtype=np.float64)[:, None] * freqs[None, :]
    parts = [np.cos(angles), np.sin(angles), np.tile(freqs, (8, 1))]
    return jnp.asarray(np.concatenate(parts, axis=0).astype(np.float32))


def rotation(table_ref, length):
    rows = (table_ref.shape[0] - 8) // 2
    start = length.astype(jnp.float32) * table_ref[2 * rows : 2 * rows + 8, :]
    cos_start, sin_start = jnp.cos(start)[0:1], jnp.sin(start)[0:1]
    cos_row, sin_row = table_ref[0:rows, :], table_ref[rows : 2 * rows, :]
    lane = lax.broadcasted_iota(jnp.int32, (1, HEAD_DIM), 1)
    sign = jnp.where(lane < HEAD_DIM // 2, -1.0, 1.0)
    cosine = cos_row * cos_start - sin_row * sin_start
    return cosine, sin_row * (cos_start * sign) + cos_row * (sin_start * sign)


def turn(x, cosine, sine):
    x = x.astype(jnp.float32)
    return (x * cosine + pltpu.roll(x, HEAD_DIM // 2, 1) * sine).astype(jnp.bfloat16)


def info_rows(new_count):
    sizes = [("cos", new_count), ("sin", new_count), ("bias", 8), ("scalars", 8), ("new", 2 * KV_HEADS * new_count)]
    at, rows = 0, {}
    for name, size in sizes:
        rows[name] = at
        at += size
    return rows, at


def fresh_rows(info_ref, base, residue, new_count, count, quarter, lanes):
    groups = new_count // count
    stack = [
        info_ref[pl.ds(base + (head + lanes) * new_count + residue, count, stride=groups), :]
        for head in range(0, 2 * KV_HEADS, quarter)
    ]
    return jnp.concatenate(stack, axis=0)


def front_kernel(
    order, me_ref, assign_any, length_any, owner_any, stripe_any, block_any, table_any, pool_any, *refs
):
    groups, slots, width = pool_any.shape
    send_refs, info_any, refs = refs[:AHEAD], refs[AHEAD], refs[AHEAD + 1 :]
    (assign_ref, length_ref, owner_ref, stripe_ref, residue_ref, block_ref, table_ref, pool_ref, pack_ref, info_ref,
     small_sems, pool_sems, send_sems, info_sems) = refs
    new_count = block_any.shape[0]
    count = new_count // groups
    quarter = width * count // slots // HEAD_DIM
    at, rows = info_rows(new_count)
    pairs = [
        (assign_any, assign_ref), (length_any, length_ref), (owner_any, owner_ref), (stripe_any, stripe_ref),
        (block_any, block_ref), (table_any, table_ref),
    ]
    smalls = [pltpu.make_async_copy(*pair, small_sems.at[i]) for i, pair in enumerate(pairs)]
    for copy in smalls:
        copy.start()
    pool_copies = [
        pltpu.make_async_copy(pool_any.at[pl.ds(low, 4)], pool_ref.at[pl.ds(low, 4)], pool_sems.at[low // 4])
        for low in range(0, groups, 4)
    ]
    for copy in pool_copies:
        copy.start()
    me = me_ref[0]
    for copy in smalls:
        copy.wait()
    request = assign_ref[me]
    length = length_ref[request]
    for residue in range(groups):
        residue_ref[owner_ref[request, residue]] = residue
    cosine, sine = rotation(table_ref, length)
    for head in range(KV_HEADS):
        low = at["new"] + head * new_count
        info_ref[low : low + new_count] = turn(block_ref[:, column(head)], cosine, sine).astype(jnp.float32)
        low += KV_HEADS * new_count
        info_ref[low : low + new_count] = block_ref[:, column(KV_HEADS + head)].astype(jnp.float32)

    def info_copy(part, low, high):
        part_rows = pl.ds(low, high - low)
        return pltpu.make_async_copy(info_ref.at[part_rows], info_any.at[part_rows], info_sems.at[part])

    info_copy(0, at["new"], rows).start()
    for copy in pool_copies:
        copy.wait()
    sends = []
    for p in range(AHEAD):
        pack_ref[p, :, 0:width] = pool_ref[assign_ref[me ^ order[p]]]
        for lanes in range(quarter):
            pack_ref[p, :, width + lanes * HEAD_DIM : width + (lanes + 1) * HEAD_DIM] = fresh_rows(
                info_ref, at["new"], residue_ref[me ^ order[p]], new_count, count, quarter, lanes
            ).astype(jnp.bfloat16)
        sends.append(pltpu.make_async_copy(pack_ref.at[p], send_refs[p], send_sems.at[p]))
        sends[-1].start()
    info_ref[at["cos"] : at["cos"] + new_count] = cosine
    info_ref[at["sin"] : at["sin"] + new_count] = sine
    per_row = HEAD_DIM // slots
    row = lax.broadcasted_iota(jnp.int32, (8, HEAD_DIM), 0)
    lane = lax.broadcasted_iota(jnp.int32, (8, HEAD_DIM), 1)
    piece, slot = row * per_row + lane // slots, lane % slots
    holder, requests, residues = jnp.zeros_like(lane), jnp.zeros_like(lane), jnp.zeros_like(lane)
    for p in range(groups):
        other = me ^ order[p]
        holder = jnp.where(piece == p, other, holder)
        requests = jnp.where(lane == p, assign_ref[other], requests)
        residues = jnp.where(lane == p, residue_ref[other], residues)
    bias = jnp.full((8, HEAD_DIM), MASKED, jnp.float32)
    for residue in range(groups):
        live = (holder == stripe_ref[request, residue]) & (slot * groups + residue < length)
        bias = jnp.where(live, 0.0, bias)
    info_ref[at["bias"] : at["bias"] + 8] = bias
    scalars = jnp.where(row == 0, requests, residues)
    info_ref[at["scalars"] : at["scalars"] + 8] = scalars.astype(jnp.float32)
    info_copy(1, 0, at["new"]).start()
    for copy in sends:
        copy.wait()
    info_copy(0, at["new"], rows).wait()
    info_copy(1, 0, at["new"]).wait()


def front(order, me, assignment, prefix_len, owner_map, stripe_map, block_kv, table, pool):
    groups, slots, width = pool.shape
    new_count = block_kv.shape[0]
    count = new_count // groups
    block = jax.ShapeDtypeStruct((slots, width + width * count // slots), jnp.bfloat16)
    info = jax.ShapeDtypeStruct((info_rows(new_count)[1], HEAD_DIM), jnp.float32)
    *blocks, info = pl.pallas_call(
        functools.partial(front_kernel, order),
        out_shape=[block] * AHEAD + [info],
        in_specs=[SMEM] + [ANY] * 7,
        out_specs=[ANY] * (AHEAD + 1),
        scratch_shapes=[
            pltpu.SMEM(assignment.shape, jnp.int32),
            pltpu.SMEM(prefix_len.shape, jnp.int32),
            pltpu.SMEM(owner_map.shape, jnp.int32),
            pltpu.SMEM(stripe_map.shape, jnp.int32),
            pltpu.SMEM(assignment.shape, jnp.int32),
            pltpu.VMEM(block_kv.shape, jnp.bfloat16),
            pltpu.VMEM(table.shape, jnp.float32),
            pltpu.VMEM(pool.shape, jnp.bfloat16),
            pltpu.VMEM((AHEAD,) + block.shape, jnp.bfloat16),
            pltpu.VMEM(info.shape, jnp.float32),
            pltpu.SemaphoreType.DMA((6,)),
            pltpu.SemaphoreType.DMA((groups // 4,)),
            pltpu.SemaphoreType.DMA((AHEAD,)),
            pltpu.SemaphoreType.DMA((2,)),
        ],
        compiler_params=params(60),
        name="front",
    )(me, assignment, prefix_len, owner_map, stripe_map, block_kv, table, pool)
    return blocks, info


def pack_kernel(info_ref, pool_ref, *refs):
    groups, slots, width = pool_ref.shape
    targets, (scalar_ref, scalar_sem) = refs[: groups - AHEAD], refs[groups - AHEAD :]
    new_count = slots * groups * (targets[0].shape[1] - width) // width
    at, _ = info_rows(new_count)
    count = new_count // groups
    quarter = (targets[0].shape[1] - width) // HEAD_DIM
    scalar_copy = pltpu.make_async_copy(info_ref.at[pl.ds(at["scalars"], 8)], scalar_ref, scalar_sem)
    scalar_copy.start()
    scalar_copy.wait()
    for p, target in enumerate(targets, AHEAD):
        target[:, 0:width] = pool_ref[scalar_ref[0, p].astype(jnp.int32)]
        residue = scalar_ref[1, p].astype(jnp.int32)
        for lanes in range(quarter):
            target[:, width + lanes * HEAD_DIM : width + (lanes + 1) * HEAD_DIM] = fresh_rows(
                info_ref, at["new"], residue, new_count, count, quarter, lanes
            ).astype(jnp.bfloat16)


def pack_others(info, pool, new_count):
    groups, slots, width = pool.shape
    block = (slots, width + width * (new_count // groups) // slots)
    return pl.pallas_call(
        pack_kernel,
        out_shape=[jax.ShapeDtypeStruct(block, jnp.bfloat16)] * (groups - AHEAD),
        in_specs=[VMEM] * 2,
        out_specs=[VMEM] * (groups - AHEAD),
        scratch_shapes=[pltpu.SMEM((8, HEAD_DIM), jnp.float32), pltpu.SemaphoreType.DMA],
        compiler_params=params(32),
        name="pack_others",
    )(info, pool)


def query_kernel(info_ref, q_ref, rot_ref, own_ref, bias_ref, request_ref):
    new_count = q_ref.shape[0]
    at, _ = info_rows(new_count)
    cosine = info_ref[at["cos"] : at["cos"] + new_count]
    sine = info_ref[at["sin"] : at["sin"] + new_count]
    for row in range(bias_ref.shape[1] // HEAD_DIM):
        line = info_ref[at["bias"] + row : at["bias"] + row + 1]
        bias_ref[:, column(row)] = jnp.broadcast_to(line, (8, HEAD_DIM))
    request_ref[...] = info_ref[at["scalars"] : at["scalars"] + 8].astype(jnp.int32)
    for head in range(2 * KV_HEADS):
        rows = at["new"] + head * new_count
        own_ref[head] = info_ref[rows : rows + new_count].astype(jnp.bfloat16)
    for head in range(Q_HEADS):
        rows = slice((head % PER_KV) * new_count, (head % PER_KV + 1) * new_count)
        rot_ref[head // PER_KV, rows, :] = turn(q_ref[:, column(head)], cosine, sine)


def rotate_queries(info, queries, span):
    new_count = queries.shape[0]
    return pl.pallas_call(
        query_kernel,
        out_shape=(
            jax.ShapeDtypeStruct((KV_HEADS, PER_KV * new_count, HEAD_DIM), jnp.bfloat16),
            jax.ShapeDtypeStruct((2 * KV_HEADS, new_count, HEAD_DIM), jnp.bfloat16),
            jax.ShapeDtypeStruct((8, span), jnp.float32),
            jax.ShapeDtypeStruct((8, HEAD_DIM), jnp.int32),
        ),
        in_specs=[VMEM] * 2,
        out_specs=[VMEM] * 4,
        compiler_params=params(32),
        name="rotate_queries",
    )(info, queries)


def quotient(summed, total):
    about = pl.reciprocal(total, approx=True)
    return summed * (about * (2.0 - total * about))


def join_keys(keys, values, got_refs, own_ref, head):
    key_parts = [got[:, column(head)] for got in got_refs]
    value_parts = [got[:, column(KV_HEADS + head)] for got in got_refs]
    if own_ref is not None:
        key_parts.append(own_ref[head])
        value_parts.append(own_ref[KV_HEADS + head])
    keys[head] = jnp.concatenate(key_parts, axis=0)
    value = jnp.concatenate(value_parts, axis=0)
    values[head] = jnp.concatenate([value, jnp.ones_like(value)], axis=1)


def dot_keys(query, keys):
    return lax.dot_general(query, keys, (((1,), (1,)), ((), ())), preferred_element_type=jnp.float32)


def staged(total, score, weigh, mix, finish, beside=None):
    scores, weights = {0: score(0)}, {}
    for at in range(total + 1):
        if at + 1 < total:
            scores[at + 1] = score(at + 1)
        if at >= 1:
            mixed = mix(at - 1, weights.pop(at - 1))
        if at < total:
            weights[at] = weigh(at, scores.pop(at))
        if at >= 1:
            finish(at - 1, mixed)
        if at == 1 and beside is not None:
            beside()


def unpacking(fresh_refs, first, request_vmem, decode_ref, rows_ref, request_ref, request_sem, decode_sems):
    count = rows_ref.shape[1]
    request_copy = pltpu.make_async_copy(request_vmem, request_ref, request_sem)
    request_copy.start()

    def decode_copy(p):
        return pltpu.make_async_copy(
            rows_ref.at[p], decode_ref.at[request_ref[0, first + p]], decode_sems.at[p]
        )

    def start():
        request_copy.wait()
        for p, fresh_ref in enumerate(fresh_refs):
            stack = fresh_ref[...]
            quarter = stack.shape[1]
            for part in range(stack.shape[0] // count):
                rows_ref[p, :, part * quarter : (part + 1) * quarter] = stack[part * count : (part + 1) * count]
            decode_copy(p).start()

    def wait():
        for p in range(len(fresh_refs)):
            decode_copy(p).wait()

    return start, wait


def spare_part(got):
    return got.at[:, pl.ds(WIDTH, got.shape[1] - WIDTH)]


def pieces_of(refs):
    pieces = []
    for ref in refs:
        pieces += [ref] if len(ref.shape) == 2 else [ref.at[i] for i in range(ref.shape[0])]
    return pieces


def attend_kernel(arrays, unpack, rot_ref, bias_ref, own_ref, *refs):
    got_refs, refs = pieces_of(refs[:arrays]), refs[arrays:]
    start, wait = None, None
    if unpack:
        request_vmem, result_ref, level_ref, decode_ref, *scratch = refs
        start, wait = unpacking([spare_part(got) for got in got_refs], 0, request_vmem, decode_ref, *scratch)
    else:
        result_ref, level_ref = refs
    new_count = rot_ref.shape[1] // PER_KV
    span = len(got_refs) * got_refs[0].shape[0]
    token = lax.broadcasted_iota(jnp.int32, (CHUNK, new_count), 0) % new_count
    causal = jnp.where(lax.broadcasted_iota(jnp.int32, (CHUNK, new_count), 1) <= token, 0.0, MASKED)
    bias = bias_ref[0:1, 0:span]
    per_head = PER_KV * new_count // CHUNK
    keys, values, highs = {}, {}, {}

    def place(at):
        return at // per_head, slice(at % per_head * CHUNK, (at % per_head + 1) * CHUNK)

    def score(at):
        head, rows = place(at)
        if at % per_head == 0:
            join_keys(keys, values, got_refs, own_ref, head)
        return dot_keys(rot_ref[head, rows, :], keys[head])

    def weigh(at, scores):
        scores = jnp.concatenate([scores[:, :span] * SCALE + bias, scores[:, span:] * SCALE + causal], axis=1)
        highs[at] = jnp.max(scores, axis=1, keepdims=True)
        return jnp.exp2(scores - highs[at]).astype(jnp.bfloat16)

    def mix(at, weights):
        return jnp.dot(weights, values[at // per_head], preferred_element_type=jnp.float32)

    def finish(at, mixed):
        head, rows = place(at)
        total = mixed[:, HEAD_DIM:]
        result_ref[head, rows, :] = quotient(mixed[:, :HEAD_DIM], total)
        level_ref[head, rows, :] = highs.pop(at) + jnp.log2(total)

    staged(KV_HEADS * per_head, score, weigh, mix, finish, start)
    if unpack:
        wait()


def attend(rot, bias, own, got, requests=None):
    rows, new_count = rot.shape[1], rot.shape[1] // PER_KV
    operands = [rot, bias, own, *got]
    shapes = [jax.ShapeDtypeStruct((KV_HEADS, rows, HEAD_DIM), jnp.float32)] * 2
    out_specs, scratch = [VMEM] * 2, []
    if requests is not None:
        operands.append(requests)
        slots, width = got[-1].shape
        count = (width - WIDTH) * slots // WIDTH
        shapes.append(jax.ShapeDtypeStruct((new_count // count, count, WIDTH), jnp.bfloat16))
        out_specs.append(ANY)
        scratch = unpack_scratch(len(pieces_of(got)), count, requests)
    return pl.pallas_call(
        functools.partial(attend_kernel, len(got), requests is not None),
        out_shape=tuple(shapes),
        in_specs=[VMEM] * len(operands),
        out_specs=tuple(out_specs),
        scratch_shapes=scratch,
        compiler_params=params(32),
        name="attend",
    )(*operands)


def unpack_scratch(pieces, count, requests):
    return [
        pltpu.VMEM((pieces, count, WIDTH), jnp.bfloat16),
        pltpu.SMEM(requests.shape, jnp.int32),
        pltpu.SemaphoreType.DMA,
        pltpu.SemaphoreType.DMA((pieces,)),
    ]


HEADROOM = 96.0


def late_kernel(pieces, first, rot_ref, bias_ref, result_ref, level_ref, *refs):
    got_refs, refs = refs[:pieces], refs[pieces:]
    request_vmem, _, out_ref, decode_ref, done_ref, out_sems, *scratch = refs
    start, wait = unpacking([spare_part(got) for got in got_refs], first, request_vmem, decode_ref, *scratch)
    slots = got_refs[0].shape[0]
    new_count = out_ref.shape[0]
    size = LATE_CHUNK
    heads_in = size // new_count
    bias = bias_ref[0:1, first * slots : (first + pieces) * slots]
    per_head = PER_KV * new_count // size
    chunks = KV_HEADS * per_head
    keys, values, excess = {}, {}, []

    def place(at):
        return at // per_head, slice(at % per_head * size, (at % per_head + 1) * size)

    def out_copy(at):
        width = heads_in * HEAD_DIM
        return pltpu.make_async_copy(
            done_ref.at[at], out_ref.at[:, pl.ds(pl.multiple_of(at * width, width), width)], out_sems.at[at]
        )

    def store(at, result):
        for row in range(heads_in):
            done_ref[at, :, column(row)] = result[row * new_count : (row + 1) * new_count].astype(jnp.bfloat16)
        out_copy(at).start()

    def score(at):
        head, rows = place(at)
        if at % per_head == 0:
            join_keys(keys, values, got_refs, None, head)
        return dot_keys(rot_ref[head, rows, :], keys[head])

    def weigh(at, scores):
        head, rows = place(at)
        powers = scores * SCALE + bias - level_ref[head, rows, :]
        excess.append(jnp.max(powers.reshape(size // 8, 8, HEAD_DIM), axis=0))
        return jnp.exp2(powers).astype(jnp.bfloat16)

    def mix(at, weights):
        return jnp.dot(weights, values[at // per_head], preferred_element_type=jnp.float32)

    def finish(at, mixed):
        head, rows = place(at)
        store(at, quotient(result_ref[head, rows, :] + mixed[:, :HEAD_DIM], 1.0 + mixed[:, HEAD_DIM:]))

    staged(chunks, score, weigh, mix, finish, start)
    most = jnp.max(functools.reduce(jnp.maximum, excess))
    wait()
    for at in range(chunks):
        out_copy(at).wait()

    @pl.when(most > HEADROOM)
    def _():
        for head in range(KV_HEADS):

            def again(chunk, carry, head=head):
                rows = pl.ds(pl.multiple_of(chunk * size, size), size)
                scores = dot_keys(rot_ref[head, rows, :], keys[head]) * SCALE + bias
                level = level_ref[head, rows, :]
                high = jnp.maximum(level, jnp.max(scores, axis=1, keepdims=True))
                factor = jnp.exp2(level - high)
                weights = jnp.exp2(scores - high).astype(jnp.bfloat16)
                mixed = jnp.dot(weights, values[head], preferred_element_type=jnp.float32)
                at = head * per_head + chunk
                summed = result_ref[head, rows, :] * factor + mixed[:, :HEAD_DIM]
                store(at, quotient(summed, factor + mixed[:, HEAD_DIM:]))
                out_copy(at).wait()
                return carry

            lax.fori_loop(0, per_head, again, 0)


def attend_late(rot, bias, result, level, got, first, requests, decode):
    rows, new_count = rot.shape[1], rot.shape[1] // PER_KV
    operands = [rot, bias, result, level, *got, requests, decode]
    chunks = KV_HEADS * rows // LATE_CHUNK
    return pl.pallas_call(
        functools.partial(late_kernel, len(got), first),
        out_shape=(
            jax.ShapeDtypeStruct((new_count, Q_HEADS * HEAD_DIM), jnp.bfloat16),
            jax.ShapeDtypeStruct(decode.shape, jnp.bfloat16),
        ),
        in_specs=[VMEM] * (len(operands) - 1) + [ANY],
        out_specs=(ANY, ANY),
        scratch_shapes=[
            pltpu.VMEM((chunks, new_count, LATE_CHUNK // new_count * HEAD_DIM), jnp.bfloat16),
            pltpu.SemaphoreType.DMA((chunks,)),
        ]
        + unpack_scratch(len(got), decode.shape[1], requests),
        input_output_aliases={len(operands) - 1: 1},
        compiler_params=params(32),
        name="attend_late",
    )(*operands)


def inverse(table):
    places = jnp.arange(table.shape[0], dtype=jnp.int32)
    return jnp.sum(jnp.where(table[None, :] == places[:, None], places, 0), axis=1)


def rotate(rows, positions, heads):
    half = HEAD_DIM // 2
    freqs = ROPE_BASE ** (-jnp.arange(half, dtype=jnp.float32) / half)
    angles = positions.astype(jnp.float32)[:, None] * freqs[None, :]
    cosine = jnp.concatenate([jnp.cos(angles)] * 2, axis=-1)[:, None, :]
    sine = jnp.concatenate([-jnp.sin(angles), jnp.sin(angles)], axis=-1)[:, None, :]
    split = rows.astype(jnp.float32).reshape(rows.shape[0], heads, HEAD_DIM)
    turned = jnp.roll(split, half, axis=-1)
    return (split * cosine + turned * sine).astype(jnp.bfloat16)


def small_pieces(me, assignment, prefix_len, stripe_map, owner_map, queries, block_kv, pool):
    groups, slots, width = pool.shape
    new_count = block_kv.shape[0]
    count = new_count // groups
    request = assignment[me[0]]
    length = prefix_len[request]
    positions = length + jnp.arange(new_count, dtype=jnp.int32)
    rot = rotate(queries, positions, Q_HEADS).reshape(new_count, KV_HEADS, PER_KV, HEAD_DIM)
    rot = jnp.transpose(rot, (1, 2, 0, 3)).reshape(KV_HEADS, PER_KV * new_count, HEAD_DIM)
    new_keys = rotate(block_kv[:, :KV_WIDTH], positions, KV_HEADS).reshape(new_count, KV_WIDTH)
    new_kv = jnp.concatenate([new_keys, block_kv[:, KV_WIDTH:]], axis=1)
    own = jnp.transpose(new_kv.reshape(new_count, 2 * KV_HEADS, HEAD_DIM), (1, 0, 2))
    spread = jnp.transpose(new_kv.reshape(count, groups, width), (1, 0, 2))
    send = jnp.concatenate([pool[assignment], spread[inverse(owner_map[request])]], axis=1)
    got = lax.all_to_all(send, "pg", split_axis=0, concat_axis=0, tiled=True)
    located = jnp.arange(slots, dtype=jnp.int32)[None, :] * groups + inverse(stripe_map[request])[:, None]
    bias = jnp.where(located < length, 0.0, MASKED).astype(jnp.float32).reshape(1, groups * slots)
    keys = got[:, :slots].reshape(groups * slots, width)
    result, _ = attend(rot, jnp.broadcast_to(bias, (8, groups * slots)), own, [keys])
    result = result.astype(jnp.bfloat16).reshape(KV_HEADS, PER_KV, new_count, HEAD_DIM)
    attended = jnp.transpose(result, (2, 0, 1, 3)).reshape(new_count, Q_HEADS * HEAD_DIM)
    return attended, got[inverse(assignment), slots:]


def shards(queries, block_kv, pool_kv, prefix_len, assignment, stripe_map, owner_map):
    queries, block_kv, pool = queries[0], block_kv[0], pool_kv[0]
    groups, slots, width = pool.shape
    new_count = queries.shape[0]
    count = new_count // groups
    me = lax.axis_index("pg").astype(jnp.int32).reshape(1)
    if groups != 16 or slots % 16 or HEAD_DIM % slots or count % 8 or slots % count:
        attended, decode_kv = small_pieces(
            me, assignment, prefix_len, stripe_map, owner_map, queries, block_kv, pool
        )
        return (attended[None], decode_kv[None])
    order = order_of(groups)
    table = rotation_tables(new_count)
    blocks, info = front(order, me, assignment, prefix_len, owner_map, stripe_map, block_kv, table, pool)
    blocks = list(blocks) + list(pack_others(info, pool, new_count))
    rot, own, bias, requests = rotate_queries(info, queries, groups * slots)
    rot, *blocks[AHEAD_OF_QUERIES:] = lax.optimization_barrier((rot, *blocks[AHEAD_OF_QUERIES:]))
    got = [
        lax.ppermute(block, "pg", [(source, source ^ t) for source in range(groups)]) if t else block
        for block, t in zip(blocks, order)
    ]
    soon = groups - LATE
    result, level, decode_kv = attend(rot, bias, own, got[:soon], requests)
    attended, decode_kv = attend_late(rot, bias, result, level, got[soon:], soon, requests, decode_kv)
    return (attended[None], decode_kv[None])


def solution(mesh):
    return jax.shard_map(
        shards,
        mesh=mesh,
        in_specs=(
            P(("rep", "pg"), None, None),
            P(("rep", "pg"), None, None),
            P(("rep", "pg"), None, None, None),
            P("rep"),
            P("rep"),
            P("rep", None),
            P("rep", None),
        ),
        out_specs=(P(("rep", "pg"), None, None), P(("rep", "pg"), None, None, None)),
        check_vma=False,
    )
```

```python
import functools
import math

import jax
import jax.numpy as jnp
import numpy as np
from jax import lax
from jax.experimental import pallas as pl
from jax.experimental.pallas import tpu as pltpu
from jax.sharding import PartitionSpec as P

Q_HEADS = 32
KV_HEADS = 4
HEAD_DIM = 128
PER_KV = Q_HEADS // KV_HEADS
KV_WIDTH = KV_HEADS * HEAD_DIM
WIDTH = 2 * KV_WIDTH

ROPE_BASE = 1000000.0
MASKED = -1e30
SCALE = HEAD_DIM ** -0.5 / math.log(2.0)
CHUNK = 256
LATE = 4
LATE_CHUNK = 512
AHEAD = 4
AHEAD_OF_QUERIES = 8

SMEM = pl.BlockSpec(memory_space=pltpu.SMEM)
VMEM = pl.BlockSpec(memory_space=pltpu.VMEM)
ANY = pl.BlockSpec(memory_space=pl.ANY)


def params(mib):
    return pltpu.CompilerParams(vmem_limit_bytes=mib * 1024 * 1024)


def column(head):
    return slice(head * HEAD_DIM, (head + 1) * HEAD_DIM)


def order_of(groups):
    half = groups // 2
    far, near = [t ^ half // 2 for t in range(half, 2 * half)], list(range(half - 1, 0, -1))
    order = [(far if kind == "f" else near).pop(0) for kind in "ffnfnfnfnfnfnfn"]
    order.insert(groups - LATE - 1, 0)
    return order


def rotation_tables(rows):
    half = HEAD_DIM // 2
    freqs = np.tile(ROPE_BASE ** (-np.arange(half, dtype=np.float64) / half), 2)
    angles = np.arange(rows, dtype=np.float64)[:, None] * freqs[None, :]
    parts = [np.cos(angles), np.sin(angles), np.tile(freqs, (8, 1))]
    return jnp.asarray(np.concatenate(parts, axis=0).astype(np.float32))


def rotation(table_ref, length):
    rows = (table_ref.shape[0] - 8) // 2
    start = length.astype(jnp.float32) * table_ref[2 * rows : 2 * rows + 8, :]
    cos_start, sin_start = jnp.cos(start)[0:1], jnp.sin(start)[0:1]
    cos_row, sin_row = table_ref[0:rows, :], table_ref[rows : 2 * rows, :]
    lane = lax.broadcasted_iota(jnp.int32, (1, HEAD_DIM), 1)
    sign = jnp.where(lane < HEAD_DIM // 2, -1.0, 1.0)
    cosine = cos_row * cos_start - sin_row * sin_start
    return cosine, sin_row * (cos_start * sign) + cos_row * (sin_start * sign)


def turn(x, cosine, sine):
    x = x.astype(jnp.float32)
    return (x * cosine + pltpu.roll(x, HEAD_DIM // 2, 1) * sine).astype(jnp.bfloat16)


def info_rows(new_count):
    sizes = [("cos", new_count), ("sin", new_count), ("bias", 8), ("scalars", 8), ("new", 2 * KV_HEADS * new_count)]
    at, rows = 0, {}
    for name, size in sizes:
        rows[name] = at
        at += size
    return rows, at


def fresh_rows(info_ref, base, residue, new_count, count, quarter, lanes):
    groups = new_count // count
    stack = [
        info_ref[pl.ds(base + (head + lanes) * new_count + residue, count, stride=groups), :]
        for head in range(0, 2 * KV_HEADS, quarter)
    ]
    return jnp.concatenate(stack, axis=0)


def front_kernel(
    order, me_ref, assign_any, length_any, owner_any, stripe_any, block_any, table_any, pool_any, *refs
):
    groups, slots, width = pool_any.shape
    send_refs, info_any, refs = refs[:AHEAD], refs[AHEAD], refs[AHEAD + 1 :]
    (assign_ref, length_ref, owner_ref, stripe_ref, residue_ref, block_ref, table_ref, pool_ref, pack_ref, info_ref,
     small_sems, pool_sems, send_sems, info_sems) = refs
    new_count = block_any.shape[0]
    count = new_count // groups
    quarter = width * count // slots // HEAD_DIM
    at, rows = info_rows(new_count)
    pairs = [
        (assign_any, assign_ref), (length_any, length_ref), (owner_any, owner_ref), (stripe_any, stripe_ref),
        (block_any, block_ref), (table_any, table_ref),
    ]
    smalls = [pltpu.make_async_copy(*pair, small_sems.at[i]) for i, pair in enumerate(pairs)]
    for copy in smalls:
        copy.start()
    pool_copies = [
        pltpu.make_async_copy(pool_any.at[pl.ds(low, 4)], pool_ref.at[pl.ds(low, 4)], pool_sems.at[low // 4])
        for low in range(0, groups, 4)
    ]
    for copy in pool_copies:
        copy.start()
    me = me_ref[0]
    for copy in smalls:
        copy.wait()
    request = assign_ref[me]
    length = length_ref[request]
    for residue in range(groups):
        residue_ref[owner_ref[request, residue]] = residue
    cosine, sine = rotation(table_ref, length)
    for head in range(KV_HEADS):
        low = at["new"] + head * new_count
        info_ref[low : low + new_count] = turn(block_ref[:, column(head)], cosine, sine).astype(jnp.float32)
        low += KV_HEADS * new_count
        info_ref[low : low + new_count] = block_ref[:, column(KV_HEADS + head)].astype(jnp.float32)

    def info_copy(part, low, high):
        part_rows = pl.ds(low, high - low)
        return pltpu.make_async_copy(info_ref.at[part_rows], info_any.at[part_rows], info_sems.at[part])

    info_copy(0, at["new"], rows).start()
    info_ref[at["cos"] : at["cos"] + new_count] = cosine
    info_ref[at["sin"] : at["sin"] + new_count] = sine
    per_row = HEAD_DIM // slots
    row = lax.broadcasted_iota(jnp.int32, (8, HEAD_DIM), 0)
    lane = lax.broadcasted_iota(jnp.int32, (8, HEAD_DIM), 1)
    piece, slot = row * per_row + lane // slots, lane % slots
    holder, requests, residues = jnp.zeros_like(lane), jnp.zeros_like(lane), jnp.zeros_like(lane)
    for p in range(groups):
        other = me ^ order[p]
        holder = jnp.where(piece == p, other, holder)
        requests = jnp.where(lane == p, assign_ref[other], requests)
        residues = jnp.where(lane == p, residue_ref[other], residues)
    bias = jnp.full((8, HEAD_DIM), MASKED, jnp.float32)
    for residue in range(groups):
        live = (holder == stripe_ref[request, residue]) & (slot * groups + residue < length)
        bias = jnp.where(live, 0.0, bias)
    info_ref[at["bias"] : at["bias"] + 8] = bias
    scalars = jnp.where(row == 0, requests, residues)
    info_ref[at["scalars"] : at["scalars"] + 8] = scalars.astype(jnp.float32)
    info_copy(1, 0, at["new"]).start()
    for copy in pool_copies:
        copy.wait()
    sends = []
    for p in range(AHEAD):
        pack_ref[p, :, 0:width] = pool_ref[assign_ref[me ^ order[p]]]
        for lanes in range(quarter):
            pack_ref[p, :, width + lanes * HEAD_DIM : width + (lanes + 1) * HEAD_DIM] = fresh_rows(
                info_ref, at["new"], residue_ref[me ^ order[p]], new_count, count, quarter, lanes
            ).astype(jnp.bfloat16)
        sends.append(pltpu.make_async_copy(pack_ref.at[p], send_refs[p], send_sems.at[p]))
        sends[-1].start()
    for copy in sends:
        copy.wait()
    info_copy(0, at["new"], rows).wait()
    info_copy(1, 0, at["new"]).wait()


def front(order, me, assignment, prefix_len, owner_map, stripe_map, block_kv, table, pool):
    groups, slots, width = pool.shape
    new_count = block_kv.shape[0]
    count = new_count // groups
    block = jax.ShapeDtypeStruct((slots, width + width * count // slots), jnp.bfloat16)
    info = jax.ShapeDtypeStruct((info_rows(new_count)[1], HEAD_DIM), jnp.float32)
    *blocks, info = pl.pallas_call(
        functools.partial(front_kernel, order),
        out_shape=[block] * AHEAD + [info],
        in_specs=[SMEM] + [ANY] * 7,
        out_specs=[ANY] * (AHEAD + 1),
        scratch_shapes=[
            pltpu.SMEM(assignment.shape, jnp.int32),
            pltpu.SMEM(prefix_len.shape, jnp.int32),
            pltpu.SMEM(owner_map.shape, jnp.int32),
            pltpu.SMEM(stripe_map.shape, jnp.int32),
            pltpu.SMEM(assignment.shape, jnp.int32),
            pltpu.VMEM(block_kv.shape, jnp.bfloat16),
            pltpu.VMEM(table.shape, jnp.float32),
            pltpu.VMEM(pool.shape, jnp.bfloat16),
            pltpu.VMEM((AHEAD,) + block.shape, jnp.bfloat16),
            pltpu.VMEM(info.shape, jnp.float32),
            pltpu.SemaphoreType.DMA((6,)),
            pltpu.SemaphoreType.DMA((groups // 4,)),
            pltpu.SemaphoreType.DMA((AHEAD,)),
            pltpu.SemaphoreType.DMA((2,)),
        ],
        compiler_params=params(60),
        name="front",
    )(me, assignment, prefix_len, owner_map, stripe_map, block_kv, table, pool)
    return blocks, info


def pack_kernel(info_ref, pool_ref, *refs):
    groups, slots, width = pool_ref.shape
    targets, (scalar_ref, scalar_sem) = refs[: groups - AHEAD], refs[groups - AHEAD :]
    new_count = slots * groups * (targets[0].shape[1] - width) // width
    at, _ = info_rows(new_count)
    count = new_count // groups
    quarter = (targets[0].shape[1] - width) // HEAD_DIM
    scalar_copy = pltpu.make_async_copy(info_ref.at[pl.ds(at["scalars"], 8)], scalar_ref, scalar_sem)
    scalar_copy.start()
    scalar_copy.wait()
    for p, target in enumerate(targets, AHEAD):
        target[:, 0:width] = pool_ref[scalar_ref[0, p].astype(jnp.int32)]
        residue = scalar_ref[1, p].astype(jnp.int32)
        for lanes in range(quarter):
            target[:, width + lanes * HEAD_DIM : width + (lanes + 1) * HEAD_DIM] = fresh_rows(
                info_ref, at["new"], residue, new_count, count, quarter, lanes
            ).astype(jnp.bfloat16)


def pack_others(info, pool, new_count):
    groups, slots, width = pool.shape
    block = (slots, width + width * (new_count // groups) // slots)
    return pl.pallas_call(
        pack_kernel,
        out_shape=[jax.ShapeDtypeStruct(block, jnp.bfloat16)] * (groups - AHEAD),
        in_specs=[VMEM] * 2,
        out_specs=[VMEM] * (groups - AHEAD),
        scratch_shapes=[pltpu.SMEM((8, HEAD_DIM), jnp.float32), pltpu.SemaphoreType.DMA],
        compiler_params=params(32),
        name="pack_others",
    )(info, pool)


def query_kernel(info_ref, q_ref, rot_ref, own_ref, bias_ref, request_ref):
    new_count = q_ref.shape[0]
    at, _ = info_rows(new_count)
    cosine = info_ref[at["cos"] : at["cos"] + new_count]
    sine = info_ref[at["sin"] : at["sin"] + new_count]
    for row in range(bias_ref.shape[1] // HEAD_DIM):
        line = info_ref[at["bias"] + row : at["bias"] + row + 1]
        bias_ref[:, column(row)] = jnp.broadcast_to(line, (8, HEAD_DIM))
    request_ref[...] = info_ref[at["scalars"] : at["scalars"] + 8].astype(jnp.int32)
    for head in range(2 * KV_HEADS):
        rows = at["new"] + head * new_count
        own_ref[head] = info_ref[rows : rows + new_count].astype(jnp.bfloat16)
    for head in range(Q_HEADS):
        rows = slice((head % PER_KV) * new_count, (head % PER_KV + 1) * new_count)
        rot_ref[head // PER_KV, rows, :] = turn(q_ref[:, column(head)], cosine, sine)


def rotate_queries(info, queries, span):
    new_count = queries.shape[0]
    return pl.pallas_call(
        query_kernel,
        out_shape=(
            jax.ShapeDtypeStruct((KV_HEADS, PER_KV * new_count, HEAD_DIM), jnp.bfloat16),
            jax.ShapeDtypeStruct((2 * KV_HEADS, new_count, HEAD_DIM), jnp.bfloat16),
            jax.ShapeDtypeStruct((8, span), jnp.float32),
            jax.ShapeDtypeStruct((8, HEAD_DIM), jnp.int32),
        ),
        in_specs=[VMEM] * 2,
        out_specs=[VMEM] * 4,
        compiler_params=params(32),
        name="rotate_queries",
    )(info, queries)


def quotient(summed, total):
    about = pl.reciprocal(total, approx=True)
    return summed * (about * (2.0 - total * about))


def join_keys(keys, values, got_refs, own_ref, head):
    key_parts = [got[:, column(head)] for got in got_refs]
    value_parts = [got[:, column(KV_HEADS + head)] for got in got_refs]
    if own_ref is not None:
        key_parts.append(own_ref[head])
        value_parts.append(own_ref[KV_HEADS + head])
    keys[head] = jnp.concatenate(key_parts, axis=0)
    value = jnp.concatenate(value_parts, axis=0)
    values[head] = jnp.concatenate([value, jnp.ones_like(value)], axis=1)


def dot_keys(query, keys):
    return lax.dot_general(query, keys, (((1,), (1,)), ((), ())), preferred_element_type=jnp.float32)


def staged(total, score, weigh, mix, finish, beside=None):
    scores, weights = {0: score(0)}, {}
    for at in range(total + 1):
        if at + 1 < total:
            scores[at + 1] = score(at + 1)
        if at >= 1:
            mixed = mix(at - 1, weights.pop(at - 1))
        if at < total:
            weights[at] = weigh(at, scores.pop(at))
        if at >= 1:
            finish(at - 1, mixed)
        if at == 1 and beside is not None:
            beside()


def unpacking(fresh_refs, first, request_vmem, decode_ref, rows_ref, request_ref, request_sem, decode_sems):
    count = rows_ref.shape[1]
    request_copy = pltpu.make_async_copy(request_vmem, request_ref, request_sem)
    request_copy.start()

    def decode_copy(p):
        return pltpu.make_async_copy(
            rows_ref.at[p], decode_ref.at[request_ref[0, first + p]], decode_sems.at[p]
        )

    def start():
        request_copy.wait()
        for p, fresh_ref in enumerate(fresh_refs):
            stack = fresh_ref[...]
            quarter = stack.shape[1]
            for part in range(stack.shape[0] // count):
                rows_ref[p, :, part * quarter : (part + 1) * quarter] = stack[part * count : (part + 1) * count]
            decode_copy(p).start()

    def wait():
        for p in range(len(fresh_refs)):
            decode_copy(p).wait()

    return start, wait


def spare_part(got):
    return got.at[:, pl.ds(WIDTH, got.shape[1] - WIDTH)]


def pieces_of(refs):
    pieces = []
    for ref in refs:
        pieces += [ref] if len(ref.shape) == 2 else [ref.at[i] for i in range(ref.shape[0])]
    return pieces


def attend_kernel(arrays, unpack, rot_ref, bias_ref, own_ref, *refs):
    got_refs, refs = pieces_of(refs[:arrays]), refs[arrays:]
    start, wait = None, None
    if unpack:
        request_vmem, result_ref, level_ref, decode_ref, *scratch = refs
        start, wait = unpacking([spare_part(got) for got in got_refs], 0, request_vmem, decode_ref, *scratch)
    else:
        result_ref, level_ref = refs
    new_count = rot_ref.shape[1] // PER_KV
    span = len(got_refs) * got_refs[0].shape[0]
    token = lax.broadcasted_iota(jnp.int32, (CHUNK, new_count), 0) % new_count
    causal = jnp.where(lax.broadcasted_iota(jnp.int32, (CHUNK, new_count), 1) <= token, 0.0, MASKED)
    bias = bias_ref[0:1, 0:span]
    per_head = PER_KV * new_count // CHUNK
    keys, values, highs = {}, {}, {}

    def place(at):
        return at // per_head, slice(at % per_head * CHUNK, (at % per_head + 1) * CHUNK)

    def score(at):
        head, rows = place(at)
        if at % per_head == 0:
            join_keys(keys, values, got_refs, own_ref, head)
        return dot_keys(rot_ref[head, rows, :], keys[head])

    def weigh(at, scores):
        scores = jnp.concatenate([scores[:, :span] * SCALE + bias, scores[:, span:] * SCALE + causal], axis=1)
        highs[at] = jnp.max(scores, axis=1, keepdims=True)
        return jnp.exp2(scores - highs[at]).astype(jnp.bfloat16)

    def mix(at, weights):
        return jnp.dot(weights, values[at // per_head], preferred_element_type=jnp.float32)

    def finish(at, mixed):
        head, rows = place(at)
        total = mixed[:, HEAD_DIM:]
        result_ref[head, rows, :] = quotient(mixed[:, :HEAD_DIM], total)
        level_ref[head, rows, :] = highs.pop(at) + jnp.log2(total)

    staged(KV_HEADS * per_head, score, weigh, mix, finish, start)
    if unpack:
        wait()


def attend(rot, bias, own, got, requests=None):
    rows, new_count = rot.shape[1], rot.shape[1] // PER_KV
    operands = [rot, bias, own, *got]
    shapes = [jax.ShapeDtypeStruct((KV_HEADS, rows, HEAD_DIM), jnp.float32)] * 2
    out_specs, scratch = [VMEM] * 2, []
    if requests is not None:
        operands.append(requests)
        slots, width = got[-1].shape
        count = (width - WIDTH) * slots // WIDTH
        shapes.append(jax.ShapeDtypeStruct((new_count // count, count, WIDTH), jnp.bfloat16))
        out_specs.append(ANY)
        scratch = unpack_scratch(len(pieces_of(got)), count, requests)
    return pl.pallas_call(
        functools.partial(attend_kernel, len(got), requests is not None),
        out_shape=tuple(shapes),
        in_specs=[VMEM] * len(operands),
        out_specs=tuple(out_specs),
        scratch_shapes=scratch,
        compiler_params=params(32),
        name="attend",
    )(*operands)


def unpack_scratch(pieces, count, requests):
    return [
        pltpu.VMEM((pieces, count, WIDTH), jnp.bfloat16),
        pltpu.SMEM(requests.shape, jnp.int32),
        pltpu.SemaphoreType.DMA,
        pltpu.SemaphoreType.DMA((pieces,)),
    ]


HEADROOM = 96.0


def late_kernel(pieces, first, rot_ref, bias_ref, result_ref, level_ref, *refs):
    got_refs, refs = refs[:pieces], refs[pieces:]
    request_vmem, _, out_ref, decode_ref, done_ref, out_sems, *scratch = refs
    start, wait = unpacking([spare_part(got) for got in got_refs], first, request_vmem, decode_ref, *scratch)
    slots = got_refs[0].shape[0]
    new_count = out_ref.shape[0]
    size = LATE_CHUNK
    heads_in = size // new_count
    bias = bias_ref[0:1, first * slots : (first + pieces) * slots]
    per_head = PER_KV * new_count // size
    chunks = KV_HEADS * per_head
    keys, values, excess = {}, {}, []

    def place(at):
        return at // per_head, slice(at % per_head * size, (at % per_head + 1) * size)

    def out_copy(at):
        width = heads_in * HEAD_DIM
        return pltpu.make_async_copy(
            done_ref.at[at], out_ref.at[:, pl.ds(pl.multiple_of(at * width, width), width)], out_sems.at[at]
        )

    def store(at, result):
        for row in range(heads_in):
            done_ref[at, :, column(row)] = result[row * new_count : (row + 1) * new_count].astype(jnp.bfloat16)
        out_copy(at).start()

    def score(at):
        head, rows = place(at)
        if at % per_head == 0:
            join_keys(keys, values, got_refs, None, head)
        return dot_keys(rot_ref[head, rows, :], keys[head])

    def weigh(at, scores):
        head, rows = place(at)
        powers = scores * SCALE + bias - level_ref[head, rows, :]
        excess.append(jnp.max(powers.reshape(size // 8, 8, HEAD_DIM), axis=0))
        return jnp.exp2(powers).astype(jnp.bfloat16)

    def mix(at, weights):
        return jnp.dot(weights, values[at // per_head], preferred_element_type=jnp.float32)

    def finish(at, mixed):
        head, rows = place(at)
        store(at, quotient(result_ref[head, rows, :] + mixed[:, :HEAD_DIM], 1.0 + mixed[:, HEAD_DIM:]))

    staged(chunks, score, weigh, mix, finish, start)
    most = jnp.max(functools.reduce(jnp.maximum, excess))
    wait()
    for at in range(chunks):
        out_copy(at).wait()

    @pl.when(most > HEADROOM)
    def _():
        for head in range(KV_HEADS):

            def again(chunk, carry, head=head):
                rows = pl.ds(pl.multiple_of(chunk * size, size), size)
                scores = dot_keys(rot_ref[head, rows, :], keys[head]) * SCALE + bias
                level = level_ref[head, rows, :]
                high = jnp.maximum(level, jnp.max(scores, axis=1, keepdims=True))
                factor = jnp.exp2(level - high)
                weights = jnp.exp2(scores - high).astype(jnp.bfloat16)
                mixed = jnp.dot(weights, values[head], preferred_element_type=jnp.float32)
                at = head * per_head + chunk
                summed = result_ref[head, rows, :] * factor + mixed[:, :HEAD_DIM]
                store(at, quotient(summed, factor + mixed[:, HEAD_DIM:]))
                out_copy(at).wait()
                return carry

            lax.fori_loop(0, per_head, again, 0)


def attend_late(rot, bias, result, level, got, first, requests, decode):
    rows, new_count = rot.shape[1], rot.shape[1] // PER_KV
    operands = [rot, bias, result, level, *got, requests, decode]
    chunks = KV_HEADS * rows // LATE_CHUNK
    return pl.pallas_call(
        functools.partial(late_kernel, len(got), first),
        out_shape=(
            jax.ShapeDtypeStruct((new_count, Q_HEADS * HEAD_DIM), jnp.bfloat16),
            jax.ShapeDtypeStruct(decode.shape, jnp.bfloat16),
        ),
        in_specs=[VMEM] * (len(operands) - 1) + [ANY],
        out_specs=(ANY, ANY),
        scratch_shapes=[
            pltpu.VMEM((chunks, new_count, LATE_CHUNK // new_count * HEAD_DIM), jnp.bfloat16),
            pltpu.SemaphoreType.DMA((chunks,)),
        ]
        + unpack_scratch(len(got), decode.shape[1], requests),
        input_output_aliases={len(operands) - 1: 1},
        compiler_params=params(32),
        name="attend_late",
    )(*operands)


def inverse(table):
    places = jnp.arange(table.shape[0], dtype=jnp.int32)
    return jnp.sum(jnp.where(table[None, :] == places[:, None], places, 0), axis=1)


def rotate(rows, positions, heads):
    half = HEAD_DIM // 2
    freqs = ROPE_BASE ** (-jnp.arange(half, dtype=jnp.float32) / half)
    angles = positions.astype(jnp.float32)[:, None] * freqs[None, :]
    cosine = jnp.concatenate([jnp.cos(angles)] * 2, axis=-1)[:, None, :]
    sine = jnp.concatenate([-jnp.sin(angles), jnp.sin(angles)], axis=-1)[:, None, :]
    split = rows.astype(jnp.float32).reshape(rows.shape[0], heads, HEAD_DIM)
    turned = jnp.roll(split, half, axis=-1)
    return (split * cosine + turned * sine).astype(jnp.bfloat16)


def small_pieces(me, assignment, prefix_len, stripe_map, owner_map, queries, block_kv, pool):
    groups, slots, width = pool.shape
    new_count = block_kv.shape[0]
    count = new_count // groups
    request = assignment[me[0]]
    length = prefix_len[request]
    positions = length + jnp.arange(new_count, dtype=jnp.int32)
    rot = rotate(queries, positions, Q_HEADS).reshape(new_count, KV_HEADS, PER_KV, HEAD_DIM)
    rot = jnp.transpose(rot, (1, 2, 0, 3)).reshape(KV_HEADS, PER_KV * new_count, HEAD_DIM)
    new_keys = rotate(block_kv[:, :KV_WIDTH], positions, KV_HEADS).reshape(new_count, KV_WIDTH)
    new_kv = jnp.concatenate([new_keys, block_kv[:, KV_WIDTH:]], axis=1)
    own = jnp.transpose(new_kv.reshape(new_count, 2 * KV_HEADS, HEAD_DIM), (1, 0, 2))
    spread = jnp.transpose(new_kv.reshape(count, groups, width), (1, 0, 2))
    send = jnp.concatenate([pool[assignment], spread[inverse(owner_map[request])]], axis=1)
    got = lax.all_to_all(send, "pg", split_axis=0, concat_axis=0, tiled=True)
    located = jnp.arange(slots, dtype=jnp.int32)[None, :] * groups + inverse(stripe_map[request])[:, None]
    bias = jnp.where(located < length, 0.0, MASKED).astype(jnp.float32).reshape(1, groups * slots)
    keys = got[:, :slots].reshape(groups * slots, width)
    result, _ = attend(rot, jnp.broadcast_to(bias, (8, groups * slots)), own, [keys])
    result = result.astype(jnp.bfloat16).reshape(KV_HEADS, PER_KV, new_count, HEAD_DIM)
    attended = jnp.transpose(result, (2, 0, 1, 3)).reshape(new_count, Q_HEADS * HEAD_DIM)
    return attended, got[inverse(assignment), slots:]


def shards(queries, block_kv, pool_kv, prefix_len, assignment, stripe_map, owner_map):
    queries, block_kv, pool = queries[0], block_kv[0], pool_kv[0]
    groups, slots, width = pool.shape
    new_count = queries.shape[0]
    count = new_count // groups
    me = lax.axis_index("pg").astype(jnp.int32).reshape(1)
    if groups != 16 or slots % 16 or HEAD_DIM % slots or count % 8 or slots % count:
        attended, decode_kv = small_pieces(
            me, assignment, prefix_len, stripe_map, owner_map, queries, block_kv, pool
        )
        return (attended[None], decode_kv[None])
    order = order_of(groups)
    table = rotation_tables(new_count)
    blocks, info = front(order, me, assignment, prefix_len, owner_map, stripe_map, block_kv, table, pool)
    blocks = list(blocks) + list(pack_others(info, pool, new_count))
    rot, own, bias, requests = rotate_queries(info, queries, groups * slots)
    rot, *blocks[AHEAD_OF_QUERIES:] = lax.optimization_barrier((rot, *blocks[AHEAD_OF_QUERIES:]))
    got = [
        lax.ppermute(block, "pg", [(source, source ^ t) for source in range(groups)]) if t else block
        for block, t in zip(blocks, order)
    ]
    soon = groups - LATE
    result, level, decode_kv = attend(rot, bias, own, got[:soon], requests)
    attended, decode_kv = attend_late(rot, bias, result, level, got[soon:], soon, requests, decode_kv)
    return (attended[None], decode_kv[None])


def solution(mesh):
    return jax.shard_map(
        shards,
        mesh=mesh,
        in_specs=(
            P(("rep", "pg"), None, None),
            P(("rep", "pg"), None, None),
            P(("rep", "pg"), None, None, None),
            P("rep"),
            P("rep"),
            P("rep", None),
            P("rep", None),
        ),
        out_specs=(P(("rep", "pg"), None, None), P(("rep", "pg"), None, None, None)),
        check_vma=False,
    )
```

```python
import functools
import math

import jax
import jax.numpy as jnp
import numpy as np
from jax import lax
from jax.experimental import pallas as pl
from jax.experimental.pallas import tpu as pltpu
from jax.sharding import PartitionSpec as P

Q_HEADS = 32
KV_HEADS = 4
HEAD_DIM = 128
PER_KV = Q_HEADS // KV_HEADS
KV_WIDTH = KV_HEADS * HEAD_DIM
WIDTH = 2 * KV_WIDTH

ROPE_BASE = 1000000.0
MASKED = -1e30
SCALE = HEAD_DIM ** -0.5 / math.log(2.0)
CHUNK = 256
LATE = 4
LATE_CHUNK = 512
AHEAD = 4
AHEAD_OF_QUERIES = 8

SMEM = pl.BlockSpec(memory_space=pltpu.SMEM)
VMEM = pl.BlockSpec(memory_space=pltpu.VMEM)
ANY = pl.BlockSpec(memory_space=pl.ANY)


def params(mib):
    return pltpu.CompilerParams(vmem_limit_bytes=mib * 1024 * 1024)


def column(head):
    return slice(head * HEAD_DIM, (head + 1) * HEAD_DIM)


def order_of(groups):
    half = groups // 2
    near = list(range(half - 1, 0, -1))
    far = [half + at // 2 + at % 2 * half // 2 for at in range(half)]
    order = [(far if kind == "f" else near).pop(0) for kind in "fnfnfnfnfnnffnf"]
    order.insert(groups - LATE - 1, 0)
    return order


def rotation_tables(rows):
    half = HEAD_DIM // 2
    freqs = np.tile(ROPE_BASE ** (-np.arange(half, dtype=np.float64) / half), 2)
    angles = np.arange(rows, dtype=np.float64)[:, None] * freqs[None, :]
    parts = [np.cos(angles), np.sin(angles), np.tile(freqs, (8, 1))]
    return jnp.asarray(np.concatenate(parts, axis=0).astype(np.float32))


def rotation(table_ref, length):
    rows = (table_ref.shape[0] - 8) // 2
    start = length.astype(jnp.float32) * table_ref[2 * rows : 2 * rows + 8, :]
    cos_start, sin_start = jnp.cos(start)[0:1], jnp.sin(start)[0:1]
    cos_row, sin_row = table_ref[0:rows, :], table_ref[rows : 2 * rows, :]
    lane = lax.broadcasted_iota(jnp.int32, (1, HEAD_DIM), 1)
    sign = jnp.where(lane < HEAD_DIM // 2, -1.0, 1.0)
    cosine = cos_row * cos_start - sin_row * sin_start
    return cosine, sin_row * (cos_start * sign) + cos_row * (sin_start * sign)


def turn(x, cosine, sine):
    x = x.astype(jnp.float32)
    return (x * cosine + pltpu.roll(x, HEAD_DIM // 2, 1) * sine).astype(jnp.bfloat16)


def info_rows(new_count):
    sizes = [("cos", new_count), ("sin", new_count), ("bias", 8), ("scalars", 8), ("new", 2 * KV_HEADS * new_count)]
    at, rows = 0, {}
    for name, size in sizes:
        rows[name] = at
        at += size
    return rows, at


def fresh_rows(info_ref, base, residue, new_count, count, quarter, lanes):
    groups = new_count // count
    stack = [
        info_ref[pl.ds(base + (head + lanes) * new_count + residue, count, stride=groups), :]
        for head in range(0, 2 * KV_HEADS, quarter)
    ]
    return jnp.concatenate(stack, axis=0)


def front_kernel(
    order, me_ref, assign_any, length_any, owner_any, stripe_any, block_any, table_any, pool_any, *refs
):
    groups, slots, width = pool_any.shape
    send_refs, info_any, refs = refs[:AHEAD], refs[AHEAD], refs[AHEAD + 1 :]
    (assign_ref, length_ref, owner_ref, stripe_ref, residue_ref, block_ref, table_ref, pool_ref, pack_ref, info_ref,
     small_sems, pool_sems, send_sems, info_sems) = refs
    new_count = block_any.shape[0]
    count = new_count // groups
    quarter = width * count // slots // HEAD_DIM
    at, rows = info_rows(new_count)
    pairs = [
        (assign_any, assign_ref), (length_any, length_ref), (owner_any, owner_ref), (stripe_any, stripe_ref),
        (block_any, block_ref), (table_any, table_ref),
    ]
    smalls = [pltpu.make_async_copy(*pair, small_sems.at[i]) for i, pair in enumerate(pairs)]
    for copy in smalls:
        copy.start()
    pool_copies = [
        pltpu.make_async_copy(pool_any.at[pl.ds(low, 4)], pool_ref.at[pl.ds(low, 4)], pool_sems.at[low // 4])
        for low in range(0, groups, 4)
    ]
    for copy in pool_copies:
        copy.start()
    me = me_ref[0]
    for copy in smalls:
        copy.wait()
    request = assign_ref[me]
    length = length_ref[request]
    for residue in range(groups):
        residue_ref[owner_ref[request, residue]] = residue
    cosine, sine = rotation(table_ref, length)
    for head in range(KV_HEADS):
        low = at["new"] + head * new_count
        info_ref[low : low + new_count] = turn(block_ref[:, column(head)], cosine, sine).astype(jnp.float32)
        low += KV_HEADS * new_count
        info_ref[low : low + new_count] = block_ref[:, column(KV_HEADS + head)].astype(jnp.float32)

    def info_copy(part, low, high):
        part_rows = pl.ds(low, high - low)
        return pltpu.make_async_copy(info_ref.at[part_rows], info_any.at[part_rows], info_sems.at[part])

    info_copy(0, at["new"], rows).start()
    info_ref[at["cos"] : at["cos"] + new_count] = cosine
    info_ref[at["sin"] : at["sin"] + new_count] = sine
    per_row = HEAD_DIM // slots
    row = lax.broadcasted_iota(jnp.int32, (8, HEAD_DIM), 0)
    lane = lax.broadcasted_iota(jnp.int32, (8, HEAD_DIM), 1)
    piece, slot = row * per_row + lane // slots, lane % slots
    holder, requests, residues = jnp.zeros_like(lane), jnp.zeros_like(lane), jnp.zeros_like(lane)
    for p in range(groups):
        other = me ^ order[p]
        holder = jnp.where(piece == p, other, holder)
        requests = jnp.where(lane == p, assign_ref[other], requests)
        residues = jnp.where(lane == p, residue_ref[other], residues)
    bias = jnp.full((8, HEAD_DIM), MASKED, jnp.float32)
    for residue in range(groups):
        live = (holder == stripe_ref[request, residue]) & (slot * groups + residue < length)
        bias = jnp.where(live, 0.0, bias)
    info_ref[at["bias"] : at["bias"] + 8] = bias
    scalars = jnp.where(row == 0, requests, residues)
    info_ref[at["scalars"] : at["scalars"] + 8] = scalars.astype(jnp.float32)
    info_copy(1, 0, at["new"]).start()
    for copy in pool_copies:
        copy.wait()
    sends = []
    for p in range(AHEAD):
        pack_ref[p, :, 0:width] = pool_ref[assign_ref[me ^ order[p]]]
        for lanes in range(quarter):
            pack_ref[p, :, width + lanes * HEAD_DIM : width + (lanes + 1) * HEAD_DIM] = fresh_rows(
                info_ref, at["new"], residue_ref[me ^ order[p]], new_count, count, quarter, lanes
            ).astype(jnp.bfloat16)
        sends.append(pltpu.make_async_copy(pack_ref.at[p], send_refs[p], send_sems.at[p]))
        sends[-1].start()
    for copy in sends:
        copy.wait()
    info_copy(0, at["new"], rows).wait()
    info_copy(1, 0, at["new"]).wait()


def front(order, me, assignment, prefix_len, owner_map, stripe_map, block_kv, table, pool):
    groups, slots, width = pool.shape
    new_count = block_kv.shape[0]
    count = new_count // groups
    block = jax.ShapeDtypeStruct((slots, width + width * count // slots), jnp.bfloat16)
    info = jax.ShapeDtypeStruct((info_rows(new_count)[1], HEAD_DIM), jnp.float32)
    *blocks, info = pl.pallas_call(
        functools.partial(front_kernel, order),
        out_shape=[block] * AHEAD + [info],
        in_specs=[SMEM] + [ANY] * 7,
        out_specs=[ANY] * (AHEAD + 1),
        scratch_shapes=[
            pltpu.SMEM(assignment.shape, jnp.int32),
            pltpu.SMEM(prefix_len.shape, jnp.int32),
            pltpu.SMEM(owner_map.shape, jnp.int32),
            pltpu.SMEM(stripe_map.shape, jnp.int32),
            pltpu.SMEM(assignment.shape, jnp.int32),
            pltpu.VMEM(block_kv.shape, jnp.bfloat16),
            pltpu.VMEM(table.shape, jnp.float32),
            pltpu.VMEM(pool.shape, jnp.bfloat16),
            pltpu.VMEM((AHEAD,) + block.shape, jnp.bfloat16),
            pltpu.VMEM(info.shape, jnp.float32),
            pltpu.SemaphoreType.DMA((6,)),
            pltpu.SemaphoreType.DMA((groups // 4,)),
            pltpu.SemaphoreType.DMA((AHEAD,)),
            pltpu.SemaphoreType.DMA((2,)),
        ],
        compiler_params=params(60),
        name="front",
    )(me, assignment, prefix_len, owner_map, stripe_map, block_kv, table, pool)
    return blocks, info


def pack_kernel(info_ref, pool_ref, *refs):
    groups, slots, width = pool_ref.shape
    targets, (scalar_ref, scalar_sem) = refs[: groups - AHEAD], refs[groups - AHEAD :]
    new_count = slots * groups * (targets[0].shape[1] - width) // width
    at, _ = info_rows(new_count)
    count = new_count // groups
    quarter = (targets[0].shape[1] - width) // HEAD_DIM
    scalar_copy = pltpu.make_async_copy(info_ref.at[pl.ds(at["scalars"], 8)], scalar_ref, scalar_sem)
    scalar_copy.start()
    scalar_copy.wait()
    for p, target in enumerate(targets, AHEAD):
        target[:, 0:width] = pool_ref[scalar_ref[0, p].astype(jnp.int32)]
        residue = scalar_ref[1, p].astype(jnp.int32)
        for lanes in range(quarter):
            target[:, width + lanes * HEAD_DIM : width + (lanes + 1) * HEAD_DIM] = fresh_rows(
                info_ref, at["new"], residue, new_count, count, quarter, lanes
            ).astype(jnp.bfloat16)


def pack_others(info, pool, new_count):
    groups, slots, width = pool.shape
    block = (slots, width + width * (new_count // groups) // slots)
    return pl.pallas_call(
        pack_kernel,
        out_shape=[jax.ShapeDtypeStruct(block, jnp.bfloat16)] * (groups - AHEAD),
        in_specs=[VMEM] * 2,
        out_specs=[VMEM] * (groups - AHEAD),
        scratch_shapes=[pltpu.SMEM((8, HEAD_DIM), jnp.float32), pltpu.SemaphoreType.DMA],
        compiler_params=params(32),
        name="pack_others",
    )(info, pool)


def query_kernel(info_ref, q_ref, rot_ref, own_ref, bias_ref, request_ref):
    new_count = q_ref.shape[0]
    at, _ = info_rows(new_count)
    cosine = info_ref[at["cos"] : at["cos"] + new_count]
    sine = info_ref[at["sin"] : at["sin"] + new_count]
    for row in range(bias_ref.shape[1] // HEAD_DIM):
        line = info_ref[at["bias"] + row : at["bias"] + row + 1]
        bias_ref[:, column(row)] = jnp.broadcast_to(line, (8, HEAD_DIM))
    request_ref[...] = info_ref[at["scalars"] : at["scalars"] + 8].astype(jnp.int32)
    for head in range(2 * KV_HEADS):
        rows = at["new"] + head * new_count
        own_ref[head] = info_ref[rows : rows + new_count].astype(jnp.bfloat16)
    for head in range(Q_HEADS):
        rows = slice((head % PER_KV) * new_count, (head % PER_KV + 1) * new_count)
        rot_ref[head // PER_KV, rows, :] = turn(q_ref[:, column(head)], cosine, sine)


def rotate_queries(info, queries, span):
    new_count = queries.shape[0]
    return pl.pallas_call(
        query_kernel,
        out_shape=(
            jax.ShapeDtypeStruct((KV_HEADS, PER_KV * new_count, HEAD_DIM), jnp.bfloat16),
            jax.ShapeDtypeStruct((2 * KV_HEADS, new_count, HEAD_DIM), jnp.bfloat16),
            jax.ShapeDtypeStruct((8, span), jnp.float32),
            jax.ShapeDtypeStruct((8, HEAD_DIM), jnp.int32),
        ),
        in_specs=[VMEM] * 2,
        out_specs=[VMEM] * 4,
        compiler_params=params(32),
        name="rotate_queries",
    )(info, queries)


def quotient(summed, total):
    about = pl.reciprocal(total, approx=True)
    return summed * (about * (2.0 - total * about))


def join_keys(keys, values, got_refs, own_ref, head):
    key_parts = [got[:, column(head)] for got in got_refs]
    value_parts = [got[:, column(KV_HEADS + head)] for got in got_refs]
    if own_ref is not None:
        key_parts.append(own_ref[head])
        value_parts.append(own_ref[KV_HEADS + head])
    keys[head] = jnp.concatenate(key_parts, axis=0)
    value = jnp.concatenate(value_parts, axis=0)
    values[head] = jnp.concatenate([value, jnp.ones_like(value)], axis=1)


def dot_keys(query, keys):
    return lax.dot_general(query, keys, (((1,), (1,)), ((), ())), preferred_element_type=jnp.float32)


def staged(total, score, weigh, mix, finish, beside=None):
    scores, weights = {0: score(0)}, {}
    for at in range(total + 1):
        if at + 1 < total:
            scores[at + 1] = score(at + 1)
        if at >= 1:
            mixed = mix(at - 1, weights.pop(at - 1))
        if at < total:
            weights[at] = weigh(at, scores.pop(at))
        if at >= 1:
            finish(at - 1, mixed)
        if at == 1 and beside is not None:
            beside()


def unpacking(fresh_refs, first, request_vmem, decode_ref, rows_ref, request_ref, request_sem, decode_sems):
    count = rows_ref.shape[1]
    request_copy = pltpu.make_async_copy(request_vmem, request_ref, request_sem)
    request_copy.start()

    def decode_copy(p):
        return pltpu.make_async_copy(
            rows_ref.at[p], decode_ref.at[request_ref[0, first + p]], decode_sems.at[p]
        )

    def start():
        request_copy.wait()
        for p, fresh_ref in enumerate(fresh_refs):
            stack = fresh_ref[...]
            quarter = stack.shape[1]
            for part in range(stack.shape[0] // count):
                rows_ref[p, :, part * quarter : (part + 1) * quarter] = stack[part * count : (part + 1) * count]
            decode_copy(p).start()

    def wait():
        for p in range(len(fresh_refs)):
            decode_copy(p).wait()

    return start, wait


def spare_part(got):
    return got.at[:, pl.ds(WIDTH, got.shape[1] - WIDTH)]


def pieces_of(refs):
    pieces = []
    for ref in refs:
        pieces += [ref] if len(ref.shape) == 2 else [ref.at[i] for i in range(ref.shape[0])]
    return pieces


def attend_kernel(arrays, unpack, rot_ref, bias_ref, own_ref, *refs):
    got_refs, refs = pieces_of(refs[:arrays]), refs[arrays:]
    start, wait = None, None
    if unpack:
        request_vmem, result_ref, level_ref, decode_ref, *scratch = refs
        start, wait = unpacking([spare_part(got) for got in got_refs], 0, request_vmem, decode_ref, *scratch)
    else:
        result_ref, level_ref = refs
    new_count = rot_ref.shape[1] // PER_KV
    span = len(got_refs) * got_refs[0].shape[0]
    token = lax.broadcasted_iota(jnp.int32, (CHUNK, new_count), 0) % new_count
    causal = jnp.where(lax.broadcasted_iota(jnp.int32, (CHUNK, new_count), 1) <= token, 0.0, MASKED)
    bias = bias_ref[0:1, 0:span]
    per_head = PER_KV * new_count // CHUNK
    keys, values, highs = {}, {}, {}

    def place(at):
        return at // per_head, slice(at % per_head * CHUNK, (at % per_head + 1) * CHUNK)

    def score(at):
        head, rows = place(at)
        if at % per_head == 0:
            join_keys(keys, values, got_refs, own_ref, head)
        return dot_keys(rot_ref[head, rows, :], keys[head])

    def weigh(at, scores):
        scores = jnp.concatenate([scores[:, :span] * SCALE + bias, scores[:, span:] * SCALE + causal], axis=1)
        highs[at] = jnp.max(scores, axis=1, keepdims=True)
        return jnp.exp2(scores - highs[at]).astype(jnp.bfloat16)

    def mix(at, weights):
        return jnp.dot(weights, values[at // per_head], preferred_element_type=jnp.float32)

    def finish(at, mixed):
        head, rows = place(at)
        total = mixed[:, HEAD_DIM:]
        result_ref[head, rows, :] = quotient(mixed[:, :HEAD_DIM], total)
        level_ref[head, rows, :] = highs.pop(at) + jnp.log2(total)

    staged(KV_HEADS * per_head, score, weigh, mix, finish, start)
    if unpack:
        wait()


def attend(rot, bias, own, got, requests=None):
    rows, new_count = rot.shape[1], rot.shape[1] // PER_KV
    operands = [rot, bias, own, *got]
    shapes = [jax.ShapeDtypeStruct((KV_HEADS, rows, HEAD_DIM), jnp.float32)] * 2
    out_specs, scratch = [VMEM] * 2, []
    if requests is not None:
        operands.append(requests)
        slots, width = got[-1].shape
        count = (width - WIDTH) * slots // WIDTH
        shapes.append(jax.ShapeDtypeStruct((new_count // count, count, WIDTH), jnp.bfloat16))
        out_specs.append(ANY)
        scratch = unpack_scratch(len(pieces_of(got)), count, requests)
    return pl.pallas_call(
        functools.partial(attend_kernel, len(got), requests is not None),
        out_shape=tuple(shapes),
        in_specs=[VMEM] * len(operands),
        out_specs=tuple(out_specs),
        scratch_shapes=scratch,
        compiler_params=params(32),
        name="attend",
    )(*operands)


def unpack_scratch(pieces, count, requests):
    return [
        pltpu.VMEM((pieces, count, WIDTH), jnp.bfloat16),
        pltpu.SMEM(requests.shape, jnp.int32),
        pltpu.SemaphoreType.DMA,
        pltpu.SemaphoreType.DMA((pieces,)),
    ]


HEADROOM = 96.0


def late_kernel(pieces, first, rot_ref, bias_ref, result_ref, level_ref, *refs):
    got_refs, refs = refs[:pieces], refs[pieces:]
    request_vmem, _, out_ref, decode_ref, done_ref, out_sems, *scratch = refs
    start, wait = unpacking([spare_part(got) for got in got_refs], first, request_vmem, decode_ref, *scratch)
    slots = got_refs[0].shape[0]
    new_count = out_ref.shape[0]
    size = LATE_CHUNK
    heads_in = size // new_count
    bias = bias_ref[0:1, first * slots : (first + pieces) * slots]
    per_head = PER_KV * new_count // size
    chunks = KV_HEADS * per_head
    keys, values, excess = {}, {}, []

    def place(at):
        return at // per_head, slice(at % per_head * size, (at % per_head + 1) * size)

    def out_copy(at):
        width = heads_in * HEAD_DIM
        return pltpu.make_async_copy(
            done_ref.at[at], out_ref.at[:, pl.ds(pl.multiple_of(at * width, width), width)], out_sems.at[at]
        )

    def store(at, result):
        for row in range(heads_in):
            done_ref[at, :, column(row)] = result[row * new_count : (row + 1) * new_count].astype(jnp.bfloat16)
        out_copy(at).start()

    def score(at):
        head, rows = place(at)
        if at % per_head == 0:
            join_keys(keys, values, got_refs, None, head)
        return dot_keys(rot_ref[head, rows, :], keys[head])

    def weigh(at, scores):
        head, rows = place(at)
        powers = scores * SCALE + bias - level_ref[head, rows, :]
        excess.append(jnp.max(powers.reshape(size // 8, 8, HEAD_DIM), axis=0))
        return jnp.exp2(powers).astype(jnp.bfloat16)

    def mix(at, weights):
        return jnp.dot(weights, values[at // per_head], preferred_element_type=jnp.float32)

    def finish(at, mixed):
        head, rows = place(at)
        store(at, quotient(result_ref[head, rows, :] + mixed[:, :HEAD_DIM], 1.0 + mixed[:, HEAD_DIM:]))

    staged(chunks, score, weigh, mix, finish, start)
    most = jnp.max(functools.reduce(jnp.maximum, excess))
    wait()
    for at in range(chunks):
        out_copy(at).wait()

    @pl.when(most > HEADROOM)
    def _():
        for head in range(KV_HEADS):

            def again(chunk, carry, head=head):
                rows = pl.ds(pl.multiple_of(chunk * size, size), size)
                scores = dot_keys(rot_ref[head, rows, :], keys[head]) * SCALE + bias
                level = level_ref[head, rows, :]
                high = jnp.maximum(level, jnp.max(scores, axis=1, keepdims=True))
                factor = jnp.exp2(level - high)
                weights = jnp.exp2(scores - high).astype(jnp.bfloat16)
                mixed = jnp.dot(weights, values[head], preferred_element_type=jnp.float32)
                at = head * per_head + chunk
                summed = result_ref[head, rows, :] * factor + mixed[:, :HEAD_DIM]
                store(at, quotient(summed, factor + mixed[:, HEAD_DIM:]))
                out_copy(at).wait()
                return carry

            lax.fori_loop(0, per_head, again, 0)


def attend_late(rot, bias, result, level, got, first, requests, decode):
    rows, new_count = rot.shape[1], rot.shape[1] // PER_KV
    operands = [rot, bias, result, level, *got, requests, decode]
    chunks = KV_HEADS * rows // LATE_CHUNK
    return pl.pallas_call(
        functools.partial(late_kernel, len(got), first),
        out_shape=(
            jax.ShapeDtypeStruct((new_count, Q_HEADS * HEAD_DIM), jnp.bfloat16),
            jax.ShapeDtypeStruct(decode.shape, jnp.bfloat16),
        ),
        in_specs=[VMEM] * (len(operands) - 1) + [ANY],
        out_specs=(ANY, ANY),
        scratch_shapes=[
            pltpu.VMEM((chunks, new_count, LATE_CHUNK // new_count * HEAD_DIM), jnp.bfloat16),
            pltpu.SemaphoreType.DMA((chunks,)),
        ]
        + unpack_scratch(len(got), decode.shape[1], requests),
        input_output_aliases={len(operands) - 1: 1},
        compiler_params=params(32),
        name="attend_late",
    )(*operands)


def inverse(table):
    places = jnp.arange(table.shape[0], dtype=jnp.int32)
    return jnp.sum(jnp.where(table[None, :] == places[:, None], places, 0), axis=1)


def rotate(rows, positions, heads):
    half = HEAD_DIM // 2
    freqs = ROPE_BASE ** (-jnp.arange(half, dtype=jnp.float32) / half)
    angles = positions.astype(jnp.float32)[:, None] * freqs[None, :]
    cosine = jnp.concatenate([jnp.cos(angles)] * 2, axis=-1)[:, None, :]
    sine = jnp.concatenate([-jnp.sin(angles), jnp.sin(angles)], axis=-1)[:, None, :]
    split = rows.astype(jnp.float32).reshape(rows.shape[0], heads, HEAD_DIM)
    turned = jnp.roll(split, half, axis=-1)
    return (split * cosine + turned * sine).astype(jnp.bfloat16)


def small_pieces(me, assignment, prefix_len, stripe_map, owner_map, queries, block_kv, pool):
    groups, slots, width = pool.shape
    new_count = block_kv.shape[0]
    count = new_count // groups
    request = assignment[me[0]]
    length = prefix_len[request]
    positions = length + jnp.arange(new_count, dtype=jnp.int32)
    rot = rotate(queries, positions, Q_HEADS).reshape(new_count, KV_HEADS, PER_KV, HEAD_DIM)
    rot = jnp.transpose(rot, (1, 2, 0, 3)).reshape(KV_HEADS, PER_KV * new_count, HEAD_DIM)
    new_keys = rotate(block_kv[:, :KV_WIDTH], positions, KV_HEADS).reshape(new_count, KV_WIDTH)
    new_kv = jnp.concatenate([new_keys, block_kv[:, KV_WIDTH:]], axis=1)
    own = jnp.transpose(new_kv.reshape(new_count, 2 * KV_HEADS, HEAD_DIM), (1, 0, 2))
    spread = jnp.transpose(new_kv.reshape(count, groups, width), (1, 0, 2))
    send = jnp.concatenate([pool[assignment], spread[inverse(owner_map[request])]], axis=1)
    got = lax.all_to_all(send, "pg", split_axis=0, concat_axis=0, tiled=True)
    located = jnp.arange(slots, dtype=jnp.int32)[None, :] * groups + inverse(stripe_map[request])[:, None]
    bias = jnp.where(located < length, 0.0, MASKED).astype(jnp.float32).reshape(1, groups * slots)
    keys = got[:, :slots].reshape(groups * slots, width)
    result, _ = attend(rot, jnp.broadcast_to(bias, (8, groups * slots)), own, [keys])
    result = result.astype(jnp.bfloat16).reshape(KV_HEADS, PER_KV, new_count, HEAD_DIM)
    attended = jnp.transpose(result, (2, 0, 1, 3)).reshape(new_count, Q_HEADS * HEAD_DIM)
    return attended, got[inverse(assignment), slots:]


def shards(queries, block_kv, pool_kv, prefix_len, assignment, stripe_map, owner_map):
    queries, block_kv, pool = queries[0], block_kv[0], pool_kv[0]
    groups, slots, width = pool.shape
    new_count = queries.shape[0]
    count = new_count // groups
    me = lax.axis_index("pg").astype(jnp.int32).reshape(1)
    if groups != 16 or slots % 16 or HEAD_DIM % slots or count % 8 or slots % count:
        attended, decode_kv = small_pieces(
            me, assignment, prefix_len, stripe_map, owner_map, queries, block_kv, pool
        )
        return (attended[None], decode_kv[None])
    order = order_of(groups)
    table = rotation_tables(new_count)
    blocks, info = front(order, me, assignment, prefix_len, owner_map, stripe_map, block_kv, table, pool)
    blocks = list(blocks) + list(pack_others(info, pool, new_count))
    rot, own, bias, requests = rotate_queries(info, queries, groups * slots)
    rot, *blocks[AHEAD_OF_QUERIES:] = lax.optimization_barrier((rot, *blocks[AHEAD_OF_QUERIES:]))
    got = [
        lax.ppermute(block, "pg", [(source, source ^ t) for source in range(groups)]) if t else block
        for block, t in zip(blocks, order)
    ]
    soon = groups - LATE
    result, level, decode_kv = attend(rot, bias, own, got[:soon], requests)
    attended, decode_kv = attend_late(rot, bias, result, level, got[soon:], soon, requests, decode_kv)
    return (attended[None], decode_kv[None])


def solution(mesh):
    return jax.shard_map(
        shards,
        mesh=mesh,
        in_specs=(
            P(("rep", "pg"), None, None),
            P(("rep", "pg"), None, None),
            P(("rep", "pg"), None, None, None),
            P("rep"),
            P("rep"),
            P("rep", None),
            P("rep", None),
        ),
        out_specs=(P(("rep", "pg"), None, None), P(("rep", "pg"), None, None, None)),
        check_vma=False,
    )
```

```python
import functools
import math

import jax
import jax.numpy as jnp
import numpy as np
from jax import lax
from jax.experimental import pallas as pl
from jax.experimental.pallas import tpu as pltpu
from jax.sharding import PartitionSpec as P

Q_HEADS = 32
KV_HEADS = 4
HEAD_DIM = 128
PER_KV = Q_HEADS // KV_HEADS
KV_WIDTH = KV_HEADS * HEAD_DIM
WIDTH = 2 * KV_WIDTH

ROPE_BASE = 1000000.0
MASKED = -1e30
SCALE = HEAD_DIM ** -0.5 / math.log(2.0)
CHUNK = 256
LATE = 4
LATE_CHUNK = 512
AHEAD = 4
AHEAD_OF_QUERIES = 8

SMEM = pl.BlockSpec(memory_space=pltpu.SMEM)
VMEM = pl.BlockSpec(memory_space=pltpu.VMEM)
ANY = pl.BlockSpec(memory_space=pl.ANY)


def params(mib):
    return pltpu.CompilerParams(vmem_limit_bytes=mib * 1024 * 1024)


def column(head):
    return slice(head * HEAD_DIM, (head + 1) * HEAD_DIM)


def order_of(groups):
    half = groups // 2
    near = list(range(half - 1, 0, -1))
    quarter, eighth = half // 2, half // 4
    far = [half + (at // 2 if at % 2 == 0 else quarter + (at // 2 ^ eighth)) for at in range(half)]
    order = [(far if kind == "f" else near).pop(0) for kind in "fnfnfnfnfnnffnf"]
    order.insert(groups - LATE - 1, 0)
    return order


def rotation_tables(rows):
    half = HEAD_DIM // 2
    freqs = np.tile(ROPE_BASE ** (-np.arange(half, dtype=np.float64) / half), 2)
    angles = np.arange(rows, dtype=np.float64)[:, None] * freqs[None, :]
    parts = [np.cos(angles), np.sin(angles), np.tile(freqs, (8, 1))]
    return jnp.asarray(np.concatenate(parts, axis=0).astype(np.float32))


def rotation(table_ref, length):
    rows = (table_ref.shape[0] - 8) // 2
    start = length.astype(jnp.float32) * table_ref[2 * rows : 2 * rows + 8, :]
    cos_start, sin_start = jnp.cos(start)[0:1], jnp.sin(start)[0:1]
    cos_row, sin_row = table_ref[0:rows, :], table_ref[rows : 2 * rows, :]
    lane = lax.broadcasted_iota(jnp.int32, (1, HEAD_DIM), 1)
    sign = jnp.where(lane < HEAD_DIM // 2, -1.0, 1.0)
    cosine = cos_row * cos_start - sin_row * sin_start
    return cosine, sin_row * (cos_start * sign) + cos_row * (sin_start * sign)


def turn(x, cosine, sine):
    x = x.astype(jnp.float32)
    return (x * cosine + pltpu.roll(x, HEAD_DIM // 2, 1) * sine).astype(jnp.bfloat16)


def info_rows(new_count):
    sizes = [("cos", new_count), ("sin", new_count), ("bias", 8), ("scalars", 8), ("new", 2 * KV_HEADS * new_count)]
    at, rows = 0, {}
    for name, size in sizes:
        rows[name] = at
        at += size
    return rows, at


def fresh_rows(info_ref, base, residue, new_count, count, quarter, lanes):
    groups = new_count // count
    stack = [
        info_ref[pl.ds(base + (head + lanes) * new_count + residue, count, stride=groups), :]
        for head in range(0, 2 * KV_HEADS, quarter)
    ]
    return jnp.concatenate(stack, axis=0)


def front_kernel(
    order, me_ref, assign_any, length_any, owner_any, stripe_any, block_any, table_any, pool_any, *refs
):
    groups, slots, width = pool_any.shape
    send_refs, info_any, refs = refs[:AHEAD], refs[AHEAD], refs[AHEAD + 1 :]
    (assign_ref, length_ref, owner_ref, stripe_ref, residue_ref, block_ref, table_ref, pool_ref, pack_ref, info_ref,
     small_sems, pool_sems, send_sems, info_sems) = refs
    new_count = block_any.shape[0]
    count = new_count // groups
    quarter = width * count // slots // HEAD_DIM
    at, rows = info_rows(new_count)
    pairs = [
        (assign_any, assign_ref), (length_any, length_ref), (owner_any, owner_ref), (stripe_any, stripe_ref),
        (block_any, block_ref), (table_any, table_ref),
    ]
    smalls = [pltpu.make_async_copy(*pair, small_sems.at[i]) for i, pair in enumerate(pairs)]
    for copy in smalls:
        copy.start()
    pool_copies = [
        pltpu.make_async_copy(pool_any.at[pl.ds(low, 4)], pool_ref.at[pl.ds(low, 4)], pool_sems.at[low // 4])
        for low in range(0, groups, 4)
    ]
    for copy in pool_copies:
        copy.start()
    me = me_ref[0]
    for copy in smalls:
        copy.wait()
    request = assign_ref[me]
    length = length_ref[request]
    for residue in range(groups):
        residue_ref[owner_ref[request, residue]] = residue
    cosine, sine = rotation(table_ref, length)
    for head in range(KV_HEADS):
        low = at["new"] + head * new_count
        info_ref[low : low + new_count] = turn(block_ref[:, column(head)], cosine, sine).astype(jnp.float32)
        low += KV_HEADS * new_count
        info_ref[low : low + new_count] = block_ref[:, column(KV_HEADS + head)].astype(jnp.float32)

    def info_copy(part, low, high):
        part_rows = pl.ds(low, high - low)
        return pltpu.make_async_copy(info_ref.at[part_rows], info_any.at[part_rows], info_sems.at[part])

    info_copy(0, at["new"], rows).start()
    info_ref[at["cos"] : at["cos"] + new_count] = cosine
    info_ref[at["sin"] : at["sin"] + new_count] = sine
    per_row = HEAD_DIM // slots
    row = lax.broadcasted_iota(jnp.int32, (8, HEAD_DIM), 0)
    lane = lax.broadcasted_iota(jnp.int32, (8, HEAD_DIM), 1)
    piece, slot = row * per_row + lane // slots, lane % slots
    holder, requests, residues = jnp.zeros_like(lane), jnp.zeros_like(lane), jnp.zeros_like(lane)
    for p in range(groups):
        other = me ^ order[p]
        holder = jnp.where(piece == p, other, holder)
        requests = jnp.where(lane == p, assign_ref[other], requests)
        residues = jnp.where(lane == p, residue_ref[other], residues)
    bias = jnp.full((8, HEAD_DIM), MASKED, jnp.float32)
    for residue in range(groups):
        live = (holder == stripe_ref[request, residue]) & (slot * groups + residue < length)
        bias = jnp.where(live, 0.0, bias)
    info_ref[at["bias"] : at["bias"] + 8] = bias
    scalars = jnp.where(row == 0, requests, residues)
    info_ref[at["scalars"] : at["scalars"] + 8] = scalars.astype(jnp.float32)
    info_copy(1, 0, at["new"]).start()
    for copy in pool_copies:
        copy.wait()
    sends = []
    for p in range(AHEAD):
        pack_ref[p, :, 0:width] = pool_ref[assign_ref[me ^ order[p]]]
        for lanes in range(quarter):
            pack_ref[p, :, width + lanes * HEAD_DIM : width + (lanes + 1) * HEAD_DIM] = fresh_rows(
                info_ref, at["new"], residue_ref[me ^ order[p]], new_count, count, quarter, lanes
            ).astype(jnp.bfloat16)
        sends.append(pltpu.make_async_copy(pack_ref.at[p], send_refs[p], send_sems.at[p]))
        sends[-1].start()
    for copy in sends:
        copy.wait()
    info_copy(0, at["new"], rows).wait()
    info_copy(1, 0, at["new"]).wait()


def front(order, me, assignment, prefix_len, owner_map, stripe_map, block_kv, table, pool):
    groups, slots, width = pool.shape
    new_count = block_kv.shape[0]
    count = new_count // groups
    block = jax.ShapeDtypeStruct((slots, width + width * count // slots), jnp.bfloat16)
    info = jax.ShapeDtypeStruct((info_rows(new_count)[1], HEAD_DIM), jnp.float32)
    *blocks, info = pl.pallas_call(
        functools.partial(front_kernel, order),
        out_shape=[block] * AHEAD + [info],
        in_specs=[SMEM] + [ANY] * 7,
        out_specs=[ANY] * (AHEAD + 1),
        scratch_shapes=[
            pltpu.SMEM(assignment.shape, jnp.int32),
            pltpu.SMEM(prefix_len.shape, jnp.int32),
            pltpu.SMEM(owner_map.shape, jnp.int32),
            pltpu.SMEM(stripe_map.shape, jnp.int32),
            pltpu.SMEM(assignment.shape, jnp.int32),
            pltpu.VMEM(block_kv.shape, jnp.bfloat16),
            pltpu.VMEM(table.shape, jnp.float32),
            pltpu.VMEM(pool.shape, jnp.bfloat16),
            pltpu.VMEM((AHEAD,) + block.shape, jnp.bfloat16),
            pltpu.VMEM(info.shape, jnp.float32),
            pltpu.SemaphoreType.DMA((6,)),
            pltpu.SemaphoreType.DMA((groups // 4,)),
            pltpu.SemaphoreType.DMA((AHEAD,)),
            pltpu.SemaphoreType.DMA((2,)),
        ],
        compiler_params=params(60),
        name="front",
    )(me, assignment, prefix_len, owner_map, stripe_map, block_kv, table, pool)
    return blocks, info


def pack_kernel(info_ref, pool_ref, *refs):
    groups, slots, width = pool_ref.shape
    targets, (scalar_ref, scalar_sem) = refs[: groups - AHEAD], refs[groups - AHEAD :]
    new_count = slots * groups * (targets[0].shape[1] - width) // width
    at, _ = info_rows(new_count)
    count = new_count // groups
    quarter = (targets[0].shape[1] - width) // HEAD_DIM
    scalar_copy = pltpu.make_async_copy(info_ref.at[pl.ds(at["scalars"], 8)], scalar_ref, scalar_sem)
    scalar_copy.start()
    scalar_copy.wait()
    for p, target in enumerate(targets, AHEAD):
        target[:, 0:width] = pool_ref[scalar_ref[0, p].astype(jnp.int32)]
        residue = scalar_ref[1, p].astype(jnp.int32)
        for lanes in range(quarter):
            target[:, width + lanes * HEAD_DIM : width + (lanes + 1) * HEAD_DIM] = fresh_rows(
                info_ref, at["new"], residue, new_count, count, quarter, lanes
            ).astype(jnp.bfloat16)


def pack_others(info, pool, new_count):
    groups, slots, width = pool.shape
    block = (slots, width + width * (new_count // groups) // slots)
    return pl.pallas_call(
        pack_kernel,
        out_shape=[jax.ShapeDtypeStruct(block, jnp.bfloat16)] * (groups - AHEAD),
        in_specs=[VMEM] * 2,
        out_specs=[VMEM] * (groups - AHEAD),
        scratch_shapes=[pltpu.SMEM((8, HEAD_DIM), jnp.float32), pltpu.SemaphoreType.DMA],
        compiler_params=params(32),
        name="pack_others",
    )(info, pool)


def query_kernel(info_ref, q_ref, rot_ref, own_ref, bias_ref, request_ref):
    new_count = q_ref.shape[0]
    at, _ = info_rows(new_count)
    cosine = info_ref[at["cos"] : at["cos"] + new_count]
    sine = info_ref[at["sin"] : at["sin"] + new_count]
    for row in range(bias_ref.shape[1] // HEAD_DIM):
        line = info_ref[at["bias"] + row : at["bias"] + row + 1]
        bias_ref[:, column(row)] = jnp.broadcast_to(line, (8, HEAD_DIM))
    request_ref[...] = info_ref[at["scalars"] : at["scalars"] + 8].astype(jnp.int32)
    for head in range(2 * KV_HEADS):
        rows = at["new"] + head * new_count
        own_ref[head] = info_ref[rows : rows + new_count].astype(jnp.bfloat16)
    for head in range(Q_HEADS):
        rows = slice((head % PER_KV) * new_count, (head % PER_KV + 1) * new_count)
        rot_ref[head // PER_KV, rows, :] = turn(q_ref[:, column(head)], cosine, sine)


def rotate_queries(info, queries, span):
    new_count = queries.shape[0]
    return pl.pallas_call(
        query_kernel,
        out_shape=(
            jax.ShapeDtypeStruct((KV_HEADS, PER_KV * new_count, HEAD_DIM), jnp.bfloat16),
            jax.ShapeDtypeStruct((2 * KV_HEADS, new_count, HEAD_DIM), jnp.bfloat16),
            jax.ShapeDtypeStruct((8, span), jnp.float32),
            jax.ShapeDtypeStruct((8, HEAD_DIM), jnp.int32),
        ),
        in_specs=[VMEM] * 2,
        out_specs=[VMEM] * 4,
        compiler_params=params(32),
        name="rotate_queries",
    )(info, queries)


def quotient(summed, total):
    about = pl.reciprocal(total, approx=True)
    return summed * (about * (2.0 - total * about))


def join_keys(keys, values, got_refs, own_ref, head):
    key_parts = [got[:, column(head)] for got in got_refs]
    value_parts = [got[:, column(KV_HEADS + head)] for got in got_refs]
    if own_ref is not None:
        key_parts.append(own_ref[head])
        value_parts.append(own_ref[KV_HEADS + head])
    keys[head] = jnp.concatenate(key_parts, axis=0)
    value = jnp.concatenate(value_parts, axis=0)
    values[head] = jnp.concatenate([value, jnp.ones_like(value)], axis=1)


def dot_keys(query, keys):
    return lax.dot_general(query, keys, (((1,), (1,)), ((), ())), preferred_element_type=jnp.float32)


def staged(total, score, weigh, mix, finish, beside=None):
    scores, weights = {0: score(0)}, {}
    for at in range(total + 1):
        if at + 1 < total:
            scores[at + 1] = score(at + 1)
        if at >= 1:
            mixed = mix(at - 1, weights.pop(at - 1))
        if at < total:
            weights[at] = weigh(at, scores.pop(at))
        if at >= 1:
            finish(at - 1, mixed)
        if at == 1 and beside is not None:
            beside()


def unpacking(fresh_refs, first, request_vmem, decode_ref, rows_ref, request_ref, request_sem, decode_sems):
    count = rows_ref.shape[1]
    request_copy = pltpu.make_async_copy(request_vmem, request_ref, request_sem)
    request_copy.start()

    def decode_copy(p):
        return pltpu.make_async_copy(
            rows_ref.at[p], decode_ref.at[request_ref[0, first + p]], decode_sems.at[p]
        )

    def start():
        request_copy.wait()
        for p, fresh_ref in enumerate(fresh_refs):
            stack = fresh_ref[...]
            quarter = stack.shape[1]
            for part in range(stack.shape[0] // count):
                rows_ref[p, :, part * quarter : (part + 1) * quarter] = stack[part * count : (part + 1) * count]
            decode_copy(p).start()

    def wait():
        for p in range(len(fresh_refs)):
            decode_copy(p).wait()

    return start, wait


def spare_part(got):
    return got.at[:, pl.ds(WIDTH, got.shape[1] - WIDTH)]


def pieces_of(refs):
    pieces = []
    for ref in refs:
        pieces += [ref] if len(ref.shape) == 2 else [ref.at[i] for i in range(ref.shape[0])]
    return pieces


def attend_kernel(arrays, unpack, rot_ref, bias_ref, own_ref, *refs):
    got_refs, refs = pieces_of(refs[:arrays]), refs[arrays:]
    start, wait = None, None
    if unpack:
        request_vmem, result_ref, level_ref, decode_ref, *scratch = refs
        start, wait = unpacking([spare_part(got) for got in got_refs], 0, request_vmem, decode_ref, *scratch)
    else:
        result_ref, level_ref = refs
    new_count = rot_ref.shape[1] // PER_KV
    span = len(got_refs) * got_refs[0].shape[0]
    token = lax.broadcasted_iota(jnp.int32, (CHUNK, new_count), 0) % new_count
    causal = jnp.where(lax.broadcasted_iota(jnp.int32, (CHUNK, new_count), 1) <= token, 0.0, MASKED)
    bias = bias_ref[0:1, 0:span]
    per_head = PER_KV * new_count // CHUNK
    keys, values, highs = {}, {}, {}

    def place(at):
        return at // per_head, slice(at % per_head * CHUNK, (at % per_head + 1) * CHUNK)

    def score(at):
        head, rows = place(at)
        if at % per_head == 0:
            join_keys(keys, values, got_refs, own_ref, head)
        return dot_keys(rot_ref[head, rows, :], keys[head])

    def weigh(at, scores):
        scores = jnp.concatenate([scores[:, :span] * SCALE + bias, scores[:, span:] * SCALE + causal], axis=1)
        highs[at] = jnp.max(scores, axis=1, keepdims=True)
        return jnp.exp2(scores - highs[at]).astype(jnp.bfloat16)

    def mix(at, weights):
        return jnp.dot(weights, values[at // per_head], preferred_element_type=jnp.float32)

    def finish(at, mixed):
        head, rows = place(at)
        total = mixed[:, HEAD_DIM:]
        result_ref[head, rows, :] = quotient(mixed[:, :HEAD_DIM], total)
        level_ref[head, rows, :] = highs.pop(at) + jnp.log2(total)

    staged(KV_HEADS * per_head, score, weigh, mix, finish, start)
    if unpack:
        wait()


def attend(rot, bias, own, got, requests=None):
    rows, new_count = rot.shape[1], rot.shape[1] // PER_KV
    operands = [rot, bias, own, *got]
    shapes = [jax.ShapeDtypeStruct((KV_HEADS, rows, HEAD_DIM), jnp.float32)] * 2
    out_specs, scratch = [VMEM] * 2, []
    if requests is not None:
        operands.append(requests)
        slots, width = got[-1].shape
        count = (width - WIDTH) * slots // WIDTH
        shapes.append(jax.ShapeDtypeStruct((new_count // count, count, WIDTH), jnp.bfloat16))
        out_specs.append(ANY)
        scratch = unpack_scratch(len(pieces_of(got)), count, requests)
    return pl.pallas_call(
        functools.partial(attend_kernel, len(got), requests is not None),
        out_shape=tuple(shapes),
        in_specs=[VMEM] * len(operands),
        out_specs=tuple(out_specs),
        scratch_shapes=scratch,
        compiler_params=params(32),
        name="attend",
    )(*operands)


def unpack_scratch(pieces, count, requests):
    return [
        pltpu.VMEM((pieces, count, WIDTH), jnp.bfloat16),
        pltpu.SMEM(requests.shape, jnp.int32),
        pltpu.SemaphoreType.DMA,
        pltpu.SemaphoreType.DMA((pieces,)),
    ]


HEADROOM = 96.0


def late_kernel(pieces, first, rot_ref, bias_ref, result_ref, level_ref, *refs):
    got_refs, refs = refs[:pieces], refs[pieces:]
    request_vmem, _, out_ref, decode_ref, done_ref, out_sems, *scratch = refs
    start, wait = unpacking([spare_part(got) for got in got_refs], first, request_vmem, decode_ref, *scratch)
    slots = got_refs[0].shape[0]
    new_count = out_ref.shape[0]
    size = LATE_CHUNK
    heads_in = size // new_count
    bias = bias_ref[0:1, first * slots : (first + pieces) * slots]
    per_head = PER_KV * new_count // size
    chunks = KV_HEADS * per_head
    keys, values, excess = {}, {}, []

    def place(at):
        return at // per_head, slice(at % per_head * size, (at % per_head + 1) * size)

    def out_copy(at):
        width = heads_in * HEAD_DIM
        return pltpu.make_async_copy(
            done_ref.at[at], out_ref.at[:, pl.ds(pl.multiple_of(at * width, width), width)], out_sems.at[at]
        )

    def store(at, result):
        for row in range(heads_in):
            done_ref[at, :, column(row)] = result[row * new_count : (row + 1) * new_count].astype(jnp.bfloat16)
        out_copy(at).start()

    def score(at):
        head, rows = place(at)
        if at % per_head == 0:
            join_keys(keys, values, got_refs, None, head)
        return dot_keys(rot_ref[head, rows, :], keys[head])

    def weigh(at, scores):
        head, rows = place(at)
        powers = scores * SCALE + bias - level_ref[head, rows, :]
        excess.append(jnp.max(powers.reshape(size // 8, 8, HEAD_DIM), axis=0))
        return jnp.exp2(powers).astype(jnp.bfloat16)

    def mix(at, weights):
        return jnp.dot(weights, values[at // per_head], preferred_element_type=jnp.float32)

    def finish(at, mixed):
        head, rows = place(at)
        store(at, quotient(result_ref[head, rows, :] + mixed[:, :HEAD_DIM], 1.0 + mixed[:, HEAD_DIM:]))

    staged(chunks, score, weigh, mix, finish, start)
    most = jnp.max(functools.reduce(jnp.maximum, excess))
    wait()
    for at in range(chunks):
        out_copy(at).wait()

    @pl.when(most > HEADROOM)
    def _():
        for head in range(KV_HEADS):

            def again(chunk, carry, head=head):
                rows = pl.ds(pl.multiple_of(chunk * size, size), size)
                scores = dot_keys(rot_ref[head, rows, :], keys[head]) * SCALE + bias
                level = level_ref[head, rows, :]
                high = jnp.maximum(level, jnp.max(scores, axis=1, keepdims=True))
                factor = jnp.exp2(level - high)
                weights = jnp.exp2(scores - high).astype(jnp.bfloat16)
                mixed = jnp.dot(weights, values[head], preferred_element_type=jnp.float32)
                at = head * per_head + chunk
                summed = result_ref[head, rows, :] * factor + mixed[:, :HEAD_DIM]
                store(at, quotient(summed, factor + mixed[:, HEAD_DIM:]))
                out_copy(at).wait()
                return carry

            lax.fori_loop(0, per_head, again, 0)


def attend_late(rot, bias, result, level, got, first, requests, decode):
    rows, new_count = rot.shape[1], rot.shape[1] // PER_KV
    operands = [rot, bias, result, level, *got, requests, decode]
    chunks = KV_HEADS * rows // LATE_CHUNK
    return pl.pallas_call(
        functools.partial(late_kernel, len(got), first),
        out_shape=(
            jax.ShapeDtypeStruct((new_count, Q_HEADS * HEAD_DIM), jnp.bfloat16),
            jax.ShapeDtypeStruct(decode.shape, jnp.bfloat16),
        ),
        in_specs=[VMEM] * (len(operands) - 1) + [ANY],
        out_specs=(ANY, ANY),
        scratch_shapes=[
            pltpu.VMEM((chunks, new_count, LATE_CHUNK // new_count * HEAD_DIM), jnp.bfloat16),
            pltpu.SemaphoreType.DMA((chunks,)),
        ]
        + unpack_scratch(len(got), decode.shape[1], requests),
        input_output_aliases={len(operands) - 1: 1},
        compiler_params=params(32),
        name="attend_late",
    )(*operands)


def inverse(table):
    places = jnp.arange(table.shape[0], dtype=jnp.int32)
    return jnp.sum(jnp.where(table[None, :] == places[:, None], places, 0), axis=1)


def rotate(rows, positions, heads):
    half = HEAD_DIM // 2
    freqs = ROPE_BASE ** (-jnp.arange(half, dtype=jnp.float32) / half)
    angles = positions.astype(jnp.float32)[:, None] * freqs[None, :]
    cosine = jnp.concatenate([jnp.cos(angles)] * 2, axis=-1)[:, None, :]
    sine = jnp.concatenate([-jnp.sin(angles), jnp.sin(angles)], axis=-1)[:, None, :]
    split = rows.astype(jnp.float32).reshape(rows.shape[0], heads, HEAD_DIM)
    turned = jnp.roll(split, half, axis=-1)
    return (split * cosine + turned * sine).astype(jnp.bfloat16)


def small_pieces(me, assignment, prefix_len, stripe_map, owner_map, queries, block_kv, pool):
    groups, slots, width = pool.shape
    new_count = block_kv.shape[0]
    count = new_count // groups
    request = assignment[me[0]]
    length = prefix_len[request]
    positions = length + jnp.arange(new_count, dtype=jnp.int32)
    rot = rotate(queries, positions, Q_HEADS).reshape(new_count, KV_HEADS, PER_KV, HEAD_DIM)
    rot = jnp.transpose(rot, (1, 2, 0, 3)).reshape(KV_HEADS, PER_KV * new_count, HEAD_DIM)
    new_keys = rotate(block_kv[:, :KV_WIDTH], positions, KV_HEADS).reshape(new_count, KV_WIDTH)
    new_kv = jnp.concatenate([new_keys, block_kv[:, KV_WIDTH:]], axis=1)
    own = jnp.transpose(new_kv.reshape(new_count, 2 * KV_HEADS, HEAD_DIM), (1, 0, 2))
    spread = jnp.transpose(new_kv.reshape(count, groups, width), (1, 0, 2))
    send = jnp.concatenate([pool[assignment], spread[inverse(owner_map[request])]], axis=1)
    got = lax.all_to_all(send, "pg", split_axis=0, concat_axis=0, tiled=True)
    located = jnp.arange(slots, dtype=jnp.int32)[None, :] * groups + inverse(stripe_map[request])[:, None]
    bias = jnp.where(located < length, 0.0, MASKED).astype(jnp.float32).reshape(1, groups * slots)
    keys = got[:, :slots].reshape(groups * slots, width)
    result, _ = attend(rot, jnp.broadcast_to(bias, (8, groups * slots)), own, [keys])
    result = result.astype(jnp.bfloat16).reshape(KV_HEADS, PER_KV, new_count, HEAD_DIM)
    attended = jnp.transpose(result, (2, 0, 1, 3)).reshape(new_count, Q_HEADS * HEAD_DIM)
    return attended, got[inverse(assignment), slots:]


def shards(queries, block_kv, pool_kv, prefix_len, assignment, stripe_map, owner_map):
    queries, block_kv, pool = queries[0], block_kv[0], pool_kv[0]
    groups, slots, width = pool.shape
    new_count = queries.shape[0]
    count = new_count // groups
    me = lax.axis_index("pg").astype(jnp.int32).reshape(1)
    if groups != 16 or slots % 16 or HEAD_DIM % slots or count % 8 or slots % count:
        attended, decode_kv = small_pieces(
            me, assignment, prefix_len, stripe_map, owner_map, queries, block_kv, pool
        )
        return (attended[None], decode_kv[None])
    order = order_of(groups)
    table = rotation_tables(new_count)
    blocks, info = front(order, me, assignment, prefix_len, owner_map, stripe_map, block_kv, table, pool)
    blocks = list(blocks) + list(pack_others(info, pool, new_count))
    rot, own, bias, requests = rotate_queries(info, queries, groups * slots)
    rot, *blocks[AHEAD_OF_QUERIES:] = lax.optimization_barrier((rot, *blocks[AHEAD_OF_QUERIES:]))
    got = [
        lax.ppermute(block, "pg", [(source, source ^ t) for source in range(groups)]) if t else block
        for block, t in zip(blocks, order)
    ]
    soon = groups - LATE
    result, level, decode_kv = attend(rot, bias, own, got[:soon], requests)
    attended, decode_kv = attend_late(rot, bias, result, level, got[soon:], soon, requests, decode_kv)
    return (attended[None], decode_kv[None])


def solution(mesh):
    return jax.shard_map(
        shards,
        mesh=mesh,
        in_specs=(
            P(("rep", "pg"), None, None),
            P(("rep", "pg"), None, None),
            P(("rep", "pg"), None, None, None),
            P("rep"),
            P("rep"),
            P("rep", None),
            P("rep", None),
        ),
        out_specs=(P(("rep", "pg"), None, None), P(("rep", "pg"), None, None, None)),
        check_vma=False,
    )
```

```python
import functools
import math

import jax
import jax.numpy as jnp
import numpy as np
from jax import lax
from jax.experimental import pallas as pl
from jax.experimental.pallas import tpu as pltpu
from jax.sharding import PartitionSpec as P

Q_HEADS = 32
KV_HEADS = 4
HEAD_DIM = 128
PER_KV = Q_HEADS // KV_HEADS
KV_WIDTH = KV_HEADS * HEAD_DIM
WIDTH = 2 * KV_WIDTH

ROPE_BASE = 1000000.0
MASKED = -1e30
SCALE = HEAD_DIM ** -0.5 / math.log(2.0)
CHUNK = 256
LATE = 4
LATE_CHUNK = 512
AHEAD = 4
AHEAD_OF_QUERIES = 8

SMEM = pl.BlockSpec(memory_space=pltpu.SMEM)
VMEM = pl.BlockSpec(memory_space=pltpu.VMEM)
ANY = pl.BlockSpec(memory_space=pl.ANY)


def params(mib):
    return pltpu.CompilerParams(vmem_limit_bytes=mib * 1024 * 1024)


def column(head):
    return slice(head * HEAD_DIM, (head + 1) * HEAD_DIM)


def order_of(groups):
    half = groups // 2
    near = list(range(half - 1, 0, -1))
    quarter, eighth = half // 2, half // 4
    far = [half + (at // 2 if at % 2 == 0 else quarter + (at // 2 ^ eighth)) for at in range(half)]
    order = [(far if kind == "f" else near).pop(0) for kind in "ffnfnfnfnfnfnfn"]
    order.insert(groups - LATE - 1, 0)
    return order


def rotation_tables(rows):
    half = HEAD_DIM // 2
    freqs = np.tile(ROPE_BASE ** (-np.arange(half, dtype=np.float64) / half), 2)
    angles = np.arange(rows, dtype=np.float64)[:, None] * freqs[None, :]
    parts = [np.cos(angles), np.sin(angles), np.tile(freqs, (8, 1))]
    return jnp.asarray(np.concatenate(parts, axis=0).astype(np.float32))


def rotation(table_ref, length):
    rows = (table_ref.shape[0] - 8) // 2
    start = length.astype(jnp.float32) * table_ref[2 * rows : 2 * rows + 8, :]
    cos_start, sin_start = jnp.cos(start)[0:1], jnp.sin(start)[0:1]
    cos_row, sin_row = table_ref[0:rows, :], table_ref[rows : 2 * rows, :]
    lane = lax.broadcasted_iota(jnp.int32, (1, HEAD_DIM), 1)
    sign = jnp.where(lane < HEAD_DIM // 2, -1.0, 1.0)
    cosine = cos_row * cos_start - sin_row * sin_start
    return cosine, sin_row * (cos_start * sign) + cos_row * (sin_start * sign)


def turn(x, cosine, sine):
    x = x.astype(jnp.float32)
    return (x * cosine + pltpu.roll(x, HEAD_DIM // 2, 1) * sine).astype(jnp.bfloat16)


def info_rows(new_count):
    sizes = [("cos", new_count), ("sin", new_count), ("bias", 8), ("scalars", 8), ("new", 2 * KV_HEADS * new_count)]
    at, rows = 0, {}
    for name, size in sizes:
        rows[name] = at
        at += size
    return rows, at


def fresh_rows(info_ref, base, residue, new_count, count, quarter, lanes):
    groups = new_count // count
    stack = [
        info_ref[pl.ds(base + (head + lanes) * new_count + residue, count, stride=groups), :]
        for head in range(0, 2 * KV_HEADS, quarter)
    ]
    return jnp.concatenate(stack, axis=0)


def front_kernel(
    order, me_ref, assign_any, length_any, owner_any, stripe_any, block_any, table_any, pool_any, *refs
):
    groups, slots, width = pool_any.shape
    send_refs, info_any, refs = refs[:AHEAD], refs[AHEAD], refs[AHEAD + 1 :]
    (assign_ref, length_ref, owner_ref, stripe_ref, residue_ref, block_ref, table_ref, pool_ref, pack_ref, info_ref,
     small_sems, pool_sems, send_sems, info_sems) = refs
    new_count = block_any.shape[0]
    count = new_count // groups
    quarter = width * count // slots // HEAD_DIM
    at, rows = info_rows(new_count)
    pairs = [
        (assign_any, assign_ref), (length_any, length_ref), (owner_any, owner_ref), (stripe_any, stripe_ref),
        (block_any, block_ref), (table_any, table_ref),
    ]
    smalls = [pltpu.make_async_copy(*pair, small_sems.at[i]) for i, pair in enumerate(pairs)]
    for copy in smalls:
        copy.start()
    pool_copies = [
        pltpu.make_async_copy(pool_any.at[pl.ds(low, 4)], pool_ref.at[pl.ds(low, 4)], pool_sems.at[low // 4])
        for low in range(0, groups, 4)
    ]
    for copy in pool_copies:
        copy.start()
    me = me_ref[0]
    for copy in smalls:
        copy.wait()
    request = assign_ref[me]
    length = length_ref[request]
    for residue in range(groups):
        residue_ref[owner_ref[request, residue]] = residue
    cosine, sine = rotation(table_ref, length)
    for head in range(KV_HEADS):
        low = at["new"] + head * new_count
        info_ref[low : low + new_count] = turn(block_ref[:, column(head)], cosine, sine).astype(jnp.float32)
        low += KV_HEADS * new_count
        info_ref[low : low + new_count] = block_ref[:, column(KV_HEADS + head)].astype(jnp.float32)

    def info_copy(part, low, high):
        part_rows = pl.ds(low, high - low)
        return pltpu.make_async_copy(info_ref.at[part_rows], info_any.at[part_rows], info_sems.at[part])

    info_copy(0, at["new"], rows).start()
    info_ref[at["cos"] : at["cos"] + new_count] = cosine
    info_ref[at["sin"] : at["sin"] + new_count] = sine
    per_row = HEAD_DIM // slots
    row = lax.broadcasted_iota(jnp.int32, (8, HEAD_DIM), 0)
    lane = lax.broadcasted_iota(jnp.int32, (8, HEAD_DIM), 1)
    piece, slot = row * per_row + lane // slots, lane % slots
    holder, requests, residues = jnp.zeros_like(lane), jnp.zeros_like(lane), jnp.zeros_like(lane)
    for p in range(groups):
        other = me ^ order[p]
        holder = jnp.where(piece == p, other, holder)
        requests = jnp.where(lane == p, assign_ref[other], requests)
        residues = jnp.where(lane == p, residue_ref[other], residues)
    bias = jnp.full((8, HEAD_DIM), MASKED, jnp.float32)
    for residue in range(groups):
        live = (holder == stripe_ref[request, residue]) & (slot * groups + residue < length)
        bias = jnp.where(live, 0.0, bias)
    info_ref[at["bias"] : at["bias"] + 8] = bias
    scalars = jnp.where(row == 0, requests, residues)
    info_ref[at["scalars"] : at["scalars"] + 8] = scalars.astype(jnp.float32)
    info_copy(1, 0, at["new"]).start()
    for copy in pool_copies:
        copy.wait()
    sends = []
    for p in range(AHEAD):
        pack_ref[p, :, 0:width] = pool_ref[assign_ref[me ^ order[p]]]
        for lanes in range(quarter):
            pack_ref[p, :, width + lanes * HEAD_DIM : width + (lanes + 1) * HEAD_DIM] = fresh_rows(
                info_ref, at["new"], residue_ref[me ^ order[p]], new_count, count, quarter, lanes
            ).astype(jnp.bfloat16)
        sends.append(pltpu.make_async_copy(pack_ref.at[p], send_refs[p], send_sems.at[p]))
        sends[-1].start()
    for copy in sends:
        copy.wait()
    info_copy(0, at["new"], rows).wait()
    info_copy(1, 0, at["new"]).wait()


def front(order, me, assignment, prefix_len, owner_map, stripe_map, block_kv, table, pool):
    groups, slots, width = pool.shape
    new_count = block_kv.shape[0]
    count = new_count // groups
    block = jax.ShapeDtypeStruct((slots, width + width * count // slots), jnp.bfloat16)
    info = jax.ShapeDtypeStruct((info_rows(new_count)[1], HEAD_DIM), jnp.float32)
    *blocks, info = pl.pallas_call(
        functools.partial(front_kernel, order),
        out_shape=[block] * AHEAD + [info],
        in_specs=[SMEM] + [ANY] * 7,
        out_specs=[ANY] * (AHEAD + 1),
        scratch_shapes=[
            pltpu.SMEM(assignment.shape, jnp.int32),
            pltpu.SMEM(prefix_len.shape, jnp.int32),
            pltpu.SMEM(owner_map.shape, jnp.int32),
            pltpu.SMEM(stripe_map.shape, jnp.int32),
            pltpu.SMEM(assignment.shape, jnp.int32),
            pltpu.VMEM(block_kv.shape, jnp.bfloat16),
            pltpu.VMEM(table.shape, jnp.float32),
            pltpu.VMEM(pool.shape, jnp.bfloat16),
            pltpu.VMEM((AHEAD,) + block.shape, jnp.bfloat16),
            pltpu.VMEM(info.shape, jnp.float32),
            pltpu.SemaphoreType.DMA((6,)),
            pltpu.SemaphoreType.DMA((groups // 4,)),
            pltpu.SemaphoreType.DMA((AHEAD,)),
            pltpu.SemaphoreType.DMA((2,)),
        ],
        compiler_params=params(60),
        name="front",
    )(me, assignment, prefix_len, owner_map, stripe_map, block_kv, table, pool)
    return blocks, info


def pack_kernel(info_ref, pool_ref, *refs):
    groups, slots, width = pool_ref.shape
    targets, (scalar_ref, scalar_sem) = refs[: groups - AHEAD], refs[groups - AHEAD :]
    new_count = slots * groups * (targets[0].shape[1] - width) // width
    at, _ = info_rows(new_count)
    count = new_count // groups
    quarter = (targets[0].shape[1] - width) // HEAD_DIM
    scalar_copy = pltpu.make_async_copy(info_ref.at[pl.ds(at["scalars"], 8)], scalar_ref, scalar_sem)
    scalar_copy.start()
    scalar_copy.wait()
    for p, target in enumerate(targets, AHEAD):
        target[:, 0:width] = pool_ref[scalar_ref[0, p].astype(jnp.int32)]
        residue = scalar_ref[1, p].astype(jnp.int32)
        for lanes in range(quarter):
            target[:, width + lanes * HEAD_DIM : width + (lanes + 1) * HEAD_DIM] = fresh_rows(
                info_ref, at["new"], residue, new_count, count, quarter, lanes
            ).astype(jnp.bfloat16)


def pack_others(info, pool, new_count):
    groups, slots, width = pool.shape
    block = (slots, width + width * (new_count // groups) // slots)
    return pl.pallas_call(
        pack_kernel,
        out_shape=[jax.ShapeDtypeStruct(block, jnp.bfloat16)] * (groups - AHEAD),
        in_specs=[VMEM] * 2,
        out_specs=[VMEM] * (groups - AHEAD),
        scratch_shapes=[pltpu.SMEM((8, HEAD_DIM), jnp.float32), pltpu.SemaphoreType.DMA],
        compiler_params=params(32),
        name="pack_others",
    )(info, pool)


def query_kernel(info_ref, q_ref, rot_ref, own_ref, bias_ref, request_ref):
    new_count = q_ref.shape[0]
    at, _ = info_rows(new_count)
    cosine = info_ref[at["cos"] : at["cos"] + new_count]
    sine = info_ref[at["sin"] : at["sin"] + new_count]
    for row in range(bias_ref.shape[1] // HEAD_DIM):
        line = info_ref[at["bias"] + row : at["bias"] + row + 1]
        bias_ref[:, column(row)] = jnp.broadcast_to(line, (8, HEAD_DIM))
    request_ref[...] = info_ref[at["scalars"] : at["scalars"] + 8].astype(jnp.int32)
    for head in range(2 * KV_HEADS):
        rows = at["new"] + head * new_count
        own_ref[head] = info_ref[rows : rows + new_count].astype(jnp.bfloat16)
    for head in range(Q_HEADS):
        rows = slice((head % PER_KV) * new_count, (head % PER_KV + 1) * new_count)
        rot_ref[head // PER_KV, rows, :] = turn(q_ref[:, column(head)], cosine, sine)


def rotate_queries(info, queries, span):
    new_count = queries.shape[0]
    return pl.pallas_call(
        query_kernel,
        out_shape=(
            jax.ShapeDtypeStruct((KV_HEADS, PER_KV * new_count, HEAD_DIM), jnp.bfloat16),
            jax.ShapeDtypeStruct((2 * KV_HEADS, new_count, HEAD_DIM), jnp.bfloat16),
            jax.ShapeDtypeStruct((8, span), jnp.float32),
            jax.ShapeDtypeStruct((8, HEAD_DIM), jnp.int32),
        ),
        in_specs=[VMEM] * 2,
        out_specs=[VMEM] * 4,
        compiler_params=params(32),
        name="rotate_queries",
    )(info, queries)


def quotient(summed, total):
    about = pl.reciprocal(total, approx=True)
    return summed * (about * (2.0 - total * about))


def join_keys(keys, values, got_refs, own_ref, head):
    key_parts = [got[:, column(head)] for got in got_refs]
    value_parts = [got[:, column(KV_HEADS + head)] for got in got_refs]
    if own_ref is not None:
        key_parts.append(own_ref[head])
        value_parts.append(own_ref[KV_HEADS + head])
    keys[head] = jnp.concatenate(key_parts, axis=0)
    value = jnp.concatenate(value_parts, axis=0)
    values[head] = jnp.concatenate([value, jnp.ones_like(value)], axis=1)


def dot_keys(query, keys):
    return lax.dot_general(query, keys, (((1,), (1,)), ((), ())), preferred_element_type=jnp.float32)


def staged(total, score, weigh, mix, finish, beside=None):
    scores, weights = {0: score(0)}, {}
    for at in range(total + 1):
        if at + 1 < total:
            scores[at + 1] = score(at + 1)
        if at >= 1:
            mixed = mix(at - 1, weights.pop(at - 1))
        if at < total:
            weights[at] = weigh(at, scores.pop(at))
        if at >= 1:
            finish(at - 1, mixed)
        if at == 1 and beside is not None:
            beside()


def unpacking(fresh_refs, first, request_vmem, decode_ref, rows_ref, request_ref, request_sem, decode_sems):
    count = rows_ref.shape[1]
    request_copy = pltpu.make_async_copy(request_vmem, request_ref, request_sem)
    request_copy.start()

    def decode_copy(p):
        return pltpu.make_async_copy(
            rows_ref.at[p], decode_ref.at[request_ref[0, first + p]], decode_sems.at[p]
        )

    def start():
        request_copy.wait()
        for p, fresh_ref in enumerate(fresh_refs):
            stack = fresh_ref[...]
            quarter = stack.shape[1]
            for part in range(stack.shape[0] // count):
                rows_ref[p, :, part * quarter : (part + 1) * quarter] = stack[part * count : (part + 1) * count]
            decode_copy(p).start()

    def wait():
        for p in range(len(fresh_refs)):
            decode_copy(p).wait()

    return start, wait


def spare_part(got):
    return got.at[:, pl.ds(WIDTH, got.shape[1] - WIDTH)]


def pieces_of(refs):
    pieces = []
    for ref in refs:
        pieces += [ref] if len(ref.shape) == 2 else [ref.at[i] for i in range(ref.shape[0])]
    return pieces


def attend_kernel(arrays, unpack, rot_ref, bias_ref, own_ref, *refs):
    got_refs, refs = pieces_of(refs[:arrays]), refs[arrays:]
    start, wait = None, None
    if unpack:
        request_vmem, result_ref, level_ref, decode_ref, *scratch = refs
        start, wait = unpacking([spare_part(got) for got in got_refs], 0, request_vmem, decode_ref, *scratch)
    else:
        result_ref, level_ref = refs
    new_count = rot_ref.shape[1] // PER_KV
    span = len(got_refs) * got_refs[0].shape[0]
    token = lax.broadcasted_iota(jnp.int32, (CHUNK, new_count), 0) % new_count
    causal = jnp.where(lax.broadcasted_iota(jnp.int32, (CHUNK, new_count), 1) <= token, 0.0, MASKED)
    bias = bias_ref[0:1, 0:span]
    per_head = PER_KV * new_count // CHUNK
    keys, values, highs = {}, {}, {}

    def place(at):
        return at // per_head, slice(at % per_head * CHUNK, (at % per_head + 1) * CHUNK)

    def score(at):
        head, rows = place(at)
        if at % per_head == 0:
            join_keys(keys, values, got_refs, own_ref, head)
        return dot_keys(rot_ref[head, rows, :], keys[head])

    def weigh(at, scores):
        scores = jnp.concatenate([scores[:, :span] * SCALE + bias, scores[:, span:] * SCALE + causal], axis=1)
        highs[at] = jnp.max(scores, axis=1, keepdims=True)
        return jnp.exp2(scores - highs[at]).astype(jnp.bfloat16)

    def mix(at, weights):
        return jnp.dot(weights, values[at // per_head], preferred_element_type=jnp.float32)

    def finish(at, mixed):
        head, rows = place(at)
        total = mixed[:, HEAD_DIM:]
        result_ref[head, rows, :] = quotient(mixed[:, :HEAD_DIM], total)
        level_ref[head, rows, :] = highs.pop(at) + jnp.log2(total)

    staged(KV_HEADS * per_head, score, weigh, mix, finish, start)
    if unpack:
        wait()


def attend(rot, bias, own, got, requests=None):
    rows, new_count = rot.shape[1], rot.shape[1] // PER_KV
    operands = [rot, bias, own, *got]
    shapes = [jax.ShapeDtypeStruct((KV_HEADS, rows, HEAD_DIM), jnp.float32)] * 2
    out_specs, scratch = [VMEM] * 2, []
    if requests is not None:
        operands.append(requests)
        slots, width = got[-1].shape
        count = (width - WIDTH) * slots // WIDTH
        shapes.append(jax.ShapeDtypeStruct((new_count // count, count, WIDTH), jnp.bfloat16))
        out_specs.append(ANY)
        scratch = unpack_scratch(len(pieces_of(got)), count, requests)
    return pl.pallas_call(
        functools.partial(attend_kernel, len(got), requests is not None),
        out_shape=tuple(shapes),
        in_specs=[VMEM] * len(operands),
        out_specs=tuple(out_specs),
        scratch_shapes=scratch,
        compiler_params=params(32),
        name="attend",
    )(*operands)


def unpack_scratch(pieces, count, requests):
    return [
        pltpu.VMEM((pieces, count, WIDTH), jnp.bfloat16),
        pltpu.SMEM(requests.shape, jnp.int32),
        pltpu.SemaphoreType.DMA,
        pltpu.SemaphoreType.DMA((pieces,)),
    ]


HEADROOM = 96.0


def late_kernel(pieces, first, rot_ref, bias_ref, result_ref, level_ref, *refs):
    got_refs, refs = refs[:pieces], refs[pieces:]
    request_vmem, _, out_ref, decode_ref, done_ref, out_sems, *scratch = refs
    start, wait = unpacking([spare_part(got) for got in got_refs], first, request_vmem, decode_ref, *scratch)
    slots = got_refs[0].shape[0]
    new_count = out_ref.shape[0]
    size = LATE_CHUNK
    heads_in = size // new_count
    bias = bias_ref[0:1, first * slots : (first + pieces) * slots]
    per_head = PER_KV * new_count // size
    chunks = KV_HEADS * per_head
    keys, values, excess = {}, {}, []

    def place(at):
        return at // per_head, slice(at % per_head * size, (at % per_head + 1) * size)

    def out_copy(at):
        width = heads_in * HEAD_DIM
        return pltpu.make_async_copy(
            done_ref.at[at], out_ref.at[:, pl.ds(pl.multiple_of(at * width, width), width)], out_sems.at[at]
        )

    def store(at, result):
        for row in range(heads_in):
            done_ref[at, :, column(row)] = result[row * new_count : (row + 1) * new_count].astype(jnp.bfloat16)
        out_copy(at).start()

    def score(at):
        head, rows = place(at)
        if at % per_head == 0:
            join_keys(keys, values, got_refs, None, head)
        return dot_keys(rot_ref[head, rows, :], keys[head])

    def weigh(at, scores):
        head, rows = place(at)
        powers = scores * SCALE + bias - level_ref[head, rows, :]
        excess.append(jnp.max(powers.reshape(size // 8, 8, HEAD_DIM), axis=0))
        return jnp.exp2(powers).astype(jnp.bfloat16)

    def mix(at, weights):
        return jnp.dot(weights, values[at // per_head], preferred_element_type=jnp.float32)

    def finish(at, mixed):
        head, rows = place(at)
        store(at, quotient(result_ref[head, rows, :] + mixed[:, :HEAD_DIM], 1.0 + mixed[:, HEAD_DIM:]))

    staged(chunks, score, weigh, mix, finish, start)
    most = jnp.max(functools.reduce(jnp.maximum, excess))
    wait()
    for at in range(chunks):
        out_copy(at).wait()

    @pl.when(most > HEADROOM)
    def _():
        for head in range(KV_HEADS):

            def again(chunk, carry, head=head):
                rows = pl.ds(pl.multiple_of(chunk * size, size), size)
                scores = dot_keys(rot_ref[head, rows, :], keys[head]) * SCALE + bias
                level = level_ref[head, rows, :]
                high = jnp.maximum(level, jnp.max(scores, axis=1, keepdims=True))
                factor = jnp.exp2(level - high)
                weights = jnp.exp2(scores - high).astype(jnp.bfloat16)
                mixed = jnp.dot(weights, values[head], preferred_element_type=jnp.float32)
                at = head * per_head + chunk
                summed = result_ref[head, rows, :] * factor + mixed[:, :HEAD_DIM]
                store(at, quotient(summed, factor + mixed[:, HEAD_DIM:]))
                out_copy(at).wait()
                return carry

            lax.fori_loop(0, per_head, again, 0)


def attend_late(rot, bias, result, level, got, first, requests, decode):
    rows, new_count = rot.shape[1], rot.shape[1] // PER_KV
    operands = [rot, bias, result, level, *got, requests, decode]
    chunks = KV_HEADS * rows // LATE_CHUNK
    return pl.pallas_call(
        functools.partial(late_kernel, len(got), first),
        out_shape=(
            jax.ShapeDtypeStruct((new_count, Q_HEADS * HEAD_DIM), jnp.bfloat16),
            jax.ShapeDtypeStruct(decode.shape, jnp.bfloat16),
        ),
        in_specs=[VMEM] * (len(operands) - 1) + [ANY],
        out_specs=(ANY, ANY),
        scratch_shapes=[
            pltpu.VMEM((chunks, new_count, LATE_CHUNK // new_count * HEAD_DIM), jnp.bfloat16),
            pltpu.SemaphoreType.DMA((chunks,)),
        ]
        + unpack_scratch(len(got), decode.shape[1], requests),
        input_output_aliases={len(operands) - 1: 1},
        compiler_params=params(32),
        name="attend_late",
    )(*operands)


def inverse(table):
    places = jnp.arange(table.shape[0], dtype=jnp.int32)
    return jnp.sum(jnp.where(table[None, :] == places[:, None], places, 0), axis=1)


def rotate(rows, positions, heads):
    half = HEAD_DIM // 2
    freqs = ROPE_BASE ** (-jnp.arange(half, dtype=jnp.float32) / half)
    angles = positions.astype(jnp.float32)[:, None] * freqs[None, :]
    cosine = jnp.concatenate([jnp.cos(angles)] * 2, axis=-1)[:, None, :]
    sine = jnp.concatenate([-jnp.sin(angles), jnp.sin(angles)], axis=-1)[:, None, :]
    split = rows.astype(jnp.float32).reshape(rows.shape[0], heads, HEAD_DIM)
    turned = jnp.roll(split, half, axis=-1)
    return (split * cosine + turned * sine).astype(jnp.bfloat16)


def small_pieces(me, assignment, prefix_len, stripe_map, owner_map, queries, block_kv, pool):
    groups, slots, width = pool.shape
    new_count = block_kv.shape[0]
    count = new_count // groups
    request = assignment[me[0]]
    length = prefix_len[request]
    positions = length + jnp.arange(new_count, dtype=jnp.int32)
    rot = rotate(queries, positions, Q_HEADS).reshape(new_count, KV_HEADS, PER_KV, HEAD_DIM)
    rot = jnp.transpose(rot, (1, 2, 0, 3)).reshape(KV_HEADS, PER_KV * new_count, HEAD_DIM)
    new_keys = rotate(block_kv[:, :KV_WIDTH], positions, KV_HEADS).reshape(new_count, KV_WIDTH)
    new_kv = jnp.concatenate([new_keys, block_kv[:, KV_WIDTH:]], axis=1)
    own = jnp.transpose(new_kv.reshape(new_count, 2 * KV_HEADS, HEAD_DIM), (1, 0, 2))
    spread = jnp.transpose(new_kv.reshape(count, groups, width), (1, 0, 2))
    send = jnp.concatenate([pool[assignment], spread[inverse(owner_map[request])]], axis=1)
    got = lax.all_to_all(send, "pg", split_axis=0, concat_axis=0, tiled=True)
    located = jnp.arange(slots, dtype=jnp.int32)[None, :] * groups + inverse(stripe_map[request])[:, None]
    bias = jnp.where(located < length, 0.0, MASKED).astype(jnp.float32).reshape(1, groups * slots)
    keys = got[:, :slots].reshape(groups * slots, width)
    result, _ = attend(rot, jnp.broadcast_to(bias, (8, groups * slots)), own, [keys])
    result = result.astype(jnp.bfloat16).reshape(KV_HEADS, PER_KV, new_count, HEAD_DIM)
    attended = jnp.transpose(result, (2, 0, 1, 3)).reshape(new_count, Q_HEADS * HEAD_DIM)
    return attended, got[inverse(assignment), slots:]


def shards(queries, block_kv, pool_kv, prefix_len, assignment, stripe_map, owner_map):
    queries, block_kv, pool = queries[0], block_kv[0], pool_kv[0]
    groups, slots, width = pool.shape
    new_count = queries.shape[0]
    count = new_count // groups
    me = lax.axis_index("pg").astype(jnp.int32).reshape(1)
    if groups != 16 or slots % 16 or HEAD_DIM % slots or count % 8 or slots % count:
        attended, decode_kv = small_pieces(
            me, assignment, prefix_len, stripe_map, owner_map, queries, block_kv, pool
        )
        return (attended[None], decode_kv[None])
    order = order_of(groups)
    table = rotation_tables(new_count)
    blocks, info = front(order, me, assignment, prefix_len, owner_map, stripe_map, block_kv, table, pool)
    blocks = list(blocks) + list(pack_others(info, pool, new_count))
    rot, own, bias, requests = rotate_queries(info, queries, groups * slots)
    rot, *blocks[AHEAD_OF_QUERIES:] = lax.optimization_barrier((rot, *blocks[AHEAD_OF_QUERIES:]))
    got = [
        lax.ppermute(block, "pg", [(source, source ^ t) for source in range(groups)]) if t else block
        for block, t in zip(blocks, order)
    ]
    soon = groups - LATE
    result, level, decode_kv = attend(rot, bias, own, got[:soon], requests)
    attended, decode_kv = attend_late(rot, bias, result, level, got[soon:], soon, requests, decode_kv)
    return (attended[None], decode_kv[None])


def solution(mesh):
    return jax.shard_map(
        shards,
        mesh=mesh,
        in_specs=(
            P(("rep", "pg"), None, None),
            P(("rep", "pg"), None, None),
            P(("rep", "pg"), None, None, None),
            P("rep"),
            P("rep"),
            P("rep", None),
            P("rep", None),
        ),
        out_specs=(P(("rep", "pg"), None, None), P(("rep", "pg"), None, None, None)),
        check_vma=False,
    )
```

```python
import functools
import math

import jax
import jax.numpy as jnp
import numpy as np
from jax import lax
from jax.experimental import pallas as pl
from jax.experimental.pallas import tpu as pltpu
from jax.sharding import PartitionSpec as P

Q_HEADS = 32
KV_HEADS = 4
HEAD_DIM = 128
PER_KV = Q_HEADS // KV_HEADS
KV_WIDTH = KV_HEADS * HEAD_DIM
WIDTH = 2 * KV_WIDTH

ROPE_BASE = 1000000.0
MASKED = -1e30
SCALE = HEAD_DIM ** -0.5 / math.log(2.0)
CHUNK = 256
LATE = 4
LATE_CHUNK = 512
AHEAD = 4
AHEAD_OF_QUERIES = 8

SMEM = pl.BlockSpec(memory_space=pltpu.SMEM)
VMEM = pl.BlockSpec(memory_space=pltpu.VMEM)
ANY = pl.BlockSpec(memory_space=pl.ANY)


def params(mib):
    return pltpu.CompilerParams(vmem_limit_bytes=mib * 1024 * 1024)


def column(head):
    return slice(head * HEAD_DIM, (head + 1) * HEAD_DIM)


def order_of(groups):
    half = groups // 2
    near = list(range(half - 1, 0, -1))
    quarter, eighth = half // 2, half // 4
    far = [half + (at // 2 if at % 2 == 0 else quarter + (at // 2 ^ eighth)) for at in range(half)]
    order = [(far if kind == "f" else near).pop(0) for kind in "ffnfnfnfnnffnfn"]
    order.insert(groups - LATE - 1, 0)
    return order


def rotation_tables(rows):
    half = HEAD_DIM // 2
    freqs = np.tile(ROPE_BASE ** (-np.arange(half, dtype=np.float64) / half), 2)
    angles = np.arange(rows, dtype=np.float64)[:, None] * freqs[None, :]
    parts = [np.cos(angles), np.sin(angles), np.tile(freqs, (8, 1))]
    return jnp.asarray(np.concatenate(parts, axis=0).astype(np.float32))


def rotation(table_ref, length):
    rows = (table_ref.shape[0] - 8) // 2
    start = length.astype(jnp.float32) * table_ref[2 * rows : 2 * rows + 8, :]
    cos_start, sin_start = jnp.cos(start)[0:1], jnp.sin(start)[0:1]
    cos_row, sin_row = table_ref[0:rows, :], table_ref[rows : 2 * rows, :]
    lane = lax.broadcasted_iota(jnp.int32, (1, HEAD_DIM), 1)
    sign = jnp.where(lane < HEAD_DIM // 2, -1.0, 1.0)
    cosine = cos_row * cos_start - sin_row * sin_start
    return cosine, sin_row * (cos_start * sign) + cos_row * (sin_start * sign)


def turn(x, cosine, sine):
    x = x.astype(jnp.float32)
    return (x * cosine + pltpu.roll(x, HEAD_DIM // 2, 1) * sine).astype(jnp.bfloat16)


def info_rows(new_count):
    sizes = [("cos", new_count), ("sin", new_count), ("bias", 8), ("scalars", 8), ("new", 2 * KV_HEADS * new_count)]
    at, rows = 0, {}
    for name, size in sizes:
        rows[name] = at
        at += size
    return rows, at


def fresh_rows(info_ref, base, residue, new_count, count, quarter, lanes):
    groups = new_count // count
    stack = [
        info_ref[pl.ds(base + (head + lanes) * new_count + residue, count, stride=groups), :]
        for head in range(0, 2 * KV_HEADS, quarter)
    ]
    return jnp.concatenate(stack, axis=0)


def front_kernel(
    order, me_ref, assign_any, length_any, owner_any, stripe_any, block_any, table_any, pool_any, *refs
):
    groups, slots, width = pool_any.shape
    send_refs, info_any, refs = refs[:AHEAD], refs[AHEAD], refs[AHEAD + 1 :]
    (assign_ref, length_ref, owner_ref, stripe_ref, residue_ref, block_ref, table_ref, pool_ref, pack_ref, info_ref,
     small_sems, pool_sems, send_sems, info_sems) = refs
    new_count = block_any.shape[0]
    count = new_count // groups
    quarter = width * count // slots // HEAD_DIM
    at, rows = info_rows(new_count)
    pairs = [
        (assign_any, assign_ref), (length_any, length_ref), (owner_any, owner_ref), (stripe_any, stripe_ref),
        (block_any, block_ref), (table_any, table_ref),
    ]
    smalls = [pltpu.make_async_copy(*pair, small_sems.at[i]) for i, pair in enumerate(pairs)]
    for copy in smalls:
        copy.start()
    pool_copies = [
        pltpu.make_async_copy(pool_any.at[pl.ds(low, 4)], pool_ref.at[pl.ds(low, 4)], pool_sems.at[low // 4])
        for low in range(0, groups, 4)
    ]
    for copy in pool_copies:
        copy.start()
    me = me_ref[0]
    for copy in smalls:
        copy.wait()
    request = assign_ref[me]
    length = length_ref[request]
    for residue in range(groups):
        residue_ref[owner_ref[request, residue]] = residue
    cosine, sine = rotation(table_ref, length)
    for head in range(KV_HEADS):
        low = at["new"] + head * new_count
        info_ref[low : low + new_count] = turn(block_ref[:, column(head)], cosine, sine).astype(jnp.float32)
        low += KV_HEADS * new_count
        info_ref[low : low + new_count] = block_ref[:, column(KV_HEADS + head)].astype(jnp.float32)

    def info_copy(part, low, high):
        part_rows = pl.ds(low, high - low)
        return pltpu.make_async_copy(info_ref.at[part_rows], info_any.at[part_rows], info_sems.at[part])

    info_copy(0, at["new"], rows).start()
    info_ref[at["cos"] : at["cos"] + new_count] = cosine
    info_ref[at["sin"] : at["sin"] + new_count] = sine
    per_row = HEAD_DIM // slots
    row = lax.broadcasted_iota(jnp.int32, (8, HEAD_DIM), 0)
    lane = lax.broadcasted_iota(jnp.int32, (8, HEAD_DIM), 1)
    piece, slot = row * per_row + lane // slots, lane % slots
    holder, requests, residues = jnp.zeros_like(lane), jnp.zeros_like(lane), jnp.zeros_like(lane)
    for p in range(groups):
        other = me ^ order[p]
        holder = jnp.where(piece == p, other, holder)
        requests = jnp.where(lane == p, assign_ref[other], requests)
        residues = jnp.where(lane == p, residue_ref[other], residues)
    bias = jnp.full((8, HEAD_DIM), MASKED, jnp.float32)
    for residue in range(groups):
        live = (holder == stripe_ref[request, residue]) & (slot * groups + residue < length)
        bias = jnp.where(live, 0.0, bias)
    info_ref[at["bias"] : at["bias"] + 8] = bias
    scalars = jnp.where(row == 0, requests, residues)
    info_ref[at["scalars"] : at["scalars"] + 8] = scalars.astype(jnp.float32)
    info_copy(1, 0, at["new"]).start()
    for copy in pool_copies:
        copy.wait()
    sends = []
    for p in range(AHEAD):
        pack_ref[p, :, 0:width] = pool_ref[assign_ref[me ^ order[p]]]
        for lanes in range(quarter):
            pack_ref[p, :, width + lanes * HEAD_DIM : width + (lanes + 1) * HEAD_DIM] = fresh_rows(
                info_ref, at["new"], residue_ref[me ^ order[p]], new_count, count, quarter, lanes
            ).astype(jnp.bfloat16)
        sends.append(pltpu.make_async_copy(pack_ref.at[p], send_refs[p], send_sems.at[p]))
        sends[-1].start()
    for copy in sends:
        copy.wait()
    info_copy(0, at["new"], rows).wait()
    info_copy(1, 0, at["new"]).wait()


def front(order, me, assignment, prefix_len, owner_map, stripe_map, block_kv, table, pool):
    groups, slots, width = pool.shape
    new_count = block_kv.shape[0]
    count = new_count // groups
    block = jax.ShapeDtypeStruct((slots, width + width * count // slots), jnp.bfloat16)
    info = jax.ShapeDtypeStruct((info_rows(new_count)[1], HEAD_DIM), jnp.float32)
    *blocks, info = pl.pallas_call(
        functools.partial(front_kernel, order),
        out_shape=[block] * AHEAD + [info],
        in_specs=[SMEM] + [ANY] * 7,
        out_specs=[ANY] * (AHEAD + 1),
        scratch_shapes=[
            pltpu.SMEM(assignment.shape, jnp.int32),
            pltpu.SMEM(prefix_len.shape, jnp.int32),
            pltpu.SMEM(owner_map.shape, jnp.int32),
            pltpu.SMEM(stripe_map.shape, jnp.int32),
            pltpu.SMEM(assignment.shape, jnp.int32),
            pltpu.VMEM(block_kv.shape, jnp.bfloat16),
            pltpu.VMEM(table.shape, jnp.float32),
            pltpu.VMEM(pool.shape, jnp.bfloat16),
            pltpu.VMEM((AHEAD,) + block.shape, jnp.bfloat16),
            pltpu.VMEM(info.shape, jnp.float32),
            pltpu.SemaphoreType.DMA((6,)),
            pltpu.SemaphoreType.DMA((groups // 4,)),
            pltpu.SemaphoreType.DMA((AHEAD,)),
            pltpu.SemaphoreType.DMA((2,)),
        ],
        compiler_params=params(60),
        name="front",
    )(me, assignment, prefix_len, owner_map, stripe_map, block_kv, table, pool)
    return blocks, info


def pack_kernel(info_ref, pool_ref, *refs):
    groups, slots, width = pool_ref.shape
    targets, (scalar_ref, scalar_sem) = refs[: groups - AHEAD], refs[groups - AHEAD :]
    new_count = slots * groups * (targets[0].shape[1] - width) // width
    at, _ = info_rows(new_count)
    count = new_count // groups
    quarter = (targets[0].shape[1] - width) // HEAD_DIM
    scalar_copy = pltpu.make_async_copy(info_ref.at[pl.ds(at["scalars"], 8)], scalar_ref, scalar_sem)
    scalar_copy.start()
    scalar_copy.wait()
    for p, target in enumerate(targets, AHEAD):
        target[:, 0:width] = pool_ref[scalar_ref[0, p].astype(jnp.int32)]
        residue = scalar_ref[1, p].astype(jnp.int32)
        for lanes in range(quarter):
            target[:, width + lanes * HEAD_DIM : width + (lanes + 1) * HEAD_DIM] = fresh_rows(
                info_ref, at["new"], residue, new_count, count, quarter, lanes
            ).astype(jnp.bfloat16)


def pack_others(info, pool, new_count):
    groups, slots, width = pool.shape
    block = (slots, width + width * (new_count // groups) // slots)
    return pl.pallas_call(
        pack_kernel,
        out_shape=[jax.ShapeDtypeStruct(block, jnp.bfloat16)] * (groups - AHEAD),
        in_specs=[VMEM] * 2,
        out_specs=[VMEM] * (groups - AHEAD),
        scratch_shapes=[pltpu.SMEM((8, HEAD_DIM), jnp.float32), pltpu.SemaphoreType.DMA],
        compiler_params=params(32),
        name="pack_others",
    )(info, pool)


def query_kernel(info_ref, q_ref, rot_ref, own_ref, bias_ref, request_ref):
    new_count = q_ref.shape[0]
    at, _ = info_rows(new_count)
    cosine = info_ref[at["cos"] : at["cos"] + new_count]
    sine = info_ref[at["sin"] : at["sin"] + new_count]
    for row in range(bias_ref.shape[1] // HEAD_DIM):
        line = info_ref[at["bias"] + row : at["bias"] + row + 1]
        bias_ref[:, column(row)] = jnp.broadcast_to(line, (8, HEAD_DIM))
    request_ref[...] = info_ref[at["scalars"] : at["scalars"] + 8].astype(jnp.int32)
    for head in range(2 * KV_HEADS):
        rows = at["new"] + head * new_count
        own_ref[head] = info_ref[rows : rows + new_count].astype(jnp.bfloat16)
    for head in range(Q_HEADS):
        rows = slice((head % PER_KV) * new_count, (head % PER_KV + 1) * new_count)
        rot_ref[head // PER_KV, rows, :] = turn(q_ref[:, column(head)], cosine, sine)


def rotate_queries(info, queries, span):
    new_count = queries.shape[0]
    return pl.pallas_call(
        query_kernel,
        out_shape=(
            jax.ShapeDtypeStruct((KV_HEADS, PER_KV * new_count, HEAD_DIM), jnp.bfloat16),
            jax.ShapeDtypeStruct((2 * KV_HEADS, new_count, HEAD_DIM), jnp.bfloat16),
            jax.ShapeDtypeStruct((8, span), jnp.float32),
            jax.ShapeDtypeStruct((8, HEAD_DIM), jnp.int32),
        ),
        in_specs=[VMEM] * 2,
        out_specs=[VMEM] * 4,
        compiler_params=params(32),
        name="rotate_queries",
    )(info, queries)


def quotient(summed, total):
    about = pl.reciprocal(total, approx=True)
    return summed * (about * (2.0 - total * about))


def join_keys(keys, values, got_refs, own_ref, head):
    key_parts = [got[:, column(head)] for got in got_refs]
    value_parts = [got[:, column(KV_HEADS + head)] for got in got_refs]
    if own_ref is not None:
        key_parts.append(own_ref[head])
        value_parts.append(own_ref[KV_HEADS + head])
    keys[head] = jnp.concatenate(key_parts, axis=0)
    value = jnp.concatenate(value_parts, axis=0)
    values[head] = jnp.concatenate([value, jnp.ones_like(value)], axis=1)


def dot_keys(query, keys):
    return lax.dot_general(query, keys, (((1,), (1,)), ((), ())), preferred_element_type=jnp.float32)


def staged(total, score, weigh, mix, finish, beside=None):
    scores, weights = {0: score(0)}, {}
    for at in range(total + 1):
        if at + 1 < total:
            scores[at + 1] = score(at + 1)
        if at >= 1:
            mixed = mix(at - 1, weights.pop(at - 1))
        if at < total:
            weights[at] = weigh(at, scores.pop(at))
        if at >= 1:
            finish(at - 1, mixed)
        if at == 1 and beside is not None:
            beside()


def unpacking(fresh_refs, first, request_vmem, decode_ref, rows_ref, request_ref, request_sem, decode_sems):
    count = rows_ref.shape[1]
    request_copy = pltpu.make_async_copy(request_vmem, request_ref, request_sem)
    request_copy.start()

    def decode_copy(p):
        return pltpu.make_async_copy(
            rows_ref.at[p], decode_ref.at[request_ref[0, first + p]], decode_sems.at[p]
        )

    def start():
        request_copy.wait()
        for p, fresh_ref in enumerate(fresh_refs):
            stack = fresh_ref[...]
            quarter = stack.shape[1]
            for part in range(stack.shape[0] // count):
                rows_ref[p, :, part * quarter : (part + 1) * quarter] = stack[part * count : (part + 1) * count]
            decode_copy(p).start()

    def wait():
        for p in range(len(fresh_refs)):
            decode_copy(p).wait()

    return start, wait


def spare_part(got):
    return got.at[:, pl.ds(WIDTH, got.shape[1] - WIDTH)]


def pieces_of(refs):
    pieces = []
    for ref in refs:
        pieces += [ref] if len(ref.shape) == 2 else [ref.at[i] for i in range(ref.shape[0])]
    return pieces


def attend_kernel(arrays, unpack, rot_ref, bias_ref, own_ref, *refs):
    got_refs, refs = pieces_of(refs[:arrays]), refs[arrays:]
    start, wait = None, None
    if unpack:
        request_vmem, result_ref, level_ref, decode_ref, *scratch = refs
        start, wait = unpacking([spare_part(got) for got in got_refs], 0, request_vmem, decode_ref, *scratch)
    else:
        result_ref, level_ref = refs
    new_count = rot_ref.shape[1] // PER_KV
    span = len(got_refs) * got_refs[0].shape[0]
    token = lax.broadcasted_iota(jnp.int32, (CHUNK, new_count), 0) % new_count
    causal = jnp.where(lax.broadcasted_iota(jnp.int32, (CHUNK, new_count), 1) <= token, 0.0, MASKED)
    bias = bias_ref[0:1, 0:span]
    per_head = PER_KV * new_count // CHUNK
    keys, values, highs = {}, {}, {}

    def place(at):
        return at // per_head, slice(at % per_head * CHUNK, (at % per_head + 1) * CHUNK)

    def score(at):
        head, rows = place(at)
        if at % per_head == 0:
            join_keys(keys, values, got_refs, own_ref, head)
        return dot_keys(rot_ref[head, rows, :], keys[head])

    def weigh(at, scores):
        scores = jnp.concatenate([scores[:, :span] * SCALE + bias, scores[:, span:] * SCALE + causal], axis=1)
        highs[at] = jnp.max(scores, axis=1, keepdims=True)
        return jnp.exp2(scores - highs[at]).astype(jnp.bfloat16)

    def mix(at, weights):
        return jnp.dot(weights, values[at // per_head], preferred_element_type=jnp.float32)

    def finish(at, mixed):
        head, rows = place(at)
        total = mixed[:, HEAD_DIM:]
        result_ref[head, rows, :] = quotient(mixed[:, :HEAD_DIM], total)
        level_ref[head, rows, :] = highs.pop(at) + jnp.log2(total)

    staged(KV_HEADS * per_head, score, weigh, mix, finish, start)
    if unpack:
        wait()


def attend(rot, bias, own, got, requests=None):
    rows, new_count = rot.shape[1], rot.shape[1] // PER_KV
    operands = [rot, bias, own, *got]
    shapes = [jax.ShapeDtypeStruct((KV_HEADS, rows, HEAD_DIM), jnp.float32)] * 2
    out_specs, scratch = [VMEM] * 2, []
    if requests is not None:
        operands.append(requests)
        slots, width = got[-1].shape
        count = (width - WIDTH) * slots // WIDTH
        shapes.append(jax.ShapeDtypeStruct((new_count // count, count, WIDTH), jnp.bfloat16))
        out_specs.append(ANY)
        scratch = unpack_scratch(len(pieces_of(got)), count, requests)
    return pl.pallas_call(
        functools.partial(attend_kernel, len(got), requests is not None),
        out_shape=tuple(shapes),
        in_specs=[VMEM] * len(operands),
        out_specs=tuple(out_specs),
        scratch_shapes=scratch,
        compiler_params=params(32),
        name="attend",
    )(*operands)


def unpack_scratch(pieces, count, requests):
    return [
        pltpu.VMEM((pieces, count, WIDTH), jnp.bfloat16),
        pltpu.SMEM(requests.shape, jnp.int32),
        pltpu.SemaphoreType.DMA,
        pltpu.SemaphoreType.DMA((pieces,)),
    ]


HEADROOM = 96.0


def late_kernel(pieces, first, rot_ref, bias_ref, result_ref, level_ref, *refs):
    got_refs, refs = refs[:pieces], refs[pieces:]
    request_vmem, _, out_ref, decode_ref, done_ref, out_sems, *scratch = refs
    start, wait = unpacking([spare_part(got) for got in got_refs], first, request_vmem, decode_ref, *scratch)
    slots = got_refs[0].shape[0]
    new_count = out_ref.shape[0]
    size = LATE_CHUNK
    heads_in = size // new_count
    bias = bias_ref[0:1, first * slots : (first + pieces) * slots]
    per_head = PER_KV * new_count // size
    chunks = KV_HEADS * per_head
    keys, values, excess = {}, {}, []

    def place(at):
        return at // per_head, slice(at % per_head * size, (at % per_head + 1) * size)

    def out_copy(at):
        width = heads_in * HEAD_DIM
        return pltpu.make_async_copy(
            done_ref.at[at], out_ref.at[:, pl.ds(pl.multiple_of(at * width, width), width)], out_sems.at[at]
        )

    def store(at, result):
        for row in range(heads_in):
            done_ref[at, :, column(row)] = result[row * new_count : (row + 1) * new_count].astype(jnp.bfloat16)
        out_copy(at).start()

    def score(at):
        head, rows = place(at)
        if at % per_head == 0:
            join_keys(keys, values, got_refs, None, head)
        return dot_keys(rot_ref[head, rows, :], keys[head])

    def weigh(at, scores):
        head, rows = place(at)
        powers = scores * SCALE + bias - level_ref[head, rows, :]
        excess.append(jnp.max(powers.reshape(size // 8, 8, HEAD_DIM), axis=0))
        return jnp.exp2(powers).astype(jnp.bfloat16)

    def mix(at, weights):
        return jnp.dot(weights, values[at // per_head], preferred_element_type=jnp.float32)

    def finish(at, mixed):
        head, rows = place(at)
        store(at, quotient(result_ref[head, rows, :] + mixed[:, :HEAD_DIM], 1.0 + mixed[:, HEAD_DIM:]))

    staged(chunks, score, weigh, mix, finish, start)
    most = jnp.max(functools.reduce(jnp.maximum, excess))
    wait()
    for at in range(chunks):
        out_copy(at).wait()

    @pl.when(most > HEADROOM)
    def _():
        for head in range(KV_HEADS):

            def again(chunk, carry, head=head):
                rows = pl.ds(pl.multiple_of(chunk * size, size), size)
                scores = dot_keys(rot_ref[head, rows, :], keys[head]) * SCALE + bias
                level = level_ref[head, rows, :]
                high = jnp.maximum(level, jnp.max(scores, axis=1, keepdims=True))
                factor = jnp.exp2(level - high)
                weights = jnp.exp2(scores - high).astype(jnp.bfloat16)
                mixed = jnp.dot(weights, values[head], preferred_element_type=jnp.float32)
                at = head * per_head + chunk
                summed = result_ref[head, rows, :] * factor + mixed[:, :HEAD_DIM]
                store(at, quotient(summed, factor + mixed[:, HEAD_DIM:]))
                out_copy(at).wait()
                return carry

            lax.fori_loop(0, per_head, again, 0)


def attend_late(rot, bias, result, level, got, first, requests, decode):
    rows, new_count = rot.shape[1], rot.shape[1] // PER_KV
    operands = [rot, bias, result, level, *got, requests, decode]
    chunks = KV_HEADS * rows // LATE_CHUNK
    return pl.pallas_call(
        functools.partial(late_kernel, len(got), first),
        out_shape=(
            jax.ShapeDtypeStruct((new_count, Q_HEADS * HEAD_DIM), jnp.bfloat16),
            jax.ShapeDtypeStruct(decode.shape, jnp.bfloat16),
        ),
        in_specs=[VMEM] * (len(operands) - 1) + [ANY],
        out_specs=(ANY, ANY),
        scratch_shapes=[
            pltpu.VMEM((chunks, new_count, LATE_CHUNK // new_count * HEAD_DIM), jnp.bfloat16),
            pltpu.SemaphoreType.DMA((chunks,)),
        ]
        + unpack_scratch(len(got), decode.shape[1], requests),
        input_output_aliases={len(operands) - 1: 1},
        compiler_params=params(32),
        name="attend_late",
    )(*operands)


def inverse(table):
    places = jnp.arange(table.shape[0], dtype=jnp.int32)
    return jnp.sum(jnp.where(table[None, :] == places[:, None], places, 0), axis=1)


def rotate(rows, positions, heads):
    half = HEAD_DIM // 2
    freqs = ROPE_BASE ** (-jnp.arange(half, dtype=jnp.float32) / half)
    angles = positions.astype(jnp.float32)[:, None] * freqs[None, :]
    cosine = jnp.concatenate([jnp.cos(angles)] * 2, axis=-1)[:, None, :]
    sine = jnp.concatenate([-jnp.sin(angles), jnp.sin(angles)], axis=-1)[:, None, :]
    split = rows.astype(jnp.float32).reshape(rows.shape[0], heads, HEAD_DIM)
    turned = jnp.roll(split, half, axis=-1)
    return (split * cosine + turned * sine).astype(jnp.bfloat16)


def small_pieces(me, assignment, prefix_len, stripe_map, owner_map, queries, block_kv, pool):
    groups, slots, width = pool.shape
    new_count = block_kv.shape[0]
    count = new_count // groups
    request = assignment[me[0]]
    length = prefix_len[request]
    positions = length + jnp.arange(new_count, dtype=jnp.int32)
    rot = rotate(queries, positions, Q_HEADS).reshape(new_count, KV_HEADS, PER_KV, HEAD_DIM)
    rot = jnp.transpose(rot, (1, 2, 0, 3)).reshape(KV_HEADS, PER_KV * new_count, HEAD_DIM)
    new_keys = rotate(block_kv[:, :KV_WIDTH], positions, KV_HEADS).reshape(new_count, KV_WIDTH)
    new_kv = jnp.concatenate([new_keys, block_kv[:, KV_WIDTH:]], axis=1)
    own = jnp.transpose(new_kv.reshape(new_count, 2 * KV_HEADS, HEAD_DIM), (1, 0, 2))
    spread = jnp.transpose(new_kv.reshape(count, groups, width), (1, 0, 2))
    send = jnp.concatenate([pool[assignment], spread[inverse(owner_map[request])]], axis=1)
    got = lax.all_to_all(send, "pg", split_axis=0, concat_axis=0, tiled=True)
    located = jnp.arange(slots, dtype=jnp.int32)[None, :] * groups + inverse(stripe_map[request])[:, None]
    bias = jnp.where(located < length, 0.0, MASKED).astype(jnp.float32).reshape(1, groups * slots)
    keys = got[:, :slots].reshape(groups * slots, width)
    result, _ = attend(rot, jnp.broadcast_to(bias, (8, groups * slots)), own, [keys])
    result = result.astype(jnp.bfloat16).reshape(KV_HEADS, PER_KV, new_count, HEAD_DIM)
    attended = jnp.transpose(result, (2, 0, 1, 3)).reshape(new_count, Q_HEADS * HEAD_DIM)
    return attended, got[inverse(assignment), slots:]


def shards(queries, block_kv, pool_kv, prefix_len, assignment, stripe_map, owner_map):
    queries, block_kv, pool = queries[0], block_kv[0], pool_kv[0]
    groups, slots, width = pool.shape
    new_count = queries.shape[0]
    count = new_count // groups
    me = lax.axis_index("pg").astype(jnp.int32).reshape(1)
    if groups != 16 or slots % 16 or HEAD_DIM % slots or count % 8 or slots % count:
        attended, decode_kv = small_pieces(
            me, assignment, prefix_len, stripe_map, owner_map, queries, block_kv, pool
        )
        return (attended[None], decode_kv[None])
    order = order_of(groups)
    table = rotation_tables(new_count)
    blocks, info = front(order, me, assignment, prefix_len, owner_map, stripe_map, block_kv, table, pool)
    blocks = list(blocks) + list(pack_others(info, pool, new_count))
    rot, own, bias, requests = rotate_queries(info, queries, groups * slots)
    rot, *blocks[AHEAD_OF_QUERIES:] = lax.optimization_barrier((rot, *blocks[AHEAD_OF_QUERIES:]))
    got = [
        lax.ppermute(block, "pg", [(source, source ^ t) for source in range(groups)]) if t else block
        for block, t in zip(blocks, order)
    ]
    soon = groups - LATE
    result, level, decode_kv = attend(rot, bias, own, got[:soon], requests)
    attended, decode_kv = attend_late(rot, bias, result, level, got[soon:], soon, requests, decode_kv)
    return (attended[None], decode_kv[None])


def solution(mesh):
    return jax.shard_map(
        shards,
        mesh=mesh,
        in_specs=(
            P(("rep", "pg"), None, None),
            P(("rep", "pg"), None, None),
            P(("rep", "pg"), None, None, None),
            P("rep"),
            P("rep"),
            P("rep", None),
            P("rep", None),
        ),
        out_specs=(P(("rep", "pg"), None, None), P(("rep", "pg"), None, None, None)),
        check_vma=False,
    )
```

```python
import functools
import math

import jax
import jax.numpy as jnp
import numpy as np
from jax import lax
from jax.experimental import pallas as pl
from jax.experimental.pallas import tpu as pltpu
from jax.sharding import PartitionSpec as P

Q_HEADS = 32
KV_HEADS = 4
HEAD_DIM = 128
PER_KV = Q_HEADS // KV_HEADS
KV_WIDTH = KV_HEADS * HEAD_DIM
WIDTH = 2 * KV_WIDTH

ROPE_BASE = 1000000.0
MASKED = -1e30
SCALE = HEAD_DIM ** -0.5 / math.log(2.0)
CHUNK = 256
LATE = 4
LATE_CHUNK = 512
AHEAD = 4
AHEAD_OF_QUERIES = 8

SMEM = pl.BlockSpec(memory_space=pltpu.SMEM)
VMEM = pl.BlockSpec(memory_space=pltpu.VMEM)
ANY = pl.BlockSpec(memory_space=pl.ANY)


def params(mib):
    return pltpu.CompilerParams(vmem_limit_bytes=mib * 1024 * 1024)


def column(head):
    return slice(head * HEAD_DIM, (head + 1) * HEAD_DIM)


def order_of(groups):
    half = groups // 2
    near = list(range(half - 1, 0, -1))
    quarter, eighth = half // 2, half // 4
    far = [half + (at // 2 if at % 2 == 0 else quarter + (at // 2 ^ eighth)) for at in range(half)]
    order = [(far if kind == "f" else near).pop(0) for kind in "ffnfnfnfnnnffnf"]
    order.insert(groups - LATE - 1, 0)
    return order


def rotation_tables(rows):
    half = HEAD_DIM // 2
    freqs = np.tile(ROPE_BASE ** (-np.arange(half, dtype=np.float64) / half), 2)
    angles = np.arange(rows, dtype=np.float64)[:, None] * freqs[None, :]
    parts = [np.cos(angles), np.sin(angles), np.tile(freqs, (8, 1))]
    return jnp.asarray(np.concatenate(parts, axis=0).astype(np.float32))


def rotation(table_ref, length):
    rows = (table_ref.shape[0] - 8) // 2
    start = length.astype(jnp.float32) * table_ref[2 * rows : 2 * rows + 8, :]
    cos_start, sin_start = jnp.cos(start)[0:1], jnp.sin(start)[0:1]
    cos_row, sin_row = table_ref[0:rows, :], table_ref[rows : 2 * rows, :]
    lane = lax.broadcasted_iota(jnp.int32, (1, HEAD_DIM), 1)
    sign = jnp.where(lane < HEAD_DIM // 2, -1.0, 1.0)
    cosine = cos_row * cos_start - sin_row * sin_start
    return cosine, sin_row * (cos_start * sign) + cos_row * (sin_start * sign)


def turn(x, cosine, sine):
    x = x.astype(jnp.float32)
    return (x * cosine + pltpu.roll(x, HEAD_DIM // 2, 1) * sine).astype(jnp.bfloat16)


def info_rows(new_count):
    sizes = [("cos", new_count), ("sin", new_count), ("bias", 8), ("scalars", 8), ("new", 2 * KV_HEADS * new_count)]
    at, rows = 0, {}
    for name, size in sizes:
        rows[name] = at
        at += size
    return rows, at


def fresh_rows(info_ref, base, residue, new_count, count, quarter, lanes):
    groups = new_count // count
    stack = [
        info_ref[pl.ds(base + (head + lanes) * new_count + residue, count, stride=groups), :]
        for head in range(0, 2 * KV_HEADS, quarter)
    ]
    return jnp.concatenate(stack, axis=0)


def front_kernel(
    order, me_ref, assign_any, length_any, owner_any, stripe_any, block_any, table_any, pool_any, *refs
):
    groups, slots, width = pool_any.shape
    send_refs, info_any, refs = refs[:AHEAD], refs[AHEAD], refs[AHEAD + 1 :]
    (assign_ref, length_ref, owner_ref, stripe_ref, residue_ref, block_ref, table_ref, pool_ref, pack_ref, info_ref,
     small_sems, pool_sems, send_sems, info_sems) = refs
    new_count = block_any.shape[0]
    count = new_count // groups
    quarter = width * count // slots // HEAD_DIM
    at, rows = info_rows(new_count)
    pairs = [
        (assign_any, assign_ref), (length_any, length_ref), (owner_any, owner_ref), (stripe_any, stripe_ref),
        (block_any, block_ref), (table_any, table_ref),
    ]
    smalls = [pltpu.make_async_copy(*pair, small_sems.at[i]) for i, pair in enumerate(pairs)]
    for copy in smalls:
        copy.start()
    pool_copies = [
        pltpu.make_async_copy(pool_any.at[pl.ds(low, 4)], pool_ref.at[pl.ds(low, 4)], pool_sems.at[low // 4])
        for low in range(0, groups, 4)
    ]
    for copy in pool_copies:
        copy.start()
    me = me_ref[0]
    for copy in smalls:
        copy.wait()
    request = assign_ref[me]
    length = length_ref[request]
    for residue in range(groups):
        residue_ref[owner_ref[request, residue]] = residue
    cosine, sine = rotation(table_ref, length)
    for head in range(KV_HEADS):
        low = at["new"] + head * new_count
        info_ref[low : low + new_count] = turn(block_ref[:, column(head)], cosine, sine).astype(jnp.float32)
        low += KV_HEADS * new_count
        info_ref[low : low + new_count] = block_ref[:, column(KV_HEADS + head)].astype(jnp.float32)

    def info_copy(part, low, high):
        part_rows = pl.ds(low, high - low)
        return pltpu.make_async_copy(info_ref.at[part_rows], info_any.at[part_rows], info_sems.at[part])

    info_copy(0, at["new"], rows).start()
    info_ref[at["cos"] : at["cos"] + new_count] = cosine
    info_ref[at["sin"] : at["sin"] + new_count] = sine
    per_row = HEAD_DIM // slots
    row = lax.broadcasted_iota(jnp.int32, (8, HEAD_DIM), 0)
    lane = lax.broadcasted_iota(jnp.int32, (8, HEAD_DIM), 1)
    piece, slot = row * per_row + lane // slots, lane % slots
    holder, requests, residues = jnp.zeros_like(lane), jnp.zeros_like(lane), jnp.zeros_like(lane)
    for p in range(groups):
        other = me ^ order[p]
        holder = jnp.where(piece == p, other, holder)
        requests = jnp.where(lane == p, assign_ref[other], requests)
        residues = jnp.where(lane == p, residue_ref[other], residues)
    bias = jnp.full((8, HEAD_DIM), MASKED, jnp.float32)
    for residue in range(groups):
        live = (holder == stripe_ref[request, residue]) & (slot * groups + residue < length)
        bias = jnp.where(live, 0.0, bias)
    info_ref[at["bias"] : at["bias"] + 8] = bias
    scalars = jnp.where(row == 0, requests, residues)
    info_ref[at["scalars"] : at["scalars"] + 8] = scalars.astype(jnp.float32)
    info_copy(1, 0, at["new"]).start()
    for copy in pool_copies:
        copy.wait()
    sends = []
    for p in range(AHEAD):
        pack_ref[p, :, 0:width] = pool_ref[assign_ref[me ^ order[p]]]
        for lanes in range(quarter):
            pack_ref[p, :, width + lanes * HEAD_DIM : width + (lanes + 1) * HEAD_DIM] = fresh_rows(
                info_ref, at["new"], residue_ref[me ^ order[p]], new_count, count, quarter, lanes
            ).astype(jnp.bfloat16)
        sends.append(pltpu.make_async_copy(pack_ref.at[p], send_refs[p], send_sems.at[p]))
        sends[-1].start()
    for copy in sends:
        copy.wait()
    info_copy(0, at["new"], rows).wait()
    info_copy(1, 0, at["new"]).wait()


def front(order, me, assignment, prefix_len, owner_map, stripe_map, block_kv, table, pool):
    groups, slots, width = pool.shape
    new_count = block_kv.shape[0]
    count = new_count // groups
    block = jax.ShapeDtypeStruct((slots, width + width * count // slots), jnp.bfloat16)
    info = jax.ShapeDtypeStruct((info_rows(new_count)[1], HEAD_DIM), jnp.float32)
    *blocks, info = pl.pallas_call(
        functools.partial(front_kernel, order),
        out_shape=[block] * AHEAD + [info],
        in_specs=[SMEM] + [ANY] * 7,
        out_specs=[ANY] * (AHEAD + 1),
        scratch_shapes=[
            pltpu.SMEM(assignment.shape, jnp.int32),
            pltpu.SMEM(prefix_len.shape, jnp.int32),
            pltpu.SMEM(owner_map.shape, jnp.int32),
            pltpu.SMEM(stripe_map.shape, jnp.int32),
            pltpu.SMEM(assignment.shape, jnp.int32),
            pltpu.VMEM(block_kv.shape, jnp.bfloat16),
            pltpu.VMEM(table.shape, jnp.float32),
            pltpu.VMEM(pool.shape, jnp.bfloat16),
            pltpu.VMEM((AHEAD,) + block.shape, jnp.bfloat16),
            pltpu.VMEM(info.shape, jnp.float32),
            pltpu.SemaphoreType.DMA((6,)),
            pltpu.SemaphoreType.DMA((groups // 4,)),
            pltpu.SemaphoreType.DMA((AHEAD,)),
            pltpu.SemaphoreType.DMA((2,)),
        ],
        compiler_params=params(60),
        name="front",
    )(me, assignment, prefix_len, owner_map, stripe_map, block_kv, table, pool)
    return blocks, info


def pack_kernel(info_ref, pool_ref, *refs):
    groups, slots, width = pool_ref.shape
    targets, (scalar_ref, scalar_sem) = refs[: groups - AHEAD], refs[groups - AHEAD :]
    new_count = slots * groups * (targets[0].shape[1] - width) // width
    at, _ = info_rows(new_count)
    count = new_count // groups
    quarter = (targets[0].shape[1] - width) // HEAD_DIM
    scalar_copy = pltpu.make_async_copy(info_ref.at[pl.ds(at["scalars"], 8)], scalar_ref, scalar_sem)
    scalar_copy.start()
    scalar_copy.wait()
    for p, target in enumerate(targets, AHEAD):
        target[:, 0:width] = pool_ref[scalar_ref[0, p].astype(jnp.int32)]
        residue = scalar_ref[1, p].astype(jnp.int32)
        for lanes in range(quarter):
            target[:, width + lanes * HEAD_DIM : width + (lanes + 1) * HEAD_DIM] = fresh_rows(
                info_ref, at["new"], residue, new_count, count, quarter, lanes
            ).astype(jnp.bfloat16)


def pack_others(info, pool, new_count):
    groups, slots, width = pool.shape
    block = (slots, width + width * (new_count // groups) // slots)
    return pl.pallas_call(
        pack_kernel,
        out_shape=[jax.ShapeDtypeStruct(block, jnp.bfloat16)] * (groups - AHEAD),
        in_specs=[VMEM] * 2,
        out_specs=[VMEM] * (groups - AHEAD),
        scratch_shapes=[pltpu.SMEM((8, HEAD_DIM), jnp.float32), pltpu.SemaphoreType.DMA],
        compiler_params=params(32),
        name="pack_others",
    )(info, pool)


def query_kernel(info_ref, q_ref, rot_ref, own_ref, bias_ref, request_ref):
    new_count = q_ref.shape[0]
    at, _ = info_rows(new_count)
    cosine = info_ref[at["cos"] : at["cos"] + new_count]
    sine = info_ref[at["sin"] : at["sin"] + new_count]
    for row in range(bias_ref.shape[1] // HEAD_DIM):
        line = info_ref[at["bias"] + row : at["bias"] + row + 1]
        bias_ref[:, column(row)] = jnp.broadcast_to(line, (8, HEAD_DIM))
    request_ref[...] = info_ref[at["scalars"] : at["scalars"] + 8].astype(jnp.int32)
    for head in range(2 * KV_HEADS):
        rows = at["new"] + head * new_count
        own_ref[head] = info_ref[rows : rows + new_count].astype(jnp.bfloat16)
    for head in range(Q_HEADS):
        rows = slice((head % PER_KV) * new_count, (head % PER_KV + 1) * new_count)
        rot_ref[head // PER_KV, rows, :] = turn(q_ref[:, column(head)], cosine, sine)


def rotate_queries(info, queries, span):
    new_count = queries.shape[0]
    return pl.pallas_call(
        query_kernel,
        out_shape=(
            jax.ShapeDtypeStruct((KV_HEADS, PER_KV * new_count, HEAD_DIM), jnp.bfloat16),
            jax.ShapeDtypeStruct((2 * KV_HEADS, new_count, HEAD_DIM), jnp.bfloat16),
            jax.ShapeDtypeStruct((8, span), jnp.float32),
            jax.ShapeDtypeStruct((8, HEAD_DIM), jnp.int32),
        ),
        in_specs=[VMEM] * 2,
        out_specs=[VMEM] * 4,
        compiler_params=params(32),
        name="rotate_queries",
    )(info, queries)


def quotient(summed, total):
    about = pl.reciprocal(total, approx=True)
    return summed * (about * (2.0 - total * about))


def join_keys(keys, values, got_refs, own_ref, head):
    key_parts = [got[:, column(head)] for got in got_refs]
    value_parts = [got[:, column(KV_HEADS + head)] for got in got_refs]
    if own_ref is not None:
        key_parts.append(own_ref[head])
        value_parts.append(own_ref[KV_HEADS + head])
    keys[head] = jnp.concatenate(key_parts, axis=0)
    value = jnp.concatenate(value_parts, axis=0)
    values[head] = jnp.concatenate([value, jnp.ones_like(value)], axis=1)


def dot_keys(query, keys):
    return lax.dot_general(query, keys, (((1,), (1,)), ((), ())), preferred_element_type=jnp.float32)


def staged(total, score, weigh, mix, finish, beside=None):
    scores, weights = {0: score(0)}, {}
    for at in range(total + 1):
        if at + 1 < total:
            scores[at + 1] = score(at + 1)
        if at >= 1:
            mixed = mix(at - 1, weights.pop(at - 1))
        if at < total:
            weights[at] = weigh(at, scores.pop(at))
        if at >= 1:
            finish(at - 1, mixed)
        if at == 1 and beside is not None:
            beside()


def unpacking(fresh_refs, first, request_vmem, decode_ref, rows_ref, request_ref, request_sem, decode_sems):
    count = rows_ref.shape[1]
    request_copy = pltpu.make_async_copy(request_vmem, request_ref, request_sem)
    request_copy.start()

    def decode_copy(p):
        return pltpu.make_async_copy(
            rows_ref.at[p], decode_ref.at[request_ref[0, first + p]], decode_sems.at[p]
        )

    def start():
        request_copy.wait()
        for p, fresh_ref in enumerate(fresh_refs):
            stack = fresh_ref[...]
            quarter = stack.shape[1]
            for part in range(stack.shape[0] // count):
                rows_ref[p, :, part * quarter : (part + 1) * quarter] = stack[part * count : (part + 1) * count]
            decode_copy(p).start()

    def wait():
        for p in range(len(fresh_refs)):
            decode_copy(p).wait()

    return start, wait


def spare_part(got):
    return got.at[:, pl.ds(WIDTH, got.shape[1] - WIDTH)]


def pieces_of(refs):
    pieces = []
    for ref in refs:
        pieces += [ref] if len(ref.shape) == 2 else [ref.at[i] for i in range(ref.shape[0])]
    return pieces


def attend_kernel(arrays, unpack, rot_ref, bias_ref, own_ref, *refs):
    got_refs, refs = pieces_of(refs[:arrays]), refs[arrays:]
    start, wait = None, None
    if unpack:
        request_vmem, result_ref, level_ref, decode_ref, *scratch = refs
        start, wait = unpacking([spare_part(got) for got in got_refs], 0, request_vmem, decode_ref, *scratch)
    else:
        result_ref, level_ref = refs
    new_count = rot_ref.shape[1] // PER_KV
    span = len(got_refs) * got_refs[0].shape[0]
    token = lax.broadcasted_iota(jnp.int32, (CHUNK, new_count), 0) % new_count
    causal = jnp.where(lax.broadcasted_iota(jnp.int32, (CHUNK, new_count), 1) <= token, 0.0, MASKED)
    bias = bias_ref[0:1, 0:span]
    per_head = PER_KV * new_count // CHUNK
    keys, values, highs = {}, {}, {}

    def place(at):
        return at // per_head, slice(at % per_head * CHUNK, (at % per_head + 1) * CHUNK)

    def score(at):
        head, rows = place(at)
        if at % per_head == 0:
            join_keys(keys, values, got_refs, own_ref, head)
        return dot_keys(rot_ref[head, rows, :], keys[head])

    def weigh(at, scores):
        scores = jnp.concatenate([scores[:, :span] * SCALE + bias, scores[:, span:] * SCALE + causal], axis=1)
        highs[at] = jnp.max(scores, axis=1, keepdims=True)
        return jnp.exp2(scores - highs[at]).astype(jnp.bfloat16)

    def mix(at, weights):
        return jnp.dot(weights, values[at // per_head], preferred_element_type=jnp.float32)

    def finish(at, mixed):
        head, rows = place(at)
        total = mixed[:, HEAD_DIM:]
        result_ref[head, rows, :] = quotient(mixed[:, :HEAD_DIM], total)
        level_ref[head, rows, :] = highs.pop(at) + jnp.log2(total)

    staged(KV_HEADS * per_head, score, weigh, mix, finish, start)
    if unpack:
        wait()


def attend(rot, bias, own, got, requests=None):
    rows, new_count = rot.shape[1], rot.shape[1] // PER_KV
    operands = [rot, bias, own, *got]
    shapes = [jax.ShapeDtypeStruct((KV_HEADS, rows, HEAD_DIM), jnp.float32)] * 2
    out_specs, scratch = [VMEM] * 2, []
    if requests is not None:
        operands.append(requests)
        slots, width = got[-1].shape
        count = (width - WIDTH) * slots // WIDTH
        shapes.append(jax.ShapeDtypeStruct((new_count // count, count, WIDTH), jnp.bfloat16))
        out_specs.append(ANY)
        scratch = unpack_scratch(len(pieces_of(got)), count, requests)
    return pl.pallas_call(
        functools.partial(attend_kernel, len(got), requests is not None),
        out_shape=tuple(shapes),
        in_specs=[VMEM] * len(operands),
        out_specs=tuple(out_specs),
        scratch_shapes=scratch,
        compiler_params=params(32),
        name="attend",
    )(*operands)


def unpack_scratch(pieces, count, requests):
    return [
        pltpu.VMEM((pieces, count, WIDTH), jnp.bfloat16),
        pltpu.SMEM(requests.shape, jnp.int32),
        pltpu.SemaphoreType.DMA,
        pltpu.SemaphoreType.DMA((pieces,)),
    ]


HEADROOM = 96.0


def late_kernel(pieces, first, rot_ref, bias_ref, result_ref, level_ref, *refs):
    got_refs, refs = refs[:pieces], refs[pieces:]
    request_vmem, _, out_ref, decode_ref, done_ref, out_sems, *scratch = refs
    start, wait = unpacking([spare_part(got) for got in got_refs], first, request_vmem, decode_ref, *scratch)
    slots = got_refs[0].shape[0]
    new_count = out_ref.shape[0]
    size = LATE_CHUNK
    heads_in = size // new_count
    bias = bias_ref[0:1, first * slots : (first + pieces) * slots]
    per_head = PER_KV * new_count // size
    chunks = KV_HEADS * per_head
    keys, values, excess = {}, {}, []

    def place(at):
        return at // per_head, slice(at % per_head * size, (at % per_head + 1) * size)

    def out_copy(at):
        width = heads_in * HEAD_DIM
        return pltpu.make_async_copy(
            done_ref.at[at], out_ref.at[:, pl.ds(pl.multiple_of(at * width, width), width)], out_sems.at[at]
        )

    def store(at, result):
        for row in range(heads_in):
            done_ref[at, :, column(row)] = result[row * new_count : (row + 1) * new_count].astype(jnp.bfloat16)
        out_copy(at).start()

    def score(at):
        head, rows = place(at)
        if at % per_head == 0:
            join_keys(keys, values, got_refs, None, head)
        return dot_keys(rot_ref[head, rows, :], keys[head])

    def weigh(at, scores):
        head, rows = place(at)
        powers = scores * SCALE + bias - level_ref[head, rows, :]
        excess.append(jnp.max(powers.reshape(size // 8, 8, HEAD_DIM), axis=0))
        return jnp.exp2(powers).astype(jnp.bfloat16)

    def mix(at, weights):
        return jnp.dot(weights, values[at // per_head], preferred_element_type=jnp.float32)

    def finish(at, mixed):
        head, rows = place(at)
        store(at, quotient(result_ref[head, rows, :] + mixed[:, :HEAD_DIM], 1.0 + mixed[:, HEAD_DIM:]))

    staged(chunks, score, weigh, mix, finish, start)
    most = jnp.max(functools.reduce(jnp.maximum, excess))
    wait()
    for at in range(chunks):
        out_copy(at).wait()

    @pl.when(most > HEADROOM)
    def _():
        for head in range(KV_HEADS):

            def again(chunk, carry, head=head):
                rows = pl.ds(pl.multiple_of(chunk * size, size), size)
                scores = dot_keys(rot_ref[head, rows, :], keys[head]) * SCALE + bias
                level = level_ref[head, rows, :]
                high = jnp.maximum(level, jnp.max(scores, axis=1, keepdims=True))
                factor = jnp.exp2(level - high)
                weights = jnp.exp2(scores - high).astype(jnp.bfloat16)
                mixed = jnp.dot(weights, values[head], preferred_element_type=jnp.float32)
                at = head * per_head + chunk
                summed = result_ref[head, rows, :] * factor + mixed[:, :HEAD_DIM]
                store(at, quotient(summed, factor + mixed[:, HEAD_DIM:]))
                out_copy(at).wait()
                return carry

            lax.fori_loop(0, per_head, again, 0)


def attend_late(rot, bias, result, level, got, first, requests, decode):
    rows, new_count = rot.shape[1], rot.shape[1] // PER_KV
    operands = [rot, bias, result, level, *got, requests, decode]
    chunks = KV_HEADS * rows // LATE_CHUNK
    return pl.pallas_call(
        functools.partial(late_kernel, len(got), first),
        out_shape=(
            jax.ShapeDtypeStruct((new_count, Q_HEADS * HEAD_DIM), jnp.bfloat16),
            jax.ShapeDtypeStruct(decode.shape, jnp.bfloat16),
        ),
        in_specs=[VMEM] * (len(operands) - 1) + [ANY],
        out_specs=(ANY, ANY),
        scratch_shapes=[
            pltpu.VMEM((chunks, new_count, LATE_CHUNK // new_count * HEAD_DIM), jnp.bfloat16),
            pltpu.SemaphoreType.DMA((chunks,)),
        ]
        + unpack_scratch(len(got), decode.shape[1], requests),
        input_output_aliases={len(operands) - 1: 1},
        compiler_params=params(32),
        name="attend_late",
    )(*operands)


def inverse(table):
    places = jnp.arange(table.shape[0], dtype=jnp.int32)
    return jnp.sum(jnp.where(table[None, :] == places[:, None], places, 0), axis=1)


def rotate(rows, positions, heads):
    half = HEAD_DIM // 2
    freqs = ROPE_BASE ** (-jnp.arange(half, dtype=jnp.float32) / half)
    angles = positions.astype(jnp.float32)[:, None] * freqs[None, :]
    cosine = jnp.concatenate([jnp.cos(angles)] * 2, axis=-1)[:, None, :]
    sine = jnp.concatenate([-jnp.sin(angles), jnp.sin(angles)], axis=-1)[:, None, :]
    split = rows.astype(jnp.float32).reshape(rows.shape[0], heads, HEAD_DIM)
    turned = jnp.roll(split, half, axis=-1)
    return (split * cosine + turned * sine).astype(jnp.bfloat16)


def small_pieces(me, assignment, prefix_len, stripe_map, owner_map, queries, block_kv, pool):
    groups, slots, width = pool.shape
    new_count = block_kv.shape[0]
    count = new_count // groups
    request = assignment[me[0]]
    length = prefix_len[request]
    positions = length + jnp.arange(new_count, dtype=jnp.int32)
    rot = rotate(queries, positions, Q_HEADS).reshape(new_count, KV_HEADS, PER_KV, HEAD_DIM)
    rot = jnp.transpose(rot, (1, 2, 0, 3)).reshape(KV_HEADS, PER_KV * new_count, HEAD_DIM)
    new_keys = rotate(block_kv[:, :KV_WIDTH], positions, KV_HEADS).reshape(new_count, KV_WIDTH)
    new_kv = jnp.concatenate([new_keys, block_kv[:, KV_WIDTH:]], axis=1)
    own = jnp.transpose(new_kv.reshape(new_count, 2 * KV_HEADS, HEAD_DIM), (1, 0, 2))
    spread = jnp.transpose(new_kv.reshape(count, groups, width), (1, 0, 2))
    send = jnp.concatenate([pool[assignment], spread[inverse(owner_map[request])]], axis=1)
    got = lax.all_to_all(send, "pg", split_axis=0, concat_axis=0, tiled=True)
    located = jnp.arange(slots, dtype=jnp.int32)[None, :] * groups + inverse(stripe_map[request])[:, None]
    bias = jnp.where(located < length, 0.0, MASKED).astype(jnp.float32).reshape(1, groups * slots)
    keys = got[:, :slots].reshape(groups * slots, width)
    result, _ = attend(rot, jnp.broadcast_to(bias, (8, groups * slots)), own, [keys])
    result = result.astype(jnp.bfloat16).reshape(KV_HEADS, PER_KV, new_count, HEAD_DIM)
    attended = jnp.transpose(result, (2, 0, 1, 3)).reshape(new_count, Q_HEADS * HEAD_DIM)
    return attended, got[inverse(assignment), slots:]


def shards(queries, block_kv, pool_kv, prefix_len, assignment, stripe_map, owner_map):
    queries, block_kv, pool = queries[0], block_kv[0], pool_kv[0]
    groups, slots, width = pool.shape
    new_count = queries.shape[0]
    count = new_count // groups
    me = lax.axis_index("pg").astype(jnp.int32).reshape(1)
    if groups != 16 or slots % 16 or HEAD_DIM % slots or count % 8 or slots % count:
        attended, decode_kv = small_pieces(
            me, assignment, prefix_len, stripe_map, owner_map, queries, block_kv, pool
        )
        return (attended[None], decode_kv[None])
    order = order_of(groups)
    table = rotation_tables(new_count)
    blocks, info = front(order, me, assignment, prefix_len, owner_map, stripe_map, block_kv, table, pool)
    blocks = list(blocks) + list(pack_others(info, pool, new_count))
    rot, own, bias, requests = rotate_queries(info, queries, groups * slots)
    rot, *blocks[AHEAD_OF_QUERIES:] = lax.optimization_barrier((rot, *blocks[AHEAD_OF_QUERIES:]))
    got = [
        lax.ppermute(block, "pg", [(source, source ^ t) for source in range(groups)]) if t else block
        for block, t in zip(blocks, order)
    ]
    soon = groups - LATE
    result, level, decode_kv = attend(rot, bias, own, got[:soon], requests)
    attended, decode_kv = attend_late(rot, bias, result, level, got[soon:], soon, requests, decode_kv)
    return (attended[None], decode_kv[None])


def solution(mesh):
    return jax.shard_map(
        shards,
        mesh=mesh,
        in_specs=(
            P(("rep", "pg"), None, None),
            P(("rep", "pg"), None, None),
            P(("rep", "pg"), None, None, None),
            P("rep"),
            P("rep"),
            P("rep", None),
            P("rep", None),
        ),
        out_specs=(P(("rep", "pg"), None, None), P(("rep", "pg"), None, None, None)),
        check_vma=False,
    )
```

```python
import functools
import math

import jax
import jax.numpy as jnp
import numpy as np
from jax import lax
from jax.experimental import pallas as pl
from jax.experimental.pallas import tpu as pltpu
from jax.sharding import PartitionSpec as P

Q_HEADS = 32
KV_HEADS = 4
HEAD_DIM = 128
PER_KV = Q_HEADS // KV_HEADS
KV_WIDTH = KV_HEADS * HEAD_DIM
WIDTH = 2 * KV_WIDTH

ROPE_BASE = 1000000.0
MASKED = -1e30
SCALE = HEAD_DIM ** -0.5 / math.log(2.0)
CHUNK = 512
LATE = 4
LATE_CHUNK = 512
AHEAD = 4
AHEAD_OF_QUERIES = 8

SMEM = pl.BlockSpec(memory_space=pltpu.SMEM)
VMEM = pl.BlockSpec(memory_space=pltpu.VMEM)
ANY = pl.BlockSpec(memory_space=pl.ANY)


def params(mib):
    return pltpu.CompilerParams(vmem_limit_bytes=mib * 1024 * 1024)


def column(head):
    return slice(head * HEAD_DIM, (head + 1) * HEAD_DIM)


def order_of(groups):
    half = groups // 2
    near = list(range(half - 1, 0, -1))
    quarter, eighth = half // 2, half // 4
    far = [half + (at // 2 if at % 2 == 0 else quarter + (at // 2 ^ eighth)) for at in range(half)]
    order = [(far if kind == "f" else near).pop(0) for kind in "ffnfnfnfnfnfnfn"]
    order.insert(groups - LATE - 1, 0)
    return order


def rotation_tables(rows):
    half = HEAD_DIM // 2
    freqs = np.tile(ROPE_BASE ** (-np.arange(half, dtype=np.float64) / half), 2)
    angles = np.arange(rows, dtype=np.float64)[:, None] * freqs[None, :]
    parts = [np.cos(angles), np.sin(angles), np.tile(freqs, (8, 1))]
    return jnp.asarray(np.concatenate(parts, axis=0).astype(np.float32))


def rotation(table_ref, length):
    rows = (table_ref.shape[0] - 8) // 2
    start = length.astype(jnp.float32) * table_ref[2 * rows : 2 * rows + 8, :]
    cos_start, sin_start = jnp.cos(start)[0:1], jnp.sin(start)[0:1]
    cos_row, sin_row = table_ref[0:rows, :], table_ref[rows : 2 * rows, :]
    lane = lax.broadcasted_iota(jnp.int32, (1, HEAD_DIM), 1)
    sign = jnp.where(lane < HEAD_DIM // 2, -1.0, 1.0)
    cosine = cos_row * cos_start - sin_row * sin_start
    return cosine, sin_row * (cos_start * sign) + cos_row * (sin_start * sign)


def turn(x, cosine, sine):
    x = x.astype(jnp.float32)
    return (x * cosine + pltpu.roll(x, HEAD_DIM // 2, 1) * sine).astype(jnp.bfloat16)


def info_rows(new_count):
    sizes = [("cos", new_count), ("sin", new_count), ("bias", 8), ("scalars", 8), ("new", 2 * KV_HEADS * new_count)]
    at, rows = 0, {}
    for name, size in sizes:
        rows[name] = at
        at += size
    return rows, at


def fresh_rows(info_ref, base, residue, new_count, count, quarter, lanes):
    groups = new_count // count
    stack = [
        info_ref[pl.ds(base + (head + lanes) * new_count + residue, count, stride=groups), :]
        for head in range(0, 2 * KV_HEADS, quarter)
    ]
    return jnp.concatenate(stack, axis=0)


def front_kernel(
    order, me_ref, assign_any, length_any, owner_any, stripe_any, block_any, table_any, pool_any, *refs
):
    groups, slots, width = pool_any.shape
    send_refs, info_any, refs = refs[:AHEAD], refs[AHEAD], refs[AHEAD + 1 :]
    (assign_ref, length_ref, owner_ref, stripe_ref, residue_ref, block_ref, table_ref, pool_ref, pack_ref, info_ref,
     small_sems, pool_sems, send_sems, info_sems) = refs
    new_count = block_any.shape[0]
    count = new_count // groups
    quarter = width * count // slots // HEAD_DIM
    at, rows = info_rows(new_count)
    pairs = [
        (assign_any, assign_ref), (length_any, length_ref), (owner_any, owner_ref), (stripe_any, stripe_ref),
        (block_any, block_ref), (table_any, table_ref),
    ]
    smalls = [pltpu.make_async_copy(*pair, small_sems.at[i]) for i, pair in enumerate(pairs)]
    for copy in smalls:
        copy.start()
    pool_copies = [
        pltpu.make_async_copy(pool_any.at[pl.ds(low, 4)], pool_ref.at[pl.ds(low, 4)], pool_sems.at[low // 4])
        for low in range(0, groups, 4)
    ]
    for copy in pool_copies:
        copy.start()
    me = me_ref[0]
    for copy in smalls:
        copy.wait()
    request = assign_ref[me]
    length = length_ref[request]
    for residue in range(groups):
        residue_ref[owner_ref[request, residue]] = residue
    cosine, sine = rotation(table_ref, length)
    for head in range(KV_HEADS):
        low = at["new"] + head * new_count
        info_ref[low : low + new_count] = turn(block_ref[:, column(head)], cosine, sine).astype(jnp.float32)
        low += KV_HEADS * new_count
        info_ref[low : low + new_count] = block_ref[:, column(KV_HEADS + head)].astype(jnp.float32)

    def info_copy(part, low, high):
        part_rows = pl.ds(low, high - low)
        return pltpu.make_async_copy(info_ref.at[part_rows], info_any.at[part_rows], info_sems.at[part])

    info_copy(0, at["new"], rows).start()
    info_ref[at["cos"] : at["cos"] + new_count] = cosine
    info_ref[at["sin"] : at["sin"] + new_count] = sine
    per_row = HEAD_DIM // slots
    row = lax.broadcasted_iota(jnp.int32, (8, HEAD_DIM), 0)
    lane = lax.broadcasted_iota(jnp.int32, (8, HEAD_DIM), 1)
    piece, slot = row * per_row + lane // slots, lane % slots
    holder, requests, residues = jnp.zeros_like(lane), jnp.zeros_like(lane), jnp.zeros_like(lane)
    for p in range(groups):
        other = me ^ order[p]
        holder = jnp.where(piece == p, other, holder)
        requests = jnp.where(lane == p, assign_ref[other], requests)
        residues = jnp.where(lane == p, residue_ref[other], residues)
    bias = jnp.full((8, HEAD_DIM), MASKED, jnp.float32)
    for residue in range(groups):
        live = (holder == stripe_ref[request, residue]) & (slot * groups + residue < length)
        bias = jnp.where(live, 0.0, bias)
    info_ref[at["bias"] : at["bias"] + 8] = bias
    scalars = jnp.where(row == 0, requests, residues)
    info_ref[at["scalars"] : at["scalars"] + 8] = scalars.astype(jnp.float32)
    info_copy(1, 0, at["new"]).start()
    for copy in pool_copies:
        copy.wait()
    sends = []
    for p in range(AHEAD):
        pack_ref[p, :, 0:width] = pool_ref[assign_ref[me ^ order[p]]]
        for lanes in range(quarter):
            pack_ref[p, :, width + lanes * HEAD_DIM : width + (lanes + 1) * HEAD_DIM] = fresh_rows(
                info_ref, at["new"], residue_ref[me ^ order[p]], new_count, count, quarter, lanes
            ).astype(jnp.bfloat16)
        sends.append(pltpu.make_async_copy(pack_ref.at[p], send_refs[p], send_sems.at[p]))
        sends[-1].start()
    for copy in sends:
        copy.wait()
    info_copy(0, at["new"], rows).wait()
    info_copy(1, 0, at["new"]).wait()


def front(order, me, assignment, prefix_len, owner_map, stripe_map, block_kv, table, pool):
    groups, slots, width = pool.shape
    new_count = block_kv.shape[0]
    count = new_count // groups
    block = jax.ShapeDtypeStruct((slots, width + width * count // slots), jnp.bfloat16)
    info = jax.ShapeDtypeStruct((info_rows(new_count)[1], HEAD_DIM), jnp.float32)
    *blocks, info = pl.pallas_call(
        functools.partial(front_kernel, order),
        out_shape=[block] * AHEAD + [info],
        in_specs=[SMEM] + [ANY] * 7,
        out_specs=[ANY] * (AHEAD + 1),
        scratch_shapes=[
            pltpu.SMEM(assignment.shape, jnp.int32),
            pltpu.SMEM(prefix_len.shape, jnp.int32),
            pltpu.SMEM(owner_map.shape, jnp.int32),
            pltpu.SMEM(stripe_map.shape, jnp.int32),
            pltpu.SMEM(assignment.shape, jnp.int32),
            pltpu.VMEM(block_kv.shape, jnp.bfloat16),
            pltpu.VMEM(table.shape, jnp.float32),
            pltpu.VMEM(pool.shape, jnp.bfloat16),
            pltpu.VMEM((AHEAD,) + block.shape, jnp.bfloat16),
            pltpu.VMEM(info.shape, jnp.float32),
            pltpu.SemaphoreType.DMA((6,)),
            pltpu.SemaphoreType.DMA((groups // 4,)),
            pltpu.SemaphoreType.DMA((AHEAD,)),
            pltpu.SemaphoreType.DMA((2,)),
        ],
        compiler_params=params(60),
        name="front",
    )(me, assignment, prefix_len, owner_map, stripe_map, block_kv, table, pool)
    return blocks, info


def pack_kernel(info_ref, pool_ref, *refs):
    groups, slots, width = pool_ref.shape
    targets, (scalar_ref, scalar_sem) = refs[: groups - AHEAD], refs[groups - AHEAD :]
    new_count = slots * groups * (targets[0].shape[1] - width) // width
    at, _ = info_rows(new_count)
    count = new_count // groups
    quarter = (targets[0].shape[1] - width) // HEAD_DIM
    scalar_copy = pltpu.make_async_copy(info_ref.at[pl.ds(at["scalars"], 8)], scalar_ref, scalar_sem)
    scalar_copy.start()
    scalar_copy.wait()
    for p, target in enumerate(targets, AHEAD):
        target[:, 0:width] = pool_ref[scalar_ref[0, p].astype(jnp.int32)]
        residue = scalar_ref[1, p].astype(jnp.int32)
        for lanes in range(quarter):
            target[:, width + lanes * HEAD_DIM : width + (lanes + 1) * HEAD_DIM] = fresh_rows(
                info_ref, at["new"], residue, new_count, count, quarter, lanes
            ).astype(jnp.bfloat16)


def pack_others(info, pool, new_count):
    groups, slots, width = pool.shape
    block = (slots, width + width * (new_count // groups) // slots)
    return pl.pallas_call(
        pack_kernel,
        out_shape=[jax.ShapeDtypeStruct(block, jnp.bfloat16)] * (groups - AHEAD),
        in_specs=[VMEM] * 2,
        out_specs=[VMEM] * (groups - AHEAD),
        scratch_shapes=[pltpu.SMEM((8, HEAD_DIM), jnp.float32), pltpu.SemaphoreType.DMA],
        compiler_params=params(32),
        name="pack_others",
    )(info, pool)


def query_kernel(info_ref, q_ref, rot_ref, own_ref, bias_ref, request_ref):
    new_count = q_ref.shape[0]
    at, _ = info_rows(new_count)
    cosine = info_ref[at["cos"] : at["cos"] + new_count]
    sine = info_ref[at["sin"] : at["sin"] + new_count]
    for row in range(bias_ref.shape[1] // HEAD_DIM):
        line = info_ref[at["bias"] + row : at["bias"] + row + 1]
        bias_ref[:, column(row)] = jnp.broadcast_to(line, (8, HEAD_DIM))
    request_ref[...] = info_ref[at["scalars"] : at["scalars"] + 8].astype(jnp.int32)
    for head in range(2 * KV_HEADS):
        rows = at["new"] + head * new_count
        own_ref[head] = info_ref[rows : rows + new_count].astype(jnp.bfloat16)
    for head in range(Q_HEADS):
        rows = slice((head % PER_KV) * new_count, (head % PER_KV + 1) * new_count)
        rot_ref[head // PER_KV, rows, :] = turn(q_ref[:, column(head)], cosine, sine)


def rotate_queries(info, queries, span):
    new_count = queries.shape[0]
    return pl.pallas_call(
        query_kernel,
        out_shape=(
            jax.ShapeDtypeStruct((KV_HEADS, PER_KV * new_count, HEAD_DIM), jnp.bfloat16),
            jax.ShapeDtypeStruct((2 * KV_HEADS, new_count, HEAD_DIM), jnp.bfloat16),
            jax.ShapeDtypeStruct((8, span), jnp.float32),
            jax.ShapeDtypeStruct((8, HEAD_DIM), jnp.int32),
        ),
        in_specs=[VMEM] * 2,
        out_specs=[VMEM] * 4,
        compiler_params=params(32),
        name="rotate_queries",
    )(info, queries)


def quotient(summed, total):
    about = pl.reciprocal(total, approx=True)
    return summed * (about * (2.0 - total * about))


def join_keys(keys, values, got_refs, own_ref, head):
    key_parts = [got[:, column(head)] for got in got_refs]
    value_parts = [got[:, column(KV_HEADS + head)] for got in got_refs]
    if own_ref is not None:
        key_parts.append(own_ref[head])
        value_parts.append(own_ref[KV_HEADS + head])
    keys[head] = jnp.concatenate(key_parts, axis=0)
    value = jnp.concatenate(value_parts, axis=0)
    values[head] = jnp.concatenate([value, jnp.ones_like(value)], axis=1)


def dot_keys(query, keys):
    return lax.dot_general(query, keys, (((1,), (1,)), ((), ())), preferred_element_type=jnp.float32)


def staged(total, score, weigh, mix, finish, beside=None):
    scores, weights = {0: score(0)}, {}
    for at in range(total + 1):
        if at + 1 < total:
            scores[at + 1] = score(at + 1)
        if at >= 1:
            mixed = mix(at - 1, weights.pop(at - 1))
        if at < total:
            weights[at] = weigh(at, scores.pop(at))
        if at >= 1:
            finish(at - 1, mixed)
        if at == 1 and beside is not None:
            beside()


def unpacking(fresh_refs, first, request_vmem, decode_ref, rows_ref, request_ref, request_sem, decode_sems):
    count = rows_ref.shape[1]
    request_copy = pltpu.make_async_copy(request_vmem, request_ref, request_sem)
    request_copy.start()

    def decode_copy(p):
        return pltpu.make_async_copy(
            rows_ref.at[p], decode_ref.at[request_ref[0, first + p]], decode_sems.at[p]
        )

    def start():
        request_copy.wait()
        for p, fresh_ref in enumerate(fresh_refs):
            stack = fresh_ref[...]
            quarter = stack.shape[1]
            for part in range(stack.shape[0] // count):
                rows_ref[p, :, part * quarter : (part + 1) * quarter] = stack[part * count : (part + 1) * count]
            decode_copy(p).start()

    def wait():
        for p in range(len(fresh_refs)):
            decode_copy(p).wait()

    return start, wait


def spare_part(got):
    return got.at[:, pl.ds(WIDTH, got.shape[1] - WIDTH)]


def pieces_of(refs):
    pieces = []
    for ref in refs:
        pieces += [ref] if len(ref.shape) == 2 else [ref.at[i] for i in range(ref.shape[0])]
    return pieces


def attend_kernel(arrays, unpack, rot_ref, bias_ref, own_ref, *refs):
    got_refs, refs = pieces_of(refs[:arrays]), refs[arrays:]
    start, wait = None, None
    if unpack:
        request_vmem, result_ref, level_ref, decode_ref, *scratch = refs
        start, wait = unpacking([spare_part(got) for got in got_refs], 0, request_vmem, decode_ref, *scratch)
    else:
        result_ref, level_ref = refs
    new_count = rot_ref.shape[1] // PER_KV
    span = len(got_refs) * got_refs[0].shape[0]
    token = lax.broadcasted_iota(jnp.int32, (CHUNK, new_count), 0) % new_count
    causal = jnp.where(lax.broadcasted_iota(jnp.int32, (CHUNK, new_count), 1) <= token, 0.0, MASKED)
    bias = bias_ref[0:1, 0:span]
    per_head = PER_KV * new_count // CHUNK
    keys, values, highs = {}, {}, {}

    def place(at):
        return at // per_head, slice(at % per_head * CHUNK, (at % per_head + 1) * CHUNK)

    def score(at):
        head, rows = place(at)
        if at % per_head == 0:
            join_keys(keys, values, got_refs, own_ref, head)
        return dot_keys(rot_ref[head, rows, :], keys[head])

    def weigh(at, scores):
        scores = jnp.concatenate([scores[:, :span] * SCALE + bias, scores[:, span:] * SCALE + causal], axis=1)
        highs[at] = jnp.max(scores, axis=1, keepdims=True)
        return jnp.exp2(scores - highs[at]).astype(jnp.bfloat16)

    def mix(at, weights):
        return jnp.dot(weights, values[at // per_head], preferred_element_type=jnp.float32)

    def finish(at, mixed):
        head, rows = place(at)
        total = mixed[:, HEAD_DIM:]
        result_ref[head, rows, :] = quotient(mixed[:, :HEAD_DIM], total)
        level_ref[head, rows, :] = highs.pop(at) + jnp.log2(total)

    staged(KV_HEADS * per_head, score, weigh, mix, finish, start)
    if unpack:
        wait()


def attend(rot, bias, own, got, requests=None):
    rows, new_count = rot.shape[1], rot.shape[1] // PER_KV
    operands = [rot, bias, own, *got]
    shapes = [jax.ShapeDtypeStruct((KV_HEADS, rows, HEAD_DIM), jnp.float32)] * 2
    out_specs, scratch = [VMEM] * 2, []
    if requests is not None:
        operands.append(requests)
        slots, width = got[-1].shape
        count = (width - WIDTH) * slots // WIDTH
        shapes.append(jax.ShapeDtypeStruct((new_count // count, count, WIDTH), jnp.bfloat16))
        out_specs.append(ANY)
        scratch = unpack_scratch(len(pieces_of(got)), count, requests)
    return pl.pallas_call(
        functools.partial(attend_kernel, len(got), requests is not None),
        out_shape=tuple(shapes),
        in_specs=[VMEM] * len(operands),
        out_specs=tuple(out_specs),
        scratch_shapes=scratch,
        compiler_params=params(32),
        name="attend",
    )(*operands)


def unpack_scratch(pieces, count, requests):
    return [
        pltpu.VMEM((pieces, count, WIDTH), jnp.bfloat16),
        pltpu.SMEM(requests.shape, jnp.int32),
        pltpu.SemaphoreType.DMA,
        pltpu.SemaphoreType.DMA((pieces,)),
    ]


HEADROOM = 96.0


def late_kernel(pieces, first, rot_ref, bias_ref, result_ref, level_ref, *refs):
    got_refs, refs = refs[:pieces], refs[pieces:]
    request_vmem, _, out_ref, decode_ref, done_ref, out_sems, *scratch = refs
    start, wait = unpacking([spare_part(got) for got in got_refs], first, request_vmem, decode_ref, *scratch)
    slots = got_refs[0].shape[0]
    new_count = out_ref.shape[0]
    size = LATE_CHUNK
    heads_in = size // new_count
    bias = bias_ref[0:1, first * slots : (first + pieces) * slots]
    per_head = PER_KV * new_count // size
    chunks = KV_HEADS * per_head
    keys, values, excess = {}, {}, []

    def place(at):
        return at // per_head, slice(at % per_head * size, (at % per_head + 1) * size)

    def out_copy(at):
        width = heads_in * HEAD_DIM
        return pltpu.make_async_copy(
            done_ref.at[at], out_ref.at[:, pl.ds(pl.multiple_of(at * width, width), width)], out_sems.at[at]
        )

    def store(at, result):
        for row in range(heads_in):
            done_ref[at, :, column(row)] = result[row * new_count : (row + 1) * new_count].astype(jnp.bfloat16)
        out_copy(at).start()

    def score(at):
        head, rows = place(at)
        if at % per_head == 0:
            join_keys(keys, values, got_refs, None, head)
        return dot_keys(rot_ref[head, rows, :], keys[head])

    def weigh(at, scores):
        head, rows = place(at)
        powers = scores * SCALE + bias - level_ref[head, rows, :]
        excess.append(jnp.max(powers.reshape(size // 8, 8, HEAD_DIM), axis=0))
        return jnp.exp2(powers).astype(jnp.bfloat16)

    def mix(at, weights):
        return jnp.dot(weights, values[at // per_head], preferred_element_type=jnp.float32)

    def finish(at, mixed):
        head, rows = place(at)
        store(at, quotient(result_ref[head, rows, :] + mixed[:, :HEAD_DIM], 1.0 + mixed[:, HEAD_DIM:]))

    staged(chunks, score, weigh, mix, finish, start)
    most = jnp.max(functools.reduce(jnp.maximum, excess))
    wait()
    for at in range(chunks):
        out_copy(at).wait()

    @pl.when(most > HEADROOM)
    def _():
        for head in range(KV_HEADS):

            def again(chunk, carry, head=head):
                rows = pl.ds(pl.multiple_of(chunk * size, size), size)
                scores = dot_keys(rot_ref[head, rows, :], keys[head]) * SCALE + bias
                level = level_ref[head, rows, :]
                high = jnp.maximum(level, jnp.max(scores, axis=1, keepdims=True))
                factor = jnp.exp2(level - high)
                weights = jnp.exp2(scores - high).astype(jnp.bfloat16)
                mixed = jnp.dot(weights, values[head], preferred_element_type=jnp.float32)
                at = head * per_head + chunk
                summed = result_ref[head, rows, :] * factor + mixed[:, :HEAD_DIM]
                store(at, quotient(summed, factor + mixed[:, HEAD_DIM:]))
                out_copy(at).wait()
                return carry

            lax.fori_loop(0, per_head, again, 0)


def attend_late(rot, bias, result, level, got, first, requests, decode):
    rows, new_count = rot.shape[1], rot.shape[1] // PER_KV
    operands = [rot, bias, result, level, *got, requests, decode]
    chunks = KV_HEADS * rows // LATE_CHUNK
    return pl.pallas_call(
        functools.partial(late_kernel, len(got), first),
        out_shape=(
            jax.ShapeDtypeStruct((new_count, Q_HEADS * HEAD_DIM), jnp.bfloat16),
            jax.ShapeDtypeStruct(decode.shape, jnp.bfloat16),
        ),
        in_specs=[VMEM] * (len(operands) - 1) + [ANY],
        out_specs=(ANY, ANY),
        scratch_shapes=[
            pltpu.VMEM((chunks, new_count, LATE_CHUNK // new_count * HEAD_DIM), jnp.bfloat16),
            pltpu.SemaphoreType.DMA((chunks,)),
        ]
        + unpack_scratch(len(got), decode.shape[1], requests),
        input_output_aliases={len(operands) - 1: 1},
        compiler_params=params(32),
        name="attend_late",
    )(*operands)


def inverse(table):
    places = jnp.arange(table.shape[0], dtype=jnp.int32)
    return jnp.sum(jnp.where(table[None, :] == places[:, None], places, 0), axis=1)


def rotate(rows, positions, heads):
    half = HEAD_DIM // 2
    freqs = ROPE_BASE ** (-jnp.arange(half, dtype=jnp.float32) / half)
    angles = positions.astype(jnp.float32)[:, None] * freqs[None, :]
    cosine = jnp.concatenate([jnp.cos(angles)] * 2, axis=-1)[:, None, :]
    sine = jnp.concatenate([-jnp.sin(angles), jnp.sin(angles)], axis=-1)[:, None, :]
    split = rows.astype(jnp.float32).reshape(rows.shape[0], heads, HEAD_DIM)
    turned = jnp.roll(split, half, axis=-1)
    return (split * cosine + turned * sine).astype(jnp.bfloat16)


def small_pieces(me, assignment, prefix_len, stripe_map, owner_map, queries, block_kv, pool):
    groups, slots, width = pool.shape
    new_count = block_kv.shape[0]
    count = new_count // groups
    request = assignment[me[0]]
    length = prefix_len[request]
    positions = length + jnp.arange(new_count, dtype=jnp.int32)
    rot = rotate(queries, positions, Q_HEADS).reshape(new_count, KV_HEADS, PER_KV, HEAD_DIM)
    rot = jnp.transpose(rot, (1, 2, 0, 3)).reshape(KV_HEADS, PER_KV * new_count, HEAD_DIM)
    new_keys = rotate(block_kv[:, :KV_WIDTH], positions, KV_HEADS).reshape(new_count, KV_WIDTH)
    new_kv = jnp.concatenate([new_keys, block_kv[:, KV_WIDTH:]], axis=1)
    own = jnp.transpose(new_kv.reshape(new_count, 2 * KV_HEADS, HEAD_DIM), (1, 0, 2))
    spread = jnp.transpose(new_kv.reshape(count, groups, width), (1, 0, 2))
    send = jnp.concatenate([pool[assignment], spread[inverse(owner_map[request])]], axis=1)
    got = lax.all_to_all(send, "pg", split_axis=0, concat_axis=0, tiled=True)
    located = jnp.arange(slots, dtype=jnp.int32)[None, :] * groups + inverse(stripe_map[request])[:, None]
    bias = jnp.where(located < length, 0.0, MASKED).astype(jnp.float32).reshape(1, groups * slots)
    keys = got[:, :slots].reshape(groups * slots, width)
    result, _ = attend(rot, jnp.broadcast_to(bias, (8, groups * slots)), own, [keys])
    result = result.astype(jnp.bfloat16).reshape(KV_HEADS, PER_KV, new_count, HEAD_DIM)
    attended = jnp.transpose(result, (2, 0, 1, 3)).reshape(new_count, Q_HEADS * HEAD_DIM)
    return attended, got[inverse(assignment), slots:]


def shards(queries, block_kv, pool_kv, prefix_len, assignment, stripe_map, owner_map):
    queries, block_kv, pool = queries[0], block_kv[0], pool_kv[0]
    groups, slots, width = pool.shape
    new_count = queries.shape[0]
    count = new_count // groups
    me = lax.axis_index("pg").astype(jnp.int32).reshape(1)
    if groups != 16 or slots % 16 or HEAD_DIM % slots or count % 8 or slots % count:
        attended, decode_kv = small_pieces(
            me, assignment, prefix_len, stripe_map, owner_map, queries, block_kv, pool
        )
        return (attended[None], decode_kv[None])
    order = order_of(groups)
    table = rotation_tables(new_count)
    blocks, info = front(order, me, assignment, prefix_len, owner_map, stripe_map, block_kv, table, pool)
    blocks = list(blocks) + list(pack_others(info, pool, new_count))
    rot, own, bias, requests = rotate_queries(info, queries, groups * slots)
    rot, *blocks[AHEAD_OF_QUERIES:] = lax.optimization_barrier((rot, *blocks[AHEAD_OF_QUERIES:]))
    got = [
        lax.ppermute(block, "pg", [(source, source ^ t) for source in range(groups)]) if t else block
        for block, t in zip(blocks, order)
    ]
    soon = groups - LATE
    result, level, decode_kv = attend(rot, bias, own, got[:soon], requests)
    attended, decode_kv = attend_late(rot, bias, result, level, got[soon:], soon, requests, decode_kv)
    return (attended[None], decode_kv[None])


def solution(mesh):
    return jax.shard_map(
        shards,
        mesh=mesh,
        in_specs=(
            P(("rep", "pg"), None, None),
            P(("rep", "pg"), None, None),
            P(("rep", "pg"), None, None, None),
            P("rep"),
            P("rep"),
            P("rep", None),
            P("rep", None),
        ),
        out_specs=(P(("rep", "pg"), None, None), P(("rep", "pg"), None, None, None)),
        check_vma=False,
    )
```

```python
import functools
import math

import jax
import jax.numpy as jnp
import numpy as np
from jax import lax
from jax.experimental import pallas as pl
from jax.experimental.pallas import tpu as pltpu
from jax.sharding import PartitionSpec as P

Q_HEADS = 32
KV_HEADS = 4
HEAD_DIM = 128
PER_KV = Q_HEADS // KV_HEADS
KV_WIDTH = KV_HEADS * HEAD_DIM
WIDTH = 2 * KV_WIDTH

ROPE_BASE = 1000000.0
MASKED = -1e30
SCALE = HEAD_DIM ** -0.5 / math.log(2.0)
CHUNK = 256
LATE = 4
LATE_CHUNK = 512
AHEAD = 4
AHEAD_OF_QUERIES = 8

SMEM = pl.BlockSpec(memory_space=pltpu.SMEM)
VMEM = pl.BlockSpec(memory_space=pltpu.VMEM)
ANY = pl.BlockSpec(memory_space=pl.ANY)


def params(mib):
    return pltpu.CompilerParams(vmem_limit_bytes=mib * 1024 * 1024)


def column(head):
    return slice(head * HEAD_DIM, (head + 1) * HEAD_DIM)


def order_of(groups):
    half = groups // 2
    near = list(range(half - 1, 0, -1))
    quarter, eighth = half // 2, half // 4
    far = [half + (at // 2 if at % 2 == 0 else quarter + (at // 2 ^ eighth)) for at in range(half)]
    far[-2:] = far[:-3:-1]
    order = [(far if kind == "f" else near).pop(0) for kind in "ffnfnfnfnfnfnfn"]
    order.insert(groups - LATE - 1, 0)
    return order


def rotation_tables(rows):
    half = HEAD_DIM // 2
    freqs = np.tile(ROPE_BASE ** (-np.arange(half, dtype=np.float64) / half), 2)
    angles = np.arange(rows, dtype=np.float64)[:, None] * freqs[None, :]
    parts = [np.cos(angles), np.sin(angles), np.tile(freqs, (8, 1))]
    return jnp.asarray(np.concatenate(parts, axis=0).astype(np.float32))


def rotation(table_ref, length):
    rows = (table_ref.shape[0] - 8) // 2
    start = length.astype(jnp.float32) * table_ref[2 * rows : 2 * rows + 8, :]
    cos_start, sin_start = jnp.cos(start)[0:1], jnp.sin(start)[0:1]
    cos_row, sin_row = table_ref[0:rows, :], table_ref[rows : 2 * rows, :]
    lane = lax.broadcasted_iota(jnp.int32, (1, HEAD_DIM), 1)
    sign = jnp.where(lane < HEAD_DIM // 2, -1.0, 1.0)
    cosine = cos_row * cos_start - sin_row * sin_start
    return cosine, sin_row * (cos_start * sign) + cos_row * (sin_start * sign)


def turn(x, cosine, sine):
    x = x.astype(jnp.float32)
    return (x * cosine + pltpu.roll(x, HEAD_DIM // 2, 1) * sine).astype(jnp.bfloat16)


def info_rows(new_count):
    sizes = [("cos", new_count), ("sin", new_count), ("bias", 8), ("scalars", 8), ("new", 2 * KV_HEADS * new_count)]
    at, rows = 0, {}
    for name, size in sizes:
        rows[name] = at
        at += size
    return rows, at


def fresh_rows(info_ref, base, residue, new_count, count, quarter, lanes):
    groups = new_count // count
    stack = [
        info_ref[pl.ds(base + (head + lanes) * new_count + residue, count, stride=groups), :]
        for head in range(0, 2 * KV_HEADS, quarter)
    ]
    return jnp.concatenate(stack, axis=0)


def front_kernel(
    order, me_ref, assign_any, length_any, owner_any, stripe_any, block_any, table_any, pool_any, *refs
):
    groups, slots, width = pool_any.shape
    send_refs, info_any, refs = refs[:AHEAD], refs[AHEAD], refs[AHEAD + 1 :]
    (assign_ref, length_ref, owner_ref, stripe_ref, residue_ref, block_ref, table_ref, pool_ref, pack_ref, info_ref,
     small_sems, pool_sems, send_sems, info_sems) = refs
    new_count = block_any.shape[0]
    count = new_count // groups
    quarter = width * count // slots // HEAD_DIM
    at, rows = info_rows(new_count)
    pairs = [
        (assign_any, assign_ref), (length_any, length_ref), (owner_any, owner_ref), (stripe_any, stripe_ref),
        (block_any, block_ref), (table_any, table_ref),
    ]
    smalls = [pltpu.make_async_copy(*pair, small_sems.at[i]) for i, pair in enumerate(pairs)]
    for copy in smalls:
        copy.start()
    pool_copies = [
        pltpu.make_async_copy(pool_any.at[pl.ds(low, 4)], pool_ref.at[pl.ds(low, 4)], pool_sems.at[low // 4])
        for low in range(0, groups, 4)
    ]
    for copy in pool_copies:
        copy.start()
    me = me_ref[0]
    for copy in smalls:
        copy.wait()
    request = assign_ref[me]
    length = length_ref[request]
    for residue in range(groups):
        residue_ref[owner_ref[request, residue]] = residue
    cosine, sine = rotation(table_ref, length)
    for head in range(KV_HEADS):
        low = at["new"] + head * new_count
        info_ref[low : low + new_count] = turn(block_ref[:, column(head)], cosine, sine).astype(jnp.float32)
        low += KV_HEADS * new_count
        info_ref[low : low + new_count] = block_ref[:, column(KV_HEADS + head)].astype(jnp.float32)

    def info_copy(part, low, high):
        part_rows = pl.ds(low, high - low)
        return pltpu.make_async_copy(info_ref.at[part_rows], info_any.at[part_rows], info_sems.at[part])

    info_copy(0, at["new"], rows).start()
    info_ref[at["cos"] : at["cos"] + new_count] = cosine
    info_ref[at["sin"] : at["sin"] + new_count] = sine
    per_row = HEAD_DIM // slots
    row = lax.broadcasted_iota(jnp.int32, (8, HEAD_DIM), 0)
    lane = lax.broadcasted_iota(jnp.int32, (8, HEAD_DIM), 1)
    piece, slot = row * per_row + lane // slots, lane % slots
    holder, requests, residues = jnp.zeros_like(lane), jnp.zeros_like(lane), jnp.zeros_like(lane)
    for p in range(groups):
        other = me ^ order[p]
        holder = jnp.where(piece == p, other, holder)
        requests = jnp.where(lane == p, assign_ref[other], requests)
        residues = jnp.where(lane == p, residue_ref[other], residues)
    bias = jnp.full((8, HEAD_DIM), MASKED, jnp.float32)
    for residue in range(groups):
        live = (holder == stripe_ref[request, residue]) & (slot * groups + residue < length)
        bias = jnp.where(live, 0.0, bias)
    info_ref[at["bias"] : at["bias"] + 8] = bias
    scalars = jnp.where(row == 0, requests, residues)
    info_ref[at["scalars"] : at["scalars"] + 8] = scalars.astype(jnp.float32)
    info_copy(1, 0, at["new"]).start()
    for copy in pool_copies:
        copy.wait()
    sends = []
    for p in range(AHEAD):
        pack_ref[p, :, 0:width] = pool_ref[assign_ref[me ^ order[p]]]
        for lanes in range(quarter):
            pack_ref[p, :, width + lanes * HEAD_DIM : width + (lanes + 1) * HEAD_DIM] = fresh_rows(
                info_ref, at["new"], residue_ref[me ^ order[p]], new_count, count, quarter, lanes
            ).astype(jnp.bfloat16)
        sends.append(pltpu.make_async_copy(pack_ref.at[p], send_refs[p], send_sems.at[p]))
        sends[-1].start()
    for copy in sends:
        copy.wait()
    info_copy(0, at["new"], rows).wait()
    info_copy(1, 0, at["new"]).wait()


def front(order, me, assignment, prefix_len, owner_map, stripe_map, block_kv, table, pool):
    groups, slots, width = pool.shape
    new_count = block_kv.shape[0]
    count = new_count // groups
    block = jax.ShapeDtypeStruct((slots, width + width * count // slots), jnp.bfloat16)
    info = jax.ShapeDtypeStruct((info_rows(new_count)[1], HEAD_DIM), jnp.float32)
    *blocks, info = pl.pallas_call(
        functools.partial(front_kernel, order),
        out_shape=[block] * AHEAD + [info],
        in_specs=[SMEM] + [ANY] * 7,
        out_specs=[ANY] * (AHEAD + 1),
        scratch_shapes=[
            pltpu.SMEM(assignment.shape, jnp.int32),
            pltpu.SMEM(prefix_len.shape, jnp.int32),
            pltpu.SMEM(owner_map.shape, jnp.int32),
            pltpu.SMEM(stripe_map.shape, jnp.int32),
            pltpu.SMEM(assignment.shape, jnp.int32),
            pltpu.VMEM(block_kv.shape, jnp.bfloat16),
            pltpu.VMEM(table.shape, jnp.float32),
            pltpu.VMEM(pool.shape, jnp.bfloat16),
            pltpu.VMEM((AHEAD,) + block.shape, jnp.bfloat16),
            pltpu.VMEM(info.shape, jnp.float32),
            pltpu.SemaphoreType.DMA((6,)),
            pltpu.SemaphoreType.DMA((groups // 4,)),
            pltpu.SemaphoreType.DMA((AHEAD,)),
            pltpu.SemaphoreType.DMA((2,)),
        ],
        compiler_params=params(60),
        name="front",
    )(me, assignment, prefix_len, owner_map, stripe_map, block_kv, table, pool)
    return blocks, info


def pack_kernel(info_ref, pool_ref, *refs):
    groups, slots, width = pool_ref.shape
    targets, (scalar_ref, scalar_sem) = refs[: groups - AHEAD], refs[groups - AHEAD :]
    new_count = slots * groups * (targets[0].shape[1] - width) // width
    at, _ = info_rows(new_count)
    count = new_count // groups
    quarter = (targets[0].shape[1] - width) // HEAD_DIM
    scalar_copy = pltpu.make_async_copy(info_ref.at[pl.ds(at["scalars"], 8)], scalar_ref, scalar_sem)
    scalar_copy.start()
    scalar_copy.wait()
    for p, target in enumerate(targets, AHEAD):
        target[:, 0:width] = pool_ref[scalar_ref[0, p].astype(jnp.int32)]
        residue = scalar_ref[1, p].astype(jnp.int32)
        for lanes in range(quarter):
            target[:, width + lanes * HEAD_DIM : width + (lanes + 1) * HEAD_DIM] = fresh_rows(
                info_ref, at["new"], residue, new_count, count, quarter, lanes
            ).astype(jnp.bfloat16)


def pack_others(info, pool, new_count):
    groups, slots, width = pool.shape
    block = (slots, width + width * (new_count // groups) // slots)
    return pl.pallas_call(
        pack_kernel,
        out_shape=[jax.ShapeDtypeStruct(block, jnp.bfloat16)] * (groups - AHEAD),
        in_specs=[VMEM] * 2,
        out_specs=[VMEM] * (groups - AHEAD),
        scratch_shapes=[pltpu.SMEM((8, HEAD_DIM), jnp.float32), pltpu.SemaphoreType.DMA],
        compiler_params=params(32),
        name="pack_others",
    )(info, pool)


def query_kernel(info_ref, q_ref, rot_ref, own_ref, bias_ref, request_ref):
    new_count = q_ref.shape[0]
    at, _ = info_rows(new_count)
    cosine = info_ref[at["cos"] : at["cos"] + new_count]
    sine = info_ref[at["sin"] : at["sin"] + new_count]
    for row in range(bias_ref.shape[1] // HEAD_DIM):
        line = info_ref[at["bias"] + row : at["bias"] + row + 1]
        bias_ref[:, column(row)] = jnp.broadcast_to(line, (8, HEAD_DIM))
    request_ref[...] = info_ref[at["scalars"] : at["scalars"] + 8].astype(jnp.int32)
    for head in range(2 * KV_HEADS):
        rows = at["new"] + head * new_count
        own_ref[head] = info_ref[rows : rows + new_count].astype(jnp.bfloat16)
    for head in range(Q_HEADS):
        rows = slice((head % PER_KV) * new_count, (head % PER_KV + 1) * new_count)
        rot_ref[head // PER_KV, rows, :] = turn(q_ref[:, column(head)], cosine, sine)


def rotate_queries(info, queries, span):
    new_count = queries.shape[0]
    return pl.pallas_call(
        query_kernel,
        out_shape=(
            jax.ShapeDtypeStruct((KV_HEADS, PER_KV * new_count, HEAD_DIM), jnp.bfloat16),
            jax.ShapeDtypeStruct((2 * KV_HEADS, new_count, HEAD_DIM), jnp.bfloat16),
            jax.ShapeDtypeStruct((8, span), jnp.float32),
            jax.ShapeDtypeStruct((8, HEAD_DIM), jnp.int32),
        ),
        in_specs=[VMEM] * 2,
        out_specs=[VMEM] * 4,
        compiler_params=params(32),
        name="rotate_queries",
    )(info, queries)


def quotient(summed, total):
    about = pl.reciprocal(total, approx=True)
    return summed * (about * (2.0 - total * about))


def join_keys(keys, values, got_refs, own_ref, head):
    key_parts = [got[:, column(head)] for got in got_refs]
    value_parts = [got[:, column(KV_HEADS + head)] for got in got_refs]
    if own_ref is not None:
        key_parts.append(own_ref[head])
        value_parts.append(own_ref[KV_HEADS + head])
    keys[head] = jnp.concatenate(key_parts, axis=0)
    value = jnp.concatenate(value_parts, axis=0)
    values[head] = jnp.concatenate([value, jnp.ones_like(value)], axis=1)


def dot_keys(query, keys):
    return lax.dot_general(query, keys, (((1,), (1,)), ((), ())), preferred_element_type=jnp.float32)


def staged(total, score, weigh, mix, finish, beside=None):
    scores, weights = {0: score(0)}, {}
    for at in range(total + 1):
        if at + 1 < total:
            scores[at + 1] = score(at + 1)
        if at >= 1:
            mixed = mix(at - 1, weights.pop(at - 1))
        if at < total:
            weights[at] = weigh(at, scores.pop(at))
        if at >= 1:
            finish(at - 1, mixed)
        if at == 1 and beside is not None:
            beside()


def unpacking(fresh_refs, first, request_vmem, decode_ref, rows_ref, request_ref, request_sem, decode_sems):
    count = rows_ref.shape[1]
    request_copy = pltpu.make_async_copy(request_vmem, request_ref, request_sem)
    request_copy.start()

    def decode_copy(p):
        return pltpu.make_async_copy(
            rows_ref.at[p], decode_ref.at[request_ref[0, first + p]], decode_sems.at[p]
        )

    def start():
        request_copy.wait()
        for p, fresh_ref in enumerate(fresh_refs):
            stack = fresh_ref[...]
            quarter = stack.shape[1]
            for part in range(stack.shape[0] // count):
                rows_ref[p, :, part * quarter : (part + 1) * quarter] = stack[part * count : (part + 1) * count]
            decode_copy(p).start()

    def wait():
        for p in range(len(fresh_refs)):
            decode_copy(p).wait()

    return start, wait


def spare_part(got):
    return got.at[:, pl.ds(WIDTH, got.shape[1] - WIDTH)]


def pieces_of(refs):
    pieces = []
    for ref in refs:
        pieces += [ref] if len(ref.shape) == 2 else [ref.at[i] for i in range(ref.shape[0])]
    return pieces


def attend_kernel(arrays, unpack, rot_ref, bias_ref, own_ref, *refs):
    got_refs, refs = pieces_of(refs[:arrays]), refs[arrays:]
    start, wait = None, None
    if unpack:
        request_vmem, result_ref, level_ref, decode_ref, *scratch = refs
        start, wait = unpacking([spare_part(got) for got in got_refs], 0, request_vmem, decode_ref, *scratch)
    else:
        result_ref, level_ref = refs
    new_count = rot_ref.shape[1] // PER_KV
    span = len(got_refs) * got_refs[0].shape[0]
    token = lax.broadcasted_iota(jnp.int32, (CHUNK, new_count), 0) % new_count
    causal = jnp.where(lax.broadcasted_iota(jnp.int32, (CHUNK, new_count), 1) <= token, 0.0, MASKED)
    bias = bias_ref[0:1, 0:span]
    per_head = PER_KV * new_count // CHUNK
    keys, values, highs = {}, {}, {}

    def place(at):
        return at // per_head, slice(at % per_head * CHUNK, (at % per_head + 1) * CHUNK)

    def score(at):
        head, rows = place(at)
        if at % per_head == 0:
            join_keys(keys, values, got_refs, own_ref, head)
        return dot_keys(rot_ref[head, rows, :], keys[head])

    def weigh(at, scores):
        scores = jnp.concatenate([scores[:, :span] * SCALE + bias, scores[:, span:] * SCALE + causal], axis=1)
        highs[at] = jnp.max(scores, axis=1, keepdims=True)
        return jnp.exp2(scores - highs[at]).astype(jnp.bfloat16)

    def mix(at, weights):
        return jnp.dot(weights, values[at // per_head], preferred_element_type=jnp.float32)

    def finish(at, mixed):
        head, rows = place(at)
        total = mixed[:, HEAD_DIM:]
        result_ref[head, rows, :] = quotient(mixed[:, :HEAD_DIM], total)
        level_ref[head, rows, :] = highs.pop(at) + jnp.log2(total)

    staged(KV_HEADS * per_head, score, weigh, mix, finish, start)
    if unpack:
        wait()


def attend(rot, bias, own, got, requests=None):
    rows, new_count = rot.shape[1], rot.shape[1] // PER_KV
    operands = [rot, bias, own, *got]
    shapes = [jax.ShapeDtypeStruct((KV_HEADS, rows, HEAD_DIM), jnp.float32)] * 2
    out_specs, scratch = [VMEM] * 2, []
    if requests is not None:
        operands.append(requests)
        slots, width = got[-1].shape
        count = (width - WIDTH) * slots // WIDTH
        shapes.append(jax.ShapeDtypeStruct((new_count // count, count, WIDTH), jnp.bfloat16))
        out_specs.append(ANY)
        scratch = unpack_scratch(len(pieces_of(got)), count, requests)
    return pl.pallas_call(
        functools.partial(attend_kernel, len(got), requests is not None),
        out_shape=tuple(shapes),
        in_specs=[VMEM] * len(operands),
        out_specs=tuple(out_specs),
        scratch_shapes=scratch,
        compiler_params=params(32),
        name="attend",
    )(*operands)


def unpack_scratch(pieces, count, requests):
    return [
        pltpu.VMEM((pieces, count, WIDTH), jnp.bfloat16),
        pltpu.SMEM(requests.shape, jnp.int32),
        pltpu.SemaphoreType.DMA,
        pltpu.SemaphoreType.DMA((pieces,)),
    ]


HEADROOM = 96.0


def late_kernel(pieces, first, rot_ref, bias_ref, result_ref, level_ref, *refs):
    got_refs, refs = refs[:pieces], refs[pieces:]
    request_vmem, _, out_ref, decode_ref, done_ref, out_sems, *scratch = refs
    start, wait = unpacking([spare_part(got) for got in got_refs], first, request_vmem, decode_ref, *scratch)
    slots = got_refs[0].shape[0]
    new_count = out_ref.shape[0]
    size = LATE_CHUNK
    heads_in = size // new_count
    bias = bias_ref[0:1, first * slots : (first + pieces) * slots]
    per_head = PER_KV * new_count // size
    chunks = KV_HEADS * per_head
    keys, values, excess = {}, {}, []

    def place(at):
        return at // per_head, slice(at % per_head * size, (at % per_head + 1) * size)

    def out_copy(at):
        width = heads_in * HEAD_DIM
        return pltpu.make_async_copy(
            done_ref.at[at], out_ref.at[:, pl.ds(pl.multiple_of(at * width, width), width)], out_sems.at[at]
        )

    def store(at, result):
        for row in range(heads_in):
            done_ref[at, :, column(row)] = result[row * new_count : (row + 1) * new_count].astype(jnp.bfloat16)
        out_copy(at).start()

    def score(at):
        head, rows = place(at)
        if at % per_head == 0:
            join_keys(keys, values, got_refs, None, head)
        return dot_keys(rot_ref[head, rows, :], keys[head])

    def weigh(at, scores):
        head, rows = place(at)
        powers = scores * SCALE + bias - level_ref[head, rows, :]
        excess.append(jnp.max(powers.reshape(size // 8, 8, HEAD_DIM), axis=0))
        return jnp.exp2(powers).astype(jnp.bfloat16)

    def mix(at, weights):
        return jnp.dot(weights, values[at // per_head], preferred_element_type=jnp.float32)

    def finish(at, mixed):
        head, rows = place(at)
        store(at, quotient(result_ref[head, rows, :] + mixed[:, :HEAD_DIM], 1.0 + mixed[:, HEAD_DIM:]))

    staged(chunks, score, weigh, mix, finish, start)
    most = jnp.max(functools.reduce(jnp.maximum, excess))
    wait()
    for at in range(chunks):
        out_copy(at).wait()

    @pl.when(most > HEADROOM)
    def _():
        for head in range(KV_HEADS):

            def again(chunk, carry, head=head):
                rows = pl.ds(pl.multiple_of(chunk * size, size), size)
                scores = dot_keys(rot_ref[head, rows, :], keys[head]) * SCALE + bias
                level = level_ref[head, rows, :]
                high = jnp.maximum(level, jnp.max(scores, axis=1, keepdims=True))
                factor = jnp.exp2(level - high)
                weights = jnp.exp2(scores - high).astype(jnp.bfloat16)
                mixed = jnp.dot(weights, values[head], preferred_element_type=jnp.float32)
                at = head * per_head + chunk
                summed = result_ref[head, rows, :] * factor + mixed[:, :HEAD_DIM]
                store(at, quotient(summed, factor + mixed[:, HEAD_DIM:]))
                out_copy(at).wait()
                return carry

            lax.fori_loop(0, per_head, again, 0)


def attend_late(rot, bias, result, level, got, first, requests, decode):
    rows, new_count = rot.shape[1], rot.shape[1] // PER_KV
    operands = [rot, bias, result, level, *got, requests, decode]
    chunks = KV_HEADS * rows // LATE_CHUNK
    return pl.pallas_call(
        functools.partial(late_kernel, len(got), first),
        out_shape=(
            jax.ShapeDtypeStruct((new_count, Q_HEADS * HEAD_DIM), jnp.bfloat16),
            jax.ShapeDtypeStruct(decode.shape, jnp.bfloat16),
        ),
        in_specs=[VMEM] * (len(operands) - 1) + [ANY],
        out_specs=(ANY, ANY),
        scratch_shapes=[
            pltpu.VMEM((chunks, new_count, LATE_CHUNK // new_count * HEAD_DIM), jnp.bfloat16),
            pltpu.SemaphoreType.DMA((chunks,)),
        ]
        + unpack_scratch(len(got), decode.shape[1], requests),
        input_output_aliases={len(operands) - 1: 1},
        compiler_params=params(32),
        name="attend_late",
    )(*operands)


def inverse(table):
    places = jnp.arange(table.shape[0], dtype=jnp.int32)
    return jnp.sum(jnp.where(table[None, :] == places[:, None], places, 0), axis=1)


def rotate(rows, positions, heads):
    half = HEAD_DIM // 2
    freqs = ROPE_BASE ** (-jnp.arange(half, dtype=jnp.float32) / half)
    angles = positions.astype(jnp.float32)[:, None] * freqs[None, :]
    cosine = jnp.concatenate([jnp.cos(angles)] * 2, axis=-1)[:, None, :]
    sine = jnp.concatenate([-jnp.sin(angles), jnp.sin(angles)], axis=-1)[:, None, :]
    split = rows.astype(jnp.float32).reshape(rows.shape[0], heads, HEAD_DIM)
    turned = jnp.roll(split, half, axis=-1)
    return (split * cosine + turned * sine).astype(jnp.bfloat16)


def small_pieces(me, assignment, prefix_len, stripe_map, owner_map, queries, block_kv, pool):
    groups, slots, width = pool.shape
    new_count = block_kv.shape[0]
    count = new_count // groups
    request = assignment[me[0]]
    length = prefix_len[request]
    positions = length + jnp.arange(new_count, dtype=jnp.int32)
    rot = rotate(queries, positions, Q_HEADS).reshape(new_count, KV_HEADS, PER_KV, HEAD_DIM)
    rot = jnp.transpose(rot, (1, 2, 0, 3)).reshape(KV_HEADS, PER_KV * new_count, HEAD_DIM)
    new_keys = rotate(block_kv[:, :KV_WIDTH], positions, KV_HEADS).reshape(new_count, KV_WIDTH)
    new_kv = jnp.concatenate([new_keys, block_kv[:, KV_WIDTH:]], axis=1)
    own = jnp.transpose(new_kv.reshape(new_count, 2 * KV_HEADS, HEAD_DIM), (1, 0, 2))
    spread = jnp.transpose(new_kv.reshape(count, groups, width), (1, 0, 2))
    send = jnp.concatenate([pool[assignment], spread[inverse(owner_map[request])]], axis=1)
    got = lax.all_to_all(send, "pg", split_axis=0, concat_axis=0, tiled=True)
    located = jnp.arange(slots, dtype=jnp.int32)[None, :] * groups + inverse(stripe_map[request])[:, None]
    bias = jnp.where(located < length, 0.0, MASKED).astype(jnp.float32).reshape(1, groups * slots)
    keys = got[:, :slots].reshape(groups * slots, width)
    result, _ = attend(rot, jnp.broadcast_to(bias, (8, groups * slots)), own, [keys])
    result = result.astype(jnp.bfloat16).reshape(KV_HEADS, PER_KV, new_count, HEAD_DIM)
    attended = jnp.transpose(result, (2, 0, 1, 3)).reshape(new_count, Q_HEADS * HEAD_DIM)
    return attended, got[inverse(assignment), slots:]


def shards(queries, block_kv, pool_kv, prefix_len, assignment, stripe_map, owner_map):
    queries, block_kv, pool = queries[0], block_kv[0], pool_kv[0]
    groups, slots, width = pool.shape
    new_count = queries.shape[0]
    count = new_count // groups
    me = lax.axis_index("pg").astype(jnp.int32).reshape(1)
    if groups != 16 or slots % 16 or HEAD_DIM % slots or count % 8 or slots % count:
        attended, decode_kv = small_pieces(
            me, assignment, prefix_len, stripe_map, owner_map, queries, block_kv, pool
        )
        return (attended[None], decode_kv[None])
    order = order_of(groups)
    table = rotation_tables(new_count)
    blocks, info = front(order, me, assignment, prefix_len, owner_map, stripe_map, block_kv, table, pool)
    blocks = list(blocks) + list(pack_others(info, pool, new_count))
    rot, own, bias, requests = rotate_queries(info, queries, groups * slots)
    rot, *blocks[AHEAD_OF_QUERIES:] = lax.optimization_barrier((rot, *blocks[AHEAD_OF_QUERIES:]))
    got = [
        lax.ppermute(block, "pg", [(source, source ^ t) for source in range(groups)]) if t else block
        for block, t in zip(blocks, order)
    ]
    soon = groups - LATE
    result, level, decode_kv = attend(rot, bias, own, got[:soon], requests)
    attended, decode_kv = attend_late(rot, bias, result, level, got[soon:], soon, requests, decode_kv)
    return (attended[None], decode_kv[None])


def solution(mesh):
    return jax.shard_map(
        shards,
        mesh=mesh,
        in_specs=(
            P(("rep", "pg"), None, None),
            P(("rep", "pg"), None, None),
            P(("rep", "pg"), None, None, None),
            P("rep"),
            P("rep"),
            P("rep", None),
            P("rep", None),
        ),
        out_specs=(P(("rep", "pg"), None, None), P(("rep", "pg"), None, None, None)),
        check_vma=False,
    )
```

```python
import functools
import math

import jax
import jax.numpy as jnp
import numpy as np
from jax import lax
from jax.experimental import pallas as pl
from jax.experimental.pallas import tpu as pltpu
from jax.sharding import PartitionSpec as P

Q_HEADS = 32
KV_HEADS = 4
HEAD_DIM = 128
PER_KV = Q_HEADS // KV_HEADS
KV_WIDTH = KV_HEADS * HEAD_DIM
WIDTH = 2 * KV_WIDTH

ROPE_BASE = 1000000.0
MASKED = -1e30
SCALE = HEAD_DIM ** -0.5 / math.log(2.0)
CHUNK = 256
LATE = 4
LATE_CHUNK = 512
AHEAD = 5
AHEAD_OF_QUERIES = 8

SMEM = pl.BlockSpec(memory_space=pltpu.SMEM)
VMEM = pl.BlockSpec(memory_space=pltpu.VMEM)
ANY = pl.BlockSpec(memory_space=pl.ANY)


def params(mib):
    return pltpu.CompilerParams(vmem_limit_bytes=mib * 1024 * 1024)


def column(head):
    return slice(head * HEAD_DIM, (head + 1) * HEAD_DIM)


def order_of(groups):
    half = groups // 2
    near = list(range(half - 1, 0, -1))
    quarter, eighth = half // 2, half // 4
    far = [half + (at // 2 if at % 2 == 0 else quarter + (at // 2 ^ eighth)) for at in range(half)]
    order = [(far if kind == "f" else near).pop(0) for kind in "ffnfnfnfnfnfnfn"]
    order.insert(groups - LATE - 1, 0)
    return order


def rotation_tables(rows):
    half = HEAD_DIM // 2
    freqs = np.tile(ROPE_BASE ** (-np.arange(half, dtype=np.float64) / half), 2)
    angles = np.arange(rows, dtype=np.float64)[:, None] * freqs[None, :]
    parts = [np.cos(angles), np.sin(angles), np.tile(freqs, (8, 1))]
    return jnp.asarray(np.concatenate(parts, axis=0).astype(np.float32))


def rotation(table_ref, length):
    rows = (table_ref.shape[0] - 8) // 2
    start = length.astype(jnp.float32) * table_ref[2 * rows : 2 * rows + 8, :]
    cos_start, sin_start = jnp.cos(start)[0:1], jnp.sin(start)[0:1]
    cos_row, sin_row = table_ref[0:rows, :], table_ref[rows : 2 * rows, :]
    lane = lax.broadcasted_iota(jnp.int32, (1, HEAD_DIM), 1)
    sign = jnp.where(lane < HEAD_DIM // 2, -1.0, 1.0)
    cosine = cos_row * cos_start - sin_row * sin_start
    return cosine, sin_row * (cos_start * sign) + cos_row * (sin_start * sign)


def turn(x, cosine, sine):
    x = x.astype(jnp.float32)
    return (x * cosine + pltpu.roll(x, HEAD_DIM // 2, 1) * sine).astype(jnp.bfloat16)


def info_rows(new_count):
    sizes = [("cos", new_count), ("sin", new_count), ("bias", 8), ("scalars", 8), ("new", 2 * KV_HEADS * new_count)]
    at, rows = 0, {}
    for name, size in sizes:
        rows[name] = at
        at += size
    return rows, at


def fresh_rows(info_ref, base, residue, new_count, count, quarter, lanes):
    groups = new_count // count
    stack = [
        info_ref[pl.ds(base + (head + lanes) * new_count + residue, count, stride=groups), :]
        for head in range(0, 2 * KV_HEADS, quarter)
    ]
    return jnp.concatenate(stack, axis=0)


def front_kernel(
    order, me_ref, assign_any, length_any, owner_any, stripe_any, block_any, table_any, pool_any, *refs
):
    groups, slots, width = pool_any.shape
    send_refs, info_any, refs = refs[:AHEAD], refs[AHEAD], refs[AHEAD + 1 :]
    (assign_ref, length_ref, owner_ref, stripe_ref, residue_ref, block_ref, table_ref, pool_ref, pack_ref, info_ref,
     small_sems, pool_sems, send_sems, info_sems) = refs
    new_count = block_any.shape[0]
    count = new_count // groups
    quarter = width * count // slots // HEAD_DIM
    at, rows = info_rows(new_count)
    pairs = [
        (assign_any, assign_ref), (length_any, length_ref), (owner_any, owner_ref), (stripe_any, stripe_ref),
        (block_any, block_ref), (table_any, table_ref),
    ]
    smalls = [pltpu.make_async_copy(*pair, small_sems.at[i]) for i, pair in enumerate(pairs)]
    for copy in smalls:
        copy.start()
    pool_copies = [
        pltpu.make_async_copy(pool_any.at[pl.ds(low, 4)], pool_ref.at[pl.ds(low, 4)], pool_sems.at[low // 4])
        for low in range(0, groups, 4)
    ]
    for copy in pool_copies:
        copy.start()
    me = me_ref[0]
    for copy in smalls:
        copy.wait()
    request = assign_ref[me]
    length = length_ref[request]
    for residue in range(groups):
        residue_ref[owner_ref[request, residue]] = residue
    cosine, sine = rotation(table_ref, length)
    for head in range(KV_HEADS):
        low = at["new"] + head * new_count
        info_ref[low : low + new_count] = turn(block_ref[:, column(head)], cosine, sine).astype(jnp.float32)
        low += KV_HEADS * new_count
        info_ref[low : low + new_count] = block_ref[:, column(KV_HEADS + head)].astype(jnp.float32)

    def info_copy(part, low, high):
        part_rows = pl.ds(low, high - low)
        return pltpu.make_async_copy(info_ref.at[part_rows], info_any.at[part_rows], info_sems.at[part])

    info_copy(0, at["new"], rows).start()
    info_ref[at["cos"] : at["cos"] + new_count] = cosine
    info_ref[at["sin"] : at["sin"] + new_count] = sine
    per_row = HEAD_DIM // slots
    row = lax.broadcasted_iota(jnp.int32, (8, HEAD_DIM), 0)
    lane = lax.broadcasted_iota(jnp.int32, (8, HEAD_DIM), 1)
    piece, slot = row * per_row + lane // slots, lane % slots
    holder, requests, residues = jnp.zeros_like(lane), jnp.zeros_like(lane), jnp.zeros_like(lane)
    for p in range(groups):
        other = me ^ order[p]
        holder = jnp.where(piece == p, other, holder)
        requests = jnp.where(lane == p, assign_ref[other], requests)
        residues = jnp.where(lane == p, residue_ref[other], residues)
    bias = jnp.full((8, HEAD_DIM), MASKED, jnp.float32)
    for residue in range(groups):
        live = (holder == stripe_ref[request, residue]) & (slot * groups + residue < length)
        bias = jnp.where(live, 0.0, bias)
    info_ref[at["bias"] : at["bias"] + 8] = bias
    scalars = jnp.where(row == 0, requests, residues)
    info_ref[at["scalars"] : at["scalars"] + 8] = scalars.astype(jnp.float32)
    info_copy(1, 0, at["new"]).start()
    for copy in pool_copies:
        copy.wait()
    sends = []
    for p in range(AHEAD):
        pack_ref[p, :, 0:width] = pool_ref[assign_ref[me ^ order[p]]]
        for lanes in range(quarter):
            pack_ref[p, :, width + lanes * HEAD_DIM : width + (lanes + 1) * HEAD_DIM] = fresh_rows(
                info_ref, at["new"], residue_ref[me ^ order[p]], new_count, count, quarter, lanes
            ).astype(jnp.bfloat16)
        sends.append(pltpu.make_async_copy(pack_ref.at[p], send_refs[p], send_sems.at[p]))
        sends[-1].start()
    for copy in sends:
        copy.wait()
    info_copy(0, at["new"], rows).wait()
    info_copy(1, 0, at["new"]).wait()


def front(order, me, assignment, prefix_len, owner_map, stripe_map, block_kv, table, pool):
    groups, slots, width = pool.shape
    new_count = block_kv.shape[0]
    count = new_count // groups
    block = jax.ShapeDtypeStruct((slots, width + width * count // slots), jnp.bfloat16)
    info = jax.ShapeDtypeStruct((info_rows(new_count)[1], HEAD_DIM), jnp.float32)
    *blocks, info = pl.pallas_call(
        functools.partial(front_kernel, order),
        out_shape=[block] * AHEAD + [info],
        in_specs=[SMEM] + [ANY] * 7,
        out_specs=[ANY] * (AHEAD + 1),
        scratch_shapes=[
            pltpu.SMEM(assignment.shape, jnp.int32),
            pltpu.SMEM(prefix_len.shape, jnp.int32),
            pltpu.SMEM(owner_map.shape, jnp.int32),
            pltpu.SMEM(stripe_map.shape, jnp.int32),
            pltpu.SMEM(assignment.shape, jnp.int32),
            pltpu.VMEM(block_kv.shape, jnp.bfloat16),
            pltpu.VMEM(table.shape, jnp.float32),
            pltpu.VMEM(pool.shape, jnp.bfloat16),
            pltpu.VMEM((AHEAD,) + block.shape, jnp.bfloat16),
            pltpu.VMEM(info.shape, jnp.float32),
            pltpu.SemaphoreType.DMA((6,)),
            pltpu.SemaphoreType.DMA((groups // 4,)),
            pltpu.SemaphoreType.DMA((AHEAD,)),
            pltpu.SemaphoreType.DMA((2,)),
        ],
        compiler_params=params(60),
        name="front",
    )(me, assignment, prefix_len, owner_map, stripe_map, block_kv, table, pool)
    return blocks, info


def pack_kernel(info_ref, pool_ref, *refs):
    groups, slots, width = pool_ref.shape
    targets, (scalar_ref, scalar_sem) = refs[: groups - AHEAD], refs[groups - AHEAD :]
    new_count = slots * groups * (targets[0].shape[1] - width) // width
    at, _ = info_rows(new_count)
    count = new_count // groups
    quarter = (targets[0].shape[1] - width) // HEAD_DIM
    scalar_copy = pltpu.make_async_copy(info_ref.at[pl.ds(at["scalars"], 8)], scalar_ref, scalar_sem)
    scalar_copy.start()
    scalar_copy.wait()
    for p, target in enumerate(targets, AHEAD):
        target[:, 0:width] = pool_ref[scalar_ref[0, p].astype(jnp.int32)]
        residue = scalar_ref[1, p].astype(jnp.int32)
        for lanes in range(quarter):
            target[:, width + lanes * HEAD_DIM : width + (lanes + 1) * HEAD_DIM] = fresh_rows(
                info_ref, at["new"], residue, new_count, count, quarter, lanes
            ).astype(jnp.bfloat16)


def pack_others(info, pool, new_count):
    groups, slots, width = pool.shape
    block = (slots, width + width * (new_count // groups) // slots)
    return pl.pallas_call(
        pack_kernel,
        out_shape=[jax.ShapeDtypeStruct(block, jnp.bfloat16)] * (groups - AHEAD),
        in_specs=[VMEM] * 2,
        out_specs=[VMEM] * (groups - AHEAD),
        scratch_shapes=[pltpu.SMEM((8, HEAD_DIM), jnp.float32), pltpu.SemaphoreType.DMA],
        compiler_params=params(32),
        name="pack_others",
    )(info, pool)


def query_kernel(info_ref, q_ref, rot_ref, own_ref, bias_ref, request_ref):
    new_count = q_ref.shape[0]
    at, _ = info_rows(new_count)
    cosine = info_ref[at["cos"] : at["cos"] + new_count]
    sine = info_ref[at["sin"] : at["sin"] + new_count]
    for row in range(bias_ref.shape[1] // HEAD_DIM):
        line = info_ref[at["bias"] + row : at["bias"] + row + 1]
        bias_ref[:, column(row)] = jnp.broadcast_to(line, (8, HEAD_DIM))
    request_ref[...] = info_ref[at["scalars"] : at["scalars"] + 8].astype(jnp.int32)
    for head in range(2 * KV_HEADS):
        rows = at["new"] + head * new_count
        own_ref[head] = info_ref[rows : rows + new_count].astype(jnp.bfloat16)
    for head in range(Q_HEADS):
        rows = slice((head % PER_KV) * new_count, (head % PER_KV + 1) * new_count)
        rot_ref[head // PER_KV, rows, :] = turn(q_ref[:, column(head)], cosine, sine)


def rotate_queries(info, queries, span):
    new_count = queries.shape[0]
    return pl.pallas_call(
        query_kernel,
        out_shape=(
            jax.ShapeDtypeStruct((KV_HEADS, PER_KV * new_count, HEAD_DIM), jnp.bfloat16),
            jax.ShapeDtypeStruct((2 * KV_HEADS, new_count, HEAD_DIM), jnp.bfloat16),
            jax.ShapeDtypeStruct((8, span), jnp.float32),
            jax.ShapeDtypeStruct((8, HEAD_DIM), jnp.int32),
        ),
        in_specs=[VMEM] * 2,
        out_specs=[VMEM] * 4,
        compiler_params=params(32),
        name="rotate_queries",
    )(info, queries)


def quotient(summed, total):
    about = pl.reciprocal(total, approx=True)
    return summed * (about * (2.0 - total * about))


def join_keys(keys, values, got_refs, own_ref, head):
    key_parts = [got[:, column(head)] for got in got_refs]
    value_parts = [got[:, column(KV_HEADS + head)] for got in got_refs]
    if own_ref is not None:
        key_parts.append(own_ref[head])
        value_parts.append(own_ref[KV_HEADS + head])
    keys[head] = jnp.concatenate(key_parts, axis=0)
    value = jnp.concatenate(value_parts, axis=0)
    values[head] = jnp.concatenate([value, jnp.ones_like(value)], axis=1)


def dot_keys(query, keys):
    return lax.dot_general(query, keys, (((1,), (1,)), ((), ())), preferred_element_type=jnp.float32)


def staged(total, score, weigh, mix, finish, beside=None):
    scores, weights = {0: score(0)}, {}
    for at in range(total + 1):
        if at + 1 < total:
            scores[at + 1] = score(at + 1)
        if at >= 1:
            mixed = mix(at - 1, weights.pop(at - 1))
        if at < total:
            weights[at] = weigh(at, scores.pop(at))
        if at >= 1:
            finish(at - 1, mixed)
        if at == 1 and beside is not None:
            beside()


def unpacking(fresh_refs, first, request_vmem, decode_ref, rows_ref, request_ref, request_sem, decode_sems):
    count = rows_ref.shape[1]
    request_copy = pltpu.make_async_copy(request_vmem, request_ref, request_sem)
    request_copy.start()

    def decode_copy(p):
        return pltpu.make_async_copy(
            rows_ref.at[p], decode_ref.at[request_ref[0, first + p]], decode_sems.at[p]
        )

    def start():
        request_copy.wait()
        for p, fresh_ref in enumerate(fresh_refs):
            stack = fresh_ref[...]
            quarter = stack.shape[1]
            for part in range(stack.shape[0] // count):
                rows_ref[p, :, part * quarter : (part + 1) * quarter] = stack[part * count : (part + 1) * count]
            decode_copy(p).start()

    def wait():
        for p in range(len(fresh_refs)):
            decode_copy(p).wait()

    return start, wait


def spare_part(got):
    return got.at[:, pl.ds(WIDTH, got.shape[1] - WIDTH)]


def pieces_of(refs):
    pieces = []
    for ref in refs:
        pieces += [ref] if len(ref.shape) == 2 else [ref.at[i] for i in range(ref.shape[0])]
    return pieces


def attend_kernel(arrays, unpack, rot_ref, bias_ref, own_ref, *refs):
    got_refs, refs = pieces_of(refs[:arrays]), refs[arrays:]
    start, wait = None, None
    if unpack:
        request_vmem, result_ref, level_ref, decode_ref, *scratch = refs
        start, wait = unpacking([spare_part(got) for got in got_refs], 0, request_vmem, decode_ref, *scratch)
    else:
        result_ref, level_ref = refs
    new_count = rot_ref.shape[1] // PER_KV
    span = len(got_refs) * got_refs[0].shape[0]
    token = lax.broadcasted_iota(jnp.int32, (CHUNK, new_count), 0) % new_count
    causal = jnp.where(lax.broadcasted_iota(jnp.int32, (CHUNK, new_count), 1) <= token, 0.0, MASKED)
    bias = bias_ref[0:1, 0:span]
    per_head = PER_KV * new_count // CHUNK
    keys, values, highs = {}, {}, {}

    def place(at):
        return at // per_head, slice(at % per_head * CHUNK, (at % per_head + 1) * CHUNK)

    def score(at):
        head, rows = place(at)
        if at % per_head == 0:
            join_keys(keys, values, got_refs, own_ref, head)
        return dot_keys(rot_ref[head, rows, :], keys[head])

    def weigh(at, scores):
        scores = jnp.concatenate([scores[:, :span] * SCALE + bias, scores[:, span:] * SCALE + causal], axis=1)
        highs[at] = jnp.max(scores, axis=1, keepdims=True)
        return jnp.exp2(scores - highs[at]).astype(jnp.bfloat16)

    def mix(at, weights):
        return jnp.dot(weights, values[at // per_head], preferred_element_type=jnp.float32)

    def finish(at, mixed):
        head, rows = place(at)
        total = mixed[:, HEAD_DIM:]
        result_ref[head, rows, :] = quotient(mixed[:, :HEAD_DIM], total)
        level_ref[head, rows, :] = highs.pop(at) + jnp.log2(total)

    staged(KV_HEADS * per_head, score, weigh, mix, finish, start)
    if unpack:
        wait()


def attend(rot, bias, own, got, requests=None):
    rows, new_count = rot.shape[1], rot.shape[1] // PER_KV
    operands = [rot, bias, own, *got]
    shapes = [jax.ShapeDtypeStruct((KV_HEADS, rows, HEAD_DIM), jnp.float32)] * 2
    out_specs, scratch = [VMEM] * 2, []
    if requests is not None:
        operands.append(requests)
        slots, width = got[-1].shape
        count = (width - WIDTH) * slots // WIDTH
        shapes.append(jax.ShapeDtypeStruct((new_count // count, count, WIDTH), jnp.bfloat16))
        out_specs.append(ANY)
        scratch = unpack_scratch(len(pieces_of(got)), count, requests)
    return pl.pallas_call(
        functools.partial(attend_kernel, len(got), requests is not None),
        out_shape=tuple(shapes),
        in_specs=[VMEM] * len(operands),
        out_specs=tuple(out_specs),
        scratch_shapes=scratch,
        compiler_params=params(32),
        name="attend",
    )(*operands)


def unpack_scratch(pieces, count, requests):
    return [
        pltpu.VMEM((pieces, count, WIDTH), jnp.bfloat16),
        pltpu.SMEM(requests.shape, jnp.int32),
        pltpu.SemaphoreType.DMA,
        pltpu.SemaphoreType.DMA((pieces,)),
    ]


HEADROOM = 96.0


def late_kernel(pieces, first, rot_ref, bias_ref, result_ref, level_ref, *refs):
    got_refs, refs = refs[:pieces], refs[pieces:]
    request_vmem, _, out_ref, decode_ref, done_ref, out_sems, *scratch = refs
    start, wait = unpacking([spare_part(got) for got in got_refs], first, request_vmem, decode_ref, *scratch)
    slots = got_refs[0].shape[0]
    new_count = out_ref.shape[0]
    size = LATE_CHUNK
    heads_in = size // new_count
    bias = bias_ref[0:1, first * slots : (first + pieces) * slots]
    per_head = PER_KV * new_count // size
    chunks = KV_HEADS * per_head
    keys, values, excess = {}, {}, []

    def place(at):
        return at // per_head, slice(at % per_head * size, (at % per_head + 1) * size)

    def out_copy(at):
        width = heads_in * HEAD_DIM
        return pltpu.make_async_copy(
            done_ref.at[at], out_ref.at[:, pl.ds(pl.multiple_of(at * width, width), width)], out_sems.at[at]
        )

    def store(at, result):
        for row in range(heads_in):
            done_ref[at, :, column(row)] = result[row * new_count : (row + 1) * new_count].astype(jnp.bfloat16)
        out_copy(at).start()

    def score(at):
        head, rows = place(at)
        if at % per_head == 0:
            join_keys(keys, values, got_refs, None, head)
        return dot_keys(rot_ref[head, rows, :], keys[head])

    def weigh(at, scores):
        head, rows = place(at)
        powers = scores * SCALE + bias - level_ref[head, rows, :]
        excess.append(jnp.max(powers.reshape(size // 8, 8, HEAD_DIM), axis=0))
        return jnp.exp2(powers).astype(jnp.bfloat16)

    def mix(at, weights):
        return jnp.dot(weights, values[at // per_head], preferred_element_type=jnp.float32)

    def finish(at, mixed):
        head, rows = place(at)
        store(at, quotient(result_ref[head, rows, :] + mixed[:, :HEAD_DIM], 1.0 + mixed[:, HEAD_DIM:]))

    staged(chunks, score, weigh, mix, finish, start)
    most = jnp.max(functools.reduce(jnp.maximum, excess))
    wait()
    for at in range(chunks):
        out_copy(at).wait()

    @pl.when(most > HEADROOM)
    def _():
        for head in range(KV_HEADS):

            def again(chunk, carry, head=head):
                rows = pl.ds(pl.multiple_of(chunk * size, size), size)
                scores = dot_keys(rot_ref[head, rows, :], keys[head]) * SCALE + bias
                level = level_ref[head, rows, :]
                high = jnp.maximum(level, jnp.max(scores, axis=1, keepdims=True))
                factor = jnp.exp2(level - high)
                weights = jnp.exp2(scores - high).astype(jnp.bfloat16)
                mixed = jnp.dot(weights, values[head], preferred_element_type=jnp.float32)
                at = head * per_head + chunk
                summed = result_ref[head, rows, :] * factor + mixed[:, :HEAD_DIM]
                store(at, quotient(summed, factor + mixed[:, HEAD_DIM:]))
                out_copy(at).wait()
                return carry

            lax.fori_loop(0, per_head, again, 0)


def attend_late(rot, bias, result, level, got, first, requests, decode):
    rows, new_count = rot.shape[1], rot.shape[1] // PER_KV
    operands = [rot, bias, result, level, *got, requests, decode]
    chunks = KV_HEADS * rows // LATE_CHUNK
    return pl.pallas_call(
        functools.partial(late_kernel, len(got), first),
        out_shape=(
            jax.ShapeDtypeStruct((new_count, Q_HEADS * HEAD_DIM), jnp.bfloat16),
            jax.ShapeDtypeStruct(decode.shape, jnp.bfloat16),
        ),
        in_specs=[VMEM] * (len(operands) - 1) + [ANY],
        out_specs=(ANY, ANY),
        scratch_shapes=[
            pltpu.VMEM((chunks, new_count, LATE_CHUNK // new_count * HEAD_DIM), jnp.bfloat16),
            pltpu.SemaphoreType.DMA((chunks,)),
        ]
        + unpack_scratch(len(got), decode.shape[1], requests),
        input_output_aliases={len(operands) - 1: 1},
        compiler_params=params(32),
        name="attend_late",
    )(*operands)


def inverse(table):
    places = jnp.arange(table.shape[0], dtype=jnp.int32)
    return jnp.sum(jnp.where(table[None, :] == places[:, None], places, 0), axis=1)


def rotate(rows, positions, heads):
    half = HEAD_DIM // 2
    freqs = ROPE_BASE ** (-jnp.arange(half, dtype=jnp.float32) / half)
    angles = positions.astype(jnp.float32)[:, None] * freqs[None, :]
    cosine = jnp.concatenate([jnp.cos(angles)] * 2, axis=-1)[:, None, :]
    sine = jnp.concatenate([-jnp.sin(angles), jnp.sin(angles)], axis=-1)[:, None, :]
    split = rows.astype(jnp.float32).reshape(rows.shape[0], heads, HEAD_DIM)
    turned = jnp.roll(split, half, axis=-1)
    return (split * cosine + turned * sine).astype(jnp.bfloat16)


def small_pieces(me, assignment, prefix_len, stripe_map, owner_map, queries, block_kv, pool):
    groups, slots, width = pool.shape
    new_count = block_kv.shape[0]
    count = new_count // groups
    request = assignment[me[0]]
    length = prefix_len[request]
    positions = length + jnp.arange(new_count, dtype=jnp.int32)
    rot = rotate(queries, positions, Q_HEADS).reshape(new_count, KV_HEADS, PER_KV, HEAD_DIM)
    rot = jnp.transpose(rot, (1, 2, 0, 3)).reshape(KV_HEADS, PER_KV * new_count, HEAD_DIM)
    new_keys = rotate(block_kv[:, :KV_WIDTH], positions, KV_HEADS).reshape(new_count, KV_WIDTH)
    new_kv = jnp.concatenate([new_keys, block_kv[:, KV_WIDTH:]], axis=1)
    own = jnp.transpose(new_kv.reshape(new_count, 2 * KV_HEADS, HEAD_DIM), (1, 0, 2))
    spread = jnp.transpose(new_kv.reshape(count, groups, width), (1, 0, 2))
    send = jnp.concatenate([pool[assignment], spread[inverse(owner_map[request])]], axis=1)
    got = lax.all_to_all(send, "pg", split_axis=0, concat_axis=0, tiled=True)
    located = jnp.arange(slots, dtype=jnp.int32)[None, :] * groups + inverse(stripe_map[request])[:, None]
    bias = jnp.where(located < length, 0.0, MASKED).astype(jnp.float32).reshape(1, groups * slots)
    keys = got[:, :slots].reshape(groups * slots, width)
    result, _ = attend(rot, jnp.broadcast_to(bias, (8, groups * slots)), own, [keys])
    result = result.astype(jnp.bfloat16).reshape(KV_HEADS, PER_KV, new_count, HEAD_DIM)
    attended = jnp.transpose(result, (2, 0, 1, 3)).reshape(new_count, Q_HEADS * HEAD_DIM)
    return attended, got[inverse(assignment), slots:]


def shards(queries, block_kv, pool_kv, prefix_len, assignment, stripe_map, owner_map):
    queries, block_kv, pool = queries[0], block_kv[0], pool_kv[0]
    groups, slots, width = pool.shape
    new_count = queries.shape[0]
    count = new_count // groups
    me = lax.axis_index("pg").astype(jnp.int32).reshape(1)
    if groups != 16 or slots % 16 or HEAD_DIM % slots or count % 8 or slots % count:
        attended, decode_kv = small_pieces(
            me, assignment, prefix_len, stripe_map, owner_map, queries, block_kv, pool
        )
        return (attended[None], decode_kv[None])
    order = order_of(groups)
    table = rotation_tables(new_count)
    blocks, info = front(order, me, assignment, prefix_len, owner_map, stripe_map, block_kv, table, pool)
    blocks = list(blocks) + list(pack_others(info, pool, new_count))
    rot, own, bias, requests = rotate_queries(info, queries, groups * slots)
    rot, *blocks[AHEAD_OF_QUERIES:] = lax.optimization_barrier((rot, *blocks[AHEAD_OF_QUERIES:]))
    got = [
        lax.ppermute(block, "pg", [(source, source ^ t) for source in range(groups)]) if t else block
        for block, t in zip(blocks, order)
    ]
    soon = groups - LATE
    result, level, decode_kv = attend(rot, bias, own, got[:soon], requests)
    attended, decode_kv = attend_late(rot, bias, result, level, got[soon:], soon, requests, decode_kv)
    return (attended[None], decode_kv[None])


def solution(mesh):
    return jax.shard_map(
        shards,
        mesh=mesh,
        in_specs=(
            P(("rep", "pg"), None, None),
            P(("rep", "pg"), None, None),
            P(("rep", "pg"), None, None, None),
            P("rep"),
            P("rep"),
            P("rep", None),
            P("rep", None),
        ),
        out_specs=(P(("rep", "pg"), None, None), P(("rep", "pg"), None, None, None)),
        check_vma=False,
    )
```

```python
import functools
import math

import jax
import jax.numpy as jnp
import numpy as np
from jax import lax
from jax.experimental import pallas as pl
from jax.experimental.pallas import tpu as pltpu
from jax.sharding import PartitionSpec as P

Q_HEADS = 32
KV_HEADS = 4
HEAD_DIM = 128
PER_KV = Q_HEADS // KV_HEADS
KV_WIDTH = KV_HEADS * HEAD_DIM
WIDTH = 2 * KV_WIDTH

ROPE_BASE = 1000000.0
MASKED = -1e30
SCALE = HEAD_DIM ** -0.5 / math.log(2.0)
CHUNK = 256
LATE = 4
LATE_CHUNK = 512
AHEAD = 4
AHEAD_OF_QUERIES = 8

SMEM = pl.BlockSpec(memory_space=pltpu.SMEM)
VMEM = pl.BlockSpec(memory_space=pltpu.VMEM)
ANY = pl.BlockSpec(memory_space=pl.ANY)


def params(mib):
    return pltpu.CompilerParams(vmem_limit_bytes=mib * 1024 * 1024)


def column(head):
    return slice(head * HEAD_DIM, (head + 1) * HEAD_DIM)


def order_of(groups):
    half = groups // 2
    near = list(range(half - 1, 0, -1))
    quarter = half // 2
    far = [half + (at // 2 if at % 2 == 0 else quarter + (at // 2 ^ (quarter - 1))) for at in range(half)]
    order = [(far if kind == "f" else near).pop(0) for kind in "ffnfnfnfnfnfnfn"]
    order.insert(groups - LATE - 1, 0)
    return order


def rotation_tables(rows):
    half = HEAD_DIM // 2
    freqs = np.tile(ROPE_BASE ** (-np.arange(half, dtype=np.float64) / half), 2)
    angles = np.arange(rows, dtype=np.float64)[:, None] * freqs[None, :]
    parts = [np.cos(angles), np.sin(angles), np.tile(freqs, (8, 1))]
    return jnp.asarray(np.concatenate(parts, axis=0).astype(np.float32))


def rotation(table_ref, length):
    rows = (table_ref.shape[0] - 8) // 2
    start = length.astype(jnp.float32) * table_ref[2 * rows : 2 * rows + 8, :]
    cos_start, sin_start = jnp.cos(start)[0:1], jnp.sin(start)[0:1]
    cos_row, sin_row = table_ref[0:rows, :], table_ref[rows : 2 * rows, :]
    lane = lax.broadcasted_iota(jnp.int32, (1, HEAD_DIM), 1)
    sign = jnp.where(lane < HEAD_DIM // 2, -1.0, 1.0)
    cosine = cos_row * cos_start - sin_row * sin_start
    return cosine, sin_row * (cos_start * sign) + cos_row * (sin_start * sign)


def turn(x, cosine, sine):
    x = x.astype(jnp.float32)
    return (x * cosine + pltpu.roll(x, HEAD_DIM // 2, 1) * sine).astype(jnp.bfloat16)


def info_rows(new_count):
    sizes = [("cos", new_count), ("sin", new_count), ("bias", 8), ("scalars", 8), ("new", 2 * KV_HEADS * new_count)]
    at, rows = 0, {}
    for name, size in sizes:
        rows[name] = at
        at += size
    return rows, at


def fresh_rows(info_ref, base, residue, new_count, count, quarter, lanes):
    groups = new_count // count
    stack = [
        info_ref[pl.ds(base + (head + lanes) * new_count + residue, count, stride=groups), :]
        for head in range(0, 2 * KV_HEADS, quarter)
    ]
    return jnp.concatenate(stack, axis=0)


def front_kernel(
    order, me_ref, assign_any, length_any, owner_any, stripe_any, block_any, table_any, pool_any, *refs
):
    groups, slots, width = pool_any.shape
    send_refs, info_any, refs = refs[:AHEAD], refs[AHEAD], refs[AHEAD + 1 :]
    (assign_ref, length_ref, owner_ref, stripe_ref, residue_ref, block_ref, table_ref, pool_ref, pack_ref, info_ref,
     small_sems, pool_sems, send_sems, info_sems) = refs
    new_count = block_any.shape[0]
    count = new_count // groups
    quarter = width * count // slots // HEAD_DIM
    at, rows = info_rows(new_count)
    pairs = [
        (assign_any, assign_ref), (length_any, length_ref), (owner_any, owner_ref), (stripe_any, stripe_ref),
        (block_any, block_ref), (table_any, table_ref),
    ]
    smalls = [pltpu.make_async_copy(*pair, small_sems.at[i]) for i, pair in enumerate(pairs)]
    for copy in smalls:
        copy.start()
    pool_copies = [
        pltpu.make_async_copy(pool_any.at[pl.ds(low, 4)], pool_ref.at[pl.ds(low, 4)], pool_sems.at[low // 4])
        for low in range(0, groups, 4)
    ]
    for copy in pool_copies:
        copy.start()
    me = me_ref[0]
    for copy in smalls:
        copy.wait()
    request = assign_ref[me]
    length = length_ref[request]
    for residue in range(groups):
        residue_ref[owner_ref[request, residue]] = residue
    cosine, sine = rotation(table_ref, length)
    for head in range(KV_HEADS):
        low = at["new"] + head * new_count
        info_ref[low : low + new_count] = turn(block_ref[:, column(head)], cosine, sine).astype(jnp.float32)
        low += KV_HEADS * new_count
        info_ref[low : low + new_count] = block_ref[:, column(KV_HEADS + head)].astype(jnp.float32)

    def info_copy(part, low, high):
        part_rows = pl.ds(low, high - low)
        return pltpu.make_async_copy(info_ref.at[part_rows], info_any.at[part_rows], info_sems.at[part])

    info_copy(0, at["new"], rows).start()
    info_ref[at["cos"] : at["cos"] + new_count] = cosine
    info_ref[at["sin"] : at["sin"] + new_count] = sine
    per_row = HEAD_DIM // slots
    row = lax.broadcasted_iota(jnp.int32, (8, HEAD_DIM), 0)
    lane = lax.broadcasted_iota(jnp.int32, (8, HEAD_DIM), 1)
    piece, slot = row * per_row + lane // slots, lane % slots
    holder, requests, residues = jnp.zeros_like(lane), jnp.zeros_like(lane), jnp.zeros_like(lane)
    for p in range(groups):
        other = me ^ order[p]
        holder = jnp.where(piece == p, other, holder)
        requests = jnp.where(lane == p, assign_ref[other], requests)
        residues = jnp.where(lane == p, residue_ref[other], residues)
    bias = jnp.full((8, HEAD_DIM), MASKED, jnp.float32)
    for residue in range(groups):
        live = (holder == stripe_ref[request, residue]) & (slot * groups + residue < length)
        bias = jnp.where(live, 0.0, bias)
    info_ref[at["bias"] : at["bias"] + 8] = bias
    scalars = jnp.where(row == 0, requests, residues)
    info_ref[at["scalars"] : at["scalars"] + 8] = scalars.astype(jnp.float32)
    info_copy(1, 0, at["new"]).start()
    for copy in pool_copies:
        copy.wait()
    sends = []
    for p in range(AHEAD):
        pack_ref[p, :, 0:width] = pool_ref[assign_ref[me ^ order[p]]]
        for lanes in range(quarter):
            pack_ref[p, :, width + lanes * HEAD_DIM : width + (lanes + 1) * HEAD_DIM] = fresh_rows(
                info_ref, at["new"], residue_ref[me ^ order[p]], new_count, count, quarter, lanes
            ).astype(jnp.bfloat16)
        sends.append(pltpu.make_async_copy(pack_ref.at[p], send_refs[p], send_sems.at[p]))
        sends[-1].start()
    for copy in sends:
        copy.wait()
    info_copy(0, at["new"], rows).wait()
    info_copy(1, 0, at["new"]).wait()


def front(order, me, assignment, prefix_len, owner_map, stripe_map, block_kv, table, pool):
    groups, slots, width = pool.shape
    new_count = block_kv.shape[0]
    count = new_count // groups
    block = jax.ShapeDtypeStruct((slots, width + width * count // slots), jnp.bfloat16)
    info = jax.ShapeDtypeStruct((info_rows(new_count)[1], HEAD_DIM), jnp.float32)
    *blocks, info = pl.pallas_call(
        functools.partial(front_kernel, order),
        out_shape=[block] * AHEAD + [info],
        in_specs=[SMEM] + [ANY] * 7,
        out_specs=[ANY] * (AHEAD + 1),
        scratch_shapes=[
            pltpu.SMEM(assignment.shape, jnp.int32),
            pltpu.SMEM(prefix_len.shape, jnp.int32),
            pltpu.SMEM(owner_map.shape, jnp.int32),
            pltpu.SMEM(stripe_map.shape, jnp.int32),
            pltpu.SMEM(assignment.shape, jnp.int32),
            pltpu.VMEM(block_kv.shape, jnp.bfloat16),
            pltpu.VMEM(table.shape, jnp.float32),
            pltpu.VMEM(pool.shape, jnp.bfloat16),
            pltpu.VMEM((AHEAD,) + block.shape, jnp.bfloat16),
            pltpu.VMEM(info.shape, jnp.float32),
            pltpu.SemaphoreType.DMA((6,)),
            pltpu.SemaphoreType.DMA((groups // 4,)),
            pltpu.SemaphoreType.DMA((AHEAD,)),
            pltpu.SemaphoreType.DMA((2,)),
        ],
        compiler_params=params(60),
        name="front",
    )(me, assignment, prefix_len, owner_map, stripe_map, block_kv, table, pool)
    return blocks, info


def pack_kernel(info_ref, pool_ref, *refs):
    groups, slots, width = pool_ref.shape
    targets, (scalar_ref, scalar_sem) = refs[: groups - AHEAD], refs[groups - AHEAD :]
    new_count = slots * groups * (targets[0].shape[1] - width) // width
    at, _ = info_rows(new_count)
    count = new_count // groups
    quarter = (targets[0].shape[1] - width) // HEAD_DIM
    scalar_copy = pltpu.make_async_copy(info_ref.at[pl.ds(at["scalars"], 8)], scalar_ref, scalar_sem)
    scalar_copy.start()
    scalar_copy.wait()
    for p, target in enumerate(targets, AHEAD):
        target[:, 0:width] = pool_ref[scalar_ref[0, p].astype(jnp.int32)]
        residue = scalar_ref[1, p].astype(jnp.int32)
        for lanes in range(quarter):
            target[:, width + lanes * HEAD_DIM : width + (lanes + 1) * HEAD_DIM] = fresh_rows(
                info_ref, at["new"], residue, new_count, count, quarter, lanes
            ).astype(jnp.bfloat16)


def pack_others(info, pool, new_count):
    groups, slots, width = pool.shape
    block = (slots, width + width * (new_count // groups) // slots)
    return pl.pallas_call(
        pack_kernel,
        out_shape=[jax.ShapeDtypeStruct(block, jnp.bfloat16)] * (groups - AHEAD),
        in_specs=[VMEM] * 2,
        out_specs=[VMEM] * (groups - AHEAD),
        scratch_shapes=[pltpu.SMEM((8, HEAD_DIM), jnp.float32), pltpu.SemaphoreType.DMA],
        compiler_params=params(32),
        name="pack_others",
    )(info, pool)


def query_kernel(info_ref, q_ref, rot_ref, own_ref, bias_ref, request_ref):
    new_count = q_ref.shape[0]
    at, _ = info_rows(new_count)
    cosine = info_ref[at["cos"] : at["cos"] + new_count]
    sine = info_ref[at["sin"] : at["sin"] + new_count]
    for row in range(bias_ref.shape[1] // HEAD_DIM):
        line = info_ref[at["bias"] + row : at["bias"] + row + 1]
        bias_ref[:, column(row)] = jnp.broadcast_to(line, (8, HEAD_DIM))
    request_ref[...] = info_ref[at["scalars"] : at["scalars"] + 8].astype(jnp.int32)
    for head in range(2 * KV_HEADS):
        rows = at["new"] + head * new_count
        own_ref[head] = info_ref[rows : rows + new_count].astype(jnp.bfloat16)
    for head in range(Q_HEADS):
        rows = slice((head % PER_KV) * new_count, (head % PER_KV + 1) * new_count)
        rot_ref[head // PER_KV, rows, :] = turn(q_ref[:, column(head)], cosine, sine)


def rotate_queries(info, queries, span):
    new_count = queries.shape[0]
    return pl.pallas_call(
        query_kernel,
        out_shape=(
            jax.ShapeDtypeStruct((KV_HEADS, PER_KV * new_count, HEAD_DIM), jnp.bfloat16),
            jax.ShapeDtypeStruct((2 * KV_HEADS, new_count, HEAD_DIM), jnp.bfloat16),
            jax.ShapeDtypeStruct((8, span), jnp.float32),
            jax.ShapeDtypeStruct((8, HEAD_DIM), jnp.int32),
        ),
        in_specs=[VMEM] * 2,
        out_specs=[VMEM] * 4,
        compiler_params=params(32),
        name="rotate_queries",
    )(info, queries)


def quotient(summed, total):
    about = pl.reciprocal(total, approx=True)
    return summed * (about * (2.0 - total * about))


def join_keys(keys, values, got_refs, own_ref, head):
    key_parts = [got[:, column(head)] for got in got_refs]
    value_parts = [got[:, column(KV_HEADS + head)] for got in got_refs]
    if own_ref is not None:
        key_parts.append(own_ref[head])
        value_parts.append(own_ref[KV_HEADS + head])
    keys[head] = jnp.concatenate(key_parts, axis=0)
    value = jnp.concatenate(value_parts, axis=0)
    values[head] = jnp.concatenate([value, jnp.ones_like(value)], axis=1)


def dot_keys(query, keys):
    return lax.dot_general(query, keys, (((1,), (1,)), ((), ())), preferred_element_type=jnp.float32)


def staged(total, score, weigh, mix, finish, beside=None):
    scores, weights = {0: score(0)}, {}
    for at in range(total + 1):
        if at + 1 < total:
            scores[at + 1] = score(at + 1)
        if at >= 1:
            mixed = mix(at - 1, weights.pop(at - 1))
        if at < total:
            weights[at] = weigh(at, scores.pop(at))
        if at >= 1:
            finish(at - 1, mixed)
        if at == 1 and beside is not None:
            beside()


def unpacking(fresh_refs, first, request_vmem, decode_ref, rows_ref, request_ref, request_sem, decode_sems):
    count = rows_ref.shape[1]
    request_copy = pltpu.make_async_copy(request_vmem, request_ref, request_sem)
    request_copy.start()

    def decode_copy(p):
        return pltpu.make_async_copy(
            rows_ref.at[p], decode_ref.at[request_ref[0, first + p]], decode_sems.at[p]
        )

    def start():
        request_copy.wait()
        for p, fresh_ref in enumerate(fresh_refs):
            stack = fresh_ref[...]
            quarter = stack.shape[1]
            for part in range(stack.shape[0] // count):
                rows_ref[p, :, part * quarter : (part + 1) * quarter] = stack[part * count : (part + 1) * count]
            decode_copy(p).start()

    def wait():
        for p in range(len(fresh_refs)):
            decode_copy(p).wait()

    return start, wait


def spare_part(got):
    return got.at[:, pl.ds(WIDTH, got.shape[1] - WIDTH)]


def pieces_of(refs):
    pieces = []
    for ref in refs:
        pieces += [ref] if len(ref.shape) == 2 else [ref.at[i] for i in range(ref.shape[0])]
    return pieces


def attend_kernel(arrays, unpack, rot_ref, bias_ref, own_ref, *refs):
    got_refs, refs = pieces_of(refs[:arrays]), refs[arrays:]
    start, wait = None, None
    if unpack:
        request_vmem, result_ref, level_ref, decode_ref, *scratch = refs
        start, wait = unpacking([spare_part(got) for got in got_refs], 0, request_vmem, decode_ref, *scratch)
    else:
        result_ref, level_ref = refs
    new_count = rot_ref.shape[1] // PER_KV
    span = len(got_refs) * got_refs[0].shape[0]
    token = lax.broadcasted_iota(jnp.int32, (CHUNK, new_count), 0) % new_count
    causal = jnp.where(lax.broadcasted_iota(jnp.int32, (CHUNK, new_count), 1) <= token, 0.0, MASKED)
    bias = bias_ref[0:1, 0:span]
    per_head = PER_KV * new_count // CHUNK
    keys, values, highs = {}, {}, {}

    def place(at):
        return at // per_head, slice(at % per_head * CHUNK, (at % per_head + 1) * CHUNK)

    def score(at):
        head, rows = place(at)
        if at % per_head == 0:
            join_keys(keys, values, got_refs, own_ref, head)
        return dot_keys(rot_ref[head, rows, :], keys[head])

    def weigh(at, scores):
        scores = jnp.concatenate([scores[:, :span] * SCALE + bias, scores[:, span:] * SCALE + causal], axis=1)
        highs[at] = jnp.max(scores, axis=1, keepdims=True)
        return jnp.exp2(scores - highs[at]).astype(jnp.bfloat16)

    def mix(at, weights):
        return jnp.dot(weights, values[at // per_head], preferred_element_type=jnp.float32)

    def finish(at, mixed):
        head, rows = place(at)
        total = mixed[:, HEAD_DIM:]
        result_ref[head, rows, :] = quotient(mixed[:, :HEAD_DIM], total)
        level_ref[head, rows, :] = highs.pop(at) + jnp.log2(total)

    staged(KV_HEADS * per_head, score, weigh, mix, finish, start)
    if unpack:
        wait()


def attend(rot, bias, own, got, requests=None):
    rows, new_count = rot.shape[1], rot.shape[1] // PER_KV
    operands = [rot, bias, own, *got]
    shapes = [jax.ShapeDtypeStruct((KV_HEADS, rows, HEAD_DIM), jnp.float32)] * 2
    out_specs, scratch = [VMEM] * 2, []
    if requests is not None:
        operands.append(requests)
        slots, width = got[-1].shape
        count = (width - WIDTH) * slots // WIDTH
        shapes.append(jax.ShapeDtypeStruct((new_count // count, count, WIDTH), jnp.bfloat16))
        out_specs.append(ANY)
        scratch = unpack_scratch(len(pieces_of(got)), count, requests)
    return pl.pallas_call(
        functools.partial(attend_kernel, len(got), requests is not None),
        out_shape=tuple(shapes),
        in_specs=[VMEM] * len(operands),
        out_specs=tuple(out_specs),
        scratch_shapes=scratch,
        compiler_params=params(32),
        name="attend",
    )(*operands)


def unpack_scratch(pieces, count, requests):
    return [
        pltpu.VMEM((pieces, count, WIDTH), jnp.bfloat16),
        pltpu.SMEM(requests.shape, jnp.int32),
        pltpu.SemaphoreType.DMA,
        pltpu.SemaphoreType.DMA((pieces,)),
    ]


HEADROOM = 96.0


def late_kernel(pieces, first, rot_ref, bias_ref, result_ref, level_ref, *refs):
    got_refs, refs = refs[:pieces], refs[pieces:]
    request_vmem, _, out_ref, decode_ref, done_ref, out_sems, *scratch = refs
    start, wait = unpacking([spare_part(got) for got in got_refs], first, request_vmem, decode_ref, *scratch)
    slots = got_refs[0].shape[0]
    new_count = out_ref.shape[0]
    size = LATE_CHUNK
    heads_in = size // new_count
    bias = bias_ref[0:1, first * slots : (first + pieces) * slots]
    per_head = PER_KV * new_count // size
    chunks = KV_HEADS * per_head
    keys, values, excess = {}, {}, []

    def place(at):
        return at // per_head, slice(at % per_head * size, (at % per_head + 1) * size)

    def out_copy(at):
        width = heads_in * HEAD_DIM
        return pltpu.make_async_copy(
            done_ref.at[at], out_ref.at[:, pl.ds(pl.multiple_of(at * width, width), width)], out_sems.at[at]
        )

    def store(at, result):
        for row in range(heads_in):
            done_ref[at, :, column(row)] = result[row * new_count : (row + 1) * new_count].astype(jnp.bfloat16)
        out_copy(at).start()

    def score(at):
        head, rows = place(at)
        if at % per_head == 0:
            join_keys(keys, values, got_refs, None, head)
        return dot_keys(rot_ref[head, rows, :], keys[head])

    def weigh(at, scores):
        head, rows = place(at)
        powers = scores * SCALE + bias - level_ref[head, rows, :]
        excess.append(jnp.max(powers.reshape(size // 8, 8, HEAD_DIM), axis=0))
        return jnp.exp2(powers).astype(jnp.bfloat16)

    def mix(at, weights):
        return jnp.dot(weights, values[at // per_head], preferred_element_type=jnp.float32)

    def finish(at, mixed):
        head, rows = place(at)
        store(at, quotient(result_ref[head, rows, :] + mixed[:, :HEAD_DIM], 1.0 + mixed[:, HEAD_DIM:]))

    staged(chunks, score, weigh, mix, finish, start)
    most = jnp.max(functools.reduce(jnp.maximum, excess))
    wait()
    for at in range(chunks):
        out_copy(at).wait()

    @pl.when(most > HEADROOM)
    def _():
        for head in range(KV_HEADS):

            def again(chunk, carry, head=head):
                rows = pl.ds(pl.multiple_of(chunk * size, size), size)
                scores = dot_keys(rot_ref[head, rows, :], keys[head]) * SCALE + bias
                level = level_ref[head, rows, :]
                high = jnp.maximum(level, jnp.max(scores, axis=1, keepdims=True))
                factor = jnp.exp2(level - high)
                weights = jnp.exp2(scores - high).astype(jnp.bfloat16)
                mixed = jnp.dot(weights, values[head], preferred_element_type=jnp.float32)
                at = head * per_head + chunk
                summed = result_ref[head, rows, :] * factor + mixed[:, :HEAD_DIM]
                store(at, quotient(summed, factor + mixed[:, HEAD_DIM:]))
                out_copy(at).wait()
                return carry

            lax.fori_loop(0, per_head, again, 0)


def attend_late(rot, bias, result, level, got, first, requests, decode):
    rows, new_count = rot.shape[1], rot.shape[1] // PER_KV
    operands = [rot, bias, result, level, *got, requests, decode]
    chunks = KV_HEADS * rows // LATE_CHUNK
    return pl.pallas_call(
        functools.partial(late_kernel, len(got), first),
        out_shape=(
            jax.ShapeDtypeStruct((new_count, Q_HEADS * HEAD_DIM), jnp.bfloat16),
            jax.ShapeDtypeStruct(decode.shape, jnp.bfloat16),
        ),
        in_specs=[VMEM] * (len(operands) - 1) + [ANY],
        out_specs=(ANY, ANY),
        scratch_shapes=[
            pltpu.VMEM((chunks, new_count, LATE_CHUNK // new_count * HEAD_DIM), jnp.bfloat16),
            pltpu.SemaphoreType.DMA((chunks,)),
        ]
        + unpack_scratch(len(got), decode.shape[1], requests),
        input_output_aliases={len(operands) - 1: 1},
        compiler_params=params(32),
        name="attend_late",
    )(*operands)


def inverse(table):
    places = jnp.arange(table.shape[0], dtype=jnp.int32)
    return jnp.sum(jnp.where(table[None, :] == places[:, None], places, 0), axis=1)


def rotate(rows, positions, heads):
    half = HEAD_DIM // 2
    freqs = ROPE_BASE ** (-jnp.arange(half, dtype=jnp.float32) / half)
    angles = positions.astype(jnp.float32)[:, None] * freqs[None, :]
    cosine = jnp.concatenate([jnp.cos(angles)] * 2, axis=-1)[:, None, :]
    sine = jnp.concatenate([-jnp.sin(angles), jnp.sin(angles)], axis=-1)[:, None, :]
    split = rows.astype(jnp.float32).reshape(rows.shape[0], heads, HEAD_DIM)
    turned = jnp.roll(split, half, axis=-1)
    return (split * cosine + turned * sine).astype(jnp.bfloat16)


def small_pieces(me, assignment, prefix_len, stripe_map, owner_map, queries, block_kv, pool):
    groups, slots, width = pool.shape
    new_count = block_kv.shape[0]
    count = new_count // groups
    request = assignment[me[0]]
    length = prefix_len[request]
    positions = length + jnp.arange(new_count, dtype=jnp.int32)
    rot = rotate(queries, positions, Q_HEADS).reshape(new_count, KV_HEADS, PER_KV, HEAD_DIM)
    rot = jnp.transpose(rot, (1, 2, 0, 3)).reshape(KV_HEADS, PER_KV * new_count, HEAD_DIM)
    new_keys = rotate(block_kv[:, :KV_WIDTH], positions, KV_HEADS).reshape(new_count, KV_WIDTH)
    new_kv = jnp.concatenate([new_keys, block_kv[:, KV_WIDTH:]], axis=1)
    own = jnp.transpose(new_kv.reshape(new_count, 2 * KV_HEADS, HEAD_DIM), (1, 0, 2))
    spread = jnp.transpose(new_kv.reshape(count, groups, width), (1, 0, 2))
    send = jnp.concatenate([pool[assignment], spread[inverse(owner_map[request])]], axis=1)
    got = lax.all_to_all(send, "pg", split_axis=0, concat_axis=0, tiled=True)
    located = jnp.arange(slots, dtype=jnp.int32)[None, :] * groups + inverse(stripe_map[request])[:, None]
    bias = jnp.where(located < length, 0.0, MASKED).astype(jnp.float32).reshape(1, groups * slots)
    keys = got[:, :slots].reshape(groups * slots, width)
    result, _ = attend(rot, jnp.broadcast_to(bias, (8, groups * slots)), own, [keys])
    result = result.astype(jnp.bfloat16).reshape(KV_HEADS, PER_KV, new_count, HEAD_DIM)
    attended = jnp.transpose(result, (2, 0, 1, 3)).reshape(new_count, Q_HEADS * HEAD_DIM)
    return attended, got[inverse(assignment), slots:]


def shards(queries, block_kv, pool_kv, prefix_len, assignment, stripe_map, owner_map):
    queries, block_kv, pool = queries[0], block_kv[0], pool_kv[0]
    groups, slots, width = pool.shape
    new_count = queries.shape[0]
    count = new_count // groups
    me = lax.axis_index("pg").astype(jnp.int32).reshape(1)
    if groups != 16 or slots % 16 or HEAD_DIM % slots or count % 8 or slots % count:
        attended, decode_kv = small_pieces(
            me, assignment, prefix_len, stripe_map, owner_map, queries, block_kv, pool
        )
        return (attended[None], decode_kv[None])
    order = order_of(groups)
    table = rotation_tables(new_count)
    blocks, info = front(order, me, assignment, prefix_len, owner_map, stripe_map, block_kv, table, pool)
    blocks = list(blocks) + list(pack_others(info, pool, new_count))
    rot, own, bias, requests = rotate_queries(info, queries, groups * slots)
    rot, *blocks[AHEAD_OF_QUERIES:] = lax.optimization_barrier((rot, *blocks[AHEAD_OF_QUERIES:]))
    got = [
        lax.ppermute(block, "pg", [(source, source ^ t) for source in range(groups)]) if t else block
        for block, t in zip(blocks, order)
    ]
    soon = groups - LATE
    result, level, decode_kv = attend(rot, bias, own, got[:soon], requests)
    attended, decode_kv = attend_late(rot, bias, result, level, got[soon:], soon, requests, decode_kv)
    return (attended[None], decode_kv[None])


def solution(mesh):
    return jax.shard_map(
        shards,
        mesh=mesh,
        in_specs=(
            P(("rep", "pg"), None, None),
            P(("rep", "pg"), None, None),
            P(("rep", "pg"), None, None, None),
            P("rep"),
            P("rep"),
            P("rep", None),
            P("rep", None),
        ),
        out_specs=(P(("rep", "pg"), None, None), P(("rep", "pg"), None, None, None)),
        check_vma=False,
    )
```

```python
import functools
import math

import jax
import jax.numpy as jnp
import numpy as np
from jax import lax
from jax.experimental import pallas as pl
from jax.experimental.pallas import tpu as pltpu
from jax.sharding import PartitionSpec as P

Q_HEADS = 32
KV_HEADS = 4
HEAD_DIM = 128
PER_KV = Q_HEADS // KV_HEADS
KV_WIDTH = KV_HEADS * HEAD_DIM
WIDTH = 2 * KV_WIDTH

ROPE_BASE = 1000000.0
MASKED = -1e30
SCALE = HEAD_DIM ** -0.5 / math.log(2.0)
CHUNK = 256
LATE = 4
LATE_CHUNK = 1024
AHEAD = 4
AHEAD_OF_QUERIES = 8

SMEM = pl.BlockSpec(memory_space=pltpu.SMEM)
VMEM = pl.BlockSpec(memory_space=pltpu.VMEM)
ANY = pl.BlockSpec(memory_space=pl.ANY)


def params(mib):
    return pltpu.CompilerParams(vmem_limit_bytes=mib * 1024 * 1024)


def column(head):
    return slice(head * HEAD_DIM, (head + 1) * HEAD_DIM)


def order_of(groups):
    half = groups // 2
    near = list(range(half - 1, 0, -1))
    quarter, eighth = half // 2, half // 4
    far = [half + (at // 2 if at % 2 == 0 else quarter + (at // 2 ^ eighth)) for at in range(half)]
    order = [(far if kind == "f" else near).pop(0) for kind in "ffnfnfnfnfnfnfn"]
    order.insert(groups - LATE - 1, 0)
    return order


def rotation_tables(rows):
    half = HEAD_DIM // 2
    freqs = np.tile(ROPE_BASE ** (-np.arange(half, dtype=np.float64) / half), 2)
    angles = np.arange(rows, dtype=np.float64)[:, None] * freqs[None, :]
    parts = [np.cos(angles), np.sin(angles), np.tile(freqs, (8, 1))]
    return jnp.asarray(np.concatenate(parts, axis=0).astype(np.float32))


def rotation(table_ref, length):
    rows = (table_ref.shape[0] - 8) // 2
    start = length.astype(jnp.float32) * table_ref[2 * rows : 2 * rows + 8, :]
    cos_start, sin_start = jnp.cos(start)[0:1], jnp.sin(start)[0:1]
    cos_row, sin_row = table_ref[0:rows, :], table_ref[rows : 2 * rows, :]
    lane = lax.broadcasted_iota(jnp.int32, (1, HEAD_DIM), 1)
    sign = jnp.where(lane < HEAD_DIM // 2, -1.0, 1.0)
    cosine = cos_row * cos_start - sin_row * sin_start
    return cosine, sin_row * (cos_start * sign) + cos_row * (sin_start * sign)


def turn(x, cosine, sine):
    x = x.astype(jnp.float32)
    return (x * cosine + pltpu.roll(x, HEAD_DIM // 2, 1) * sine).astype(jnp.bfloat16)


def info_rows(new_count):
    sizes = [("cos", new_count), ("sin", new_count), ("bias", 8), ("scalars", 8), ("new", 2 * KV_HEADS * new_count)]
    at, rows = 0, {}
    for name, size in sizes:
        rows[name] = at
        at += size
    return rows, at


def fresh_rows(info_ref, base, residue, new_count, count, quarter, lanes):
    groups = new_count // count
    stack = [
        info_ref[pl.ds(base + (head + lanes) * new_count + residue, count, stride=groups), :]
        for head in range(0, 2 * KV_HEADS, quarter)
    ]
    return jnp.concatenate(stack, axis=0)


def front_kernel(
    order, me_ref, assign_any, length_any, owner_any, stripe_any, block_any, table_any, pool_any, *refs
):
    groups, slots, width = pool_any.shape
    send_refs, info_any, refs = refs[:AHEAD], refs[AHEAD], refs[AHEAD + 1 :]
    (assign_ref, length_ref, owner_ref, stripe_ref, residue_ref, block_ref, table_ref, pool_ref, pack_ref, info_ref,
     small_sems, pool_sems, send_sems, info_sems) = refs
    new_count = block_any.shape[0]
    count = new_count // groups
    quarter = width * count // slots // HEAD_DIM
    at, rows = info_rows(new_count)
    pairs = [
        (assign_any, assign_ref), (length_any, length_ref), (owner_any, owner_ref), (stripe_any, stripe_ref),
        (block_any, block_ref), (table_any, table_ref),
    ]
    smalls = [pltpu.make_async_copy(*pair, small_sems.at[i]) for i, pair in enumerate(pairs)]
    for copy in smalls:
        copy.start()
    pool_copies = [
        pltpu.make_async_copy(pool_any.at[pl.ds(low, 4)], pool_ref.at[pl.ds(low, 4)], pool_sems.at[low // 4])
        for low in range(0, groups, 4)
    ]
    for copy in pool_copies:
        copy.start()
    me = me_ref[0]
    for copy in smalls:
        copy.wait()
    request = assign_ref[me]
    length = length_ref[request]
    for residue in range(groups):
        residue_ref[owner_ref[request, residue]] = residue
    cosine, sine = rotation(table_ref, length)
    for head in range(KV_HEADS):
        low = at["new"] + head * new_count
        info_ref[low : low + new_count] = turn(block_ref[:, column(head)], cosine, sine).astype(jnp.float32)
        low += KV_HEADS * new_count
        info_ref[low : low + new_count] = block_ref[:, column(KV_HEADS + head)].astype(jnp.float32)

    def info_copy(part, low, high):
        part_rows = pl.ds(low, high - low)
        return pltpu.make_async_copy(info_ref.at[part_rows], info_any.at[part_rows], info_sems.at[part])

    info_copy(0, at["new"], rows).start()
    info_ref[at["cos"] : at["cos"] + new_count] = cosine
    info_ref[at["sin"] : at["sin"] + new_count] = sine
    per_row = HEAD_DIM // slots
    row = lax.broadcasted_iota(jnp.int32, (8, HEAD_DIM), 0)
    lane = lax.broadcasted_iota(jnp.int32, (8, HEAD_DIM), 1)
    piece, slot = row * per_row + lane // slots, lane % slots
    holder, requests, residues = jnp.zeros_like(lane), jnp.zeros_like(lane), jnp.zeros_like(lane)
    for p in range(groups):
        other = me ^ order[p]
        holder = jnp.where(piece == p, other, holder)
        requests = jnp.where(lane == p, assign_ref[other], requests)
        residues = jnp.where(lane == p, residue_ref[other], residues)
    bias = jnp.full((8, HEAD_DIM), MASKED, jnp.float32)
    for residue in range(groups):
        live = (holder == stripe_ref[request, residue]) & (slot * groups + residue < length)
        bias = jnp.where(live, 0.0, bias)
    info_ref[at["bias"] : at["bias"] + 8] = bias
    scalars = jnp.where(row == 0, requests, residues)
    info_ref[at["scalars"] : at["scalars"] + 8] = scalars.astype(jnp.float32)
    info_copy(1, 0, at["new"]).start()
    for copy in pool_copies:
        copy.wait()
    sends = []
    for p in range(AHEAD):
        pack_ref[p, :, 0:width] = pool_ref[assign_ref[me ^ order[p]]]
        for lanes in range(quarter):
            pack_ref[p, :, width + lanes * HEAD_DIM : width + (lanes + 1) * HEAD_DIM] = fresh_rows(
                info_ref, at["new"], residue_ref[me ^ order[p]], new_count, count, quarter, lanes
            ).astype(jnp.bfloat16)
        sends.append(pltpu.make_async_copy(pack_ref.at[p], send_refs[p], send_sems.at[p]))
        sends[-1].start()
    for copy in sends:
        copy.wait()
    info_copy(0, at["new"], rows).wait()
    info_copy(1, 0, at["new"]).wait()


def front(order, me, assignment, prefix_len, owner_map, stripe_map, block_kv, table, pool):
    groups, slots, width = pool.shape
    new_count = block_kv.shape[0]
    count = new_count // groups
    block = jax.ShapeDtypeStruct((slots, width + width * count // slots), jnp.bfloat16)
    info = jax.ShapeDtypeStruct((info_rows(new_count)[1], HEAD_DIM), jnp.float32)
    *blocks, info = pl.pallas_call(
        functools.partial(front_kernel, order),
        out_shape=[block] * AHEAD + [info],
        in_specs=[SMEM] + [ANY] * 7,
        out_specs=[ANY] * (AHEAD + 1),
        scratch_shapes=[
            pltpu.SMEM(assignment.shape, jnp.int32),
            pltpu.SMEM(prefix_len.shape, jnp.int32),
            pltpu.SMEM(owner_map.shape, jnp.int32),
            pltpu.SMEM(stripe_map.shape, jnp.int32),
            pltpu.SMEM(assignment.shape, jnp.int32),
            pltpu.VMEM(block_kv.shape, jnp.bfloat16),
            pltpu.VMEM(table.shape, jnp.float32),
            pltpu.VMEM(pool.shape, jnp.bfloat16),
            pltpu.VMEM((AHEAD,) + block.shape, jnp.bfloat16),
            pltpu.VMEM(info.shape, jnp.float32),
            pltpu.SemaphoreType.DMA((6,)),
            pltpu.SemaphoreType.DMA((groups // 4,)),
            pltpu.SemaphoreType.DMA((AHEAD,)),
            pltpu.SemaphoreType.DMA((2,)),
        ],
        compiler_params=params(60),
        name="front",
    )(me, assignment, prefix_len, owner_map, stripe_map, block_kv, table, pool)
    return blocks, info


def pack_kernel(info_ref, pool_ref, *refs):
    groups, slots, width = pool_ref.shape
    targets, (scalar_ref, scalar_sem) = refs[: groups - AHEAD], refs[groups - AHEAD :]
    new_count = slots * groups * (targets[0].shape[1] - width) // width
    at, _ = info_rows(new_count)
    count = new_count // groups
    quarter = (targets[0].shape[1] - width) // HEAD_DIM
    scalar_copy = pltpu.make_async_copy(info_ref.at[pl.ds(at["scalars"], 8)], scalar_ref, scalar_sem)
    scalar_copy.start()
    scalar_copy.wait()
    for p, target in enumerate(targets, AHEAD):
        target[:, 0:width] = pool_ref[scalar_ref[0, p].astype(jnp.int32)]
        residue = scalar_ref[1, p].astype(jnp.int32)
        for lanes in range(quarter):
            target[:, width + lanes * HEAD_DIM : width + (lanes + 1) * HEAD_DIM] = fresh_rows(
                info_ref, at["new"], residue, new_count, count, quarter, lanes
            ).astype(jnp.bfloat16)


def pack_others(info, pool, new_count):
    groups, slots, width = pool.shape
    block = (slots, width + width * (new_count // groups) // slots)
    return pl.pallas_call(
        pack_kernel,
        out_shape=[jax.ShapeDtypeStruct(block, jnp.bfloat16)] * (groups - AHEAD),
        in_specs=[VMEM] * 2,
        out_specs=[VMEM] * (groups - AHEAD),
        scratch_shapes=[pltpu.SMEM((8, HEAD_DIM), jnp.float32), pltpu.SemaphoreType.DMA],
        compiler_params=params(32),
        name="pack_others",
    )(info, pool)


def query_kernel(info_ref, q_ref, rot_ref, own_ref, bias_ref, request_ref):
    new_count = q_ref.shape[0]
    at, _ = info_rows(new_count)
    cosine = info_ref[at["cos"] : at["cos"] + new_count]
    sine = info_ref[at["sin"] : at["sin"] + new_count]
    for row in range(bias_ref.shape[1] // HEAD_DIM):
        line = info_ref[at["bias"] + row : at["bias"] + row + 1]
        bias_ref[:, column(row)] = jnp.broadcast_to(line, (8, HEAD_DIM))
    request_ref[...] = info_ref[at["scalars"] : at["scalars"] + 8].astype(jnp.int32)
    for head in range(2 * KV_HEADS):
        rows = at["new"] + head * new_count
        own_ref[head] = info_ref[rows : rows + new_count].astype(jnp.bfloat16)
    for head in range(Q_HEADS):
        rows = slice((head % PER_KV) * new_count, (head % PER_KV + 1) * new_count)
        rot_ref[head // PER_KV, rows, :] = turn(q_ref[:, column(head)], cosine, sine)


def rotate_queries(info, queries, span):
    new_count = queries.shape[0]
    return pl.pallas_call(
        query_kernel,
        out_shape=(
            jax.ShapeDtypeStruct((KV_HEADS, PER_KV * new_count, HEAD_DIM), jnp.bfloat16),
            jax.ShapeDtypeStruct((2 * KV_HEADS, new_count, HEAD_DIM), jnp.bfloat16),
            jax.ShapeDtypeStruct((8, span), jnp.float32),
            jax.ShapeDtypeStruct((8, HEAD_DIM), jnp.int32),
        ),
        in_specs=[VMEM] * 2,
        out_specs=[VMEM] * 4,
        compiler_params=params(32),
        name="rotate_queries",
    )(info, queries)


def quotient(summed, total):
    about = pl.reciprocal(total, approx=True)
    return summed * (about * (2.0 - total * about))


def join_keys(keys, values, got_refs, own_ref, head):
    key_parts = [got[:, column(head)] for got in got_refs]
    value_parts = [got[:, column(KV_HEADS + head)] for got in got_refs]
    if own_ref is not None:
        key_parts.append(own_ref[head])
        value_parts.append(own_ref[KV_HEADS + head])
    keys[head] = jnp.concatenate(key_parts, axis=0)
    value = jnp.concatenate(value_parts, axis=0)
    values[head] = jnp.concatenate([value, jnp.ones_like(value)], axis=1)


def dot_keys(query, keys):
    return lax.dot_general(query, keys, (((1,), (1,)), ((), ())), preferred_element_type=jnp.float32)


def staged(total, score, weigh, mix, finish, beside=None):
    scores, weights = {0: score(0)}, {}
    for at in range(total + 1):
        if at + 1 < total:
            scores[at + 1] = score(at + 1)
        if at >= 1:
            mixed = mix(at - 1, weights.pop(at - 1))
        if at < total:
            weights[at] = weigh(at, scores.pop(at))
        if at >= 1:
            finish(at - 1, mixed)
        if at == 1 and beside is not None:
            beside()


def unpacking(fresh_refs, first, request_vmem, decode_ref, rows_ref, request_ref, request_sem, decode_sems):
    count = rows_ref.shape[1]
    request_copy = pltpu.make_async_copy(request_vmem, request_ref, request_sem)
    request_copy.start()

    def decode_copy(p):
        return pltpu.make_async_copy(
            rows_ref.at[p], decode_ref.at[request_ref[0, first + p]], decode_sems.at[p]
        )

    def start():
        request_copy.wait()
        for p, fresh_ref in enumerate(fresh_refs):
            stack = fresh_ref[...]
            quarter = stack.shape[1]
            for part in range(stack.shape[0] // count):
                rows_ref[p, :, part * quarter : (part + 1) * quarter] = stack[part * count : (part + 1) * count]
            decode_copy(p).start()

    def wait():
        for p in range(len(fresh_refs)):
            decode_copy(p).wait()

    return start, wait


def spare_part(got):
    return got.at[:, pl.ds(WIDTH, got.shape[1] - WIDTH)]


def pieces_of(refs):
    pieces = []
    for ref in refs:
        pieces += [ref] if len(ref.shape) == 2 else [ref.at[i] for i in range(ref.shape[0])]
    return pieces


def attend_kernel(arrays, unpack, rot_ref, bias_ref, own_ref, *refs):
    got_refs, refs = pieces_of(refs[:arrays]), refs[arrays:]
    start, wait = None, None
    if unpack:
        request_vmem, result_ref, level_ref, decode_ref, *scratch = refs
        start, wait = unpacking([spare_part(got) for got in got_refs], 0, request_vmem, decode_ref, *scratch)
    else:
        result_ref, level_ref = refs
    new_count = rot_ref.shape[1] // PER_KV
    span = len(got_refs) * got_refs[0].shape[0]
    token = lax.broadcasted_iota(jnp.int32, (CHUNK, new_count), 0) % new_count
    causal = jnp.where(lax.broadcasted_iota(jnp.int32, (CHUNK, new_count), 1) <= token, 0.0, MASKED)
    bias = bias_ref[0:1, 0:span]
    per_head = PER_KV * new_count // CHUNK
    keys, values, highs = {}, {}, {}

    def place(at):
        return at // per_head, slice(at % per_head * CHUNK, (at % per_head + 1) * CHUNK)

    def score(at):
        head, rows = place(at)
        if at % per_head == 0:
            join_keys(keys, values, got_refs, own_ref, head)
        return dot_keys(rot_ref[head, rows, :], keys[head])

    def weigh(at, scores):
        scores = jnp.concatenate([scores[:, :span] * SCALE + bias, scores[:, span:] * SCALE + causal], axis=1)
        highs[at] = jnp.max(scores, axis=1, keepdims=True)
        return jnp.exp2(scores - highs[at]).astype(jnp.bfloat16)

    def mix(at, weights):
        return jnp.dot(weights, values[at // per_head], preferred_element_type=jnp.float32)

    def finish(at, mixed):
        head, rows = place(at)
        total = mixed[:, HEAD_DIM:]
        result_ref[head, rows, :] = quotient(mixed[:, :HEAD_DIM], total)
        level_ref[head, rows, :] = highs.pop(at) + jnp.log2(total)

    staged(KV_HEADS * per_head, score, weigh, mix, finish, start)
    if unpack:
        wait()


def attend(rot, bias, own, got, requests=None):
    rows, new_count = rot.shape[1], rot.shape[1] // PER_KV
    operands = [rot, bias, own, *got]
    shapes = [jax.ShapeDtypeStruct((KV_HEADS, rows, HEAD_DIM), jnp.float32)] * 2
    out_specs, scratch = [VMEM] * 2, []
    if requests is not None:
        operands.append(requests)
        slots, width = got[-1].shape
        count = (width - WIDTH) * slots // WIDTH
        shapes.append(jax.ShapeDtypeStruct((new_count // count, count, WIDTH), jnp.bfloat16))
        out_specs.append(ANY)
        scratch = unpack_scratch(len(pieces_of(got)), count, requests)
    return pl.pallas_call(
        functools.partial(attend_kernel, len(got), requests is not None),
        out_shape=tuple(shapes),
        in_specs=[VMEM] * len(operands),
        out_specs=tuple(out_specs),
        scratch_shapes=scratch,
        compiler_params=params(32),
        name="attend",
    )(*operands)


def unpack_scratch(pieces, count, requests):
    return [
        pltpu.VMEM((pieces, count, WIDTH), jnp.bfloat16),
        pltpu.SMEM(requests.shape, jnp.int32),
        pltpu.SemaphoreType.DMA,
        pltpu.SemaphoreType.DMA((pieces,)),
    ]


HEADROOM = 96.0


def late_kernel(pieces, first, rot_ref, bias_ref, result_ref, level_ref, *refs):
    got_refs, refs = refs[:pieces], refs[pieces:]
    request_vmem, _, out_ref, decode_ref, done_ref, out_sems, *scratch = refs
    start, wait = unpacking([spare_part(got) for got in got_refs], first, request_vmem, decode_ref, *scratch)
    slots = got_refs[0].shape[0]
    new_count = out_ref.shape[0]
    size = LATE_CHUNK
    heads_in = size // new_count
    bias = bias_ref[0:1, first * slots : (first + pieces) * slots]
    per_head = PER_KV * new_count // size
    chunks = KV_HEADS * per_head
    keys, values, excess = {}, {}, []

    def place(at):
        return at // per_head, slice(at % per_head * size, (at % per_head + 1) * size)

    def out_copy(at):
        width = heads_in * HEAD_DIM
        return pltpu.make_async_copy(
            done_ref.at[at], out_ref.at[:, pl.ds(pl.multiple_of(at * width, width), width)], out_sems.at[at]
        )

    def store(at, result):
        for row in range(heads_in):
            done_ref[at, :, column(row)] = result[row * new_count : (row + 1) * new_count].astype(jnp.bfloat16)
        out_copy(at).start()

    def score(at):
        head, rows = place(at)
        if at % per_head == 0:
            join_keys(keys, values, got_refs, None, head)
        return dot_keys(rot_ref[head, rows, :], keys[head])

    def weigh(at, scores):
        head, rows = place(at)
        powers = scores * SCALE + bias - level_ref[head, rows, :]
        excess.append(jnp.max(powers.reshape(size // 8, 8, HEAD_DIM), axis=0))
        return jnp.exp2(powers).astype(jnp.bfloat16)

    def mix(at, weights):
        return jnp.dot(weights, values[at // per_head], preferred_element_type=jnp.float32)

    def finish(at, mixed):
        head, rows = place(at)
        store(at, quotient(result_ref[head, rows, :] + mixed[:, :HEAD_DIM], 1.0 + mixed[:, HEAD_DIM:]))

    staged(chunks, score, weigh, mix, finish, start)
    most = jnp.max(functools.reduce(jnp.maximum, excess))
    wait()
    for at in range(chunks):
        out_copy(at).wait()

    @pl.when(most > HEADROOM)
    def _():
        for head in range(KV_HEADS):

            def again(chunk, carry, head=head):
                rows = pl.ds(pl.multiple_of(chunk * size, size), size)
                scores = dot_keys(rot_ref[head, rows, :], keys[head]) * SCALE + bias
                level = level_ref[head, rows, :]
                high = jnp.maximum(level, jnp.max(scores, axis=1, keepdims=True))
                factor = jnp.exp2(level - high)
                weights = jnp.exp2(scores - high).astype(jnp.bfloat16)
                mixed = jnp.dot(weights, values[head], preferred_element_type=jnp.float32)
                at = head * per_head + chunk
                summed = result_ref[head, rows, :] * factor + mixed[:, :HEAD_DIM]
                store(at, quotient(summed, factor + mixed[:, HEAD_DIM:]))
                out_copy(at).wait()
                return carry

            lax.fori_loop(0, per_head, again, 0)


def attend_late(rot, bias, result, level, got, first, requests, decode):
    rows, new_count = rot.shape[1], rot.shape[1] // PER_KV
    operands = [rot, bias, result, level, *got, requests, decode]
    chunks = KV_HEADS * rows // LATE_CHUNK
    return pl.pallas_call(
        functools.partial(late_kernel, len(got), first),
        out_shape=(
            jax.ShapeDtypeStruct((new_count, Q_HEADS * HEAD_DIM), jnp.bfloat16),
            jax.ShapeDtypeStruct(decode.shape, jnp.bfloat16),
        ),
        in_specs=[VMEM] * (len(operands) - 1) + [ANY],
        out_specs=(ANY, ANY),
        scratch_shapes=[
            pltpu.VMEM((chunks, new_count, LATE_CHUNK // new_count * HEAD_DIM), jnp.bfloat16),
            pltpu.SemaphoreType.DMA((chunks,)),
        ]
        + unpack_scratch(len(got), decode.shape[1], requests),
        input_output_aliases={len(operands) - 1: 1},
        compiler_params=params(32),
        name="attend_late",
    )(*operands)


def inverse(table):
    places = jnp.arange(table.shape[0], dtype=jnp.int32)
    return jnp.sum(jnp.where(table[None, :] == places[:, None], places, 0), axis=1)


def rotate(rows, positions, heads):
    half = HEAD_DIM // 2
    freqs = ROPE_BASE ** (-jnp.arange(half, dtype=jnp.float32) / half)
    angles = positions.astype(jnp.float32)[:, None] * freqs[None, :]
    cosine = jnp.concatenate([jnp.cos(angles)] * 2, axis=-1)[:, None, :]
    sine = jnp.concatenate([-jnp.sin(angles), jnp.sin(angles)], axis=-1)[:, None, :]
    split = rows.astype(jnp.float32).reshape(rows.shape[0], heads, HEAD_DIM)
    turned = jnp.roll(split, half, axis=-1)
    return (split * cosine + turned * sine).astype(jnp.bfloat16)


def small_pieces(me, assignment, prefix_len, stripe_map, owner_map, queries, block_kv, pool):
    groups, slots, width = pool.shape
    new_count = block_kv.shape[0]
    count = new_count // groups
    request = assignment[me[0]]
    length = prefix_len[request]
    positions = length + jnp.arange(new_count, dtype=jnp.int32)
    rot = rotate(queries, positions, Q_HEADS).reshape(new_count, KV_HEADS, PER_KV, HEAD_DIM)
    rot = jnp.transpose(rot, (1, 2, 0, 3)).reshape(KV_HEADS, PER_KV * new_count, HEAD_DIM)
    new_keys = rotate(block_kv[:, :KV_WIDTH], positions, KV_HEADS).reshape(new_count, KV_WIDTH)
    new_kv = jnp.concatenate([new_keys, block_kv[:, KV_WIDTH:]], axis=1)
    own = jnp.transpose(new_kv.reshape(new_count, 2 * KV_HEADS, HEAD_DIM), (1, 0, 2))
    spread = jnp.transpose(new_kv.reshape(count, groups, width), (1, 0, 2))
    send = jnp.concatenate([pool[assignment], spread[inverse(owner_map[request])]], axis=1)
    got = lax.all_to_all(send, "pg", split_axis=0, concat_axis=0, tiled=True)
    located = jnp.arange(slots, dtype=jnp.int32)[None, :] * groups + inverse(stripe_map[request])[:, None]
    bias = jnp.where(located < length, 0.0, MASKED).astype(jnp.float32).reshape(1, groups * slots)
    keys = got[:, :slots].reshape(groups * slots, width)
    result, _ = attend(rot, jnp.broadcast_to(bias, (8, groups * slots)), own, [keys])
    result = result.astype(jnp.bfloat16).reshape(KV_HEADS, PER_KV, new_count, HEAD_DIM)
    attended = jnp.transpose(result, (2, 0, 1, 3)).reshape(new_count, Q_HEADS * HEAD_DIM)
    return attended, got[inverse(assignment), slots:]


def shards(queries, block_kv, pool_kv, prefix_len, assignment, stripe_map, owner_map):
    queries, block_kv, pool = queries[0], block_kv[0], pool_kv[0]
    groups, slots, width = pool.shape
    new_count = queries.shape[0]
    count = new_count // groups
    me = lax.axis_index("pg").astype(jnp.int32).reshape(1)
    if groups != 16 or slots % 16 or HEAD_DIM % slots or count % 8 or slots % count:
        attended, decode_kv = small_pieces(
            me, assignment, prefix_len, stripe_map, owner_map, queries, block_kv, pool
        )
        return (attended[None], decode_kv[None])
    order = order_of(groups)
    table = rotation_tables(new_count)
    blocks, info = front(order, me, assignment, prefix_len, owner_map, stripe_map, block_kv, table, pool)
    blocks = list(blocks) + list(pack_others(info, pool, new_count))
    rot, own, bias, requests = rotate_queries(info, queries, groups * slots)
    rot, *blocks[AHEAD_OF_QUERIES:] = lax.optimization_barrier((rot, *blocks[AHEAD_OF_QUERIES:]))
    got = [
        lax.ppermute(block, "pg", [(source, source ^ t) for source in range(groups)]) if t else block
        for block, t in zip(blocks, order)
    ]
    soon = groups - LATE
    result, level, decode_kv = attend(rot, bias, own, got[:soon], requests)
    attended, decode_kv = attend_late(rot, bias, result, level, got[soon:], soon, requests, decode_kv)
    return (attended[None], decode_kv[None])


def solution(mesh):
    return jax.shard_map(
        shards,
        mesh=mesh,
        in_specs=(
            P(("rep", "pg"), None, None),
            P(("rep", "pg"), None, None),
            P(("rep", "pg"), None, None, None),
            P("rep"),
            P("rep"),
            P("rep", None),
            P("rep", None),
        ),
        out_specs=(P(("rep", "pg"), None, None), P(("rep", "pg"), None, None, None)),
        check_vma=False,
    )
```
